32 devices in a mesh: dp: 4 (over y, core), space: 8 (over z, x).
Axes of the slice: x: 2, y: 2, z: 4, core: 2. Of those that a mesh axis runs over, the one named last changes fastest.
Arguments:
- features: bfloat16 [4, 8, 48, 512], P('dp', 'space'), may hold values from -6 to 6
- device_block: int32 [4, 8], P('dp'), may hold values from 0 to 15, as said below
- conv_first: bfloat16 [48, 27, 48], replicated, may hold values from -0.15625 to 0.15625
- conv_second: bfloat16 [48, 27, 48], replicated, may hold values from -0.15625 to 0.15625
- head_weight: bfloat16 [3, 48], replicated, may hold values from -0.875 to 0.875
- targets: int32 [4, 8, 3, 512], P('dp', 'space'), may hold values 0 or 1
Outputs:
- affinity_logits: float32 [4, 8, 3, 512], P('dp', 'space')
- grad_first: float32 [48, 27, 48], replicated
- grad_second: float32 [48, 27, 48], replicated
- grad_head: float32 [3, 48], replicated
The draws below stay inside these ranges and needn't reach their ends.
Inputs may be any that keep to these rules, and one draw needn't show every extreme that they name: `device_block`: row n lists 8 distinct block ids of crop n, one for each device; id = (4 * bx + by) + bz. Blocks that no device lists hold no tissue.
All inputs are finite; a program needn't handle non-finite values. No bound on the sum of `targets` on one device may be relied on, other than what follows from the above.
Results may differ from the reference program's by a relative error of at most 0.0041.
Values may be sent and summed in bfloat16 or wider, within the bound.
No kernel may reach another device: no remote copies, remote signals or barrier semaphores. Data moves between devices by JAX's collectives and lax.ppermute only.
A program may use at most 64 MiB of HBM per device.

```python
import jax
import jax.numpy as jnp
from jax import lax

C = 48
TAPS = 27
BS = 8
VOX = 512
GX = 4
GY = 4
GZ = 1
N_DP = 4
N_SPACE = 8


def draw_device_block(key, part):
    block_total = GX * GY * GZ
    crop_keys = jax.random.split(key, N_DP)

    def one_crop(crop_key):
        first_key, second_key = jax.random.split(crop_key)
        middle = jax.random.permutation(first_key, block_total - 2)[:N_SPACE - 2] + 1
        chosen = jnp.concatenate([jnp.array([0, block_total - 1], jnp.int32), middle.astype(jnp.int32)])
        return jax.random.permutation(second_key, chosen)
    return jax.vmap(one_crop)(crop_keys).astype(jnp.int32)


def touch_ends(drawn, rng, smallest, top_value):
    longest = drawn.shape.index(max(drawn.shape))
    spots = []
    for shift in (0, 1):
        where = [jax.random.randint(jax.random.fold_in(rng, axis), (), 0, length) for axis, length in enumerate(drawn.shape)]
        where[longest] = (where[longest] + shift) % drawn.shape[longest]
        spots.append(tuple(where))
    return drawn.at[spots[0]].set(smallest).at[spots[1]].set(top_value)


def levels(own_key, dims, cuts, least, top_value):
    loudness, own = 1.0, jax.random.fold_in(own_key, 6)
    for position, shards_of in cuts:
        heights = jnp.exp(jax.random.uniform(jax.random.fold_in(own, position), (shards_of,), jnp.float32, least / len(cuts), top_value / len(cuts)))
        loudness = loudness * jnp.repeat(heights, dims[position] // shards_of).reshape([-1 if axis == position else 1 for axis in range(len(dims))])
    return loudness


def centred(rng, dims, width, limit, cuts=(), held_as=jnp.bfloat16):
    entries = jax.random.normal(rng, dims, jnp.float32) * width
    if len(cuts) > 0:
        entries = levels(rng, dims, cuts, -0.22, 0.18) * entries
    return jnp.clip(entries, min=-limit, max=limit).astype(held_as)


def setup_inputs(seed: int = 0) -> dict:
    streams_of = jax.random.split(jax.random.key(seed), 7)
    return {
        "features": centred(streams_of[0], (N_DP, N_SPACE, C, VOX), 1.0, 6.0, ((0, 4), (1, 8))),
        "device_block": draw_device_block(jax.random.fold_in(streams_of[6], 71), 0),
        "conv_first": centred(streams_of[2], (C, TAPS, C), (27 * C) ** -0.5, 0.15625),
        "conv_second": centred(streams_of[3], (C, TAPS, C), (27 * C) ** -0.5, 0.15625),
        "head_weight": centred(streams_of[4], (3, C), C ** -0.5, 0.875),
        "targets": touch_ends((jax.random.randint(streams_of[5], (N_DP, N_SPACE, 3, VOX), 0, 2) < 1).astype(jnp.int32), jax.random.fold_in(streams_of[5], 1), 0, 1),
    }


def conv_volume(volume, weight, dilation):
    kernel = weight.reshape(C, 3, 3, 3, C).transpose(0, 4, 1, 2, 3)
    return lax.conv_general_dilated(volume[None], kernel, (1, 1, 1), [(dilation, dilation)] * 3, rhs_dilation=(dilation, dilation, dilation), dimension_numbers=('NCDHW', 'OIDHW', 'NCDHW'), precision=lax.Precision.HIGHEST)[0]

def elu_pair(values):
    negative = jnp.exp(jnp.minimum(values, 0.0))
    return (jnp.where(values > 0, values, negative - 1.0), jnp.where(values > 0, 1.0, negative))

def rounded(values):
    return lax.optimization_barrier(values.astype(jnp.bfloat16)).astype(jnp.float32)

def place_blocks(rows, block_ids, channels):
    grid = jnp.zeros((GX * GY * GZ, channels, BS, BS, BS), rows.dtype)
    grid = grid.at[block_ids].set(rows.reshape(N_SPACE, channels, BS, BS, BS))
    grid = grid.reshape(GX, GY, GZ, channels, BS, BS, BS).transpose(3, 0, 4, 1, 5, 2, 6)
    return grid.reshape(channels, GX * BS, GY * BS, GZ * BS)

def take_blocks(volume, block_ids, channels):
    grid = volume.reshape(channels, GX, BS, GY, BS, GZ, BS).transpose(1, 3, 5, 0, 2, 4, 6)
    return grid.reshape(GX * GY * GZ, channels, VOX)[block_ids]

def reference(features, device_block, conv_first, conv_second, head_weight, targets):
    first_w = conv_first.astype(jnp.float32)
    second_w = conv_second.astype(jnp.float32)
    head_w = head_weight.astype(jnp.float32)
    scale = 1.0 / jnp.sqrt(jnp.float32(N_DP * N_SPACE * 3 * VOX))

    def one_crop(crop_inputs):
        crop_features, block_ids, crop_targets = crop_inputs
        mask = place_blocks(jnp.ones((N_SPACE, 1, VOX), jnp.float32), block_ids, 1)
        volume = place_blocks(crop_features.astype(jnp.float32), block_ids, C)
        pre_first, pull_first = jax.vjp(lambda weight: conv_volume(volume, weight, 1), first_w)
        act_first, slope_first = elu_pair(pre_first)
        hid_first = rounded(act_first * mask)
        pre_second, pull_second = jax.vjp(lambda field, weight: conv_volume(field, weight, 2), hid_first, second_w)
        act_second, slope_second = elu_pair(pre_second)
        hid_second = rounded(act_second * mask)
        logits = jnp.einsum('jc,cxyz->jxyz', head_w, hid_second, precision=lax.Precision.HIGHEST)
        target_vol = place_blocks(crop_targets.astype(jnp.float32), block_ids, 3)
        grad_logit = rounded((jax.nn.sigmoid(logits) - target_vol) * mask * scale)
        grad_head = jnp.einsum('jxyz,cxyz->jc', grad_logit, hid_second, precision=lax.Precision.HIGHEST)
        back_second = jnp.einsum('jc,jxyz->cxyz', head_w, grad_logit, precision=lax.Precision.HIGHEST)
        grad_pre_second = rounded(back_second * slope_second * mask)
        back_first, grad_second = pull_second(grad_pre_second)
        grad_pre_first = rounded(back_first * slope_first * mask)
        grad_first = pull_first(grad_pre_first)[0]
        return (take_blocks(logits, block_ids, 3), grad_first, grad_second, grad_head)
    logit_rows, grad_first, grad_second, grad_head = lax.map(one_crop, (features, device_block, targets))
    return (logit_rows, lax.optimization_barrier(jnp.sum(grad_first, axis=0)), lax.optimization_barrier(jnp.sum(grad_second, axis=0)), lax.optimization_barrier(jnp.sum(grad_head, axis=0)))
```

```python
import functools

import jax
import jax.numpy as jnp
from jax import lax
from jax.experimental import pallas as pl
from jax.experimental.pallas import tpu as pltpu
from jax.sharding import PartitionSpec as P

BS = 8


tap_offsets = [
    (tap_index // 9 - 1, tap_index // 3 % 3 - 1, tap_index % 3 - 1) for tap_index in range(27)
]


def elu_pair(values):
    negative = jnp.exp(jnp.minimum(values, 0.0))
    return (jnp.where(values > 0, values, negative - 1.0), jnp.where(values > 0, 1.0, negative))


def neighbor_tables(device_block):
    space_count = lax.axis_size("space")
    depth_z = space_count // 8
    self_index = lax.axis_index("space")
    blocks = device_block[0]
    coords = jnp.stack([blocks // (4 * depth_z), blocks // depth_z % 4, blocks % depth_z])
    own_coords = lax.dynamic_index_in_dim(coords, self_index, 1, keepdims=False)
    offsets = jnp.array(tap_offsets, jnp.int32)
    limits = jnp.array([4, 4, depth_z], jnp.int32)
    wanted = own_coords[None, :] + offsets
    inside = jnp.all((wanted >= 0) & (wanted < limits[None, :]), axis=1) & (jnp.arange(27) != 13)
    wanted_id = (wanted[:, 0] * 4 + wanted[:, 1]) * depth_z + wanted[:, 2]
    matches = (blocks[None, :] == wanted_id[:, None]) & inside[:, None]
    devices = jnp.arange(space_count, dtype=jnp.int32)
    owner_row = jnp.sum(jnp.where(matches, devices[None, :], 0), axis=1)
    present = jnp.any(matches, axis=1)
    relative = coords - own_coords[:, None]
    adjacent = jnp.all(jnp.abs(relative) <= 1, axis=0) & (devices != self_index)
    send_tap = jnp.where(
        adjacent, (relative[0] + 1) * 9 + (relative[1] + 1) * 3 + relative[2] + 1, 13
    )
    return (owner_row, present, send_tap)


def region_slice(block_data, offset, depth_cells):
    span_list = []
    for step_value in offset:
        if step_value == 1:
            span_list.append(slice(BS - depth_cells, BS))
        elif step_value == -1:
            span_list.append(slice(0, depth_cells))
        else:
            span_list.append(slice(0, BS))
    return block_data[:, span_list[0], span_list[1], span_list[2]]


def surround(block_data, depth_cells, tables):
    owner_row, present, send_tap = tables
    channels = block_data.shape[0]
    length = depth_cells * BS * BS
    pieces = []
    for tap_index in range(27):
        if tap_index == 13:
            pieces.append(jnp.zeros((channels, length), block_data.dtype))
        else:
            region = region_slice(block_data, tap_offsets[tap_index], depth_cells).reshape(
                channels, -1
            )
            pieces.append(jnp.pad(region, ((0, 0), (0, length - region.shape[1]))))
    outgoing = jnp.stack(pieces)
    sending = outgoing[send_tap]
    by_source = lax.all_to_all(sending, "space", split_axis=0, concat_axis=0, tiled=True)
    incoming = jnp.where(
        present[:, None, None], by_source[owner_row], jnp.zeros((), block_data.dtype)
    )
    rows_x = []
    for step_x in range(3):
        rows_y = []
        for step_y in range(3):
            rows_z = []
            for step_z in range(3):
                tap_index = step_x * 9 + step_y * 3 + step_z
                if tap_index == 13:
                    rows_z.append(block_data)
                else:
                    extent_list = [
                        BS if step_value == 1 else depth_cells
                        for step_value in (step_x, step_y, step_z)
                    ]
                    count_cells = extent_list[0] * extent_list[1] * extent_list[2]
                    rows_z.append(
                        incoming[tap_index][:, :count_cells].reshape(
                            channels, extent_list[0], extent_list[1], extent_list[2]
                        )
                    )
            rows_y.append(jnp.concatenate(rows_z, axis=3))
        rows_x.append(jnp.concatenate(rows_y, axis=2))
    return jnp.concatenate(rows_x, axis=1)


def conv_padded(padded, kernel, dilation):
    result = lax.conv_general_dilated(
        padded[None],
        kernel,
        (1, 1, 1),
        "VALID",
        rhs_dilation=(dilation, dilation, dilation),
        dimension_numbers=("NCDHW", "OIDHW", "NCDHW"),
        preferred_element_type=jnp.float32,
    )
    return result[0].reshape(kernel.shape[0], BS * BS * BS)


def kernel_grad(padded, grad_rows, dilation):
    channels = padded.shape[0]
    outputs = grad_rows.shape[0]
    grad_block = grad_rows.reshape(outputs, 1, BS, BS, BS)
    result = lax.conv_general_dilated(
        padded[None],
        grad_block,
        (dilation, dilation, dilation),
        "VALID",
        dimension_numbers=("CNDHW", "OIDHW", "NCDHW"),
        preferred_element_type=jnp.float32,
    )
    return result.reshape(channels, outputs, 27).transpose(1, 2, 0)


def on_device_deep(features, device_block, conv_first, conv_second, head_weight, targets):
    channels = features.shape[2]
    tables = neighbor_tables(device_block)
    kernel_first = conv_first.reshape(channels, 3, 3, 3, channels).transpose(0, 4, 1, 2, 3)
    kernel_second = conv_second.reshape(channels, 3, 3, 3, channels).transpose(0, 4, 1, 2, 3)
    block_in = features[0, 0].reshape(channels, BS, BS, BS)
    padded_in = surround(block_in, 1, tables)
    pre_first = conv_padded(padded_in, kernel_first, 1)
    act_first, slope_first = elu_pair(pre_first)
    hid_first = act_first.astype(jnp.bfloat16)
    padded_first = surround(hid_first.reshape(channels, BS, BS, BS), 2, tables)
    pre_second = conv_padded(padded_first, kernel_second, 2)
    act_second, slope_second = elu_pair(pre_second)
    hid_second = act_second.astype(jnp.bfloat16)
    logits = jnp.dot(head_weight, hid_second, preferred_element_type=jnp.float32)
    scale = (lax.axis_size("dp") * lax.axis_size("space") * 3 * BS * BS * BS) ** (-0.5)
    grad_logit = ((jax.nn.sigmoid(logits) - targets[0, 0].astype(jnp.float32)) * scale).astype(
        jnp.bfloat16
    )
    grad_head = lax.dot_general(
        grad_logit, hid_second, (((1,), (1,)), ((), ())), preferred_element_type=jnp.float32
    )
    back_second = lax.dot_general(
        head_weight, grad_logit, (((0,), (0,)), ((), ())), preferred_element_type=jnp.float32
    )
    grad_pre_second = (back_second * slope_second).astype(jnp.bfloat16)
    grad_second = kernel_grad(padded_first, grad_pre_second, 2)
    padded_grad = surround(grad_pre_second.reshape(channels, BS, BS, BS), 2, tables)
    kernel_back = jnp.transpose(kernel_second[:, :, ::-1, ::-1, ::-1], (1, 0, 2, 3, 4))
    back_first = conv_padded(padded_grad, kernel_back, 2)
    grad_pre_first = (back_first * slope_first).astype(jnp.bfloat16)
    grad_first = kernel_grad(padded_in, grad_pre_first, 1)
    grad_first, grad_second, grad_head = lax.psum(
        (grad_first, grad_second, grad_head), ("dp", "space")
    )
    return (logits[None, None], grad_first, grad_second, grad_head)


C = 48
CELLS = 512
ROWS = 1008
LANES = 128


def lanes(rows=1):
    return lax.broadcasted_iota(jnp.int32, (rows, LANES), 1)


def pack_kernel(features_ref, targets_ref, out_ref):
    copies = out_ref.shape[0]
    targets = targets_ref[...].astype(jnp.float32)
    targets = jnp.concatenate([targets, jnp.zeros((1, CELLS), jnp.float32)], axis=0)
    pieces = [targets[:, LANES * q : LANES * (q + 1)] for q in range(4)]
    target_tile = jnp.concatenate(pieces, axis=0).astype(jnp.bfloat16)
    for s in range(copies):
        for ct in range(3):
            for q in range(4):
                out_ref[s, 4 * ct + q] = features_ref[
                    16 * ct : 16 * (ct + 1), LANES * q : LANES * (q + 1)
                ]
        out_ref[s, 12] = target_tile


def weights_kernel(first_ref, second_ref, head_ref, w1_ref, w2_ref, w2t_ref, h_ref, ht_ref):
    for ref, out in ((first_ref, w1_ref), (second_ref, w2_ref)):
        stacked = []
        for a in range(3):
            taps = [ref[9 * a + t].astype(jnp.float32) for t in range(9)]
            stacked.append(jnp.concatenate(taps, axis=1))
        whole = jnp.concatenate(stacked, axis=0)
        out[...] = whole.astype(jnp.bfloat16)
        if out is w2_ref:
            w2t_ref[...] = whole.T.astype(jnp.bfloat16)
    head = jnp.concatenate(
        [head_ref[...].astype(jnp.float32), jnp.zeros((13, C), jnp.float32)], axis=0
    )
    h_ref[...] = head.astype(jnp.bfloat16)
    ht_ref[...] = head.T.astype(jnp.bfloat16)


def matmul(left, right):
    return lax.dot_general(
        left, right, (((1,), (0,)), ((), ())), preferred_element_type=jnp.float32
    )


def matmul_lanes(left, right):
    return lax.dot_general(
        left, right, (((1,), (1,)), ((), ())), preferred_element_type=jnp.float32
    )


def roll(values, shift):
    return pltpu.roll(values, shift % LANES, 1)


def crop_kernel(
    scale,
    block_ref,
    gathered_ref,
    w1_ref,
    w2_ref,
    w2t_ref,
    h_ref,
    ht_ref,
    logits_ref,
    packed_ref,
    table_ref,
    present_ref,
    x9_ref,
    h9_ref,
    product_ref,
    slope1_ref,
    slope2_ref,
    hid2_ref,
    grad2_ref,
    shifted_ref,
    back_ref,
):
    count = gathered_ref.shape[0]
    me = lax.axis_index("space")
    own = block_ref[0, me]
    for slot in range(10):
        table_ref[slot] = 0
        present_ref[slot] = 0
    for s in range(count):
        block = block_ref[0, s]
        dx = (block >> 2) - (own >> 2) + 1
        dy = (block & 3) - (own & 3) + 1
        near = (dx >= 0) & (dx <= 2) & (dy >= 0) & (dy <= 2)
        slot = jnp.where(near, dx * 3 + dy, 9)
        table_ref[slot] = s
        present_ref[slot] = 1
    owner = [table_ref[q] for q in range(9)]
    there = [present_ref[q].astype(jnp.float32) for q in range(9)]

    lane = lanes()
    depth = lane & 7
    low, mid = lane < 32, lane < 96
    own_lanes = ((lane >= 32) & (lane < 96)).astype(jnp.float32)
    left_half = lane < 64
    masks = [
        jnp.where(low, there[3 * bx], jnp.where(mid, there[3 * bx + 1], there[3 * bx + 2]))
        for bx in range(3)
    ]
    edge_masks = [jnp.where(left_half, there[3 * bx + 2], there[3 * bx]) for bx in range(3)]

    for plane in range(18):
        bx, i = (plane + 3) // 8, (plane + 3) % 8
        q, half = i // 2, i % 2
        for ct in range(3):
            parts = [
                gathered_ref[owner[3 * bx + by], 4 * ct + q].astype(jnp.float32) for by in range(3)
            ]
            before = roll(parts[0], 96 - 64 * half)
            middle = roll(parts[1], 32 - 64 * half)
            after = roll(parts[2], 96 - 64 * half)
            main = jnp.where(low, before, jnp.where(mid, middle, after)) * masks[bx]
            edge = jnp.where(left_half, after, before) * edge_masks[bx]
            for c in (-1, 0, 1):
                if c == 0:
                    main_c, edge_c = main, edge
                else:
                    keep = depth >= 1 if c == 1 else depth <= 6
                    main_c, edge_c = jnp.where(keep, main, 0.0), jnp.where(keep, edge, 0.0)
                for b in (-1, 0, 1):
                    step = 8 * b + c
                    if b == 1:
                        source = jnp.where(lane < step, edge_c, main_c)
                    elif b == -1:
                        source = jnp.where(lane >= LANES + step, edge_c, main_c)
                    else:
                        source = main_c
                    row = (3 * (b + 1) + c + 1) * C + 16 * ct
                    x9_ref[row : row + 16, LANES * plane : LANES * (plane + 1)] = (
                        roll(source, -step) if step else source
                    ).astype(jnp.bfloat16)

    def plane_cols(plane):
        return slice(LANES * plane, LANES * (plane + 1))

    def summed(plane, stride):
        return (
            product_ref[0:C, plane_cols(plane)]
            + product_ref[C : 2 * C, plane_cols(plane + stride)]
            + product_ref[2 * C : 3 * C, plane_cols(plane + 2 * stride)]
        )

    for n in range(9):
        cols = slice(256 * n, 256 * (n + 1))
        product_ref[:, cols] = matmul(w1_ref[...], x9_ref[:, cols])

    for plane in range(16):
        bx = (plane + 4) // 8
        pre = summed(plane, 1)
        negative = jnp.exp(jnp.minimum(pre, 0.0))
        if 4 <= plane < 12:
            slope1_ref[:, plane_cols(plane - 4)] = jnp.where(pre > 0, 1.0, negative)
        hidden = jnp.where(pre > 0, pre, negative - 1.0) * masks[bx]
        hidden = hidden.astype(jnp.bfloat16).astype(jnp.float32)
        for c in (-1, 0, 1):
            if c == 0:
                source = hidden
            else:
                source = jnp.where(depth >= 2 if c == 1 else depth <= 5, hidden, 0.0)
            for b in (-1, 0, 1):
                step = 16 * b + 2 * c
                row = (3 * (b + 1) + c + 1) * C
                h9_ref[row : row + C, plane_cols(plane)] = (
                    roll(source, -step) if step else source
                ).astype(jnp.bfloat16)

    for n in range(8):
        cols = slice(256 * n, 256 * (n + 1))
        product_ref[:, cols] = matmul(w2_ref[...], h9_ref[:, cols])

    for plane in range(12):
        bx = (plane + 6) // 8
        pre = summed(plane, 2)
        negative = jnp.exp(jnp.minimum(pre, 0.0))
        slope2_ref[:, plane_cols(plane)] = jnp.where(pre > 0, 1.0, negative) * masks[bx]
        hidden = jnp.where(pre > 0, pre, negative - 1.0) * masks[bx]
        hid2_ref[:, plane_cols(plane)] = hidden.astype(jnp.bfloat16)

    logits = matmul(h_ref[...], hid2_ref[...])
    targets = []
    for half in range(2):
        row = []
        for bx in range(3):
            parts = [gathered_ref[owner[3 * bx + by], 12].astype(jnp.float32) for by in range(3)]
            before = roll(parts[0], 96 - 64 * half)
            middle = roll(parts[1], 32 - 64 * half)
            after = roll(parts[2], 96 - 64 * half)
            row.append(jnp.where(low, before, jnp.where(mid, middle, after)))
        targets.append(row)
    grads = []
    for plane in range(12):
        bx, i = (plane + 6) // 8, (plane + 6) % 8
        value = logits[:, plane_cols(plane)]
        wanted = targets[i % 2][bx][4 * (i // 2) : 4 * (i // 2) + 4]
        wanted = jnp.concatenate([wanted, jnp.zeros((12, LANES), jnp.float32)], axis=0)
        sigmoid = 1.0 / (1.0 + jnp.exp(-value))
        grads.append((sigmoid - wanted) * masks[bx] * scale)
    for q in range(4):
        first = roll(logits[:, plane_cols(2 + 2 * q)], -32)
        second = roll(logits[:, plane_cols(3 + 2 * q)], 32)
        logits_ref[:, plane_cols(q)] = jnp.where(left_half, first, second)[0:3]

    grad_logit = jnp.concatenate(grads, axis=1).astype(jnp.bfloat16)
    back = matmul(ht_ref[...], grad_logit)
    grad2_ref[...] = (back * slope2_ref[...]).astype(jnp.bfloat16)
    own_grads = jnp.concatenate([grads[2 + x] * own_lanes for x in range(8)], axis=1)
    head_part = matmul_lanes(hid2_ref[:, 2 * LANES : 10 * LANES], own_grads.astype(jnp.bfloat16))

    own_bf16 = own_lanes.astype(jnp.bfloat16)
    shifted_ref[...] = jnp.zeros_like(shifted_ref)
    for a in range(3):
        for x in range(8):
            shifted_ref[C * a : C * (a + 1), plane_cols(x + 2 * a)] = (
                grad2_ref[:, plane_cols(x + 2)] * own_bf16
            )
    second_part = matmul_lanes(shifted_ref[...], h9_ref[:, 2 * LANES : 14 * LANES])

    for a in range(3):
        for x in range(8):
            shifted_ref[C * a : C * (a + 1), plane_cols(x)] = grad2_ref[:, plane_cols(x + 4 - 2 * a)]
    for n in range(4):
        cols = slice(256 * n, 256 * (n + 1))
        back_ref[:, cols] = matmul(w2t_ref[...], shifted_ref[:, cols])
    grad1 = []
    for x in range(8):
        total = jnp.zeros((C, LANES), jnp.float32)
        for c in (-1, 0, 1):
            part = jnp.zeros((C, LANES), jnp.float32)
            for b in (-1, 0, 1):
                row = (3 * (b + 1) + c + 1) * C
                step = 16 * b + 2 * c
                piece = back_ref[row : row + C, plane_cols(x)]
                part += roll(piece, step) if step else piece
            if c:
                part = jnp.where(depth >= 2 if c == 1 else depth <= 5, part, 0.0)
            total += part
        grad1.append((total * slope1_ref[:, plane_cols(x)] * own_lanes).astype(jnp.bfloat16))

    shifted_ref[...] = jnp.zeros_like(shifted_ref)
    for a in range(3):
        for x in range(8):
            shifted_ref[C * a : C * (a + 1), plane_cols(x + a)] = grad1[x]
    first_part = matmul_lanes(
        shifted_ref[:, 0 : 10 * LANES], x9_ref[:, 4 * LANES : 14 * LANES]
    )

    for q in range(3):
        cols = plane_cols(q)
        packed_ref[144 * q : 144 * (q + 1), :] = first_part[:, cols].astype(jnp.bfloat16)
        packed_ref[144 * (q + 3) : 144 * (q + 4), :] = second_part[:, cols].astype(jnp.bfloat16)
    head_part = jnp.concatenate([head_part, jnp.zeros((96, 16), jnp.float32)], axis=0)
    tail = jnp.concatenate(
        [first_part[:, 384:], second_part[:, 384:], head_part, jnp.zeros((144, 16), jnp.float32)],
        axis=1,
    )
    packed_ref[144 * 6 : ROWS, :] = tail.astype(jnp.bfloat16)
    packed_ref[ROWS:, :] = jnp.zeros((packed_ref.shape[0] - ROWS, LANES), jnp.bfloat16)


def sum_kernel(parts_ref, out_ref):
    total = parts_ref[0].astype(jnp.float32)
    for s in range(1, parts_ref.shape[0]):
        total += parts_ref[s].astype(jnp.float32)
    total = total.astype(jnp.bfloat16)
    for s in range(out_ref.shape[0]):
        out_ref[s] = total


def unpack_kernel(rows_ref, first_ref, second_ref, head_ref):
    tail = rows_ref[144 * 6 : ROWS, :].astype(jnp.float32)
    for k, out in ((0, first_ref), (1, second_ref)):
        tiles = [rows_ref[144 * (3 * k + q) : 144 * (3 * k + q + 1), :].astype(jnp.float32) for q in range(3)]
        whole = jnp.concatenate(tiles + [tail[:, C * k : C * (k + 1)]], axis=1)
        for a in range(3):
            for t in range(9):
                out[9 * a + t] = whole[C * a : C * (a + 1), C * t : C * (t + 1)]
    head_ref[...] = tail[0:C, 96:112].T[0:3]


def on_device_flat(features, device_block, conv_first, conv_second, head_weight, targets):
    space_count = lax.axis_size("space")
    device_count = lax.axis_size("dp") * space_count
    bf16, f32 = jnp.bfloat16, jnp.float32
    shape = jax.ShapeDtypeStruct
    vmem = pl.BlockSpec(memory_space=pltpu.VMEM)
    smem = pl.BlockSpec(memory_space=pltpu.SMEM)

    packed_block = pl.pallas_call(
        pack_kernel,
        out_shape=shape((space_count, 13, 16, LANES), bf16),
        in_specs=[vmem] * 2,
        out_specs=vmem,
        name="pack_block",
    )(features[0, 0], targets[0, 0])
    gathered = lax.all_to_all(packed_block, "space", split_axis=0, concat_axis=0, tiled=True)
    w1, w2, w2t, head, head_t = pl.pallas_call(
        weights_kernel,
        out_shape=(
            shape((3 * C, 9 * C), bf16),
            shape((3 * C, 9 * C), bf16),
            shape((9 * C, 3 * C), bf16),
            shape((16, C), bf16),
            shape((C, 16), bf16),
        ),
        in_specs=[vmem] * 3,
        out_specs=(vmem,) * 5,
        name="lay_out_weights",
    )(conv_first.transpose(1, 0, 2), conv_second.transpose(1, 0, 2), head_weight)

    chunk = -(-ROWS // (16 * device_count)) * 16
    scale = (device_count * 3 * CELLS) ** (-0.5)
    logits, packed = pl.pallas_call(
        functools.partial(crop_kernel, scale),
        out_shape=(shape((3, CELLS), f32), shape((chunk * device_count, LANES), bf16)),
        in_specs=[smem] + [vmem] * 6,
        out_specs=(vmem, vmem),
        scratch_shapes=[
            pltpu.SMEM((10,), jnp.int32),
            pltpu.SMEM((10,), jnp.int32),
            pltpu.VMEM((9 * C, 18 * LANES), bf16),
            pltpu.VMEM((9 * C, 16 * LANES), bf16),
            pltpu.VMEM((3 * C, 18 * LANES), f32),
            pltpu.VMEM((C, 8 * LANES), f32),
            pltpu.VMEM((C, 12 * LANES), f32),
            pltpu.VMEM((C, 12 * LANES), bf16),
            pltpu.VMEM((C, 12 * LANES), bf16),
            pltpu.VMEM((3 * C, 12 * LANES), bf16),
            pltpu.VMEM((9 * C, 8 * LANES), f32),
        ],
        compiler_params=pltpu.CompilerParams(vmem_limit_bytes=40 * 1024 * 1024),
        name="forward_backward",
    )(device_block, gathered, w1, w2, w2t, head, head_t)

    terms = lax.all_to_all(
        packed.reshape(device_count, chunk, LANES), ("dp", "space"), 0, 0, tiled=True
    )
    summed = pl.pallas_call(
        sum_kernel,
        out_shape=shape((device_count, chunk, LANES), bf16),
        in_specs=[vmem],
        out_specs=vmem,
        name="sum_terms",
    )(terms)
    rows = lax.all_to_all(summed, ("dp", "space"), 0, 0, tiled=True)
    grad_first, grad_second, grad_head = pl.pallas_call(
        unpack_kernel,
        out_shape=(shape((27, C, C), f32), shape((27, C, C), f32), shape((3, C), f32)),
        in_specs=[vmem],
        out_specs=(vmem,) * 3,
        name="unpack_gradients",
    )(rows.reshape(device_count * chunk, LANES))
    return (
        logits[None, None],
        grad_first.transpose(1, 0, 2),
        grad_second.transpose(1, 0, 2),
        grad_head,
    )


def solution(mesh):
    in_specs = (
        P("dp", "space", None, None),
        P("dp", None),
        P(),
        P(),
        P(),
        P("dp", "space", None, None),
    )
    out_specs = (P("dp", "space", None, None), P(), P(), P())
    depth_z = mesh.shape["space"] // 8
    return jax.shard_map(
        on_device_flat if depth_z == 1 else on_device_deep,
        mesh=mesh,
        in_specs=in_specs,
        out_specs=out_specs,
        check_vma=False,
    )
```

```python
import functools

import jax
import jax.numpy as jnp
from jax import lax
from jax.experimental import pallas as pl
from jax.experimental.pallas import tpu as pltpu
from jax.sharding import PartitionSpec as P

BS = 8


tap_offsets = [
    (tap_index // 9 - 1, tap_index // 3 % 3 - 1, tap_index % 3 - 1) for tap_index in range(27)
]


def elu_pair(values):
    negative = jnp.exp(jnp.minimum(values, 0.0))
    return (jnp.where(values > 0, values, negative - 1.0), jnp.where(values > 0, 1.0, negative))


def neighbor_tables(device_block):
    space_count = lax.axis_size("space")
    depth_z = space_count // 8
    self_index = lax.axis_index("space")
    blocks = device_block[0]
    coords = jnp.stack([blocks // (4 * depth_z), blocks // depth_z % 4, blocks % depth_z])
    own_coords = lax.dynamic_index_in_dim(coords, self_index, 1, keepdims=False)
    offsets = jnp.array(tap_offsets, jnp.int32)
    limits = jnp.array([4, 4, depth_z], jnp.int32)
    wanted = own_coords[None, :] + offsets
    inside = jnp.all((wanted >= 0) & (wanted < limits[None, :]), axis=1) & (jnp.arange(27) != 13)
    wanted_id = (wanted[:, 0] * 4 + wanted[:, 1]) * depth_z + wanted[:, 2]
    matches = (blocks[None, :] == wanted_id[:, None]) & inside[:, None]
    devices = jnp.arange(space_count, dtype=jnp.int32)
    owner_row = jnp.sum(jnp.where(matches, devices[None, :], 0), axis=1)
    present = jnp.any(matches, axis=1)
    relative = coords - own_coords[:, None]
    adjacent = jnp.all(jnp.abs(relative) <= 1, axis=0) & (devices != self_index)
    send_tap = jnp.where(
        adjacent, (relative[0] + 1) * 9 + (relative[1] + 1) * 3 + relative[2] + 1, 13
    )
    return (owner_row, present, send_tap)


def region_slice(block_data, offset, depth_cells):
    span_list = []
    for step_value in offset:
        if step_value == 1:
            span_list.append(slice(BS - depth_cells, BS))
        elif step_value == -1:
            span_list.append(slice(0, depth_cells))
        else:
            span_list.append(slice(0, BS))
    return block_data[:, span_list[0], span_list[1], span_list[2]]


def surround(block_data, depth_cells, tables):
    owner_row, present, send_tap = tables
    channels = block_data.shape[0]
    length = depth_cells * BS * BS
    pieces = []
    for tap_index in range(27):
        if tap_index == 13:
            pieces.append(jnp.zeros((channels, length), block_data.dtype))
        else:
            region = region_slice(block_data, tap_offsets[tap_index], depth_cells).reshape(
                channels, -1
            )
            pieces.append(jnp.pad(region, ((0, 0), (0, length - region.shape[1]))))
    outgoing = jnp.stack(pieces)
    sending = outgoing[send_tap]
    by_source = lax.all_to_all(sending, "space", split_axis=0, concat_axis=0, tiled=True)
    incoming = jnp.where(
        present[:, None, None], by_source[owner_row], jnp.zeros((), block_data.dtype)
    )
    rows_x = []
    for step_x in range(3):
        rows_y = []
        for step_y in range(3):
            rows_z = []
            for step_z in range(3):
                tap_index = step_x * 9 + step_y * 3 + step_z
                if tap_index == 13:
                    rows_z.append(block_data)
                else:
                    extent_list = [
                        BS if step_value == 1 else depth_cells
                        for step_value in (step_x, step_y, step_z)
                    ]
                    count_cells = extent_list[0] * extent_list[1] * extent_list[2]
                    rows_z.append(
                        incoming[tap_index][:, :count_cells].reshape(
                            channels, extent_list[0], extent_list[1], extent_list[2]
                        )
                    )
            rows_y.append(jnp.concatenate(rows_z, axis=3))
        rows_x.append(jnp.concatenate(rows_y, axis=2))
    return jnp.concatenate(rows_x, axis=1)


def conv_padded(padded, kernel, dilation):
    result = lax.conv_general_dilated(
        padded[None],
        kernel,
        (1, 1, 1),
        "VALID",
        rhs_dilation=(dilation, dilation, dilation),
        dimension_numbers=("NCDHW", "OIDHW", "NCDHW"),
        preferred_element_type=jnp.float32,
    )
    return result[0].reshape(kernel.shape[0], BS * BS * BS)


def kernel_grad(padded, grad_rows, dilation):
    channels = padded.shape[0]
    outputs = grad_rows.shape[0]
    grad_block = grad_rows.reshape(outputs, 1, BS, BS, BS)
    result = lax.conv_general_dilated(
        padded[None],
        grad_block,
        (dilation, dilation, dilation),
        "VALID",
        dimension_numbers=("CNDHW", "OIDHW", "NCDHW"),
        preferred_element_type=jnp.float32,
    )
    return result.reshape(channels, outputs, 27).transpose(1, 2, 0)


def on_device_deep(features, device_block, conv_first, conv_second, head_weight, targets):
    channels = features.shape[2]
    tables = neighbor_tables(device_block)
    kernel_first = conv_first.reshape(channels, 3, 3, 3, channels).transpose(0, 4, 1, 2, 3)
    kernel_second = conv_second.reshape(channels, 3, 3, 3, channels).transpose(0, 4, 1, 2, 3)
    block_in = features[0, 0].reshape(channels, BS, BS, BS)
    padded_in = surround(block_in, 1, tables)
    pre_first = conv_padded(padded_in, kernel_first, 1)
    act_first, slope_first = elu_pair(pre_first)
    hid_first = act_first.astype(jnp.bfloat16)
    padded_first = surround(hid_first.reshape(channels, BS, BS, BS), 2, tables)
    pre_second = conv_padded(padded_first, kernel_second, 2)
    act_second, slope_second = elu_pair(pre_second)
    hid_second = act_second.astype(jnp.bfloat16)
    logits = jnp.dot(head_weight, hid_second, preferred_element_type=jnp.float32)
    scale = (lax.axis_size("dp") * lax.axis_size("space") * 3 * BS * BS * BS) ** (-0.5)
    grad_logit = ((jax.nn.sigmoid(logits) - targets[0, 0].astype(jnp.float32)) * scale).astype(
        jnp.bfloat16
    )
    grad_head = lax.dot_general(
        grad_logit, hid_second, (((1,), (1,)), ((), ())), preferred_element_type=jnp.float32
    )
    back_second = lax.dot_general(
        head_weight, grad_logit, (((0,), (0,)), ((), ())), preferred_element_type=jnp.float32
    )
    grad_pre_second = (back_second * slope_second).astype(jnp.bfloat16)
    grad_second = kernel_grad(padded_first, grad_pre_second, 2)
    padded_grad = surround(grad_pre_second.reshape(channels, BS, BS, BS), 2, tables)
    kernel_back = jnp.transpose(kernel_second[:, :, ::-1, ::-1, ::-1], (1, 0, 2, 3, 4))
    back_first = conv_padded(padded_grad, kernel_back, 2)
    grad_pre_first = (back_first * slope_first).astype(jnp.bfloat16)
    grad_first = kernel_grad(padded_in, grad_pre_first, 1)
    grad_first, grad_second, grad_head = lax.psum(
        (grad_first, grad_second, grad_head), ("dp", "space")
    )
    return (logits[None, None], grad_first, grad_second, grad_head)


C = 48
CELLS = 512
ROWS = 1008
LANES = 128


def lanes(rows=1):
    return lax.broadcasted_iota(jnp.int32, (rows, LANES), 1)


def pack_kernel(features_ref, targets_ref, out_ref):
    targets = targets_ref[:, 0, :].astype(jnp.float32)
    targets = jnp.concatenate([targets, jnp.zeros((1, CELLS), jnp.float32)], axis=0)
    pieces = [targets[:, LANES * q : LANES * (q + 1)] for q in range(4)]
    target_tile = jnp.concatenate(pieces, axis=0).astype(jnp.bfloat16)
    for ct in range(3):
        for q in range(4):
            out_ref[4 * ct + q] = features_ref[
                16 * ct : 16 * (ct + 1), LANES * q : LANES * (q + 1)
            ]
    out_ref[12] = target_tile


def weights_kernel(first_ref, second_ref, head_ref, w1_ref, w2_ref, w2t_ref, h_ref, ht_ref):
    for ref, out in ((first_ref, w1_ref), (second_ref, w2_ref)):
        stacked = []
        for a in range(3):
            taps = [ref[9 * a + t].astype(jnp.float32) for t in range(9)]
            stacked.append(jnp.concatenate(taps, axis=1))
        whole = jnp.concatenate(stacked, axis=0)
        out[...] = whole.astype(jnp.bfloat16)
        if out is w2_ref:
            w2t_ref[...] = whole.T.astype(jnp.bfloat16)
    head = jnp.concatenate(
        [head_ref[...].astype(jnp.float32), jnp.zeros((13, C), jnp.float32)], axis=0
    )
    h_ref[...] = head.astype(jnp.bfloat16)
    ht_ref[...] = head.T.astype(jnp.bfloat16)


def matmul(left, right):
    return lax.dot_general(
        left, right, (((1,), (0,)), ((), ())), preferred_element_type=jnp.float32
    )


def matmul_lanes(left, right):
    return lax.dot_general(
        left, right, (((1,), (1,)), ((), ())), preferred_element_type=jnp.float32
    )


def roll(values, shift):
    return pltpu.roll(values, shift % LANES, 1)


def crop_kernel(
    scale,
    block_ref,
    gathered_ref,
    w1_hbm,
    w2_hbm,
    w2t_hbm,
    h_hbm,
    ht_hbm,
    logits_ref,
    packed_ref,
    table_ref,
    present_ref,
    x9_ref,
    h9_ref,
    product_ref,
    slope1_ref,
    slope2_ref,
    hid2_ref,
    grad2_ref,
    shifted_ref,
    back_ref,
    w1_ref,
    w2_ref,
    w2t_ref,
    h_ref,
    ht_ref,
    sems,
):
    sources = (w1_hbm, w2_hbm, w2t_hbm, h_hbm, ht_hbm)
    copies = [
        pltpu.make_async_copy(source, target, sems.at[k])
        for k, (source, target) in enumerate(zip(sources, (w1_ref, w2_ref, w2t_ref, h_ref, ht_ref)))
    ]
    for copy in copies:
        copy.start()

    count = gathered_ref.shape[0]
    me = lax.axis_index("space")
    own = block_ref[0, me]
    for slot in range(10):
        table_ref[slot] = 0
        present_ref[slot] = 0
    for s in range(count):
        block = block_ref[0, s]
        dx = (block >> 2) - (own >> 2) + 1
        dy = (block & 3) - (own & 3) + 1
        near = (dx >= 0) & (dx <= 2) & (dy >= 0) & (dy <= 2)
        slot = jnp.where(near, dx * 3 + dy, 9)
        table_ref[slot] = s
        present_ref[slot] = 1
    owner = [table_ref[q] for q in range(9)]
    there = [present_ref[q].astype(jnp.float32) for q in range(9)]

    lane = lanes()
    depth = lane & 7
    low, mid = lane < 32, lane < 96
    own_lanes = ((lane >= 32) & (lane < 96)).astype(jnp.float32)
    left_half = lane < 64
    masks = [
        jnp.where(low, there[3 * bx], jnp.where(mid, there[3 * bx + 1], there[3 * bx + 2]))
        for bx in range(3)
    ]
    edge_masks = [jnp.where(left_half, there[3 * bx + 2], there[3 * bx]) for bx in range(3)]

    for plane in range(18):
        bx, i = (plane + 3) // 8, (plane + 3) % 8
        q, half = i // 2, i % 2
        for ct in range(3):
            parts = [
                gathered_ref[owner[3 * bx + by], 4 * ct + q].astype(jnp.float32) for by in range(3)
            ]
            before = roll(parts[0], 96 - 64 * half)
            middle = roll(parts[1], 32 - 64 * half)
            after = roll(parts[2], 96 - 64 * half)
            main = jnp.where(low, before, jnp.where(mid, middle, after)) * masks[bx]
            edge = jnp.where(left_half, after, before) * edge_masks[bx]
            for c in (-1, 0, 1):
                if c == 0:
                    main_c, edge_c = main, edge
                else:
                    keep = depth >= 1 if c == 1 else depth <= 6
                    main_c, edge_c = jnp.where(keep, main, 0.0), jnp.where(keep, edge, 0.0)
                for b in (-1, 0, 1):
                    step = 8 * b + c
                    if b == 1:
                        source = jnp.where(lane < step, edge_c, main_c)
                    elif b == -1:
                        source = jnp.where(lane >= LANES + step, edge_c, main_c)
                    else:
                        source = main_c
                    row = (3 * (b + 1) + c + 1) * C + 16 * ct
                    x9_ref[row : row + 16, LANES * plane : LANES * (plane + 1)] = (
                        roll(source, -step) if step else source
                    ).astype(jnp.bfloat16)

    def plane_cols(plane):
        return slice(LANES * plane, LANES * (plane + 1))

    def summed(plane, stride):
        return (
            product_ref[0:C, plane_cols(plane)]
            + product_ref[C : 2 * C, plane_cols(plane + stride)]
            + product_ref[2 * C : 3 * C, plane_cols(plane + 2 * stride)]
        )

    for copy in copies:
        copy.wait()
    for n in range(9):
        cols = slice(256 * n, 256 * (n + 1))
        product_ref[:, cols] = matmul(w1_ref[...], x9_ref[:, cols])

    for plane in range(16):
        bx = (plane + 4) // 8
        pre = summed(plane, 1)
        negative = jnp.exp(jnp.minimum(pre, 0.0))
        if 4 <= plane < 12:
            slope1_ref[:, plane_cols(plane - 4)] = jnp.where(pre > 0, 1.0, negative)
        hidden = jnp.where(pre > 0, pre, negative - 1.0) * masks[bx]
        hidden = hidden.astype(jnp.bfloat16).astype(jnp.float32)
        for c in (-1, 0, 1):
            if c == 0:
                source = hidden
            else:
                source = jnp.where(depth >= 2 if c == 1 else depth <= 5, hidden, 0.0)
            for b in (-1, 0, 1):
                step = 16 * b + 2 * c
                row = (3 * (b + 1) + c + 1) * C
                h9_ref[row : row + C, plane_cols(plane)] = (
                    roll(source, -step) if step else source
                ).astype(jnp.bfloat16)

    for n in range(8):
        cols = slice(256 * n, 256 * (n + 1))
        product_ref[:, cols] = matmul(w2_ref[...], h9_ref[:, cols])

    for plane in range(12):
        bx = (plane + 6) // 8
        pre = summed(plane, 2)
        negative = jnp.exp(jnp.minimum(pre, 0.0))
        slope2_ref[:, plane_cols(plane)] = jnp.where(pre > 0, 1.0, negative) * masks[bx]
        hidden = jnp.where(pre > 0, pre, negative - 1.0) * masks[bx]
        hid2_ref[:, plane_cols(plane)] = hidden.astype(jnp.bfloat16)

    logits = matmul(h_ref[...], hid2_ref[...])
    targets = []
    for half in range(2):
        row = []
        for bx in range(3):
            parts = [gathered_ref[owner[3 * bx + by], 12].astype(jnp.float32) for by in range(3)]
            before = roll(parts[0], 96 - 64 * half)
            middle = roll(parts[1], 32 - 64 * half)
            after = roll(parts[2], 96 - 64 * half)
            row.append(jnp.where(low, before, jnp.where(mid, middle, after)))
        targets.append(row)
    grads = []
    for plane in range(12):
        bx, i = (plane + 6) // 8, (plane + 6) % 8
        value = logits[:, plane_cols(plane)]
        wanted = targets[i % 2][bx][4 * (i // 2) : 4 * (i // 2) + 4]
        wanted = jnp.concatenate([wanted, jnp.zeros((12, LANES), jnp.float32)], axis=0)
        sigmoid = 1.0 / (1.0 + jnp.exp(-value))
        grads.append((sigmoid - wanted) * masks[bx] * scale)
    for q in range(4):
        first = roll(logits[:, plane_cols(2 + 2 * q)], -32)
        second = roll(logits[:, plane_cols(3 + 2 * q)], 32)
        logits_ref[:, 0, plane_cols(q)] = jnp.where(left_half, first, second)[0:3]

    grad_logit = jnp.concatenate(grads, axis=1).astype(jnp.bfloat16)
    back = matmul(ht_ref[...], grad_logit)
    grad2_ref[...] = (back * slope2_ref[...]).astype(jnp.bfloat16)
    own_grads = jnp.concatenate([grads[2 + x] * own_lanes for x in range(8)], axis=1)
    head_part = matmul_lanes(hid2_ref[:, 2 * LANES : 10 * LANES], own_grads.astype(jnp.bfloat16))

    own_bf16 = own_lanes.astype(jnp.bfloat16)
    shifted_ref[...] = jnp.zeros_like(shifted_ref)
    for a in range(3):
        for x in range(8):
            shifted_ref[C * a : C * (a + 1), plane_cols(x + 2 * a)] = (
                grad2_ref[:, plane_cols(x + 2)] * own_bf16
            )
    second_part = matmul_lanes(shifted_ref[...], h9_ref[:, 2 * LANES : 14 * LANES])

    for a in range(3):
        for x in range(8):
            shifted_ref[C * a : C * (a + 1), plane_cols(x)] = grad2_ref[:, plane_cols(x + 4 - 2 * a)]
    for n in range(4):
        cols = slice(256 * n, 256 * (n + 1))
        back_ref[:, cols] = matmul(w2t_ref[...], shifted_ref[:, cols])
    grad1 = []
    for x in range(8):
        total = jnp.zeros((C, LANES), jnp.float32)
        for c in (-1, 0, 1):
            part = jnp.zeros((C, LANES), jnp.float32)
            for b in (-1, 0, 1):
                row = (3 * (b + 1) + c + 1) * C
                step = 16 * b + 2 * c
                piece = back_ref[row : row + C, plane_cols(x)]
                part += roll(piece, step) if step else piece
            if c:
                part = jnp.where(depth >= 2 if c == 1 else depth <= 5, part, 0.0)
            total += part
        grad1.append((total * slope1_ref[:, plane_cols(x)] * own_lanes).astype(jnp.bfloat16))

    shifted_ref[...] = jnp.zeros_like(shifted_ref)
    for a in range(3):
        for x in range(8):
            shifted_ref[C * a : C * (a + 1), plane_cols(x + a)] = grad1[x]
    first_part = matmul_lanes(
        shifted_ref[:, 0 : 10 * LANES], x9_ref[:, 4 * LANES : 14 * LANES]
    )

    for q in range(3):
        cols = plane_cols(q)
        packed_ref[144 * q : 144 * (q + 1), :] = first_part[:, cols].astype(jnp.bfloat16)
        packed_ref[144 * (q + 3) : 144 * (q + 4), :] = second_part[:, cols].astype(jnp.bfloat16)
    head_part = jnp.concatenate([head_part, jnp.zeros((96, 16), jnp.float32)], axis=0)
    tail = jnp.concatenate(
        [first_part[:, 384:], second_part[:, 384:], head_part, jnp.zeros((144, 16), jnp.float32)],
        axis=1,
    )
    packed_ref[144 * 6 : ROWS, :] = tail.astype(jnp.bfloat16)
    packed_ref[ROWS:, :] = jnp.zeros((packed_ref.shape[0] - ROWS, LANES), jnp.bfloat16)


def sum_kernel(parts_ref, out_ref):
    total = parts_ref[0].astype(jnp.float32)
    for s in range(1, parts_ref.shape[0]):
        total += parts_ref[s].astype(jnp.float32)
    out_ref[...] = total.astype(jnp.bfloat16)


def unpack_kernel(rows_ref, first_ref, second_ref, head_ref):
    tail = rows_ref[144 * 6 : ROWS, :].astype(jnp.float32)
    for k, out in ((0, first_ref), (1, second_ref)):
        tiles = [rows_ref[144 * (3 * k + q) : 144 * (3 * k + q + 1), :].astype(jnp.float32) for q in range(3)]
        whole = jnp.concatenate(tiles + [tail[:, C * k : C * (k + 1)]], axis=1)
        for a in range(3):
            for t in range(9):
                out[9 * a + t] = whole[C * a : C * (a + 1), C * t : C * (t + 1)]
    head_ref[...] = tail[0:C, 96:112].T[0:3]


def on_device_flat(features, device_block, conv_first, conv_second, head_weight, targets):
    space_count = lax.axis_size("space")
    device_count = lax.axis_size("dp") * space_count
    bf16, f32 = jnp.bfloat16, jnp.float32
    shape = jax.ShapeDtypeStruct
    vmem = pl.BlockSpec(memory_space=pltpu.VMEM)
    smem = pl.BlockSpec(memory_space=pltpu.SMEM)

    packed_block = pl.pallas_call(
        pack_kernel,
        out_shape=shape((13, 16, LANES), bf16),
        in_specs=[vmem] * 2,
        out_specs=vmem,
        name="pack_block",
    )(features[0, 0], targets[0].transpose(1, 0, 2))
    gathered = lax.all_gather(packed_block, "space")
    w1, w2, w2t, head, head_t = pl.pallas_call(
        weights_kernel,
        out_shape=(
            shape((3 * C, 9 * C), bf16),
            shape((3 * C, 9 * C), bf16),
            shape((9 * C, 3 * C), bf16),
            shape((16, C), bf16),
            shape((C, 16), bf16),
        ),
        in_specs=[vmem] * 3,
        out_specs=(vmem,) * 5,
        name="lay_out_weights",
    )(conv_first.transpose(1, 0, 2), conv_second.transpose(1, 0, 2), head_weight)

    chunk = -(-ROWS // (16 * device_count)) * 16
    scale = (device_count * 3 * CELLS) ** (-0.5)
    logits, packed = pl.pallas_call(
        functools.partial(crop_kernel, scale),
        out_shape=(shape((3, 1, CELLS), f32), shape((chunk * device_count, LANES), bf16)),
        in_specs=[smem, vmem] + [pl.BlockSpec(memory_space=pltpu.HBM)] * 5,
        out_specs=(vmem, vmem),
        scratch_shapes=[
            pltpu.SMEM((10,), jnp.int32),
            pltpu.SMEM((10,), jnp.int32),
            pltpu.VMEM((9 * C, 18 * LANES), bf16),
            pltpu.VMEM((9 * C, 16 * LANES), bf16),
            pltpu.VMEM((3 * C, 18 * LANES), f32),
            pltpu.VMEM((C, 8 * LANES), f32),
            pltpu.VMEM((C, 12 * LANES), f32),
            pltpu.VMEM((C, 12 * LANES), bf16),
            pltpu.VMEM((C, 12 * LANES), bf16),
            pltpu.VMEM((3 * C, 12 * LANES), bf16),
            pltpu.VMEM((9 * C, 8 * LANES), f32),
            pltpu.VMEM((3 * C, 9 * C), bf16),
            pltpu.VMEM((3 * C, 9 * C), bf16),
            pltpu.VMEM((9 * C, 3 * C), bf16),
            pltpu.VMEM((16, C), bf16),
            pltpu.VMEM((C, 16), bf16),
            pltpu.SemaphoreType.DMA((5,)),
        ],
        compiler_params=pltpu.CompilerParams(vmem_limit_bytes=40 * 1024 * 1024),
        name="forward_backward",
    )(device_block, gathered, w1, w2, w2t, head, head_t)

    terms = lax.all_to_all(
        packed.reshape(device_count, chunk, LANES), ("dp", "space"), 0, 0, tiled=True
    )
    summed = pl.pallas_call(
        sum_kernel,
        out_shape=shape((chunk, LANES), bf16),
        in_specs=[vmem],
        out_specs=vmem,
        compiler_params=pltpu.CompilerParams(vmem_limit_bytes=16 * 1024 * 1024),
        name="sum_terms",
    )(terms)
    rows = lax.all_gather(summed, ("dp", "space"))
    grad_first, grad_second, grad_head = pl.pallas_call(
        unpack_kernel,
        out_shape=(shape((27, C, C), f32), shape((27, C, C), f32), shape((3, C), f32)),
        in_specs=[vmem],
        out_specs=(vmem,) * 3,
        compiler_params=pltpu.CompilerParams(vmem_limit_bytes=16 * 1024 * 1024),
        name="unpack_gradients",
    )(rows.reshape(device_count * chunk, LANES))
    return (
        logits.transpose(1, 0, 2)[None],
        grad_first.transpose(1, 0, 2),
        grad_second.transpose(1, 0, 2),
        grad_head,
    )


def solution(mesh):
    in_specs = (
        P("dp", "space", None, None),
        P("dp", None),
        P(),
        P(),
        P(),
        P("dp", "space", None, None),
    )
    out_specs = (P("dp", "space", None, None), P(), P(), P())
    depth_z = mesh.shape["space"] // 8
    return jax.shard_map(
        on_device_flat if depth_z == 1 else on_device_deep,
        mesh=mesh,
        in_specs=in_specs,
        out_specs=out_specs,
        check_vma=False,
    )
```

```python
import functools

import jax
import jax.numpy as jnp
from jax import lax
from jax.experimental import pallas as pl
from jax.experimental.pallas import tpu as pltpu
from jax.sharding import PartitionSpec as P

BS = 8


tap_offsets = [
    (tap_index // 9 - 1, tap_index // 3 % 3 - 1, tap_index % 3 - 1) for tap_index in range(27)
]


def elu_pair(values):
    negative = jnp.exp(jnp.minimum(values, 0.0))
    return (jnp.where(values > 0, values, negative - 1.0), jnp.where(values > 0, 1.0, negative))


def neighbor_tables(device_block):
    space_count = lax.axis_size("space")
    depth_z = space_count // 8
    self_index = lax.axis_index("space")
    blocks = device_block[0]
    coords = jnp.stack([blocks // (4 * depth_z), blocks // depth_z % 4, blocks % depth_z])
    own_coords = lax.dynamic_index_in_dim(coords, self_index, 1, keepdims=False)
    offsets = jnp.array(tap_offsets, jnp.int32)
    limits = jnp.array([4, 4, depth_z], jnp.int32)
    wanted = own_coords[None, :] + offsets
    inside = jnp.all((wanted >= 0) & (wanted < limits[None, :]), axis=1) & (jnp.arange(27) != 13)
    wanted_id = (wanted[:, 0] * 4 + wanted[:, 1]) * depth_z + wanted[:, 2]
    matches = (blocks[None, :] == wanted_id[:, None]) & inside[:, None]
    devices = jnp.arange(space_count, dtype=jnp.int32)
    owner_row = jnp.sum(jnp.where(matches, devices[None, :], 0), axis=1)
    present = jnp.any(matches, axis=1)
    relative = coords - own_coords[:, None]
    adjacent = jnp.all(jnp.abs(relative) <= 1, axis=0) & (devices != self_index)
    send_tap = jnp.where(
        adjacent, (relative[0] + 1) * 9 + (relative[1] + 1) * 3 + relative[2] + 1, 13
    )
    return (owner_row, present, send_tap)


def region_slice(block_data, offset, depth_cells):
    span_list = []
    for step_value in offset:
        if step_value == 1:
            span_list.append(slice(BS - depth_cells, BS))
        elif step_value == -1:
            span_list.append(slice(0, depth_cells))
        else:
            span_list.append(slice(0, BS))
    return block_data[:, span_list[0], span_list[1], span_list[2]]


def surround(block_data, depth_cells, tables):
    owner_row, present, send_tap = tables
    channels = block_data.shape[0]
    length = depth_cells * BS * BS
    pieces = []
    for tap_index in range(27):
        if tap_index == 13:
            pieces.append(jnp.zeros((channels, length), block_data.dtype))
        else:
            region = region_slice(block_data, tap_offsets[tap_index], depth_cells).reshape(
                channels, -1
            )
            pieces.append(jnp.pad(region, ((0, 0), (0, length - region.shape[1]))))
    outgoing = jnp.stack(pieces)
    sending = outgoing[send_tap]
    by_source = lax.all_to_all(sending, "space", split_axis=0, concat_axis=0, tiled=True)
    incoming = jnp.where(
        present[:, None, None], by_source[owner_row], jnp.zeros((), block_data.dtype)
    )
    rows_x = []
    for step_x in range(3):
        rows_y = []
        for step_y in range(3):
            rows_z = []
            for step_z in range(3):
                tap_index = step_x * 9 + step_y * 3 + step_z
                if tap_index == 13:
                    rows_z.append(block_data)
                else:
                    extent_list = [
                        BS if step_value == 1 else depth_cells
                        for step_value in (step_x, step_y, step_z)
                    ]
                    count_cells = extent_list[0] * extent_list[1] * extent_list[2]
                    rows_z.append(
                        incoming[tap_index][:, :count_cells].reshape(
                            channels, extent_list[0], extent_list[1], extent_list[2]
                        )
                    )
            rows_y.append(jnp.concatenate(rows_z, axis=3))
        rows_x.append(jnp.concatenate(rows_y, axis=2))
    return jnp.concatenate(rows_x, axis=1)


def conv_padded(padded, kernel, dilation):
    result = lax.conv_general_dilated(
        padded[None],
        kernel,
        (1, 1, 1),
        "VALID",
        rhs_dilation=(dilation, dilation, dilation),
        dimension_numbers=("NCDHW", "OIDHW", "NCDHW"),
        preferred_element_type=jnp.float32,
    )
    return result[0].reshape(kernel.shape[0], BS * BS * BS)


def kernel_grad(padded, grad_rows, dilation):
    channels = padded.shape[0]
    outputs = grad_rows.shape[0]
    grad_block = grad_rows.reshape(outputs, 1, BS, BS, BS)
    result = lax.conv_general_dilated(
        padded[None],
        grad_block,
        (dilation, dilation, dilation),
        "VALID",
        dimension_numbers=("CNDHW", "OIDHW", "NCDHW"),
        preferred_element_type=jnp.float32,
    )
    return result.reshape(channels, outputs, 27).transpose(1, 2, 0)


def on_device_deep(features, device_block, conv_first, conv_second, head_weight, targets):
    channels = features.shape[2]
    tables = neighbor_tables(device_block)
    kernel_first = conv_first.reshape(channels, 3, 3, 3, channels).transpose(0, 4, 1, 2, 3)
    kernel_second = conv_second.reshape(channels, 3, 3, 3, channels).transpose(0, 4, 1, 2, 3)
    block_in = features[0, 0].reshape(channels, BS, BS, BS)
    padded_in = surround(block_in, 1, tables)
    pre_first = conv_padded(padded_in, kernel_first, 1)
    act_first, slope_first = elu_pair(pre_first)
    hid_first = act_first.astype(jnp.bfloat16)
    padded_first = surround(hid_first.reshape(channels, BS, BS, BS), 2, tables)
    pre_second = conv_padded(padded_first, kernel_second, 2)
    act_second, slope_second = elu_pair(pre_second)
    hid_second = act_second.astype(jnp.bfloat16)
    logits = jnp.dot(head_weight, hid_second, preferred_element_type=jnp.float32)
    scale = (lax.axis_size("dp") * lax.axis_size("space") * 3 * BS * BS * BS) ** (-0.5)
    grad_logit = ((jax.nn.sigmoid(logits) - targets[0, 0].astype(jnp.float32)) * scale).astype(
        jnp.bfloat16
    )
    grad_head = lax.dot_general(
        grad_logit, hid_second, (((1,), (1,)), ((), ())), preferred_element_type=jnp.float32
    )
    back_second = lax.dot_general(
        head_weight, grad_logit, (((0,), (0,)), ((), ())), preferred_element_type=jnp.float32
    )
    grad_pre_second = (back_second * slope_second).astype(jnp.bfloat16)
    grad_second = kernel_grad(padded_first, grad_pre_second, 2)
    padded_grad = surround(grad_pre_second.reshape(channels, BS, BS, BS), 2, tables)
    kernel_back = jnp.transpose(kernel_second[:, :, ::-1, ::-1, ::-1], (1, 0, 2, 3, 4))
    back_first = conv_padded(padded_grad, kernel_back, 2)
    grad_pre_first = (back_first * slope_first).astype(jnp.bfloat16)
    grad_first = kernel_grad(padded_in, grad_pre_first, 1)
    grad_first, grad_second, grad_head = lax.psum(
        (grad_first, grad_second, grad_head), ("dp", "space")
    )
    return (logits[None, None], grad_first, grad_second, grad_head)


C = 48
CELLS = 512
ROWS = 1008
LANES = 128


def lanes(rows=1):
    return lax.broadcasted_iota(jnp.int32, (rows, LANES), 1)


def pack_kernel(features_ref, targets_ref, out_ref):
    targets = targets_ref[:, 0, :].astype(jnp.float32)
    targets = jnp.concatenate([targets, jnp.zeros((1, CELLS), jnp.float32)], axis=0)
    pieces = [targets[:, LANES * q : LANES * (q + 1)] for q in range(4)]
    target_tile = jnp.concatenate(pieces, axis=0).astype(jnp.bfloat16)
    for ct in range(3):
        for q in range(4):
            out_ref[4 * ct + q] = features_ref[
                16 * ct : 16 * (ct + 1), LANES * q : LANES * (q + 1)
            ]
    out_ref[12] = target_tile


def stacked_taps(ref):
    rows = []
    for a in range(3):
        taps = [ref[9 * a + t].astype(jnp.float32) for t in range(9)]
        rows.append(jnp.concatenate(taps, axis=1))
    return jnp.concatenate(rows, axis=0)


def matmul(left, right):
    return lax.dot_general(
        left, right, (((1,), (0,)), ((), ())), preferred_element_type=jnp.float32
    )


def matmul_lanes(left, right):
    return lax.dot_general(
        left, right, (((1,), (1,)), ((), ())), preferred_element_type=jnp.float32
    )


def roll(values, shift):
    return pltpu.roll(values, shift % LANES, 1)


def crop_kernel(
    scale,
    count,
    *refs,
):
    blocks, refs = refs[1 : 1 + count], refs[:1] + refs[1 + count :]
    crop_body(scale, blocks, *refs)


def crop_body(
    scale,
    blocks,
    block_ref,
    first_ref,
    second_ref,
    head_ref,
    logits_ref,
    packed_ref,
    table_ref,
    present_ref,
    x9_ref,
    h9_ref,
    product_ref,
    slope1_ref,
    slope2_ref,
    hid2_ref,
    grad2_ref,
    shifted_ref,
    back_ref,
    gathered_ref,
    w1_ref,
    w2_ref,
    w2t_ref,
):
    count = len(blocks)
    for k in range(count):
        gathered_ref[k] = blocks[k][...]
    w1_ref[...] = stacked_taps(first_ref).astype(jnp.bfloat16)
    whole = stacked_taps(second_ref)
    w2_ref[...] = whole.astype(jnp.bfloat16)
    w2t_ref[...] = whole.T.astype(jnp.bfloat16)
    head = head_ref[...].astype(jnp.float32)
    head = jnp.concatenate([head, jnp.zeros((13, C), jnp.float32)], axis=0)
    head_t = head.T.astype(jnp.bfloat16)
    head = head.astype(jnp.bfloat16)

    me = lax.axis_index("space")
    own = block_ref[0, me]
    for slot in range(10):
        table_ref[slot] = 0
        present_ref[slot] = 0
    for s in range(count):
        block = block_ref[0, s]
        dx = (block >> 2) - (own >> 2) + 1
        dy = (block & 3) - (own & 3) + 1
        near = (dx >= 0) & (dx <= 2) & (dy >= 0) & (dy <= 2)
        slot = jnp.where(near, dx * 3 + dy, 9)
        table_ref[slot] = s ^ me
        present_ref[slot] = 1
    owner = [table_ref[q] for q in range(9)]
    there = [present_ref[q].astype(jnp.float32) for q in range(9)]

    lane = lanes()
    depth = lane & 7
    low, mid = lane < 32, lane < 96
    own_lanes = ((lane >= 32) & (lane < 96)).astype(jnp.float32)
    left_half = lane < 64
    masks = [
        jnp.where(low, there[3 * bx], jnp.where(mid, there[3 * bx + 1], there[3 * bx + 2]))
        for bx in range(3)
    ]
    edge_masks = [jnp.where(left_half, there[3 * bx + 2], there[3 * bx]) for bx in range(3)]

    for plane in range(18):
        bx, i = (plane + 3) // 8, (plane + 3) % 8
        q, half = i // 2, i % 2
        for ct in range(3):
            parts = [
                gathered_ref[owner[3 * bx + by], 4 * ct + q].astype(jnp.float32) for by in range(3)
            ]
            before = roll(parts[0], 96 - 64 * half)
            middle = roll(parts[1], 32 - 64 * half)
            after = roll(parts[2], 96 - 64 * half)
            main = jnp.where(low, before, jnp.where(mid, middle, after)) * masks[bx]
            edge = jnp.where(left_half, after, before) * edge_masks[bx]
            for c in (-1, 0, 1):
                if c == 0:
                    main_c, edge_c = main, edge
                else:
                    keep = depth >= 1 if c == 1 else depth <= 6
                    main_c, edge_c = jnp.where(keep, main, 0.0), jnp.where(keep, edge, 0.0)
                for b in (-1, 0, 1):
                    step = 8 * b + c
                    if b == 1:
                        source = jnp.where(lane < step, edge_c, main_c)
                    elif b == -1:
                        source = jnp.where(lane >= LANES + step, edge_c, main_c)
                    else:
                        source = main_c
                    row = (3 * (b + 1) + c + 1) * C + 16 * ct
                    x9_ref[row : row + 16, LANES * plane : LANES * (plane + 1)] = (
                        roll(source, -step) if step else source
                    ).astype(jnp.bfloat16)

    def plane_cols(plane):
        return slice(LANES * plane, LANES * (plane + 1))

    def summed(plane, stride):
        return (
            product_ref[0:C, plane_cols(plane)]
            + product_ref[C : 2 * C, plane_cols(plane + stride)]
            + product_ref[2 * C : 3 * C, plane_cols(plane + 2 * stride)]
        )

    for n in range(9):
        cols = slice(256 * n, 256 * (n + 1))
        product_ref[:, cols] = matmul(w1_ref[...], x9_ref[:, cols])

    for plane in range(16):
        bx = (plane + 4) // 8
        pre = summed(plane, 1)
        negative = jnp.exp(jnp.minimum(pre, 0.0))
        if 4 <= plane < 12:
            slope1_ref[:, plane_cols(plane - 4)] = jnp.where(pre > 0, 1.0, negative)
        hidden = jnp.where(pre > 0, pre, negative - 1.0) * masks[bx]
        hidden = hidden.astype(jnp.bfloat16).astype(jnp.float32)
        for c in (-1, 0, 1):
            if c == 0:
                source = hidden
            else:
                source = jnp.where(depth >= 2 if c == 1 else depth <= 5, hidden, 0.0)
            for b in (-1, 0, 1):
                step = 16 * b + 2 * c
                row = (3 * (b + 1) + c + 1) * C
                h9_ref[row : row + C, plane_cols(plane)] = (
                    roll(source, -step) if step else source
                ).astype(jnp.bfloat16)

    for n in range(8):
        cols = slice(256 * n, 256 * (n + 1))
        product_ref[:, cols] = matmul(w2_ref[...], h9_ref[:, cols])

    for plane in range(12):
        bx = (plane + 6) // 8
        pre = summed(plane, 2)
        negative = jnp.exp(jnp.minimum(pre, 0.0))
        slope2_ref[:, plane_cols(plane)] = jnp.where(pre > 0, 1.0, negative) * masks[bx]
        hidden = jnp.where(pre > 0, pre, negative - 1.0) * masks[bx]
        hid2_ref[:, plane_cols(plane)] = hidden.astype(jnp.bfloat16)

    logits = matmul(head, hid2_ref[...])
    targets = []
    for half in range(2):
        row = []
        for bx in range(3):
            parts = [gathered_ref[owner[3 * bx + by], 12].astype(jnp.float32) for by in range(3)]
            before = roll(parts[0], 96 - 64 * half)
            middle = roll(parts[1], 32 - 64 * half)
            after = roll(parts[2], 96 - 64 * half)
            row.append(jnp.where(low, before, jnp.where(mid, middle, after)))
        targets.append(row)
    grads = []
    for plane in range(12):
        bx, i = (plane + 6) // 8, (plane + 6) % 8
        value = logits[:, plane_cols(plane)]
        wanted = targets[i % 2][bx][4 * (i // 2) : 4 * (i // 2) + 4]
        wanted = jnp.concatenate([wanted, jnp.zeros((12, LANES), jnp.float32)], axis=0)
        sigmoid = 1.0 / (1.0 + jnp.exp(-value))
        grads.append((sigmoid - wanted) * masks[bx] * scale)
    for q in range(4):
        first = roll(logits[:, plane_cols(2 + 2 * q)], -32)
        second = roll(logits[:, plane_cols(3 + 2 * q)], 32)
        logits_ref[:, 0, plane_cols(q)] = jnp.where(left_half, first, second)[0:3]

    grad_logit = jnp.concatenate(grads, axis=1).astype(jnp.bfloat16)
    back = matmul(head_t, grad_logit)
    grad2_ref[...] = (back * slope2_ref[...]).astype(jnp.bfloat16)
    own_grads = jnp.concatenate([grads[2 + x] * own_lanes for x in range(8)], axis=1)
    head_part = matmul_lanes(hid2_ref[:, 2 * LANES : 10 * LANES], own_grads.astype(jnp.bfloat16))

    own_bf16 = own_lanes.astype(jnp.bfloat16)
    shifted_ref[...] = jnp.zeros_like(shifted_ref)
    for a in range(3):
        for x in range(8):
            shifted_ref[C * a : C * (a + 1), plane_cols(x + 2 * a)] = (
                grad2_ref[:, plane_cols(x + 2)] * own_bf16
            )
    second_part = matmul_lanes(shifted_ref[...], h9_ref[:, 2 * LANES : 14 * LANES])

    for a in range(3):
        for x in range(8):
            shifted_ref[C * a : C * (a + 1), plane_cols(x)] = grad2_ref[:, plane_cols(x + 4 - 2 * a)]
    for n in range(4):
        cols = slice(256 * n, 256 * (n + 1))
        back_ref[:, cols] = matmul(w2t_ref[...], shifted_ref[:, cols])
    grad1 = []
    for x in range(8):
        total = jnp.zeros((C, LANES), jnp.float32)
        for c in (-1, 0, 1):
            part = jnp.zeros((C, LANES), jnp.float32)
            for b in (-1, 0, 1):
                row = (3 * (b + 1) + c + 1) * C
                step = 16 * b + 2 * c
                piece = back_ref[row : row + C, plane_cols(x)]
                part += roll(piece, step) if step else piece
            if c:
                part = jnp.where(depth >= 2 if c == 1 else depth <= 5, part, 0.0)
            total += part
        grad1.append((total * slope1_ref[:, plane_cols(x)] * own_lanes).astype(jnp.bfloat16))

    shifted_ref[...] = jnp.zeros_like(shifted_ref)
    for a in range(3):
        for x in range(8):
            shifted_ref[C * a : C * (a + 1), plane_cols(x + a)] = grad1[x]
    first_part = matmul_lanes(
        shifted_ref[:, 0 : 10 * LANES], x9_ref[:, 4 * LANES : 14 * LANES]
    )

    for q in range(3):
        cols = plane_cols(q)
        packed_ref[144 * q : 144 * (q + 1), :] = first_part[:, cols].astype(jnp.bfloat16)
        packed_ref[144 * (q + 3) : 144 * (q + 4), :] = second_part[:, cols].astype(jnp.bfloat16)
    head_part = jnp.concatenate([head_part, jnp.zeros((96, 16), jnp.float32)], axis=0)
    tail = jnp.concatenate(
        [first_part[:, 384:], second_part[:, 384:], head_part, jnp.zeros((144, 16), jnp.float32)],
        axis=1,
    )
    packed_ref[144 * 6 : ROWS, :] = tail.astype(jnp.bfloat16)
    packed_ref[ROWS:, :] = jnp.zeros((packed_ref.shape[0] - ROWS, LANES), jnp.bfloat16)


def sum_kernel(parts_ref, out_ref):
    total = parts_ref[0].astype(jnp.float32)
    for s in range(1, parts_ref.shape[0]):
        total += parts_ref[s].astype(jnp.float32)
    total = total.astype(jnp.bfloat16)
    for s in range(out_ref.shape[0]):
        out_ref[s] = total


def unpack_kernel(rows_ref, first_ref, second_ref, head_ref):
    tail = rows_ref[144 * 6 : ROWS, :].astype(jnp.float32)
    for k, out in ((0, first_ref), (1, second_ref)):
        tiles = [rows_ref[144 * (3 * k + q) : 144 * (3 * k + q + 1), :].astype(jnp.float32) for q in range(3)]
        whole = jnp.concatenate(tiles + [tail[:, C * k : C * (k + 1)]], axis=1)
        for a in range(3):
            for t in range(9):
                out[9 * a + t] = whole[C * a : C * (a + 1), C * t : C * (t + 1)]
    head_ref[...] = tail[0:C, 96:112].T[0:3]


def on_device_flat(features, device_block, conv_first, conv_second, head_weight, targets):
    space_count = lax.axis_size("space")
    device_count = lax.axis_size("dp") * space_count
    bf16, f32 = jnp.bfloat16, jnp.float32
    small = pltpu.CompilerParams(vmem_limit_bytes=8 * 1024 * 1024)
    shape = jax.ShapeDtypeStruct
    vmem = pl.BlockSpec(memory_space=pltpu.VMEM)
    smem = pl.BlockSpec(memory_space=pltpu.SMEM)

    packed_block = pl.pallas_call(
        pack_kernel,
        out_shape=shape((13, 16, LANES), bf16),
        in_specs=[vmem] * 2,
        out_specs=vmem,
        compiler_params=small,
        name="pack_block",
    )(features[0, 0], targets[0].transpose(1, 0, 2))
    blocks = [packed_block] + [
        lax.ppermute(packed_block, "space", [(s, s ^ k) for s in range(space_count)])
        for k in range(1, space_count)
    ]

    chunk = -(-ROWS // (16 * device_count)) * 16
    scale = (device_count * 3 * CELLS) ** (-0.5)
    logits, packed = pl.pallas_call(
        functools.partial(crop_kernel, scale, space_count),
        out_shape=(shape((3, 1, CELLS), f32), shape((chunk * device_count, LANES), bf16)),
        in_specs=[smem] + [vmem] * (space_count + 3),
        out_specs=(vmem, vmem),
        scratch_shapes=[
            pltpu.SMEM((10,), jnp.int32),
            pltpu.SMEM((10,), jnp.int32),
            pltpu.VMEM((9 * C, 18 * LANES), bf16),
            pltpu.VMEM((9 * C, 16 * LANES), bf16),
            pltpu.VMEM((3 * C, 18 * LANES), f32),
            pltpu.VMEM((C, 8 * LANES), f32),
            pltpu.VMEM((C, 12 * LANES), f32),
            pltpu.VMEM((C, 12 * LANES), bf16),
            pltpu.VMEM((C, 12 * LANES), bf16),
            pltpu.VMEM((3 * C, 12 * LANES), bf16),
            pltpu.VMEM((9 * C, 8 * LANES), f32),
            pltpu.VMEM((space_count, 13, 16, LANES), bf16),
            pltpu.VMEM((3 * C, 9 * C), bf16),
            pltpu.VMEM((3 * C, 9 * C), bf16),
            pltpu.VMEM((9 * C, 3 * C), bf16),
        ],
        compiler_params=pltpu.CompilerParams(vmem_limit_bytes=20 * 1024 * 1024),
        name="forward_backward",
    )(
        device_block,
        *blocks,
        conv_first.transpose(1, 0, 2),
        conv_second.transpose(1, 0, 2),
        head_weight,
    )

    terms = lax.all_to_all(
        packed.reshape(device_count, chunk, LANES), ("dp", "space"), 0, 0, tiled=True
    )
    summed = pl.pallas_call(
        sum_kernel,
        out_shape=shape((device_count, chunk, LANES), bf16),
        in_specs=[vmem],
        out_specs=vmem,
        compiler_params=small,
        name="sum_terms",
    )(terms)
    rows = lax.all_to_all(summed, ("dp", "space"), 0, 0, tiled=True)
    grad_first, grad_second, grad_head = pl.pallas_call(
        unpack_kernel,
        out_shape=(shape((27, C, C), f32), shape((27, C, C), f32), shape((3, C), f32)),
        in_specs=[vmem],
        out_specs=(vmem,) * 3,
        compiler_params=small,
        name="unpack_gradients",
    )(rows.reshape(device_count * chunk, LANES))
    return (
        logits.transpose(1, 0, 2)[None],
        grad_first.transpose(1, 0, 2),
        grad_second.transpose(1, 0, 2),
        grad_head,
    )


def solution(mesh):
    in_specs = (
        P("dp", "space", None, None),
        P("dp", None),
        P(),
        P(),
        P(),
        P("dp", "space", None, None),
    )
    out_specs = (P("dp", "space", None, None), P(), P(), P())
    depth_z = mesh.shape["space"] // 8
    return jax.shard_map(
        on_device_flat if depth_z == 1 else on_device_deep,
        mesh=mesh,
        in_specs=in_specs,
        out_specs=out_specs,
        check_vma=False,
    )
```

```python
import functools

import jax
import jax.numpy as jnp
from jax import lax
from jax.experimental import pallas as pl
from jax.experimental.pallas import tpu as pltpu
from jax.sharding import PartitionSpec as P

BS = 8


tap_offsets = [
    (tap_index // 9 - 1, tap_index // 3 % 3 - 1, tap_index % 3 - 1) for tap_index in range(27)
]


def elu_pair(values):
    negative = jnp.exp(jnp.minimum(values, 0.0))
    return (jnp.where(values > 0, values, negative - 1.0), jnp.where(values > 0, 1.0, negative))


def neighbor_tables(device_block):
    space_count = lax.axis_size("space")
    depth_z = space_count // 8
    self_index = lax.axis_index("space")
    blocks = device_block[0]
    coords = jnp.stack([blocks // (4 * depth_z), blocks // depth_z % 4, blocks % depth_z])
    own_coords = lax.dynamic_index_in_dim(coords, self_index, 1, keepdims=False)
    offsets = jnp.array(tap_offsets, jnp.int32)
    limits = jnp.array([4, 4, depth_z], jnp.int32)
    wanted = own_coords[None, :] + offsets
    inside = jnp.all((wanted >= 0) & (wanted < limits[None, :]), axis=1) & (jnp.arange(27) != 13)
    wanted_id = (wanted[:, 0] * 4 + wanted[:, 1]) * depth_z + wanted[:, 2]
    matches = (blocks[None, :] == wanted_id[:, None]) & inside[:, None]
    devices = jnp.arange(space_count, dtype=jnp.int32)
    owner_row = jnp.sum(jnp.where(matches, devices[None, :], 0), axis=1)
    present = jnp.any(matches, axis=1)
    relative = coords - own_coords[:, None]
    adjacent = jnp.all(jnp.abs(relative) <= 1, axis=0) & (devices != self_index)
    send_tap = jnp.where(
        adjacent, (relative[0] + 1) * 9 + (relative[1] + 1) * 3 + relative[2] + 1, 13
    )
    return (owner_row, present, send_tap)


def region_slice(block_data, offset, depth_cells):
    span_list = []
    for step_value in offset:
        if step_value == 1:
            span_list.append(slice(BS - depth_cells, BS))
        elif step_value == -1:
            span_list.append(slice(0, depth_cells))
        else:
            span_list.append(slice(0, BS))
    return block_data[:, span_list[0], span_list[1], span_list[2]]


def surround(block_data, depth_cells, tables):
    owner_row, present, send_tap = tables
    channels = block_data.shape[0]
    length = depth_cells * BS * BS
    pieces = []
    for tap_index in range(27):
        if tap_index == 13:
            pieces.append(jnp.zeros((channels, length), block_data.dtype))
        else:
            region = region_slice(block_data, tap_offsets[tap_index], depth_cells).reshape(
                channels, -1
            )
            pieces.append(jnp.pad(region, ((0, 0), (0, length - region.shape[1]))))
    outgoing = jnp.stack(pieces)
    sending = outgoing[send_tap]
    by_source = lax.all_to_all(sending, "space", split_axis=0, concat_axis=0, tiled=True)
    incoming = jnp.where(
        present[:, None, None], by_source[owner_row], jnp.zeros((), block_data.dtype)
    )
    rows_x = []
    for step_x in range(3):
        rows_y = []
        for step_y in range(3):
            rows_z = []
            for step_z in range(3):
                tap_index = step_x * 9 + step_y * 3 + step_z
                if tap_index == 13:
                    rows_z.append(block_data)
                else:
                    extent_list = [
                        BS if step_value == 1 else depth_cells
                        for step_value in (step_x, step_y, step_z)
                    ]
                    count_cells = extent_list[0] * extent_list[1] * extent_list[2]
                    rows_z.append(
                        incoming[tap_index][:, :count_cells].reshape(
                            channels, extent_list[0], extent_list[1], extent_list[2]
                        )
                    )
            rows_y.append(jnp.concatenate(rows_z, axis=3))
        rows_x.append(jnp.concatenate(rows_y, axis=2))
    return jnp.concatenate(rows_x, axis=1)


def conv_padded(padded, kernel, dilation):
    result = lax.conv_general_dilated(
        padded[None],
        kernel,
        (1, 1, 1),
        "VALID",
        rhs_dilation=(dilation, dilation, dilation),
        dimension_numbers=("NCDHW", "OIDHW", "NCDHW"),
        preferred_element_type=jnp.float32,
    )
    return result[0].reshape(kernel.shape[0], BS * BS * BS)


def kernel_grad(padded, grad_rows, dilation):
    channels = padded.shape[0]
    outputs = grad_rows.shape[0]
    grad_block = grad_rows.reshape(outputs, 1, BS, BS, BS)
    result = lax.conv_general_dilated(
        padded[None],
        grad_block,
        (dilation, dilation, dilation),
        "VALID",
        dimension_numbers=("CNDHW", "OIDHW", "NCDHW"),
        preferred_element_type=jnp.float32,
    )
    return result.reshape(channels, outputs, 27).transpose(1, 2, 0)


def on_device_deep(features, device_block, conv_first, conv_second, head_weight, targets):
    channels = features.shape[2]
    tables = neighbor_tables(device_block)
    kernel_first = conv_first.reshape(channels, 3, 3, 3, channels).transpose(0, 4, 1, 2, 3)
    kernel_second = conv_second.reshape(channels, 3, 3, 3, channels).transpose(0, 4, 1, 2, 3)
    block_in = features[0, 0].reshape(channels, BS, BS, BS)
    padded_in = surround(block_in, 1, tables)
    pre_first = conv_padded(padded_in, kernel_first, 1)
    act_first, slope_first = elu_pair(pre_first)
    hid_first = act_first.astype(jnp.bfloat16)
    padded_first = surround(hid_first.reshape(channels, BS, BS, BS), 2, tables)
    pre_second = conv_padded(padded_first, kernel_second, 2)
    act_second, slope_second = elu_pair(pre_second)
    hid_second = act_second.astype(jnp.bfloat16)
    logits = jnp.dot(head_weight, hid_second, preferred_element_type=jnp.float32)
    scale = (lax.axis_size("dp") * lax.axis_size("space") * 3 * BS * BS * BS) ** (-0.5)
    grad_logit = ((jax.nn.sigmoid(logits) - targets[0, 0].astype(jnp.float32)) * scale).astype(
        jnp.bfloat16
    )
    grad_head = lax.dot_general(
        grad_logit, hid_second, (((1,), (1,)), ((), ())), preferred_element_type=jnp.float32
    )
    back_second = lax.dot_general(
        head_weight, grad_logit, (((0,), (0,)), ((), ())), preferred_element_type=jnp.float32
    )
    grad_pre_second = (back_second * slope_second).astype(jnp.bfloat16)
    grad_second = kernel_grad(padded_first, grad_pre_second, 2)
    padded_grad = surround(grad_pre_second.reshape(channels, BS, BS, BS), 2, tables)
    kernel_back = jnp.transpose(kernel_second[:, :, ::-1, ::-1, ::-1], (1, 0, 2, 3, 4))
    back_first = conv_padded(padded_grad, kernel_back, 2)
    grad_pre_first = (back_first * slope_first).astype(jnp.bfloat16)
    grad_first = kernel_grad(padded_in, grad_pre_first, 1)
    grad_first, grad_second, grad_head = lax.psum(
        (grad_first, grad_second, grad_head), ("dp", "space")
    )
    return (logits[None, None], grad_first, grad_second, grad_head)


C = 48
CELLS = 512
HALF = 512
LANES = 128


def lanes(rows=1):
    return lax.broadcasted_iota(jnp.int32, (rows, LANES), 1)


def pack_kernel(features_ref, targets_ref, out_ref):
    targets = targets_ref[:, 0, :].astype(jnp.float32)
    targets = jnp.concatenate([targets, jnp.zeros((1, CELLS), jnp.float32)], axis=0)
    pieces = [targets[:, LANES * q : LANES * (q + 1)] for q in range(4)]
    target_tile = jnp.concatenate(pieces, axis=0).astype(jnp.bfloat16)
    for ct in range(3):
        for q in range(4):
            out_ref[4 * ct + q] = features_ref[
                16 * ct : 16 * (ct + 1), LANES * q : LANES * (q + 1)
            ]
    out_ref[12] = target_tile


def stacked_taps(ref):
    rows = []
    for a in range(3):
        taps = [ref[9 * a + t].astype(jnp.float32) for t in range(9)]
        rows.append(jnp.concatenate(taps, axis=1))
    return jnp.concatenate(rows, axis=0)


def weights_kernel(
    block_ref, first_ref, second_ref, head_ref, table_ref, w1_ref, w2_ref, w2t_ref, h_ref, ht_ref
):
    me = lax.axis_index("space")
    own = block_ref[0, me]
    for slot in range(10):
        table_ref[0, slot] = 0
        table_ref[1, slot] = 0
    for s in range(block_ref.shape[1]):
        block = block_ref[0, s]
        dx = (block >> 2) - (own >> 2) + 1
        dy = (block & 3) - (own & 3) + 1
        near = (dx >= 0) & (dx <= 2) & (dy >= 0) & (dy <= 2)
        slot = jnp.where(near, dx * 3 + dy, 9)
        table_ref[0, slot] = s ^ me
        table_ref[1, slot] = 1
    w1_ref[...] = stacked_taps(first_ref).astype(jnp.bfloat16)
    whole = stacked_taps(second_ref)
    w2_ref[...] = whole.astype(jnp.bfloat16)
    w2t_ref[...] = whole.T.astype(jnp.bfloat16)
    head = head_ref[...].astype(jnp.float32)
    head = jnp.concatenate([head, jnp.zeros((13, C), jnp.float32)], axis=0)
    h_ref[...] = head.astype(jnp.bfloat16)
    ht_ref[...] = head.T.astype(jnp.bfloat16)


def matmul(left, right):
    return lax.dot_general(
        left, right, (((1,), (0,)), ((), ())), preferred_element_type=jnp.float32
    )


def matmul_lanes(left, right):
    return lax.dot_general(
        left, right, (((1,), (1,)), ((), ())), preferred_element_type=jnp.float32
    )


def roll(values, shift):
    return pltpu.roll(values, shift % LANES, 1)


def crop_kernel(scale, count, table_ref, *refs):
    crop_body(scale, table_ref, refs[:count], *refs[count:])


def crop_body(
    scale,
    table_ref,
    blocks,
    w1_ref,
    w2_ref,
    w2t_ref,
    h_ref,
    ht_ref,
    logits_ref,
    keep_ref,
    send_ref,
    gathered_ref,
    x9_ref,
    h9_ref,
    product_ref,
    slope1_ref,
    slope2_ref,
    hid2_ref,
    grad2_ref,
    shifted_ref,
    back_ref,
):
    for k, block in enumerate(blocks):
        gathered_ref[k] = block[...]

    owner = [table_ref[0, q] for q in range(9)]
    there = [table_ref[1, q].astype(jnp.float32) for q in range(9)]

    lane = lanes()
    depth = lane & 7
    low, mid = lane < 32, lane < 96
    own_lanes = ((lane >= 32) & (lane < 96)).astype(jnp.float32)
    left_half = lane < 64
    masks = [
        jnp.where(low, there[3 * bx], jnp.where(mid, there[3 * bx + 1], there[3 * bx + 2]))
        for bx in range(3)
    ]
    edge_masks = [jnp.where(left_half, there[3 * bx + 2], there[3 * bx]) for bx in range(3)]

    for plane in range(18):
        bx, i = (plane + 3) // 8, (plane + 3) % 8
        q, half = i // 2, i % 2
        for ct in range(3):
            parts = [
                gathered_ref[owner[3 * bx + by], 4 * ct + q].astype(jnp.float32) for by in range(3)
            ]
            before = roll(parts[0], 96 - 64 * half)
            middle = roll(parts[1], 32 - 64 * half)
            after = roll(parts[2], 96 - 64 * half)
            main = jnp.where(low, before, jnp.where(mid, middle, after)) * masks[bx]
            edge = jnp.where(left_half, after, before) * edge_masks[bx]
            for c in (-1, 0, 1):
                if c == 0:
                    main_c, edge_c = main, edge
                else:
                    keep = depth >= 1 if c == 1 else depth <= 6
                    main_c, edge_c = jnp.where(keep, main, 0.0), jnp.where(keep, edge, 0.0)
                for b in (-1, 0, 1):
                    step = 8 * b + c
                    if b == 1:
                        source = jnp.where(lane < step, edge_c, main_c)
                    elif b == -1:
                        source = jnp.where(lane >= LANES + step, edge_c, main_c)
                    else:
                        source = main_c
                    row = (3 * (b + 1) + c + 1) * C + 16 * ct
                    x9_ref[row : row + 16, LANES * plane : LANES * (plane + 1)] = (
                        roll(source, -step) if step else source
                    ).astype(jnp.bfloat16)

    def plane_cols(plane):
        return slice(LANES * plane, LANES * (plane + 1))

    def summed(plane, stride):
        return (
            product_ref[0:C, plane_cols(plane)]
            + product_ref[C : 2 * C, plane_cols(plane + stride)]
            + product_ref[2 * C : 3 * C, plane_cols(plane + 2 * stride)]
        )

    for n in range(9):
        cols = slice(256 * n, 256 * (n + 1))
        product_ref[:, cols] = matmul(w1_ref[...], x9_ref[:, cols])

    for plane in range(16):
        bx = (plane + 4) // 8
        pre = summed(plane, 1)
        negative = jnp.exp(jnp.minimum(pre, 0.0))
        if 4 <= plane < 12:
            slope1_ref[:, plane_cols(plane - 4)] = jnp.where(pre > 0, 1.0, negative)
        hidden = jnp.where(pre > 0, pre, negative - 1.0) * masks[bx]
        hidden = hidden.astype(jnp.bfloat16).astype(jnp.float32)
        for c in (-1, 0, 1):
            if c == 0:
                source = hidden
            else:
                source = jnp.where(depth >= 2 if c == 1 else depth <= 5, hidden, 0.0)
            for b in (-1, 0, 1):
                step = 16 * b + 2 * c
                row = (3 * (b + 1) + c + 1) * C
                h9_ref[row : row + C, plane_cols(plane)] = (
                    roll(source, -step) if step else source
                ).astype(jnp.bfloat16)

    for n in range(8):
        cols = slice(256 * n, 256 * (n + 1))
        product_ref[:, cols] = matmul(w2_ref[...], h9_ref[:, cols])

    for plane in range(12):
        bx = (plane + 6) // 8
        pre = summed(plane, 2)
        negative = jnp.exp(jnp.minimum(pre, 0.0))
        slope2_ref[:, plane_cols(plane)] = jnp.where(pre > 0, 1.0, negative) * masks[bx]
        hidden = jnp.where(pre > 0, pre, negative - 1.0) * masks[bx]
        hid2_ref[:, plane_cols(plane)] = hidden.astype(jnp.bfloat16)

    logits = matmul(h_ref[...], hid2_ref[...])
    targets = []
    for half in range(2):
        row = []
        for bx in range(3):
            parts = [gathered_ref[owner[3 * bx + by], 12].astype(jnp.float32) for by in range(3)]
            before = roll(parts[0], 96 - 64 * half)
            middle = roll(parts[1], 32 - 64 * half)
            after = roll(parts[2], 96 - 64 * half)
            row.append(jnp.where(low, before, jnp.where(mid, middle, after)))
        targets.append(row)
    grads = []
    for plane in range(12):
        bx, i = (plane + 6) // 8, (plane + 6) % 8
        value = logits[:, plane_cols(plane)]
        wanted = targets[i % 2][bx][4 * (i // 2) : 4 * (i // 2) + 4]
        wanted = jnp.concatenate([wanted, jnp.zeros((12, LANES), jnp.float32)], axis=0)
        sigmoid = 1.0 / (1.0 + jnp.exp(-value))
        grads.append((sigmoid - wanted) * masks[bx] * scale)
    for q in range(4):
        first = roll(logits[:, plane_cols(2 + 2 * q)], -32)
        second = roll(logits[:, plane_cols(3 + 2 * q)], 32)
        logits_ref[:, 0, plane_cols(q)] = jnp.where(left_half, first, second)[0:3]

    grad_logit = jnp.concatenate(grads, axis=1).astype(jnp.bfloat16)
    back = matmul(ht_ref[...], grad_logit)
    grad2_ref[...] = (back * slope2_ref[...]).astype(jnp.bfloat16)
    own_grads = jnp.concatenate([grads[2 + x] * own_lanes for x in range(8)], axis=1)
    head_part = matmul_lanes(hid2_ref[:, 2 * LANES : 10 * LANES], own_grads.astype(jnp.bfloat16))

    own_bf16 = own_lanes.astype(jnp.bfloat16)
    shifted_ref[...] = jnp.zeros_like(shifted_ref)
    for a in range(3):
        for x in range(8):
            shifted_ref[C * a : C * (a + 1), plane_cols(x + 2 * a)] = (
                grad2_ref[:, plane_cols(x + 2)] * own_bf16
            )
    second_part = matmul_lanes(shifted_ref[...], h9_ref[:, 2 * LANES : 14 * LANES])

    for a in range(3):
        for x in range(8):
            shifted_ref[C * a : C * (a + 1), plane_cols(x)] = grad2_ref[:, plane_cols(x + 4 - 2 * a)]
    for n in range(4):
        cols = slice(256 * n, 256 * (n + 1))
        back_ref[:, cols] = matmul(w2t_ref[...], shifted_ref[:, cols])
    grad1 = []
    for x in range(8):
        total = jnp.zeros((C, LANES), jnp.float32)
        for c in (-1, 0, 1):
            part = jnp.zeros((C, LANES), jnp.float32)
            for b in (-1, 0, 1):
                row = (3 * (b + 1) + c + 1) * C
                step = 16 * b + 2 * c
                piece = back_ref[row : row + C, plane_cols(x)]
                part += roll(piece, step) if step else piece
            if c:
                part = jnp.where(depth >= 2 if c == 1 else depth <= 5, part, 0.0)
            total += part
        grad1.append((total * slope1_ref[:, plane_cols(x)] * own_lanes).astype(jnp.bfloat16))

    shifted_ref[...] = jnp.zeros_like(shifted_ref)
    for a in range(3):
        for x in range(8):
            shifted_ref[C * a : C * (a + 1), plane_cols(x + a)] = grad1[x]
    first_part = matmul_lanes(
        shifted_ref[:, 0 : 10 * LANES], x9_ref[:, 4 * LANES : 14 * LANES]
    )

    first_core = (lax.axis_index("dp") & 1) == 0
    for q in range(3):
        rows, cols = slice(144 * q, 144 * (q + 1)), plane_cols(q)
        keep_ref[rows, :] = jnp.where(first_core, first_part[:, cols], second_part[:, cols])
        send_ref[rows, :] = jnp.where(first_core, second_part[:, cols], first_part[:, cols])
    head_part = jnp.concatenate([head_part, jnp.zeros((24, 16), jnp.float32)], axis=0)
    nothing = jnp.zeros((72, 16), jnp.float32)
    tails = [
        jnp.concatenate([part[0:72, 384:], part[72:144, 384:], extra, nothing], axis=1)
        for part, extra in ((first_part, nothing), (second_part, head_part))
    ]
    keep_ref[432:504, :] = jnp.where(first_core, tails[0], tails[1])
    send_ref[432:504, :] = jnp.where(first_core, tails[1], tails[0])
    keep_ref[504:HALF, :] = jnp.zeros((HALF - 504, LANES), jnp.float32)
    send_ref[504:HALF, :] = jnp.zeros((HALF - 504, LANES), jnp.float32)


def side_position():
    return (lax.axis_index("dp") >> 1) * 2 + (lax.axis_index("space") & 1)


def deal_kernel(position, parts, *refs):
    terms, (own_ref, *sends) = refs[:parts], refs[parts:]
    own = position()
    quarter = own_ref.shape[0]
    for k, out_ref in enumerate([own_ref] + sends):
        rows = pl.ds(pl.multiple_of((own ^ k) * quarter, quarter), quarter)
        total = terms[0][rows, :].astype(jnp.float32)
        for term in terms[1:]:
            total += term[rows, :].astype(jnp.float32)
        out_ref[...] = total.astype(out_ref.dtype)


def add_kernel(*refs):
    total = refs[0][...].astype(jnp.float32)
    for ref in refs[1:-1]:
        total += ref[...].astype(jnp.float32)
    refs[-1][...] = total.astype(refs[-1].dtype)


def join_kernel(position, *refs):
    parts, out_ref = refs[:-1], refs[-1]
    own = position()
    quarter = parts[0].shape[0]
    for k, part in enumerate(parts):
        rows = pl.ds(pl.multiple_of((own ^ k) * quarter, quarter), quarter)
        out_ref[rows, :] = part[...]


def unpack_kernel(mine_ref, other_ref, first_ref, second_ref, head_ref):
    first_core = (lax.axis_index("dp") & 1) == 0
    mine = mine_ref[...].astype(jnp.float32)
    other = other_ref[...].astype(jnp.float32)
    for k, out in ((0, first_ref), (1, second_ref)):
        half = jnp.where(first_core, other if k else mine, mine if k else other)
        tail = jnp.concatenate([half[432:504, 0:C], half[432:504, C : 2 * C]], axis=0)
        tiles = [half[144 * q : 144 * (q + 1), :] for q in range(3)]
        whole = jnp.concatenate(tiles + [tail], axis=1)
        for a in range(3):
            for t in range(9):
                out[9 * a + t] = whole[C * a : C * (a + 1), C * t : C * (t + 1)]
        if k:
            head_ref[...] = half[432 : 432 + C, 96:112].T[0:3]


def on_device_flat(features, device_block, conv_first, conv_second, head_weight, targets):
    space_count = lax.axis_size("space")
    device_count = lax.axis_size("dp") * space_count
    bf16, f32 = jnp.bfloat16, jnp.float32
    small = pltpu.CompilerParams(vmem_limit_bytes=8 * 1024 * 1024)
    shape = jax.ShapeDtypeStruct
    vmem = pl.BlockSpec(memory_space=pltpu.VMEM)
    smem = pl.BlockSpec(memory_space=pltpu.SMEM)

    packed_block = pl.pallas_call(
        pack_kernel,
        out_shape=shape((13, 16, LANES), bf16),
        in_specs=[vmem] * 2,
        out_specs=vmem,
        compiler_params=small,
        name="pack_block",
    )(features[0, 0], targets[0].transpose(1, 0, 2))
    blocks = [packed_block] + [
        lax.ppermute(packed_block, "space", [(s, s ^ k) for s in range(space_count)])
        for k in range(1, space_count)
    ]

    table, w1, w2, w2t, head, head_t = pl.pallas_call(
        weights_kernel,
        out_shape=(
            shape((2, 16), jnp.int32),
            shape((3 * C, 9 * C), bf16),
            shape((3 * C, 9 * C), bf16),
            shape((9 * C, 3 * C), bf16),
            shape((16, C), bf16),
            shape((C, 16), bf16),
        ),
        in_specs=[smem] + [vmem] * 3,
        out_specs=(smem,) + (vmem,) * 5,
        compiler_params=small,
        cost_estimate=pl.CostEstimate(flops=2_000_000, bytes_accessed=4_000_000, transcendentals=0),
        name="lay_out_weights",
    )(device_block, conv_first.transpose(1, 0, 2), conv_second.transpose(1, 0, 2), head_weight)

    scale = (device_count * 3 * CELLS) ** (-0.5)
    logits, keep, send = pl.pallas_call(
        functools.partial(crop_kernel, scale, space_count),
        out_shape=(shape((3, 1, CELLS), f32), shape((HALF, LANES), f32), shape((HALF, LANES), f32)),
        in_specs=[smem] + [vmem] * (space_count + 5),
        out_specs=(vmem,) * 3,
        scratch_shapes=[
            pltpu.VMEM((space_count, 13, 16, LANES), bf16),
            pltpu.VMEM((9 * C, 18 * LANES), bf16),
            pltpu.VMEM((9 * C, 16 * LANES), bf16),
            pltpu.VMEM((3 * C, 18 * LANES), f32),
            pltpu.VMEM((C, 8 * LANES), f32),
            pltpu.VMEM((C, 12 * LANES), f32),
            pltpu.VMEM((C, 12 * LANES), bf16),
            pltpu.VMEM((C, 12 * LANES), bf16),
            pltpu.VMEM((3 * C, 12 * LANES), bf16),
            pltpu.VMEM((9 * C, 8 * LANES), f32),
        ],
        compiler_params=pltpu.CompilerParams(vmem_limit_bytes=20 * 1024 * 1024),
        name="forward_backward",
    )(table, *blocks, w1, w2, w2t, head, head_t)

    def swap(values, mask):
        return lax.ppermute(values, ("dp", "space"), [(s, s ^ mask) for s in range(device_count)])

    def step(kernel, outs, *operands):
        return pl.pallas_call(
            kernel,
            out_shape=outs,
            in_specs=[vmem] * len(operands),
            out_specs=jax.tree.map(lambda _: vmem, outs),
            compiler_params=small,
            name="gradient_sum",
        )(*operands)

    core, y, x, z = space_count, 2 * space_count, 1, 2
    sides, depths = (x, y, x ^ y), (z, 2 * z, 3 * z)
    depth_position = lambda: lax.axis_index("space") >> 1

    quarter, piece = HALF // 4, HALF // 16
    other = swap(send, core)
    own, *sends = step(
        functools.partial(deal_kernel, side_position, 2),
        [shape((quarter, LANES), f32)] + [shape((quarter, LANES), bf16)] * 3,
        keep,
        other,
    )
    terms = [swap(part, mask) for part, mask in zip(sends, sides)]
    own, *sends = step(
        functools.partial(deal_kernel, depth_position, 4),
        [shape((piece, LANES), f32)] * 4,
        own,
        *terms,
    )
    terms = [swap(part, mask) for part, mask in zip(sends, depths)]
    total = step(add_kernel, shape((piece, LANES), bf16), own, *terms)
    total = step(
        functools.partial(join_kernel, depth_position),
        shape((quarter, LANES), bf16),
        total,
        *[swap(total, mask) for mask in depths],
    )
    total = step(
        functools.partial(join_kernel, side_position),
        shape((HALF, LANES), bf16),
        total,
        *[swap(total, mask) for mask in sides],
    )
    grad_first, grad_second, grad_head = pl.pallas_call(
        unpack_kernel,
        out_shape=(shape((27, C, C), f32), shape((27, C, C), f32), shape((3, C), f32)),
        in_specs=[vmem] * 2,
        out_specs=(vmem,) * 3,
        compiler_params=small,
        name="unpack_gradients",
    )(total, swap(total, core))
    return (
        logits.transpose(1, 0, 2)[None],
        grad_first.transpose(1, 0, 2),
        grad_second.transpose(1, 0, 2),
        grad_head,
    )


def solution(mesh):
    in_specs = (
        P("dp", "space", None, None),
        P("dp", None),
        P(),
        P(),
        P(),
        P("dp", "space", None, None),
    )
    out_specs = (P("dp", "space", None, None), P(), P(), P())
    flat = mesh.shape["space"] == 8 and mesh.shape["dp"] == 4
    return jax.shard_map(
        on_device_flat if flat else on_device_deep,
        mesh=mesh,
        in_specs=in_specs,
        out_specs=out_specs,
        check_vma=False,
    )
```

```python
import functools

import jax
import jax.numpy as jnp
from jax import lax
from jax.experimental import pallas as pl
from jax.experimental.pallas import tpu as pltpu
from jax.sharding import PartitionSpec as P

BS = 8


tap_offsets = [
    (tap_index // 9 - 1, tap_index // 3 % 3 - 1, tap_index % 3 - 1) for tap_index in range(27)
]


def elu_pair(values):
    negative = jnp.exp(jnp.minimum(values, 0.0))
    return (jnp.where(values > 0, values, negative - 1.0), jnp.where(values > 0, 1.0, negative))


def neighbor_tables(device_block):
    space_count = lax.axis_size("space")
    depth_z = space_count // 8
    self_index = lax.axis_index("space")
    blocks = device_block[0]
    coords = jnp.stack([blocks // (4 * depth_z), blocks // depth_z % 4, blocks % depth_z])
    own_coords = lax.dynamic_index_in_dim(coords, self_index, 1, keepdims=False)
    offsets = jnp.array(tap_offsets, jnp.int32)
    limits = jnp.array([4, 4, depth_z], jnp.int32)
    wanted = own_coords[None, :] + offsets
    inside = jnp.all((wanted >= 0) & (wanted < limits[None, :]), axis=1) & (jnp.arange(27) != 13)
    wanted_id = (wanted[:, 0] * 4 + wanted[:, 1]) * depth_z + wanted[:, 2]
    matches = (blocks[None, :] == wanted_id[:, None]) & inside[:, None]
    devices = jnp.arange(space_count, dtype=jnp.int32)
    owner_row = jnp.sum(jnp.where(matches, devices[None, :], 0), axis=1)
    present = jnp.any(matches, axis=1)
    relative = coords - own_coords[:, None]
    adjacent = jnp.all(jnp.abs(relative) <= 1, axis=0) & (devices != self_index)
    send_tap = jnp.where(
        adjacent, (relative[0] + 1) * 9 + (relative[1] + 1) * 3 + relative[2] + 1, 13
    )
    return (owner_row, present, send_tap)


def region_slice(block_data, offset, depth_cells):
    span_list = []
    for step_value in offset:
        if step_value == 1:
            span_list.append(slice(BS - depth_cells, BS))
        elif step_value == -1:
            span_list.append(slice(0, depth_cells))
        else:
            span_list.append(slice(0, BS))
    return block_data[:, span_list[0], span_list[1], span_list[2]]


def surround(block_data, depth_cells, tables):
    owner_row, present, send_tap = tables
    channels = block_data.shape[0]
    length = depth_cells * BS * BS
    pieces = []
    for tap_index in range(27):
        if tap_index == 13:
            pieces.append(jnp.zeros((channels, length), block_data.dtype))
        else:
            region = region_slice(block_data, tap_offsets[tap_index], depth_cells).reshape(
                channels, -1
            )
            pieces.append(jnp.pad(region, ((0, 0), (0, length - region.shape[1]))))
    outgoing = jnp.stack(pieces)
    sending = outgoing[send_tap]
    by_source = lax.all_to_all(sending, "space", split_axis=0, concat_axis=0, tiled=True)
    incoming = jnp.where(
        present[:, None, None], by_source[owner_row], jnp.zeros((), block_data.dtype)
    )
    rows_x = []
    for step_x in range(3):
        rows_y = []
        for step_y in range(3):
            rows_z = []
            for step_z in range(3):
                tap_index = step_x * 9 + step_y * 3 + step_z
                if tap_index == 13:
                    rows_z.append(block_data)
                else:
                    extent_list = [
                        BS if step_value == 1 else depth_cells
                        for step_value in (step_x, step_y, step_z)
                    ]
                    count_cells = extent_list[0] * extent_list[1] * extent_list[2]
                    rows_z.append(
                        incoming[tap_index][:, :count_cells].reshape(
                            channels, extent_list[0], extent_list[1], extent_list[2]
                        )
                    )
            rows_y.append(jnp.concatenate(rows_z, axis=3))
        rows_x.append(jnp.concatenate(rows_y, axis=2))
    return jnp.concatenate(rows_x, axis=1)


def conv_padded(padded, kernel, dilation):
    result = lax.conv_general_dilated(
        padded[None],
        kernel,
        (1, 1, 1),
        "VALID",
        rhs_dilation=(dilation, dilation, dilation),
        dimension_numbers=("NCDHW", "OIDHW", "NCDHW"),
        preferred_element_type=jnp.float32,
    )
    return result[0].reshape(kernel.shape[0], BS * BS * BS)


def kernel_grad(padded, grad_rows, dilation):
    channels = padded.shape[0]
    outputs = grad_rows.shape[0]
    grad_block = grad_rows.reshape(outputs, 1, BS, BS, BS)
    result = lax.conv_general_dilated(
        padded[None],
        grad_block,
        (dilation, dilation, dilation),
        "VALID",
        dimension_numbers=("CNDHW", "OIDHW", "NCDHW"),
        preferred_element_type=jnp.float32,
    )
    return result.reshape(channels, outputs, 27).transpose(1, 2, 0)


def on_device_deep(features, device_block, conv_first, conv_second, head_weight, targets):
    channels = features.shape[2]
    tables = neighbor_tables(device_block)
    kernel_first = conv_first.reshape(channels, 3, 3, 3, channels).transpose(0, 4, 1, 2, 3)
    kernel_second = conv_second.reshape(channels, 3, 3, 3, channels).transpose(0, 4, 1, 2, 3)
    block_in = features[0, 0].reshape(channels, BS, BS, BS)
    padded_in = surround(block_in, 1, tables)
    pre_first = conv_padded(padded_in, kernel_first, 1)
    act_first, slope_first = elu_pair(pre_first)
    hid_first = act_first.astype(jnp.bfloat16)
    padded_first = surround(hid_first.reshape(channels, BS, BS, BS), 2, tables)
    pre_second = conv_padded(padded_first, kernel_second, 2)
    act_second, slope_second = elu_pair(pre_second)
    hid_second = act_second.astype(jnp.bfloat16)
    logits = jnp.dot(head_weight, hid_second, preferred_element_type=jnp.float32)
    scale = (lax.axis_size("dp") * lax.axis_size("space") * 3 * BS * BS * BS) ** (-0.5)
    grad_logit = ((jax.nn.sigmoid(logits) - targets[0, 0].astype(jnp.float32)) * scale).astype(
        jnp.bfloat16
    )
    grad_head = lax.dot_general(
        grad_logit, hid_second, (((1,), (1,)), ((), ())), preferred_element_type=jnp.float32
    )
    back_second = lax.dot_general(
        head_weight, grad_logit, (((0,), (0,)), ((), ())), preferred_element_type=jnp.float32
    )
    grad_pre_second = (back_second * slope_second).astype(jnp.bfloat16)
    grad_second = kernel_grad(padded_first, grad_pre_second, 2)
    padded_grad = surround(grad_pre_second.reshape(channels, BS, BS, BS), 2, tables)
    kernel_back = jnp.transpose(kernel_second[:, :, ::-1, ::-1, ::-1], (1, 0, 2, 3, 4))
    back_first = conv_padded(padded_grad, kernel_back, 2)
    grad_pre_first = (back_first * slope_first).astype(jnp.bfloat16)
    grad_first = kernel_grad(padded_in, grad_pre_first, 1)
    grad_first, grad_second, grad_head = lax.psum(
        (grad_first, grad_second, grad_head), ("dp", "space")
    )
    return (logits[None, None], grad_first, grad_second, grad_head)


C = 48
CELLS = 512
HALF = 512
LANES = 128


def lanes(rows=1):
    return lax.broadcasted_iota(jnp.int32, (rows, LANES), 1)


def pack_kernel(features_ref, targets_ref, out_ref):
    targets = targets_ref[:, 0, :].astype(jnp.float32)
    targets = jnp.concatenate([targets, jnp.zeros((1, CELLS), jnp.float32)], axis=0)
    pieces = [targets[:, LANES * q : LANES * (q + 1)] for q in range(4)]
    target_tile = jnp.concatenate(pieces, axis=0).astype(jnp.bfloat16)
    for ct in range(3):
        for q in range(4):
            out_ref[4 * ct + q] = features_ref[
                16 * ct : 16 * (ct + 1), LANES * q : LANES * (q + 1)
            ]
    out_ref[12] = target_tile


def stacked_taps(ref):
    rows = []
    for a in range(3):
        taps = [ref[9 * a + t].astype(jnp.float32) for t in range(9)]
        rows.append(jnp.concatenate(taps, axis=1))
    return jnp.concatenate(rows, axis=0)


def weights_kernel(
    block_ref, first_ref, second_ref, head_ref, table_ref, w1_ref, w2_ref, w2t_ref, h_ref, ht_ref
):
    me = lax.axis_index("space")
    own = block_ref[0, me]
    for slot in range(10):
        table_ref[0, slot] = 0
        table_ref[1, slot] = 0
    for s in range(block_ref.shape[1]):
        block = block_ref[0, s]
        dx = (block >> 2) - (own >> 2) + 1
        dy = (block & 3) - (own & 3) + 1
        near = (dx >= 0) & (dx <= 2) & (dy >= 0) & (dy <= 2)
        slot = jnp.where(near, dx * 3 + dy, 9)
        table_ref[0, slot] = s ^ me
        table_ref[1, slot] = 1
    w1_ref[...] = stacked_taps(first_ref).astype(jnp.bfloat16)
    whole = stacked_taps(second_ref)
    w2_ref[...] = whole.astype(jnp.bfloat16)
    w2t_ref[...] = whole.T.astype(jnp.bfloat16)
    head = head_ref[...].astype(jnp.float32)
    head = jnp.concatenate([head, jnp.zeros((13, C), jnp.float32)], axis=0)
    h_ref[...] = head.astype(jnp.bfloat16)
    ht_ref[...] = head.T.astype(jnp.bfloat16)


def matmul(left, right):
    return lax.dot_general(
        left, right, (((1,), (0,)), ((), ())), preferred_element_type=jnp.float32
    )


def matmul_lanes(left, right):
    return lax.dot_general(
        left, right, (((1,), (1,)), ((), ())), preferred_element_type=jnp.float32
    )


def roll(values, shift):
    return pltpu.roll(values, shift % LANES, 1)


def crop_kernel(scale, count, table_ref, *refs):
    crop_body(scale, table_ref, refs[:count], *refs[count:])


def crop_body(
    scale,
    table_ref,
    blocks,
    w1_ref,
    w2_ref,
    w2t_ref,
    h_ref,
    ht_ref,
    logits_ref,
    packed_ref,
    gathered_ref,
    x9_ref,
    h9_ref,
    product_ref,
    slope1_ref,
    slope2_ref,
    hid2_ref,
    grad2_ref,
    shifted_ref,
    back_ref,
):
    for k, block in enumerate(blocks):
        gathered_ref[k] = block[...]

    owner = [table_ref[0, q] for q in range(9)]
    there = [table_ref[1, q].astype(jnp.float32) for q in range(9)]

    bf16 = jnp.bfloat16
    lane = lanes(16)
    depth = lane & 7
    depth48 = lanes(C) & 7
    low, mid, left_half = lane < 32, lane < 96, lane < 64
    own_lanes = jnp.where((lane >= 32) & mid, 1.0, 0.0)
    masks = [
        jnp.where(low, there[3 * bx], jnp.where(mid, there[3 * bx + 1], there[3 * bx + 2]))
        for bx in range(3)
    ]
    edge_masks = [
        jnp.where(left_half, there[3 * bx + 2], there[3 * bx]).astype(bf16) for bx in range(3)
    ]
    main_masks = [mask.astype(bf16) for mask in masks]
    masks = [mask[0:1] for mask in masks]
    own_row = own_lanes[0:1]

    def placed(tile, bx, half):
        before, middle, after = [gathered_ref[owner[3 * bx + by], tile] for by in range(3)]
        outer = 96 - 64 * half
        return roll(before, outer), roll(middle, 32 - 64 * half), roll(after, outer)

    zero = jnp.zeros((16, LANES), bf16)
    for plane in range(18):
        bx, i = (plane + 3) // 8, (plane + 3) % 8
        for ct in range(3):
            before, middle, after = placed(4 * ct + i // 2, bx, i % 2)
            main = jnp.where(low, before, jnp.where(mid, middle, after)) * main_masks[bx]
            edge = jnp.where(left_half, after, before) * edge_masks[bx]
            for c in (-1, 0, 1):
                if c == 0:
                    main_c, edge_c = main, edge
                else:
                    keep = depth >= 1 if c == 1 else depth <= 6
                    main_c, edge_c = jnp.where(keep, main, zero), jnp.where(keep, edge, zero)
                for b in (-1, 0, 1):
                    step = 8 * b + c
                    if b == 1:
                        source = jnp.where(lane < step, edge_c, main_c)
                    elif b == -1:
                        source = jnp.where(lane >= LANES + step, edge_c, main_c)
                    else:
                        source = main_c
                    row = (3 * (b + 1) + c + 1) * C + 16 * ct
                    x9_ref[row : row + 16, LANES * plane : LANES * (plane + 1)] = (
                        roll(source, -step) if step else source
                    )

    def plane_cols(plane):
        return slice(LANES * plane, LANES * (plane + 1))

    def summed(plane, stride):
        return (
            product_ref[0:C, plane_cols(plane)]
            + product_ref[C : 2 * C, plane_cols(plane + stride)]
            + product_ref[2 * C : 3 * C, plane_cols(plane + 2 * stride)]
        )

    for n in range(9):
        cols = slice(256 * n, 256 * (n + 1))
        product_ref[:, cols] = matmul(w1_ref[...], x9_ref[:, cols])

    for plane in range(16):
        bx = (plane + 4) // 8
        pre = summed(plane, 1)
        negative = jnp.exp(jnp.minimum(pre, 0.0))
        if 4 <= plane < 12:
            slope1_ref[:, plane_cols(plane - 4)] = jnp.where(pre > 0, 1.0, negative)
        hidden = jnp.where(pre > 0, pre, negative - 1.0) * masks[bx]
        hidden = hidden.astype(bf16)
        for c in (-1, 0, 1):
            if c == 0:
                source = hidden
            else:
                keep = depth48 >= 2 if c == 1 else depth48 <= 5
                source = jnp.where(keep, hidden, jnp.zeros((C, LANES), bf16))
            for b in (-1, 0, 1):
                step = 16 * b + 2 * c
                row = (3 * (b + 1) + c + 1) * C
                h9_ref[row : row + C, plane_cols(plane)] = roll(source, -step) if step else source

    for n in range(8):
        cols = slice(256 * n, 256 * (n + 1))
        product_ref[:, cols] = matmul(w2_ref[...], h9_ref[:, cols])

    for plane in range(12):
        bx = (plane + 6) // 8
        pre = summed(plane, 2)
        negative = jnp.exp(jnp.minimum(pre, 0.0))
        slope2_ref[:, plane_cols(plane)] = jnp.where(pre > 0, 1.0, negative) * masks[bx]
        hidden = jnp.where(pre > 0, pre, negative - 1.0) * masks[bx]
        hid2_ref[:, plane_cols(plane)] = hidden.astype(jnp.bfloat16)

    logits = matmul(h_ref[...], hid2_ref[...])
    targets = []
    for half in range(2):
        row = []
        for bx in range(3):
            before, middle, after = placed(12, bx, half)
            cells = jnp.where(low, before, jnp.where(mid, middle, after))
            row.append(cells.astype(jnp.float32))
        targets.append(row)
    grads = []
    for plane in range(12):
        bx, i = (plane + 6) // 8, (plane + 6) % 8
        value = logits[:, plane_cols(plane)]
        wanted = targets[i % 2][bx][4 * (i // 2) : 4 * (i // 2) + 4]
        wanted = jnp.concatenate([wanted, jnp.zeros((12, LANES), jnp.float32)], axis=0)
        sigmoid = 1.0 / (1.0 + jnp.exp(-value))
        grads.append((sigmoid - wanted) * masks[bx] * scale)
    for q in range(4):
        first = roll(logits[:, plane_cols(2 + 2 * q)], -32)
        second = roll(logits[:, plane_cols(3 + 2 * q)], 32)
        logits_ref[:, 0, plane_cols(q)] = jnp.where(left_half, first, second)[0:3]

    grad_logit = jnp.concatenate(grads, axis=1).astype(jnp.bfloat16)
    back = matmul(ht_ref[...], grad_logit)
    grad2_ref[...] = (back * slope2_ref[...]).astype(jnp.bfloat16)
    own_grads = jnp.concatenate([grads[2 + x] * own_row for x in range(8)], axis=1)
    head_part = matmul_lanes(hid2_ref[:, 2 * LANES : 10 * LANES], own_grads.astype(jnp.bfloat16))

    own_bf16 = jnp.broadcast_to(own_row, (C, LANES)).astype(bf16)
    shifted_ref[...] = jnp.zeros_like(shifted_ref)
    for a in range(3):
        for x in range(8):
            shifted_ref[C * a : C * (a + 1), plane_cols(x + 2 * a)] = (
                grad2_ref[:, plane_cols(x + 2)] * own_bf16
            )
    second_part = matmul_lanes(shifted_ref[...], h9_ref[:, 2 * LANES : 14 * LANES])

    for a in range(3):
        for x in range(8):
            shifted_ref[C * a : C * (a + 1), plane_cols(x)] = grad2_ref[:, plane_cols(x + 4 - 2 * a)]
    for n in range(4):
        cols = slice(256 * n, 256 * (n + 1))
        back_ref[:, cols] = matmul(w2t_ref[...], shifted_ref[:, cols])
    grad1 = []
    for x in range(8):
        total = jnp.zeros((C, LANES), jnp.float32)
        for c in (-1, 0, 1):
            part = jnp.zeros((C, LANES), jnp.float32)
            for b in (-1, 0, 1):
                row = (3 * (b + 1) + c + 1) * C
                step = 16 * b + 2 * c
                piece = back_ref[row : row + C, plane_cols(x)]
                part += roll(piece, step) if step else piece
            if c:
                part = jnp.where(depth48 >= 2 if c == 1 else depth48 <= 5, part, 0.0)
            total += part
        grad1.append((total * slope1_ref[:, plane_cols(x)] * own_row).astype(jnp.bfloat16))

    shifted_ref[...] = jnp.zeros_like(shifted_ref)
    for a in range(3):
        for x in range(8):
            shifted_ref[C * a : C * (a + 1), plane_cols(x + a)] = grad1[x]
    first_part = matmul_lanes(
        shifted_ref[:, 0 : 10 * LANES], x9_ref[:, 4 * LANES : 14 * LANES]
    )

    head_part = jnp.concatenate([head_part, jnp.zeros((24, 16), jnp.float32)], axis=0)
    nothing = jnp.zeros((72, 16), jnp.float32)
    for base, part, extra in ((0, first_part, nothing), (HALF, second_part, head_part)):
        for q in range(3):
            packed_ref[base + 144 * q : base + 144 * (q + 1), :] = part[:, plane_cols(q)].astype(bf16)
        tail = [part[0:72, 384:], part[72:144, 384:], extra, nothing]
        tail = jnp.concatenate([jnp.concatenate(tail, axis=1), jnp.zeros((8, LANES))], axis=0)
        packed_ref[base + 432 : base + HALF, :] = tail.astype(bf16)


def sum_kernel(parts_ref, out_ref):
    total = parts_ref[0].astype(jnp.float32)
    for s in range(1, parts_ref.shape[0]):
        total += parts_ref[s].astype(jnp.float32)
    total = total.astype(jnp.bfloat16)
    for s in range(out_ref.shape[0]):
        out_ref[s] = total


def unpack_kernel(rows_ref, first_hbm, second_hbm, head_ref, whole_ref, sems):
    copies = []
    for k, out in ((0, first_hbm), (1, second_hbm)):
        half = rows_ref[HALF * k : HALF * (k + 1), :].astype(jnp.float32)
        tail = jnp.concatenate([half[432:504, 0:C], half[432:504, C : 2 * C]], axis=0)
        tiles = [half[144 * q : 144 * (q + 1), :] for q in range(3)]
        whole = jnp.concatenate(tiles + [tail], axis=1)
        for a in range(3):
            for t in range(9):
                whole_ref[k, 9 * a + t] = whole[C * a : C * (a + 1), C * t : C * (t + 1)]
            taps = pl.ds(9 * a, 9)
            copy = pltpu.make_async_copy(whole_ref.at[k, taps], out.at[taps], sems.at[k, a])
            copy.start()
            copies.append(copy)
        if k:
            head_ref[...] = half[432 : 432 + C, 96:112].T[0:3]
    for copy in copies:
        copy.wait()


def on_device_flat(features, device_block, conv_first, conv_second, head_weight, targets):
    space_count = lax.axis_size("space")
    device_count = lax.axis_size("dp") * space_count
    bf16, f32 = jnp.bfloat16, jnp.float32
    small = pltpu.CompilerParams(vmem_limit_bytes=8 * 1024 * 1024)
    shape = jax.ShapeDtypeStruct
    vmem = pl.BlockSpec(memory_space=pltpu.VMEM)
    smem = pl.BlockSpec(memory_space=pltpu.SMEM)

    packed_block = pl.pallas_call(
        pack_kernel,
        out_shape=shape((13, 16, LANES), bf16),
        in_specs=[vmem] * 2,
        out_specs=vmem,
        compiler_params=small,
        name="pack_block",
    )(features[0, 0], targets[0].transpose(1, 0, 2))
    blocks = [packed_block] + [
        lax.ppermute(packed_block, "space", [(s, s ^ k) for s in range(space_count)])
        for k in range(1, space_count)
    ]

    table, w1, w2, w2t, head, head_t = pl.pallas_call(
        weights_kernel,
        out_shape=(
            shape((2, 16), jnp.int32),
            shape((3 * C, 9 * C), bf16),
            shape((3 * C, 9 * C), bf16),
            shape((9 * C, 3 * C), bf16),
            shape((16, C), bf16),
            shape((C, 16), bf16),
        ),
        in_specs=[smem] + [vmem] * 3,
        out_specs=(smem,) + (vmem,) * 5,
        compiler_params=small,
        cost_estimate=pl.CostEstimate(flops=2_000_000, bytes_accessed=4_000_000, transcendentals=0),
        name="lay_out_weights",
    )(device_block, conv_first.transpose(1, 0, 2), conv_second.transpose(1, 0, 2), head_weight)

    scale = (device_count * 3 * CELLS) ** (-0.5)
    logits, packed = pl.pallas_call(
        functools.partial(crop_kernel, scale, space_count),
        out_shape=(shape((3, 1, CELLS), f32), shape((2 * HALF, LANES), bf16)),
        in_specs=[smem] + [vmem] * (space_count + 5),
        out_specs=(vmem,) * 2,
        scratch_shapes=[
            pltpu.VMEM((space_count, 13, 16, LANES), bf16),
            pltpu.VMEM((9 * C, 18 * LANES), bf16),
            pltpu.VMEM((9 * C, 16 * LANES), bf16),
            pltpu.VMEM((3 * C, 18 * LANES), f32),
            pltpu.VMEM((C, 8 * LANES), f32),
            pltpu.VMEM((C, 12 * LANES), f32),
            pltpu.VMEM((C, 12 * LANES), bf16),
            pltpu.VMEM((C, 12 * LANES), bf16),
            pltpu.VMEM((3 * C, 12 * LANES), bf16),
            pltpu.VMEM((9 * C, 8 * LANES), f32),
        ],
        compiler_params=pltpu.CompilerParams(vmem_limit_bytes=20 * 1024 * 1024),
        name="forward_backward",
    )(table, *blocks, w1, w2, w2t, head, head_t)

    rows = HALF * 2 // device_count
    terms = lax.all_to_all(
        packed.reshape(device_count, rows, LANES), ("dp", "space"), 0, 0, tiled=True
    )
    summed = pl.pallas_call(
        sum_kernel,
        out_shape=shape((device_count, rows, LANES), bf16),
        in_specs=[vmem],
        out_specs=vmem,
        compiler_params=small,
        name="sum_terms",
    )(terms)
    total = lax.all_to_all(summed, ("dp", "space"), 0, 0, tiled=True)
    grad_first, grad_second, grad_head = pl.pallas_call(
        unpack_kernel,
        out_shape=(shape((27, C, C), f32), shape((27, C, C), f32), shape((3, C), f32)),
        in_specs=[vmem],
        out_specs=(pl.BlockSpec(memory_space=pl.ANY),) * 2 + (vmem,),
        scratch_shapes=[pltpu.VMEM((2, 27, C, C), f32), pltpu.SemaphoreType.DMA((2, 3))],
        compiler_params=small,
        name="unpack_gradients",
    )(total.reshape(2 * HALF, LANES))
    return (
        logits.transpose(1, 0, 2)[None],
        grad_first.transpose(1, 0, 2),
        grad_second.transpose(1, 0, 2),
        grad_head,
    )


def solution(mesh):
    in_specs = (
        P("dp", "space", None, None),
        P("dp", None),
        P(),
        P(),
        P(),
        P("dp", "space", None, None),
    )
    out_specs = (P("dp", "space", None, None), P(), P(), P())
    flat = mesh.shape["space"] == 8 and mesh.shape["dp"] == 4
    return jax.shard_map(
        on_device_flat if flat else on_device_deep,
        mesh=mesh,
        in_specs=in_specs,
        out_specs=out_specs,
        check_vma=False,
    )
```

```python
import functools

import jax
import jax.numpy as jnp
from jax import lax
from jax.experimental import pallas as pl
from jax.experimental.pallas import tpu as pltpu
from jax.sharding import PartitionSpec as P

BS = 8


tap_offsets = [
    (tap_index // 9 - 1, tap_index // 3 % 3 - 1, tap_index % 3 - 1) for tap_index in range(27)
]


def elu_pair(values):
    negative = jnp.exp(jnp.minimum(values, 0.0))
    return (jnp.where(values > 0, values, negative - 1.0), jnp.where(values > 0, 1.0, negative))


def neighbor_tables(device_block):
    space_count = lax.axis_size("space")
    depth_z = space_count // 8
    self_index = lax.axis_index("space")
    blocks = device_block[0]
    coords = jnp.stack([blocks // (4 * depth_z), blocks // depth_z % 4, blocks % depth_z])
    own_coords = lax.dynamic_index_in_dim(coords, self_index, 1, keepdims=False)
    offsets = jnp.array(tap_offsets, jnp.int32)
    limits = jnp.array([4, 4, depth_z], jnp.int32)
    wanted = own_coords[None, :] + offsets
    inside = jnp.all((wanted >= 0) & (wanted < limits[None, :]), axis=1) & (jnp.arange(27) != 13)
    wanted_id = (wanted[:, 0] * 4 + wanted[:, 1]) * depth_z + wanted[:, 2]
    matches = (blocks[None, :] == wanted_id[:, None]) & inside[:, None]
    devices = jnp.arange(space_count, dtype=jnp.int32)
    owner_row = jnp.sum(jnp.where(matches, devices[None, :], 0), axis=1)
    present = jnp.any(matches, axis=1)
    relative = coords - own_coords[:, None]
    adjacent = jnp.all(jnp.abs(relative) <= 1, axis=0) & (devices != self_index)
    send_tap = jnp.where(
        adjacent, (relative[0] + 1) * 9 + (relative[1] + 1) * 3 + relative[2] + 1, 13
    )
    return (owner_row, present, send_tap)


def region_slice(block_data, offset, depth_cells):
    span_list = []
    for step_value in offset:
        if step_value == 1:
            span_list.append(slice(BS - depth_cells, BS))
        elif step_value == -1:
            span_list.append(slice(0, depth_cells))
        else:
            span_list.append(slice(0, BS))
    return block_data[:, span_list[0], span_list[1], span_list[2]]


def surround(block_data, depth_cells, tables):
    owner_row, present, send_tap = tables
    channels = block_data.shape[0]
    length = depth_cells * BS * BS
    pieces = []
    for tap_index in range(27):
        if tap_index == 13:
            pieces.append(jnp.zeros((channels, length), block_data.dtype))
        else:
            region = region_slice(block_data, tap_offsets[tap_index], depth_cells).reshape(
                channels, -1
            )
            pieces.append(jnp.pad(region, ((0, 0), (0, length - region.shape[1]))))
    outgoing = jnp.stack(pieces)
    sending = outgoing[send_tap]
    by_source = lax.all_to_all(sending, "space", split_axis=0, concat_axis=0, tiled=True)
    incoming = jnp.where(
        present[:, None, None], by_source[owner_row], jnp.zeros((), block_data.dtype)
    )
    rows_x = []
    for step_x in range(3):
        rows_y = []
        for step_y in range(3):
            rows_z = []
            for step_z in range(3):
                tap_index = step_x * 9 + step_y * 3 + step_z
                if tap_index == 13:
                    rows_z.append(block_data)
                else:
                    extent_list = [
                        BS if step_value == 1 else depth_cells
                        for step_value in (step_x, step_y, step_z)
                    ]
                    count_cells = extent_list[0] * extent_list[1] * extent_list[2]
                    rows_z.append(
                        incoming[tap_index][:, :count_cells].reshape(
                            channels, extent_list[0], extent_list[1], extent_list[2]
                        )
                    )
            rows_y.append(jnp.concatenate(rows_z, axis=3))
        rows_x.append(jnp.concatenate(rows_y, axis=2))
    return jnp.concatenate(rows_x, axis=1)


def conv_padded(padded, kernel, dilation):
    result = lax.conv_general_dilated(
        padded[None],
        kernel,
        (1, 1, 1),
        "VALID",
        rhs_dilation=(dilation, dilation, dilation),
        dimension_numbers=("NCDHW", "OIDHW", "NCDHW"),
        preferred_element_type=jnp.float32,
    )
    return result[0].reshape(kernel.shape[0], BS * BS * BS)


def kernel_grad(padded, grad_rows, dilation):
    channels = padded.shape[0]
    outputs = grad_rows.shape[0]
    grad_block = grad_rows.reshape(outputs, 1, BS, BS, BS)
    result = lax.conv_general_dilated(
        padded[None],
        grad_block,
        (dilation, dilation, dilation),
        "VALID",
        dimension_numbers=("CNDHW", "OIDHW", "NCDHW"),
        preferred_element_type=jnp.float32,
    )
    return result.reshape(channels, outputs, 27).transpose(1, 2, 0)


def on_device_deep(features, device_block, conv_first, conv_second, head_weight, targets):
    channels = features.shape[2]
    tables = neighbor_tables(device_block)
    kernel_first = conv_first.reshape(channels, 3, 3, 3, channels).transpose(0, 4, 1, 2, 3)
    kernel_second = conv_second.reshape(channels, 3, 3, 3, channels).transpose(0, 4, 1, 2, 3)
    block_in = features[0, 0].reshape(channels, BS, BS, BS)
    padded_in = surround(block_in, 1, tables)
    pre_first = conv_padded(padded_in, kernel_first, 1)
    act_first, slope_first = elu_pair(pre_first)
    hid_first = act_first.astype(jnp.bfloat16)
    padded_first = surround(hid_first.reshape(channels, BS, BS, BS), 2, tables)
    pre_second = conv_padded(padded_first, kernel_second, 2)
    act_second, slope_second = elu_pair(pre_second)
    hid_second = act_second.astype(jnp.bfloat16)
    logits = jnp.dot(head_weight, hid_second, preferred_element_type=jnp.float32)
    scale = (lax.axis_size("dp") * lax.axis_size("space") * 3 * BS * BS * BS) ** (-0.5)
    grad_logit = ((jax.nn.sigmoid(logits) - targets[0, 0].astype(jnp.float32)) * scale).astype(
        jnp.bfloat16
    )
    grad_head = lax.dot_general(
        grad_logit, hid_second, (((1,), (1,)), ((), ())), preferred_element_type=jnp.float32
    )
    back_second = lax.dot_general(
        head_weight, grad_logit, (((0,), (0,)), ((), ())), preferred_element_type=jnp.float32
    )
    grad_pre_second = (back_second * slope_second).astype(jnp.bfloat16)
    grad_second = kernel_grad(padded_first, grad_pre_second, 2)
    padded_grad = surround(grad_pre_second.reshape(channels, BS, BS, BS), 2, tables)
    kernel_back = jnp.transpose(kernel_second[:, :, ::-1, ::-1, ::-1], (1, 0, 2, 3, 4))
    back_first = conv_padded(padded_grad, kernel_back, 2)
    grad_pre_first = (back_first * slope_first).astype(jnp.bfloat16)
    grad_first = kernel_grad(padded_in, grad_pre_first, 1)
    grad_first, grad_second, grad_head = lax.psum(
        (grad_first, grad_second, grad_head), ("dp", "space")
    )
    return (logits[None, None], grad_first, grad_second, grad_head)


C = 48
CELLS = 512
HALF = 512
LANES = 128


def lanes(rows=1):
    return lax.broadcasted_iota(jnp.int32, (rows, LANES), 1)


def roll(values, shift):
    return pltpu.roll(values, shift % LANES, 1) if shift % LANES else values


def pack_kernel(block_ref, features_ref, targets_ref, head_ref, *refs):
    own_ref, *slab_refs, table_ref, h_ref, ht_ref, cases_ref = refs
    me = lax.axis_index("space")
    own = block_ref[0, me]
    for slot in range(10):
        table_ref[0, slot] = 1
        table_ref[1, slot] = 0
    table_ref[0, 4] = 0
    table_ref[1, 4] = 1
    picks = []
    for k in range(1, len(slab_refs) + 1):
        block = block_ref[0, me ^ k]
        dx = (block >> 2) - (own >> 2)
        dy = (block & 3) - (own & 3)
        near = (dx >= -1) & (dx <= 1) & (dy >= -1) & (dy <= 1)
        slot = jnp.where(near, dx * 3 + dy + 4, 9)
        table_ref[0, slot] = k
        table_ref[1, slot] = 1
        along_y = jnp.where(dy > 0, 2, 3)
        picks.append(jnp.where(dx > 0, 0, jnp.where(dx < 0, 1, along_y)))

    bf16 = jnp.bfloat16
    lane = lanes(16)
    left = lane < 64
    cell = lane & 63
    tiles = [
        [features_ref[16 * ct : 16 * (ct + 1), LANES * q : LANES * (q + 1)] for q in range(4)]
        for ct in range(3)
    ]
    targets = targets_ref[:, 0, :].astype(jnp.float32)
    targets = jnp.concatenate([targets, jnp.zeros((1, CELLS), jnp.float32)], axis=0)
    rows = [targets[:, LANES * q : LANES * (q + 1)] for q in range(4)]
    target_tile = jnp.concatenate(rows, axis=0)
    for ct in range(3):
        for q in range(4):
            own_ref[4 * ct + q] = tiles[ct][q]
    own_ref[12] = target_tile.astype(bf16)

    def write(case, pairs, halves, wanted):
        for ct in range(3):
            cases_ref[case, 2 * ct] = pairs[ct][0]
            cases_ref[case, 2 * ct + 1] = pairs[ct][1]
        cases_ref[case, 6] = jnp.where(left, halves[0], halves[1])
        cases_ref[case, 7] = jnp.where(left, halves[2], wanted.astype(bf16))

    for case, pair, single, q in ((0, (2, 3), 1, 3), (1, (0, 1), 2, 0)):
        turns = (64, 0, 64) if case == 0 else (0, 64, 0)
        halves = [roll(tiles[ct][single], turns[ct]) for ct in range(3)]
        both = [roll(rows[q], 64), rows[q], jnp.zeros((8, LANES), jnp.float32)]
        wanted = jnp.concatenate(both, axis=0)
        write(case, [(t[pair[0]], t[pair[1]]) for t in tiles], halves, wanted)
    for case, spare, turn, turns, target_turns in (
        (2, cell < 24, -24, (-48, -96, -16, -64), (16, -32)),
        (3, cell >= 40, 40, (-24, -72, 8, -40), (64, 16)),
    ):
        pairs, halves = [], []
        for ct, t in enumerate(tiles):
            pairs.append([jnp.where(spare, roll(t[q + 2], turn), t[q]) for q in range(2)])
            moved = [roll(t[2 + n // 2], turns[n] + (64 if ct == 1 else 0)) for n in range(4)]
            half = jnp.where(cell < 16, moved[0], jnp.where(cell < 32, moved[1], moved[2]))
            halves.append(jnp.where(cell < 48, half, moved[3]))
        wanted = [roll(target_tile, n) for n in target_turns]
        write(case, pairs, halves, jnp.where(lane < 80, wanted[0], wanted[1]))
    for pick, ref in zip(picks, slab_refs):
        ref[...] = cases_ref[pick]

    head = head_ref[...].astype(jnp.float32)
    head = jnp.concatenate([head, jnp.zeros((13, C), jnp.float32)], axis=0)
    h_ref[...] = head.astype(bf16)
    ht_ref[...] = head.T.astype(bf16)


def stacked_taps(ref):
    rows = []
    for a in range(3):
        taps = [ref[9 * a + t] for t in range(9)]
        rows.append(jnp.concatenate(taps, axis=1))
    return jnp.concatenate(rows, axis=0)


def weights_kernel(first_ref, second_ref, w1_ref, w2_ref, w2t_ref):
    w1_ref[...] = stacked_taps(first_ref)
    whole = stacked_taps(second_ref)
    w2_ref[...] = whole
    w2t_ref[...] = whole.T


def matmul(left, right):
    return lax.dot_general(
        left, right, (((1,), (0,)), ((), ())), preferred_element_type=jnp.float32
    )


def matmul_lanes(left, right):
    return lax.dot_general(
        left, right, (((1,), (1,)), ((), ())), preferred_element_type=jnp.float32
    )


def crop_kernel(scale, count, table_ref, *refs):
    crop_body(scale, table_ref, refs[0], refs[1:count], *refs[count:])


def crop_body(
    scale,
    table_ref,
    own_ref,
    slabs,
    w1_ref,
    w2_ref,
    w2t_ref,
    h_ref,
    ht_ref,
    logits_ref,
    packed_ref,
    gathered_ref,
    sides_ref,
    x9_ref,
    h9_ref,
    product_ref,
    slope1_ref,
    slope2_ref,
    hid2_ref,
    grad2_ref,
    shifted_ref,
    back_ref,
):
    for k, slab in enumerate(slabs):
        gathered_ref[k + 1] = slab[...]

    owner = [table_ref[0, q] for q in range(9)]
    there = [table_ref[1, q].astype(jnp.float32) for q in range(9)]

    bf16 = jnp.bfloat16
    lane = lanes(16)
    depth = lane & 7
    depth48 = lanes(C) & 7
    low, mid, left_half = lane < 32, lane < 96, lane < 64
    own_lanes = jnp.where((lane >= 32) & mid, 1.0, 0.0)
    masks = [
        jnp.where(low, there[3 * bx], jnp.where(mid, there[3 * bx + 1], there[3 * bx + 2]))
        for bx in range(3)
    ]
    edge_masks = [
        jnp.where(left_half, there[3 * bx + 2], there[3 * bx]).astype(bf16) for bx in range(3)
    ]
    main_masks = [mask.astype(bf16) for mask in masks]
    masks = [mask[0:1] for mask in masks]
    own_row = own_lanes[0:1]

    cell = lane & 63
    for side, by, in_place, turn, turns in (
        (0, 0, cell < 48, 24, (48, 96, 16, 64)),
        (1, 2, cell < 24, -40, (24, 72, -8, 40)),
    ):
        slab = owner[3 + by]
        for ct in range(3):
            half = gathered_ref[slab, 6 + ct // 2]
            for q in range(2):
                sides_ref[side, 4 * ct + q] = gathered_ref[slab, 2 * ct + q]
                moved = [roll(half, turns[2 * q + n] - (64 if ct == 1 else 0)) for n in range(2)]
                sides_ref[side, 4 * ct + q + 2] = jnp.where(
                    in_place,
                    roll(gathered_ref[slab, 2 * ct + q], turn),
                    jnp.where(left_half, moved[0], moved[1]),
                )

    def placed(ct, bx, i):
        if bx == 1:
            tile, half = 4 * ct + i // 2, i % 2
            parts = [sides_ref[0, tile], own_ref[tile], sides_ref[1, tile]]
        else:
            if i == (3 if bx == 0 else 4):
                tile, half = 6 + ct // 2, ct % 2
            else:
                tile, half = 2 * ct + (i // 2 - 2 if bx == 0 else i // 2), i % 2
            parts = [gathered_ref[owner[3 * bx + by], tile] for by in range(3)]
        outer = 96 - 64 * half
        return roll(parts[0], outer), roll(parts[1], 32 - 64 * half), roll(parts[2], outer)

    zero = jnp.zeros((16, LANES), bf16)
    for plane in range(18):
        bx, i = (plane + 3) // 8, (plane + 3) % 8
        for ct in range(3):
            before, middle, after = placed(ct, bx, i)
            main = jnp.where(low, before, jnp.where(mid, middle, after)) * main_masks[bx]
            edge = jnp.where(left_half, after, before) * edge_masks[bx]
            for c in (-1, 0, 1):
                if c == 0:
                    main_c, edge_c = main, edge
                else:
                    keep = depth >= 1 if c == 1 else depth <= 6
                    main_c, edge_c = jnp.where(keep, main, zero), jnp.where(keep, edge, zero)
                for b in (-1, 0, 1):
                    step = 8 * b + c
                    if b == 1:
                        source = jnp.where(lane < step, edge_c, main_c)
                    elif b == -1:
                        source = jnp.where(lane >= LANES + step, edge_c, main_c)
                    else:
                        source = main_c
                    row = (3 * (b + 1) + c + 1) * C + 16 * ct
                    x9_ref[row : row + 16, LANES * plane : LANES * (plane + 1)] = (
                        roll(source, -step) if step else source
                    )

    def plane_cols(plane):
        return slice(LANES * plane, LANES * (plane + 1))

    def summed(plane, stride):
        return (
            product_ref[0:C, plane_cols(plane)]
            + product_ref[C : 2 * C, plane_cols(plane + stride)]
            + product_ref[2 * C : 3 * C, plane_cols(plane + 2 * stride)]
        )

    for n in range(9):
        cols = slice(256 * n, 256 * (n + 1))
        product_ref[:, cols] = matmul(w1_ref[...], x9_ref[:, cols])

    for plane in range(16):
        bx = (plane + 4) // 8
        pre = summed(plane, 1)
        negative = jnp.exp(jnp.minimum(pre, 0.0))
        if 4 <= plane < 12:
            slope1_ref[:, plane_cols(plane - 4)] = jnp.where(pre > 0, 1.0, negative)
        hidden = jnp.where(pre > 0, pre, negative - 1.0) * masks[bx]
        hidden = hidden.astype(bf16)
        for c in (-1, 0, 1):
            if c == 0:
                source = hidden
            else:
                keep = depth48 >= 2 if c == 1 else depth48 <= 5
                source = jnp.where(keep, hidden, jnp.zeros((C, LANES), bf16))
            for b in (-1, 0, 1):
                step = 16 * b + 2 * c
                row = (3 * (b + 1) + c + 1) * C
                h9_ref[row : row + C, plane_cols(plane)] = roll(source, -step) if step else source

    for n in range(8):
        cols = slice(256 * n, 256 * (n + 1))
        product_ref[:, cols] = matmul(w2_ref[...], h9_ref[:, cols])

    for plane in range(12):
        bx = (plane + 6) // 8
        pre = summed(plane, 2)
        negative = jnp.exp(jnp.minimum(pre, 0.0))
        slope2_ref[:, plane_cols(plane)] = jnp.where(pre > 0, 1.0, negative) * masks[bx]
        hidden = jnp.where(pre > 0, pre, negative - 1.0) * masks[bx]
        hid2_ref[:, plane_cols(plane)] = hidden.astype(jnp.bfloat16)

    logits = matmul(h_ref[...], hid2_ref[...])
    targets = []
    for bx, half in ((0, 1), (1, 0), (1, 1), (2, 1)):
        if bx == 1:
            before = roll(gathered_ref[owner[3], 7], -48 - 16 * half)
            middle = roll(own_ref[12], 32 - 64 * half)
            after = roll(gathered_ref[owner[5], 7], 32 - 16 * half)
        else:
            parts = [gathered_ref[owner[3 * bx + by], 7] for by in range(3)]
            before, middle, after = roll(parts[0], 32), roll(parts[1], -32), roll(parts[2], 32)
        cells = jnp.where(low, before, jnp.where(mid, middle, after))
        targets.append(cells.astype(jnp.float32))
    grads = []
    for plane in range(12):
        bx, i = (plane + 6) // 8, (plane + 6) % 8
        value = logits[:, plane_cols(plane)]
        if bx == 1:
            wanted = targets[1 + i % 2][4 * (i // 2) : 4 * (i // 2) + 4]
        else:
            wanted = targets[0 if bx == 0 else 3][4 * (i % 2) : 4 * (i % 2) + 4]
        wanted = jnp.concatenate([wanted, jnp.zeros((12, LANES), jnp.float32)], axis=0)
        sigmoid = 1.0 / (1.0 + jnp.exp(-value))
        grads.append((sigmoid - wanted) * masks[bx] * scale)
    for q in range(4):
        first = roll(logits[:, plane_cols(2 + 2 * q)], -32)
        second = roll(logits[:, plane_cols(3 + 2 * q)], 32)
        logits_ref[:, 0, plane_cols(q)] = jnp.where(left_half, first, second)[0:3]

    grad_logit = jnp.concatenate(grads, axis=1).astype(jnp.bfloat16)
    back = matmul(ht_ref[...], grad_logit)
    grad2_ref[...] = (back * slope2_ref[...]).astype(jnp.bfloat16)
    own_grads = jnp.concatenate([grads[2 + x] * own_row for x in range(8)], axis=1)
    head_part = matmul_lanes(hid2_ref[:, 2 * LANES : 10 * LANES], own_grads.astype(jnp.bfloat16))

    own_bf16 = jnp.broadcast_to(own_row, (C, LANES)).astype(bf16)
    shifted_ref[...] = jnp.zeros_like(shifted_ref)
    for a in range(3):
        for x in range(8):
            shifted_ref[C * a : C * (a + 1), plane_cols(x + 2 * a)] = (
                grad2_ref[:, plane_cols(x + 2)] * own_bf16
            )
    second_part = matmul_lanes(shifted_ref[...], h9_ref[:, 2 * LANES : 14 * LANES])

    for a in range(3):
        for x in range(8):
            shifted_ref[C * a : C * (a + 1), plane_cols(x)] = grad2_ref[:, plane_cols(x + 4 - 2 * a)]
    for n in range(4):
        cols = slice(256 * n, 256 * (n + 1))
        back_ref[:, cols] = matmul(w2t_ref[...], shifted_ref[:, cols])
    grad1 = []
    for x in range(8):
        total = jnp.zeros((C, LANES), jnp.float32)
        for c in (-1, 0, 1):
            part = jnp.zeros((C, LANES), jnp.float32)
            for b in (-1, 0, 1):
                row = (3 * (b + 1) + c + 1) * C
                step = 16 * b + 2 * c
                piece = back_ref[row : row + C, plane_cols(x)]
                part += roll(piece, step) if step else piece
            if c:
                part = jnp.where(depth48 >= 2 if c == 1 else depth48 <= 5, part, 0.0)
            total += part
        grad1.append((total * slope1_ref[:, plane_cols(x)] * own_row).astype(jnp.bfloat16))

    shifted_ref[...] = jnp.zeros_like(shifted_ref)
    for a in range(3):
        for x in range(8):
            shifted_ref[C * a : C * (a + 1), plane_cols(x + a)] = grad1[x]
    first_part = matmul_lanes(
        shifted_ref[:, 0 : 10 * LANES], x9_ref[:, 4 * LANES : 14 * LANES]
    )

    head_part = jnp.concatenate([head_part, jnp.zeros((24, 16), jnp.float32)], axis=0)
    nothing = jnp.zeros((72, 16), jnp.float32)
    for base, part, extra in ((0, first_part, nothing), (HALF, second_part, head_part)):
        for q in range(3):
            packed_ref[base + 144 * q : base + 144 * (q + 1), :] = part[:, plane_cols(q)].astype(bf16)
        tail = [part[0:72, 384:], part[72:144, 384:], extra, nothing]
        tail = jnp.concatenate([jnp.concatenate(tail, axis=1), jnp.zeros((8, LANES))], axis=0)
        packed_ref[base + 432 : base + HALF, :] = tail.astype(bf16)


def sum_kernel(parts_ref, out_ref):
    total = parts_ref[0].astype(jnp.float32)
    for s in range(1, parts_ref.shape[0]):
        total += parts_ref[s].astype(jnp.float32)
    total = total.astype(jnp.bfloat16)
    for s in range(out_ref.shape[0]):
        out_ref[s] = total


def unpack_kernel(rows_ref, first_ref, second_ref, head_ref):
    for k, out in ((0, first_ref), (1, second_ref)):
        half = rows_ref[HALF * k : HALF * (k + 1), :].astype(jnp.float32)
        tail = jnp.concatenate([half[432:504, 0:C], half[432:504, C : 2 * C]], axis=0)
        tiles = [half[144 * q : 144 * (q + 1), :] for q in range(3)]
        whole = jnp.concatenate(tiles + [tail], axis=1)
        for a in range(3):
            for t in range(9):
                out[9 * a + t] = whole[C * a : C * (a + 1), C * t : C * (t + 1)]
        if k:
            head_ref[...] = half[432 : 432 + C, 96:112].T[0:3]


def on_device_flat(features, device_block, conv_first, conv_second, head_weight, targets):
    space_count = lax.axis_size("space")
    device_count = lax.axis_size("dp") * space_count
    bf16, f32 = jnp.bfloat16, jnp.float32
    small = pltpu.CompilerParams(vmem_limit_bytes=8 * 1024 * 1024)
    shape = jax.ShapeDtypeStruct
    vmem = pl.BlockSpec(memory_space=pltpu.VMEM)
    smem = pl.BlockSpec(memory_space=pltpu.SMEM)

    partners = range(1, space_count)
    own, *slabs, table, head, head_t = pl.pallas_call(
        pack_kernel,
        out_shape=(
            shape((13, 16, LANES), bf16),
            *[shape((8, 16, LANES), bf16) for _ in partners],
            shape((2, 16), jnp.int32),
            shape((16, C), bf16),
            shape((C, 16), bf16),
        ),
        in_specs=[smem] + [vmem] * 3,
        out_specs=(vmem,) * space_count + (smem, vmem, vmem),
        scratch_shapes=[pltpu.VMEM((4, 8, 16, LANES), bf16)],
        compiler_params=small,
        name="pack_block",
    )(device_block, features[0, 0], targets[0].transpose(1, 0, 2), head_weight)
    slabs = [
        lax.ppermute(slab, "space", [(s, s ^ k) for s in range(space_count)])
        for k, slab in zip(partners, slabs)
    ]

    w1, w2, w2t = pl.pallas_call(
        weights_kernel,
        out_shape=(
            shape((3 * C, 9 * C), bf16),
            shape((3 * C, 9 * C), bf16),
            shape((9 * C, 3 * C), bf16),
        ),
        in_specs=[vmem] * 2,
        out_specs=(vmem,) * 3,
        compiler_params=small,
        cost_estimate=pl.CostEstimate(flops=2_000_000, bytes_accessed=4_000_000, transcendentals=0),
        name="lay_out_weights",
    )(conv_first.transpose(1, 0, 2), conv_second.transpose(1, 0, 2))

    scale = (device_count * 3 * CELLS) ** (-0.5)
    logits, packed = pl.pallas_call(
        functools.partial(crop_kernel, scale, space_count),
        out_shape=(shape((3, 1, CELLS), f32), shape((2 * HALF, LANES), bf16)),
        in_specs=[smem] + [vmem] * (space_count + 5),
        out_specs=(vmem,) * 2,
        scratch_shapes=[
            pltpu.VMEM((space_count, 8, 16, LANES), bf16),
            pltpu.VMEM((2, 12, 16, LANES), bf16),
            pltpu.VMEM((9 * C, 18 * LANES), bf16),
            pltpu.VMEM((9 * C, 16 * LANES), bf16),
            pltpu.VMEM((3 * C, 18 * LANES), f32),
            pltpu.VMEM((C, 8 * LANES), f32),
            pltpu.VMEM((C, 12 * LANES), f32),
            pltpu.VMEM((C, 12 * LANES), bf16),
            pltpu.VMEM((C, 12 * LANES), bf16),
            pltpu.VMEM((3 * C, 12 * LANES), bf16),
            pltpu.VMEM((9 * C, 8 * LANES), f32),
        ],
        compiler_params=pltpu.CompilerParams(vmem_limit_bytes=20 * 1024 * 1024),
        name="forward_backward",
    )(table, own, *slabs, w1, w2, w2t, head, head_t)

    rows = HALF * 2 // device_count
    terms = lax.all_to_all(
        packed.reshape(device_count, rows, LANES), ("dp", "space"), 0, 0, tiled=True
    )
    summed = pl.pallas_call(
        sum_kernel,
        out_shape=shape((device_count, rows, LANES), bf16),
        in_specs=[vmem],
        out_specs=vmem,
        compiler_params=small,
        name="sum_terms",
    )(terms)
    total = lax.all_to_all(summed, ("dp", "space"), 0, 0, tiled=True)
    grad_first, grad_second, grad_head = pl.pallas_call(
        unpack_kernel,
        out_shape=(shape((27, C, C), f32), shape((27, C, C), f32), shape((3, C), f32)),
        in_specs=[vmem],
        out_specs=(vmem,) * 3,
        compiler_params=small,
        name="unpack_gradients",
    )(total.reshape(2 * HALF, LANES))
    return (
        logits.transpose(1, 0, 2)[None],
        grad_first.transpose(1, 0, 2),
        grad_second.transpose(1, 0, 2),
        grad_head,
    )


def solution(mesh):
    in_specs = (
        P("dp", "space", None, None),
        P("dp", None),
        P(),
        P(),
        P(),
        P("dp", "space", None, None),
    )
    out_specs = (P("dp", "space", None, None), P(), P(), P())
    flat = mesh.shape["space"] == 8 and mesh.shape["dp"] == 4
    return jax.shard_map(
        on_device_flat if flat else on_device_deep,
        mesh=mesh,
        in_specs=in_specs,
        out_specs=out_specs,
        check_vma=False,
    )
```

```python
import functools

import jax
import jax.numpy as jnp
from jax import lax
from jax.experimental import pallas as pl
from jax.experimental.pallas import tpu as pltpu
from jax.sharding import PartitionSpec as P

BS = 8


tap_offsets = [
    (tap_index // 9 - 1, tap_index // 3 % 3 - 1, tap_index % 3 - 1) for tap_index in range(27)
]


def elu_pair(values):
    negative = jnp.exp(jnp.minimum(values, 0.0))
    return (jnp.where(values > 0, values, negative - 1.0), jnp.where(values > 0, 1.0, negative))


def neighbor_tables(device_block):
    space_count = lax.axis_size("space")
    depth_z = space_count // 8
    self_index = lax.axis_index("space")
    blocks = device_block[0]
    coords = jnp.stack([blocks // (4 * depth_z), blocks // depth_z % 4, blocks % depth_z])
    own_coords = lax.dynamic_index_in_dim(coords, self_index, 1, keepdims=False)
    offsets = jnp.array(tap_offsets, jnp.int32)
    limits = jnp.array([4, 4, depth_z], jnp.int32)
    wanted = own_coords[None, :] + offsets
    inside = jnp.all((wanted >= 0) & (wanted < limits[None, :]), axis=1) & (jnp.arange(27) != 13)
    wanted_id = (wanted[:, 0] * 4 + wanted[:, 1]) * depth_z + wanted[:, 2]
    matches = (blocks[None, :] == wanted_id[:, None]) & inside[:, None]
    devices = jnp.arange(space_count, dtype=jnp.int32)
    owner_row = jnp.sum(jnp.where(matches, devices[None, :], 0), axis=1)
    present = jnp.any(matches, axis=1)
    relative = coords - own_coords[:, None]
    adjacent = jnp.all(jnp.abs(relative) <= 1, axis=0) & (devices != self_index)
    send_tap = jnp.where(
        adjacent, (relative[0] + 1) * 9 + (relative[1] + 1) * 3 + relative[2] + 1, 13
    )
    return (owner_row, present, send_tap)


def region_slice(block_data, offset, depth_cells):
    span_list = []
    for step_value in offset:
        if step_value == 1:
            span_list.append(slice(BS - depth_cells, BS))
        elif step_value == -1:
            span_list.append(slice(0, depth_cells))
        else:
            span_list.append(slice(0, BS))
    return block_data[:, span_list[0], span_list[1], span_list[2]]


def surround(block_data, depth_cells, tables):
    owner_row, present, send_tap = tables
    channels = block_data.shape[0]
    length = depth_cells * BS * BS
    pieces = []
    for tap_index in range(27):
        if tap_index == 13:
            pieces.append(jnp.zeros((channels, length), block_data.dtype))
        else:
            region = region_slice(block_data, tap_offsets[tap_index], depth_cells).reshape(
                channels, -1
            )
            pieces.append(jnp.pad(region, ((0, 0), (0, length - region.shape[1]))))
    outgoing = jnp.stack(pieces)
    sending = outgoing[send_tap]
    by_source = lax.all_to_all(sending, "space", split_axis=0, concat_axis=0, tiled=True)
    incoming = jnp.where(
        present[:, None, None], by_source[owner_row], jnp.zeros((), block_data.dtype)
    )
    rows_x = []
    for step_x in range(3):
        rows_y = []
        for step_y in range(3):
            rows_z = []
            for step_z in range(3):
                tap_index = step_x * 9 + step_y * 3 + step_z
                if tap_index == 13:
                    rows_z.append(block_data)
                else:
                    extent_list = [
                        BS if step_value == 1 else depth_cells
                        for step_value in (step_x, step_y, step_z)
                    ]
                    count_cells = extent_list[0] * extent_list[1] * extent_list[2]
                    rows_z.append(
                        incoming[tap_index][:, :count_cells].reshape(
                            channels, extent_list[0], extent_list[1], extent_list[2]
                        )
                    )
            rows_y.append(jnp.concatenate(rows_z, axis=3))
        rows_x.append(jnp.concatenate(rows_y, axis=2))
    return jnp.concatenate(rows_x, axis=1)


def conv_padded(padded, kernel, dilation):
    result = lax.conv_general_dilated(
        padded[None],
        kernel,
        (1, 1, 1),
        "VALID",
        rhs_dilation=(dilation, dilation, dilation),
        dimension_numbers=("NCDHW", "OIDHW", "NCDHW"),
        preferred_element_type=jnp.float32,
    )
    return result[0].reshape(kernel.shape[0], BS * BS * BS)


def kernel_grad(padded, grad_rows, dilation):
    channels = padded.shape[0]
    outputs = grad_rows.shape[0]
    grad_block = grad_rows.reshape(outputs, 1, BS, BS, BS)
    result = lax.conv_general_dilated(
        padded[None],
        grad_block,
        (dilation, dilation, dilation),
        "VALID",
        dimension_numbers=("CNDHW", "OIDHW", "NCDHW"),
        preferred_element_type=jnp.float32,
    )
    return result.reshape(channels, outputs, 27).transpose(1, 2, 0)


def on_device_deep(features, device_block, conv_first, conv_second, head_weight, targets):
    channels = features.shape[2]
    tables = neighbor_tables(device_block)
    kernel_first = conv_first.reshape(channels, 3, 3, 3, channels).transpose(0, 4, 1, 2, 3)
    kernel_second = conv_second.reshape(channels, 3, 3, 3, channels).transpose(0, 4, 1, 2, 3)
    block_in = features[0, 0].reshape(channels, BS, BS, BS)
    padded_in = surround(block_in, 1, tables)
    pre_first = conv_padded(padded_in, kernel_first, 1)
    act_first, slope_first = elu_pair(pre_first)
    hid_first = act_first.astype(jnp.bfloat16)
    padded_first = surround(hid_first.reshape(channels, BS, BS, BS), 2, tables)
    pre_second = conv_padded(padded_first, kernel_second, 2)
    act_second, slope_second = elu_pair(pre_second)
    hid_second = act_second.astype(jnp.bfloat16)
    logits = jnp.dot(head_weight, hid_second, preferred_element_type=jnp.float32)
    scale = (lax.axis_size("dp") * lax.axis_size("space") * 3 * BS * BS * BS) ** (-0.5)
    grad_logit = ((jax.nn.sigmoid(logits) - targets[0, 0].astype(jnp.float32)) * scale).astype(
        jnp.bfloat16
    )
    grad_head = lax.dot_general(
        grad_logit, hid_second, (((1,), (1,)), ((), ())), preferred_element_type=jnp.float32
    )
    back_second = lax.dot_general(
        head_weight, grad_logit, (((0,), (0,)), ((), ())), preferred_element_type=jnp.float32
    )
    grad_pre_second = (back_second * slope_second).astype(jnp.bfloat16)
    grad_second = kernel_grad(padded_first, grad_pre_second, 2)
    padded_grad = surround(grad_pre_second.reshape(channels, BS, BS, BS), 2, tables)
    kernel_back = jnp.transpose(kernel_second[:, :, ::-1, ::-1, ::-1], (1, 0, 2, 3, 4))
    back_first = conv_padded(padded_grad, kernel_back, 2)
    grad_pre_first = (back_first * slope_first).astype(jnp.bfloat16)
    grad_first = kernel_grad(padded_in, grad_pre_first, 1)
    grad_first, grad_second, grad_head = lax.psum(
        (grad_first, grad_second, grad_head), ("dp", "space")
    )
    return (logits[None, None], grad_first, grad_second, grad_head)


C = 48
CELLS = 512
HALF = 512
LANES = 128


def lanes(rows=1):
    return lax.broadcasted_iota(jnp.int32, (rows, LANES), 1)


def roll(values, shift):
    return pltpu.roll(values, shift % LANES, 1) if shift % LANES else values


def listed_blocks(block_ref, me):
    ids = block_ref[...].astype(jnp.float32)
    index = lax.broadcasted_iota(jnp.int32, ids.shape, 1)
    return [
        jnp.sum(jnp.where(index == (me ^ k), ids, 0.0)).astype(jnp.int32)
        for k in range(ids.shape[1])
    ]


def apart(source, target):
    return (target >> 2) - (source >> 2), (target & 3) - (source & 3)


def pack_kernel(
    block_ref, own_f_ref, own_t_ref, mate_f_ref, mate_t_ref, own_ref, mate_ref, *refs
):
    *pair_refs, cases_ref = refs
    blocks = listed_blocks(block_ref, lax.axis_index("space"))
    bf16 = jnp.bfloat16
    lane = lanes(16)
    left = lane < 64
    cell = lane & 63
    for j, (features_ref, targets_ref) in enumerate(
        ((own_f_ref, own_t_ref), (mate_f_ref, mate_t_ref))
    ):
        tiles = [
            [features_ref[16 * ct : 16 * (ct + 1), LANES * q : LANES * (q + 1)] for q in range(4)]
            for ct in range(3)
        ]
        targets = targets_ref[:, 0, :].astype(jnp.float32)
        targets = jnp.concatenate([targets, jnp.zeros((1, CELLS), jnp.float32)], axis=0)
        rows = [targets[:, LANES * q : LANES * (q + 1)] for q in range(4)]
        target_tile = jnp.concatenate(rows, axis=0)
        if j == 0:
            for ct in range(3):
                for q in range(4):
                    own_ref[4 * ct + q] = tiles[ct][q]
            own_ref[12] = target_tile.astype(bf16)

        def write(case, pairs, halves, wanted):
            for ct in range(3):
                cases_ref[4 * j + case, 2 * ct] = pairs[ct][0]
                cases_ref[4 * j + case, 2 * ct + 1] = pairs[ct][1]
            cases_ref[4 * j + case, 6] = jnp.where(left, halves[0], halves[1])
            cases_ref[4 * j + case, 7] = jnp.where(left, halves[2], wanted.astype(bf16))

        for case, pair, single, q in ((0, (2, 3), 1, 3), (1, (0, 1), 2, 0)):
            turns = (64, 0, 64) if case == 0 else (0, 64, 0)
            halves = [roll(tiles[ct][single], turns[ct]) for ct in range(3)]
            both = [roll(rows[q], 64), rows[q], jnp.zeros((8, LANES), jnp.float32)]
            wanted = jnp.concatenate(both, axis=0)
            write(case, [(t[pair[0]], t[pair[1]]) for t in tiles], halves, wanted)
        for case, spare, turn, turns, target_turns in (
            (2, cell < 24, -24, (-48, -96, -16, -64), (16, -32)),
            (3, cell >= 40, 40, (-24, -72, 8, -40), (64, 16)),
        ):
            pairs, halves = [], []
            for ct, t in enumerate(tiles):
                pairs.append([jnp.where(spare, roll(t[q + 2], turn), t[q]) for q in range(2)])
                moved = [roll(t[2 + n // 2], turns[n] + (64 if ct == 1 else 0)) for n in range(4)]
                half = jnp.where(cell < 16, moved[0], jnp.where(cell < 32, moved[1], moved[2]))
                halves.append(jnp.where(cell < 48, half, moved[3]))
            wanted = [roll(target_tile, n) for n in target_turns]
            write(case, pairs, halves, jnp.where(lane < 80, wanted[0], wanted[1]))

    def pick(source, k):
        dx, dy = apart(blocks[source], blocks[k])
        along_y = jnp.where(dy > 0, 2, 3)
        return 4 * source + jnp.where(dx > 0, 0, jnp.where(dx < 0, 1, along_y))

    mate_ref[...] = cases_ref[pick(1, 0)]
    for n, ref in enumerate(pair_refs):
        ref[0] = cases_ref[pick(0, 2 * n + 2)]
        ref[1] = cases_ref[pick(1, 2 * n + 2)]


def stacked_taps(ref):
    rows = []
    for a in range(3):
        taps = [ref[9 * a + t] for t in range(9)]
        rows.append(jnp.concatenate(taps, axis=1))
    return jnp.concatenate(rows, axis=0)


def weights_kernel(first_ref, second_ref, head_ref, w1_ref, w2_ref, w2t_ref, h_ref, ht_ref):
    w1_ref[...] = stacked_taps(first_ref)
    whole = stacked_taps(second_ref)
    w2_ref[...] = whole
    w2t_ref[...] = whole.T
    head = head_ref[...].astype(jnp.float32)
    head = jnp.concatenate([head, jnp.zeros((13, C), jnp.float32)], axis=0)
    h_ref[...] = head.astype(jnp.bfloat16)
    ht_ref[...] = head.T.astype(jnp.bfloat16)


def matmul(left, right):
    return lax.dot_general(
        left, right, (((1,), (0,)), ((), ())), preferred_element_type=jnp.float32
    )


def matmul_lanes(left, right):
    return lax.dot_general(
        left, right, (((1,), (1,)), ((), ())), preferred_element_type=jnp.float32
    )


def crop_kernel(scale, block_ref, own_ref, mate_ref, *refs):
    crop_body(scale, block_ref, own_ref, mate_ref, refs[:3], *refs[3:])


def crop_body(
    scale,
    block_ref,
    own_ref,
    mate_ref,
    pairs,
    w1_ref,
    w2_ref,
    w2t_ref,
    h_ref,
    ht_ref,
    logits_ref,
    packed_ref,
    table_ref,
    gathered_ref,
    sides_ref,
    x9_ref,
    h9_ref,
    product_ref,
    slope1_ref,
    slope2_ref,
    hid2_ref,
    grad2_ref,
    shifted_ref,
    back_ref,
):
    gathered_ref[1] = mate_ref[...]
    for n, pair in enumerate(pairs):
        for j in range(2):
            gathered_ref[2 * n + 2 + j] = pair[j]
    blocks = listed_blocks(block_ref, lax.axis_index("space"))
    for slot in range(10):
        table_ref[0, slot] = 1
        table_ref[1, slot] = 0
    table_ref[1, 4] = 1
    for k in range(1, len(blocks)):
        dx, dy = apart(blocks[0], blocks[k])
        near = (dx >= -1) & (dx <= 1) & (dy >= -1) & (dy <= 1)
        slot = jnp.where(near, dx * 3 + dy + 4, 9)
        table_ref[0, slot] = k
        table_ref[1, slot] = 1

    owner = [table_ref[0, q] for q in range(9)]
    there = [table_ref[1, q].astype(jnp.float32) for q in range(9)]

    bf16 = jnp.bfloat16
    lane = lanes(16)
    depth = lane & 7
    depth48 = lanes(C) & 7
    low, mid, left_half = lane < 32, lane < 96, lane < 64
    own_lanes = jnp.where((lane >= 32) & mid, 1.0, 0.0)
    masks = [
        jnp.where(low, there[3 * bx], jnp.where(mid, there[3 * bx + 1], there[3 * bx + 2]))
        for bx in range(3)
    ]
    edge_masks = [
        jnp.where(left_half, there[3 * bx + 2], there[3 * bx]).astype(bf16) for bx in range(3)
    ]
    main_masks = [mask.astype(bf16) for mask in masks]
    masks = [mask[0:1] for mask in masks]
    own_row = own_lanes[0:1]

    cell = lane & 63
    for side, by, in_place, turn, turns in (
        (0, 0, cell < 48, 24, (48, 96, 16, 64)),
        (1, 2, cell < 24, -40, (24, 72, -8, 40)),
    ):
        slab = owner[3 + by]
        for ct in range(3):
            half = gathered_ref[slab, 6 + ct // 2]
            for q in range(2):
                sides_ref[side, 4 * ct + q] = gathered_ref[slab, 2 * ct + q]
                moved = [roll(half, turns[2 * q + n] - (64 if ct == 1 else 0)) for n in range(2)]
                sides_ref[side, 4 * ct + q + 2] = jnp.where(
                    in_place,
                    roll(gathered_ref[slab, 2 * ct + q], turn),
                    jnp.where(left_half, moved[0], moved[1]),
                )

    def placed(ct, bx, i):
        if bx == 1:
            tile, half = 4 * ct + i // 2, i % 2
            parts = [sides_ref[0, tile], own_ref[tile], sides_ref[1, tile]]
        else:
            if i == (3 if bx == 0 else 4):
                tile, half = 6 + ct // 2, ct % 2
            else:
                tile, half = 2 * ct + (i // 2 - 2 if bx == 0 else i // 2), i % 2
            parts = [gathered_ref[owner[3 * bx + by], tile] for by in range(3)]
        outer = 96 - 64 * half
        return roll(parts[0], outer), roll(parts[1], 32 - 64 * half), roll(parts[2], outer)

    zero = jnp.zeros((16, LANES), bf16)
    for plane in range(18):
        bx, i = (plane + 3) // 8, (plane + 3) % 8
        for ct in range(3):
            before, middle, after = placed(ct, bx, i)
            main = jnp.where(low, before, jnp.where(mid, middle, after)) * main_masks[bx]
            edge = jnp.where(left_half, after, before) * edge_masks[bx]
            for c in (-1, 0, 1):
                if c == 0:
                    main_c, edge_c = main, edge
                else:
                    keep = depth >= 1 if c == 1 else depth <= 6
                    main_c, edge_c = jnp.where(keep, main, zero), jnp.where(keep, edge, zero)
                for b in (-1, 0, 1):
                    step = 8 * b + c
                    if b == 1:
                        source = jnp.where(lane < step, edge_c, main_c)
                    elif b == -1:
                        source = jnp.where(lane >= LANES + step, edge_c, main_c)
                    else:
                        source = main_c
                    row = (3 * (b + 1) + c + 1) * C + 16 * ct
                    x9_ref[row : row + 16, LANES * plane : LANES * (plane + 1)] = (
                        roll(source, -step) if step else source
                    )

    def plane_cols(plane):
        return slice(LANES * plane, LANES * (plane + 1))

    def summed(plane, stride):
        return (
            product_ref[0:C, plane_cols(plane)]
            + product_ref[C : 2 * C, plane_cols(plane + stride)]
            + product_ref[2 * C : 3 * C, plane_cols(plane + 2 * stride)]
        )

    for n in range(9):
        cols = slice(256 * n, 256 * (n + 1))
        product_ref[:, cols] = matmul(w1_ref[...], x9_ref[:, cols])

    for plane in range(16):
        bx = (plane + 4) // 8
        pre = summed(plane, 1)
        negative = jnp.exp(jnp.minimum(pre, 0.0))
        if 4 <= plane < 12:
            slope1_ref[:, plane_cols(plane - 4)] = jnp.where(pre > 0, 1.0, negative)
        hidden = jnp.where(pre > 0, pre, negative - 1.0) * masks[bx]
        hidden = hidden.astype(bf16)
        for c in (-1, 0, 1):
            if c == 0:
                source = hidden
            else:
                keep = depth48 >= 2 if c == 1 else depth48 <= 5
                source = jnp.where(keep, hidden, jnp.zeros((C, LANES), bf16))
            for b in (-1, 0, 1):
                step = 16 * b + 2 * c
                row = (3 * (b + 1) + c + 1) * C
                h9_ref[row : row + C, plane_cols(plane)] = roll(source, -step) if step else source

    for n in range(8):
        cols = slice(256 * n, 256 * (n + 1))
        product_ref[:, cols] = matmul(w2_ref[...], h9_ref[:, cols])

    for plane in range(12):
        bx = (plane + 6) // 8
        pre = summed(plane, 2)
        negative = jnp.exp(jnp.minimum(pre, 0.0))
        slope2_ref[:, plane_cols(plane)] = jnp.where(pre > 0, 1.0, negative) * masks[bx]
        hidden = jnp.where(pre > 0, pre, negative - 1.0) * masks[bx]
        hid2_ref[:, plane_cols(plane)] = hidden.astype(jnp.bfloat16)

    logits = matmul(h_ref[...], hid2_ref[...])
    targets = []
    for bx, half in ((0, 1), (1, 0), (1, 1), (2, 1)):
        if bx == 1:
            before = roll(gathered_ref[owner[3], 7], -48 - 16 * half)
            middle = roll(own_ref[12], 32 - 64 * half)
            after = roll(gathered_ref[owner[5], 7], 32 - 16 * half)
        else:
            parts = [gathered_ref[owner[3 * bx + by], 7] for by in range(3)]
            before, middle, after = roll(parts[0], 32), roll(parts[1], -32), roll(parts[2], 32)
        cells = jnp.where(low, before, jnp.where(mid, middle, after))
        targets.append(cells.astype(jnp.float32))
    grads = []
    for plane in range(12):
        bx, i = (plane + 6) // 8, (plane + 6) % 8
        value = logits[:, plane_cols(plane)]
        if bx == 1:
            wanted = targets[1 + i % 2][4 * (i // 2) : 4 * (i // 2) + 4]
        else:
            wanted = targets[0 if bx == 0 else 3][4 * (i % 2) : 4 * (i % 2) + 4]
        wanted = jnp.concatenate([wanted, jnp.zeros((12, LANES), jnp.float32)], axis=0)
        sigmoid = 1.0 / (1.0 + jnp.exp(-value))
        grads.append((sigmoid - wanted) * masks[bx] * scale)
    for q in range(4):
        first = roll(logits[:, plane_cols(2 + 2 * q)], -32)
        second = roll(logits[:, plane_cols(3 + 2 * q)], 32)
        logits_ref[:, 0, plane_cols(q)] = jnp.where(left_half, first, second)[0:3]

    grad_logit = jnp.concatenate(grads, axis=1).astype(jnp.bfloat16)
    back = matmul(ht_ref[...], grad_logit)
    grad2_ref[...] = (back * slope2_ref[...]).astype(jnp.bfloat16)
    own_grads = jnp.concatenate([grads[2 + x] * own_row for x in range(8)], axis=1)
    head_part = matmul_lanes(hid2_ref[:, 2 * LANES : 10 * LANES], own_grads.astype(jnp.bfloat16))

    own_bf16 = jnp.broadcast_to(own_row, (C, LANES)).astype(bf16)
    shifted_ref[...] = jnp.zeros_like(shifted_ref)
    for a in range(3):
        for x in range(8):
            shifted_ref[C * a : C * (a + 1), plane_cols(x + 2 * a)] = (
                grad2_ref[:, plane_cols(x + 2)] * own_bf16
            )
    second_part = matmul_lanes(shifted_ref[...], h9_ref[:, 2 * LANES : 14 * LANES])

    for a in range(3):
        for x in range(8):
            shifted_ref[C * a : C * (a + 1), plane_cols(x)] = grad2_ref[:, plane_cols(x + 4 - 2 * a)]
    for n in range(4):
        cols = slice(256 * n, 256 * (n + 1))
        back_ref[:, cols] = matmul(w2t_ref[...], shifted_ref[:, cols])
    grad1 = []
    for x in range(8):
        total = jnp.zeros((C, LANES), jnp.float32)
        for c in (-1, 0, 1):
            part = jnp.zeros((C, LANES), jnp.float32)
            for b in (-1, 0, 1):
                row = (3 * (b + 1) + c + 1) * C
                step = 16 * b + 2 * c
                piece = back_ref[row : row + C, plane_cols(x)]
                part += roll(piece, step) if step else piece
            if c:
                part = jnp.where(depth48 >= 2 if c == 1 else depth48 <= 5, part, 0.0)
            total += part
        grad1.append((total * slope1_ref[:, plane_cols(x)] * own_row).astype(jnp.bfloat16))

    shifted_ref[...] = jnp.zeros_like(shifted_ref)
    for a in range(3):
        for x in range(8):
            shifted_ref[C * a : C * (a + 1), plane_cols(x + a)] = grad1[x]
    first_part = matmul_lanes(
        shifted_ref[:, 0 : 10 * LANES], x9_ref[:, 4 * LANES : 14 * LANES]
    )

    head_part = jnp.concatenate([head_part, jnp.zeros((24, 16), jnp.float32)], axis=0)
    nothing = jnp.zeros((72, 16), jnp.float32)
    for base, part, extra in ((0, first_part, nothing), (HALF, second_part, head_part)):
        for q in range(3):
            packed_ref[base + 144 * q : base + 144 * (q + 1), :] = part[:, plane_cols(q)].astype(bf16)
        tail = [part[0:72, 384:], part[72:144, 384:], extra, nothing]
        tail = jnp.concatenate([jnp.concatenate(tail, axis=1), jnp.zeros((8, LANES))], axis=0)
        packed_ref[base + 432 : base + HALF, :] = tail.astype(bf16)


def sum_kernel(parts_ref, out_ref):
    total = parts_ref[0].astype(jnp.float32)
    for s in range(1, parts_ref.shape[0]):
        total += parts_ref[s].astype(jnp.float32)
    total = total.astype(jnp.bfloat16)
    for s in range(out_ref.shape[0]):
        out_ref[s] = total


def unpack_kernel(rows_ref, first_ref, second_ref, head_ref):
    for k, out in ((0, first_ref), (1, second_ref)):
        half = rows_ref[HALF * k : HALF * (k + 1), :].astype(jnp.float32)
        tail = jnp.concatenate([half[432:504, 0:C], half[432:504, C : 2 * C]], axis=0)
        tiles = [half[144 * q : 144 * (q + 1), :] for q in range(3)]
        whole = jnp.concatenate(tiles + [tail], axis=1)
        for a in range(3):
            for t in range(9):
                out[9 * a + t] = whole[C * a : C * (a + 1), C * t : C * (t + 1)]
        if k:
            head_ref[...] = half[432 : 432 + C, 96:112].T[0:3]


def on_device_flat(features, device_block, conv_first, conv_second, head_weight, targets):
    space_count = lax.axis_size("space")
    device_count = lax.axis_size("dp") * space_count
    bf16, f32 = jnp.bfloat16, jnp.float32
    small = pltpu.CompilerParams(vmem_limit_bytes=8 * 1024 * 1024)
    shape = jax.ShapeDtypeStruct
    vmem = pl.BlockSpec(memory_space=pltpu.VMEM)

    def swap(values, mask):
        return lax.ppermute(values, "space", [(s, s ^ mask) for s in range(space_count)])

    mate_features, mate_targets = swap(features, 1), swap(targets, 1)
    partners = (2, 4, 6)
    own, mate_slab, *pairs = pl.pallas_call(
        pack_kernel,
        out_shape=(
            shape((13, 16, LANES), bf16),
            shape((8, 16, LANES), bf16),
            *[shape((2, 8, 16, LANES), bf16) for _ in partners],
        ),
        in_specs=[vmem] * 5,
        out_specs=(vmem,) * 5,
        scratch_shapes=[pltpu.VMEM((8, 8, 16, LANES), bf16)],
        compiler_params=small,
        name="pack_slabs",
    )(
        device_block,
        features[0, 0],
        targets[0].transpose(1, 0, 2),
        mate_features[0, 0],
        mate_targets[0].transpose(1, 0, 2),
    )
    pairs = [swap(pair, mask) for pair, mask in zip(pairs, partners)]

    w1, w2, w2t, head, head_t = pl.pallas_call(
        weights_kernel,
        out_shape=(
            shape((3 * C, 9 * C), bf16),
            shape((3 * C, 9 * C), bf16),
            shape((9 * C, 3 * C), bf16),
            shape((16, C), bf16),
            shape((C, 16), bf16),
        ),
        in_specs=[vmem] * 3,
        out_specs=(vmem,) * 5,
        compiler_params=small,
        cost_estimate=pl.CostEstimate(flops=2_000_000, bytes_accessed=4_000_000, transcendentals=0),
        name="lay_out_weights",
    )(conv_first.transpose(1, 0, 2), conv_second.transpose(1, 0, 2), head_weight)

    scale = (device_count * 3 * CELLS) ** (-0.5)
    logits, packed = pl.pallas_call(
        functools.partial(crop_kernel, scale),
        out_shape=(shape((3, 1, CELLS), f32), shape((2 * HALF, LANES), bf16)),
        in_specs=[vmem] * 11,
        out_specs=(vmem,) * 2,
        scratch_shapes=[
            pltpu.SMEM((2, 16), jnp.int32),
            pltpu.VMEM((space_count, 8, 16, LANES), bf16),
            pltpu.VMEM((2, 12, 16, LANES), bf16),
            pltpu.VMEM((9 * C, 18 * LANES), bf16),
            pltpu.VMEM((9 * C, 16 * LANES), bf16),
            pltpu.VMEM((3 * C, 18 * LANES), f32),
            pltpu.VMEM((C, 8 * LANES), f32),
            pltpu.VMEM((C, 12 * LANES), f32),
            pltpu.VMEM((C, 12 * LANES), bf16),
            pltpu.VMEM((C, 12 * LANES), bf16),
            pltpu.VMEM((3 * C, 12 * LANES), bf16),
            pltpu.VMEM((9 * C, 8 * LANES), f32),
        ],
        compiler_params=pltpu.CompilerParams(vmem_limit_bytes=20 * 1024 * 1024),
        name="forward_backward",
    )(device_block, own, mate_slab, *pairs, w1, w2, w2t, head, head_t)

    rows = HALF * 2 // device_count
    terms = lax.all_to_all(
        packed.reshape(device_count, rows, LANES), ("dp", "space"), 0, 0, tiled=True
    )
    summed = pl.pallas_call(
        sum_kernel,
        out_shape=shape((device_count, rows, LANES), bf16),
        in_specs=[vmem],
        out_specs=vmem,
        compiler_params=small,
        name="sum_terms",
    )(terms)
    total = lax.all_to_all(summed, ("dp", "space"), 0, 0, tiled=True)
    grad_first, grad_second, grad_head = pl.pallas_call(
        unpack_kernel,
        out_shape=(shape((27, C, C), f32), shape((27, C, C), f32), shape((3, C), f32)),
        in_specs=[vmem],
        out_specs=(vmem,) * 3,
        compiler_params=small,
        name="unpack_gradients",
    )(total.reshape(2 * HALF, LANES))
    return (
        logits.transpose(1, 0, 2)[None],
        grad_first.transpose(1, 0, 2),
        grad_second.transpose(1, 0, 2),
        grad_head,
    )


def solution(mesh):
    in_specs = (
        P("dp", "space", None, None),
        P("dp", None),
        P(),
        P(),
        P(),
        P("dp", "space", None, None),
    )
    out_specs = (P("dp", "space", None, None), P(), P(), P())
    flat = mesh.shape["space"] == 8 and mesh.shape["dp"] == 4
    return jax.shard_map(
        on_device_flat if flat else on_device_deep,
        mesh=mesh,
        in_specs=in_specs,
        out_specs=out_specs,
        check_vma=False,
    )
```

```python
import functools

import jax
import jax.numpy as jnp
from jax import lax
from jax.experimental import pallas as pl
from jax.experimental.pallas import tpu as pltpu
from jax.sharding import PartitionSpec as P

BS = 8


tap_offsets = [
    (tap_index // 9 - 1, tap_index // 3 % 3 - 1, tap_index % 3 - 1) for tap_index in range(27)
]


def elu_pair(values):
    negative = jnp.exp(jnp.minimum(values, 0.0))
    return (jnp.where(values > 0, values, negative - 1.0), jnp.where(values > 0, 1.0, negative))


def neighbor_tables(device_block):
    space_count = lax.axis_size("space")
    depth_z = space_count // 8
    self_index = lax.axis_index("space")
    blocks = device_block[0]
    coords = jnp.stack([blocks // (4 * depth_z), blocks // depth_z % 4, blocks % depth_z])
    own_coords = lax.dynamic_index_in_dim(coords, self_index, 1, keepdims=False)
    offsets = jnp.array(tap_offsets, jnp.int32)
    limits = jnp.array([4, 4, depth_z], jnp.int32)
    wanted = own_coords[None, :] + offsets
    inside = jnp.all((wanted >= 0) & (wanted < limits[None, :]), axis=1) & (jnp.arange(27) != 13)
    wanted_id = (wanted[:, 0] * 4 + wanted[:, 1]) * depth_z + wanted[:, 2]
    matches = (blocks[None, :] == wanted_id[:, None]) & inside[:, None]
    devices = jnp.arange(space_count, dtype=jnp.int32)
    owner_row = jnp.sum(jnp.where(matches, devices[None, :], 0), axis=1)
    present = jnp.any(matches, axis=1)
    relative = coords - own_coords[:, None]
    adjacent = jnp.all(jnp.abs(relative) <= 1, axis=0) & (devices != self_index)
    send_tap = jnp.where(
        adjacent, (relative[0] + 1) * 9 + (relative[1] + 1) * 3 + relative[2] + 1, 13
    )
    return (owner_row, present, send_tap)


def region_slice(block_data, offset, depth_cells):
    span_list = []
    for step_value in offset:
        if step_value == 1:
            span_list.append(slice(BS - depth_cells, BS))
        elif step_value == -1:
            span_list.append(slice(0, depth_cells))
        else:
            span_list.append(slice(0, BS))
    return block_data[:, span_list[0], span_list[1], span_list[2]]


def surround(block_data, depth_cells, tables):
    owner_row, present, send_tap = tables
    channels = block_data.shape[0]
    length = depth_cells * BS * BS
    pieces = []
    for tap_index in range(27):
        if tap_index == 13:
            pieces.append(jnp.zeros((channels, length), block_data.dtype))
        else:
            region = region_slice(block_data, tap_offsets[tap_index], depth_cells).reshape(
                channels, -1
            )
            pieces.append(jnp.pad(region, ((0, 0), (0, length - region.shape[1]))))
    outgoing = jnp.stack(pieces)
    sending = outgoing[send_tap]
    by_source = lax.all_to_all(sending, "space", split_axis=0, concat_axis=0, tiled=True)
    incoming = jnp.where(
        present[:, None, None], by_source[owner_row], jnp.zeros((), block_data.dtype)
    )
    rows_x = []
    for step_x in range(3):
        rows_y = []
        for step_y in range(3):
            rows_z = []
            for step_z in range(3):
                tap_index = step_x * 9 + step_y * 3 + step_z
                if tap_index == 13:
                    rows_z.append(block_data)
                else:
                    extent_list = [
                        BS if step_value == 1 else depth_cells
                        for step_value in (step_x, step_y, step_z)
                    ]
                    count_cells = extent_list[0] * extent_list[1] * extent_list[2]
                    rows_z.append(
                        incoming[tap_index][:, :count_cells].reshape(
                            channels, extent_list[0], extent_list[1], extent_list[2]
                        )
                    )
            rows_y.append(jnp.concatenate(rows_z, axis=3))
        rows_x.append(jnp.concatenate(rows_y, axis=2))
    return jnp.concatenate(rows_x, axis=1)


def conv_padded(padded, kernel, dilation):
    result = lax.conv_general_dilated(
        padded[None],
        kernel,
        (1, 1, 1),
        "VALID",
        rhs_dilation=(dilation, dilation, dilation),
        dimension_numbers=("NCDHW", "OIDHW", "NCDHW"),
        preferred_element_type=jnp.float32,
    )
    return result[0].reshape(kernel.shape[0], BS * BS * BS)


def kernel_grad(padded, grad_rows, dilation):
    channels = padded.shape[0]
    outputs = grad_rows.shape[0]
    grad_block = grad_rows.reshape(outputs, 1, BS, BS, BS)
    result = lax.conv_general_dilated(
        padded[None],
        grad_block,
        (dilation, dilation, dilation),
        "VALID",
        dimension_numbers=("CNDHW", "OIDHW", "NCDHW"),
        preferred_element_type=jnp.float32,
    )
    return result.reshape(channels, outputs, 27).transpose(1, 2, 0)


def on_device_deep(features, device_block, conv_first, conv_second, head_weight, targets):
    channels = features.shape[2]
    tables = neighbor_tables(device_block)
    kernel_first = conv_first.reshape(channels, 3, 3, 3, channels).transpose(0, 4, 1, 2, 3)
    kernel_second = conv_second.reshape(channels, 3, 3, 3, channels).transpose(0, 4, 1, 2, 3)
    block_in = features[0, 0].reshape(channels, BS, BS, BS)
    padded_in = surround(block_in, 1, tables)
    pre_first = conv_padded(padded_in, kernel_first, 1)
    act_first, slope_first = elu_pair(pre_first)
    hid_first = act_first.astype(jnp.bfloat16)
    padded_first = surround(hid_first.reshape(channels, BS, BS, BS), 2, tables)
    pre_second = conv_padded(padded_first, kernel_second, 2)
    act_second, slope_second = elu_pair(pre_second)
    hid_second = act_second.astype(jnp.bfloat16)
    logits = jnp.dot(head_weight, hid_second, preferred_element_type=jnp.float32)
    scale = (lax.axis_size("dp") * lax.axis_size("space") * 3 * BS * BS * BS) ** (-0.5)
    grad_logit = ((jax.nn.sigmoid(logits) - targets[0, 0].astype(jnp.float32)) * scale).astype(
        jnp.bfloat16
    )
    grad_head = lax.dot_general(
        grad_logit, hid_second, (((1,), (1,)), ((), ())), preferred_element_type=jnp.float32
    )
    back_second = lax.dot_general(
        head_weight, grad_logit, (((0,), (0,)), ((), ())), preferred_element_type=jnp.float32
    )
    grad_pre_second = (back_second * slope_second).astype(jnp.bfloat16)
    grad_second = kernel_grad(padded_first, grad_pre_second, 2)
    padded_grad = surround(grad_pre_second.reshape(channels, BS, BS, BS), 2, tables)
    kernel_back = jnp.transpose(kernel_second[:, :, ::-1, ::-1, ::-1], (1, 0, 2, 3, 4))
    back_first = conv_padded(padded_grad, kernel_back, 2)
    grad_pre_first = (back_first * slope_first).astype(jnp.bfloat16)
    grad_first = kernel_grad(padded_in, grad_pre_first, 1)
    grad_first, grad_second, grad_head = lax.psum(
        (grad_first, grad_second, grad_head), ("dp", "space")
    )
    return (logits[None, None], grad_first, grad_second, grad_head)


C = 48
CELLS = 512
HALF = 512
LANES = 128


def lanes(rows=1):
    return lax.broadcasted_iota(jnp.int32, (rows, LANES), 1)


def roll(values, shift):
    return pltpu.roll(values, shift % LANES, 1) if shift % LANES else values


def listed_blocks(block_ref, me):
    ids = block_ref[...].astype(jnp.float32)
    index = lax.broadcasted_iota(jnp.int32, ids.shape, 1)
    return [
        jnp.sum(jnp.where(index == (me ^ k), ids, 0.0)).astype(jnp.int32)
        for k in range(ids.shape[1])
    ]


def apart(source, target):
    return (target >> 2) - (source >> 2), (target & 3) - (source & 3)


PARTNERS = (6, 4, 2)


def block_tiles(features_ref, targets_ref):
    tiles = [
        [features_ref[16 * ct : 16 * (ct + 1), LANES * q : LANES * (q + 1)] for q in range(4)]
        for ct in range(3)
    ]
    targets = targets_ref[:, 0, :].astype(jnp.float32)
    targets = jnp.concatenate([targets, jnp.zeros((1, CELLS), jnp.float32)], axis=0)
    return tiles, [targets[:, LANES * q : LANES * (q + 1)] for q in range(4)]


def write_cases(tiles, rows, cases_ref):
    lane = lanes(16)
    left = lane < 64
    cell = lane & 63
    target_tile = jnp.concatenate(rows, axis=0)

    def write(case, pairs, halves, wanted):
        for ct in range(3):
            cases_ref[case, 2 * ct] = pairs[ct][0]
            cases_ref[case, 2 * ct + 1] = pairs[ct][1]
        cases_ref[case, 6] = jnp.where(left, halves[0], halves[1])
        cases_ref[case, 7] = jnp.where(left, halves[2], wanted.astype(jnp.bfloat16))

    for case, pair, single, q in ((0, (2, 3), 1, 3), (1, (0, 1), 2, 0)):
        turns = (64, 0, 64) if case == 0 else (0, 64, 0)
        halves = [roll(tiles[ct][single], turns[ct]) for ct in range(3)]
        both = [roll(rows[q], 64), rows[q], jnp.zeros((8, LANES), jnp.float32)]
        wanted = jnp.concatenate(both, axis=0)
        write(case, [(t[pair[0]], t[pair[1]]) for t in tiles], halves, wanted)
    for case, spare, turn, turns, target_turns in (
        (2, cell < 24, -24, (-48, -96, -16, -64), (16, -32)),
        (3, cell >= 40, 40, (-24, -72, 8, -40), (64, 16)),
    ):
        pairs, halves = [], []
        for ct, t in enumerate(tiles):
            pairs.append([jnp.where(spare, roll(t[q + 2], turn), t[q]) for q in range(2)])
            moved = [roll(t[2 + n // 2], turns[n] + (64 if ct == 1 else 0)) for n in range(4)]
            half = jnp.where(cell < 16, moved[0], jnp.where(cell < 32, moved[1], moved[2]))
            halves.append(jnp.where(cell < 48, half, moved[3]))
        wanted = [roll(target_tile, n) for n in target_turns]
        write(case, pairs, halves, jnp.where(lane < 80, wanted[0], wanted[1]))


def case_of(source, target):
    dx, dy = apart(source, target)
    return jnp.where(dx > 0, 0, jnp.where(dx < 0, 1, jnp.where(dy > 0, 2, 3)))


def pack_own_kernel(block_ref, features_ref, targets_ref, own_ref, slabs_ref, cases_ref):
    blocks = listed_blocks(block_ref, lax.axis_index("space"))
    tiles, rows = block_tiles(features_ref, targets_ref)
    for ct in range(3):
        for q in range(4):
            own_ref[4 * ct + q] = tiles[ct][q]
    own_ref[12] = jnp.concatenate(rows, axis=0).astype(jnp.bfloat16)
    write_cases(tiles, rows, cases_ref)
    for n, k in enumerate(PARTNERS):
        slabs_ref[n] = cases_ref[case_of(blocks[0], blocks[k])]


def pack_mate_kernel(block_ref, features_ref, targets_ref, slabs_ref, mate_ref, *refs):
    *pair_refs, cases_ref = refs
    blocks = listed_blocks(block_ref, lax.axis_index("space"))
    write_cases(*block_tiles(features_ref, targets_ref), cases_ref)
    mate_ref[...] = cases_ref[case_of(blocks[1], blocks[0])]
    for n, (k, ref) in enumerate(zip(PARTNERS, pair_refs)):
        ref[0] = slabs_ref[n]
        ref[1] = cases_ref[case_of(blocks[1], blocks[k])]


def stacked_taps(ref):
    rows = []
    for a in range(3):
        taps = [ref[9 * a + t] for t in range(9)]
        rows.append(jnp.concatenate(taps, axis=1))
    return jnp.concatenate(rows, axis=0)


def weights_kernel(first_ref, second_ref, head_ref, w1_ref, w2_ref, w2t_ref, h_ref, ht_ref):
    w1_ref[...] = stacked_taps(first_ref)
    whole = stacked_taps(second_ref)
    w2_ref[...] = whole
    w2t_ref[...] = whole.T
    head = head_ref[...].astype(jnp.float32)
    head = jnp.concatenate([head, jnp.zeros((13, C), jnp.float32)], axis=0)
    h_ref[...] = head.astype(jnp.bfloat16)
    ht_ref[...] = head.T.astype(jnp.bfloat16)


def matmul(left, right):
    return lax.dot_general(
        left, right, (((1,), (0,)), ((), ())), preferred_element_type=jnp.float32
    )


def matmul_lanes(left, right):
    return lax.dot_general(
        left, right, (((1,), (1,)), ((), ())), preferred_element_type=jnp.float32
    )


def crop_kernel(scale, block_ref, own_ref, mate_ref, *refs):
    crop_body(scale, block_ref, own_ref, mate_ref, refs[:3], *refs[3:])


def crop_body(
    scale,
    block_ref,
    own_ref,
    mate_ref,
    pairs,
    w1_ref,
    w2_ref,
    w2t_ref,
    h_ref,
    ht_ref,
    logits_ref,
    packed_ref,
    table_ref,
    gathered_ref,
    sides_ref,
    x9_ref,
    h9_ref,
    product_ref,
    slope1_ref,
    slope2_ref,
    hid2_ref,
    grad2_ref,
    shifted_ref,
    back_ref,
):
    gathered_ref[1] = mate_ref[...]
    for k, pair in zip(PARTNERS, pairs):
        for j in range(2):
            gathered_ref[k + j] = pair[j]
    blocks = listed_blocks(block_ref, lax.axis_index("space"))
    for slot in range(10):
        table_ref[0, slot] = 1
        table_ref[1, slot] = 0
    table_ref[1, 4] = 1
    for k in range(1, len(blocks)):
        dx, dy = apart(blocks[0], blocks[k])
        near = (dx >= -1) & (dx <= 1) & (dy >= -1) & (dy <= 1)
        slot = jnp.where(near, dx * 3 + dy + 4, 9)
        table_ref[0, slot] = k
        table_ref[1, slot] = 1

    owner = [table_ref[0, q] for q in range(9)]
    there = [table_ref[1, q].astype(jnp.float32) for q in range(9)]

    bf16 = jnp.bfloat16
    lane = lanes(16)
    depth = lane & 7
    depth48 = lanes(C) & 7
    low, mid, left_half = lane < 32, lane < 96, lane < 64
    own_lanes = jnp.where((lane >= 32) & mid, 1.0, 0.0)
    masks = [
        jnp.where(low, there[3 * bx], jnp.where(mid, there[3 * bx + 1], there[3 * bx + 2]))
        for bx in range(3)
    ]
    edge_masks = [
        jnp.where(left_half, there[3 * bx + 2], there[3 * bx]).astype(bf16) for bx in range(3)
    ]
    main_masks = [mask.astype(bf16) for mask in masks]
    masks = [mask[0:1] for mask in masks]
    own_row = own_lanes[0:1]

    cell = lane & 63
    for side, by, in_place, turn, turns in (
        (0, 0, cell < 48, 24, (48, 96, 16, 64)),
        (1, 2, cell < 24, -40, (24, 72, -8, 40)),
    ):
        slab = owner[3 + by]
        for ct in range(3):
            half = gathered_ref[slab, 6 + ct // 2]
            for q in range(2):
                sides_ref[side, 4 * ct + q] = gathered_ref[slab, 2 * ct + q]
                moved = [roll(half, turns[2 * q + n] - (64 if ct == 1 else 0)) for n in range(2)]
                sides_ref[side, 4 * ct + q + 2] = jnp.where(
                    in_place,
                    roll(gathered_ref[slab, 2 * ct + q], turn),
                    jnp.where(left_half, moved[0], moved[1]),
                )

    def placed(ct, bx, i):
        if bx == 1:
            tile, half = 4 * ct + i // 2, i % 2
            parts = [sides_ref[0, tile], own_ref[tile], sides_ref[1, tile]]
        else:
            if i == (3 if bx == 0 else 4):
                tile, half = 6 + ct // 2, ct % 2
            else:
                tile, half = 2 * ct + (i // 2 - 2 if bx == 0 else i // 2), i % 2
            parts = [gathered_ref[owner[3 * bx + by], tile] for by in range(3)]
        outer = 96 - 64 * half
        return roll(parts[0], outer), roll(parts[1], 32 - 64 * half), roll(parts[2], outer)

    zero = jnp.zeros((16, LANES), bf16)
    for plane in range(18):
        bx, i = (plane + 3) // 8, (plane + 3) % 8
        for ct in range(3):
            before, middle, after = placed(ct, bx, i)
            main = jnp.where(low, before, jnp.where(mid, middle, after)) * main_masks[bx]
            edge = jnp.where(left_half, after, before) * edge_masks[bx]
            for c in (-1, 0, 1):
                if c == 0:
                    main_c, edge_c = main, edge
                else:
                    keep = depth >= 1 if c == 1 else depth <= 6
                    main_c, edge_c = jnp.where(keep, main, zero), jnp.where(keep, edge, zero)
                for b in (-1, 0, 1):
                    step = 8 * b + c
                    if b == 1:
                        source = jnp.where(lane < step, edge_c, main_c)
                    elif b == -1:
                        source = jnp.where(lane >= LANES + step, edge_c, main_c)
                    else:
                        source = main_c
                    row = (3 * (b + 1) + c + 1) * C + 16 * ct
                    x9_ref[row : row + 16, LANES * plane : LANES * (plane + 1)] = (
                        roll(source, -step) if step else source
                    )

    def plane_cols(plane):
        return slice(LANES * plane, LANES * (plane + 1))

    def summed(plane, stride):
        return (
            product_ref[0:C, plane_cols(plane)]
            + product_ref[C : 2 * C, plane_cols(plane + stride)]
            + product_ref[2 * C : 3 * C, plane_cols(plane + 2 * stride)]
        )

    for n in range(9):
        cols = slice(256 * n, 256 * (n + 1))
        product_ref[:, cols] = matmul(w1_ref[...], x9_ref[:, cols])

    for plane in range(16):
        bx = (plane + 4) // 8
        pre = summed(plane, 1)
        negative = jnp.exp(jnp.minimum(pre, 0.0))
        if 4 <= plane < 12:
            slope1_ref[:, plane_cols(plane - 4)] = jnp.where(pre > 0, 1.0, negative)
        hidden = jnp.where(pre > 0, pre, negative - 1.0) * masks[bx]
        hidden = hidden.astype(bf16)
        for c in (-1, 0, 1):
            if c == 0:
                source = hidden
            else:
                keep = depth48 >= 2 if c == 1 else depth48 <= 5
                source = jnp.where(keep, hidden, jnp.zeros((C, LANES), bf16))
            for b in (-1, 0, 1):
                step = 16 * b + 2 * c
                row = (3 * (b + 1) + c + 1) * C
                h9_ref[row : row + C, plane_cols(plane)] = roll(source, -step) if step else source

    for n in range(8):
        cols = slice(256 * n, 256 * (n + 1))
        product_ref[:, cols] = matmul(w2_ref[...], h9_ref[:, cols])

    for plane in range(12):
        bx = (plane + 6) // 8
        pre = summed(plane, 2)
        negative = jnp.exp(jnp.minimum(pre, 0.0))
        slope2_ref[:, plane_cols(plane)] = jnp.where(pre > 0, 1.0, negative) * masks[bx]
        hidden = jnp.where(pre > 0, pre, negative - 1.0) * masks[bx]
        hid2_ref[:, plane_cols(plane)] = hidden.astype(jnp.bfloat16)

    logits = matmul(h_ref[...], hid2_ref[...])
    targets = []
    for bx, half in ((0, 1), (1, 0), (1, 1), (2, 1)):
        if bx == 1:
            before = roll(gathered_ref[owner[3], 7], -48 - 16 * half)
            middle = roll(own_ref[12], 32 - 64 * half)
            after = roll(gathered_ref[owner[5], 7], 32 - 16 * half)
        else:
            parts = [gathered_ref[owner[3 * bx + by], 7] for by in range(3)]
            before, middle, after = roll(parts[0], 32), roll(parts[1], -32), roll(parts[2], 32)
        cells = jnp.where(low, before, jnp.where(mid, middle, after))
        targets.append(cells.astype(jnp.float32))
    grads = []
    for plane in range(12):
        bx, i = (plane + 6) // 8, (plane + 6) % 8
        value = logits[:, plane_cols(plane)]
        if bx == 1:
            wanted = targets[1 + i % 2][4 * (i // 2) : 4 * (i // 2) + 4]
        else:
            wanted = targets[0 if bx == 0 else 3][4 * (i % 2) : 4 * (i % 2) + 4]
        wanted = jnp.concatenate([wanted, jnp.zeros((12, LANES), jnp.float32)], axis=0)
        sigmoid = 1.0 / (1.0 + jnp.exp(-value))
        grads.append((sigmoid - wanted) * masks[bx] * scale)
    for q in range(4):
        first = roll(logits[:, plane_cols(2 + 2 * q)], -32)
        second = roll(logits[:, plane_cols(3 + 2 * q)], 32)
        logits_ref[:, 0, plane_cols(q)] = jnp.where(left_half, first, second)[0:3]

    grad_logit = jnp.concatenate(grads, axis=1).astype(jnp.bfloat16)
    back = matmul(ht_ref[...], grad_logit)
    grad2_ref[...] = (back * slope2_ref[...]).astype(jnp.bfloat16)
    own_grads = jnp.concatenate([grads[2 + x] * own_row for x in range(8)], axis=1)
    head_part = matmul_lanes(hid2_ref[:, 2 * LANES : 10 * LANES], own_grads.astype(jnp.bfloat16))

    own_bf16 = jnp.broadcast_to(own_row, (C, LANES)).astype(bf16)
    shifted_ref[...] = jnp.zeros_like(shifted_ref)
    for a in range(3):
        for x in range(8):
            shifted_ref[C * a : C * (a + 1), plane_cols(x + 2 * a)] = (
                grad2_ref[:, plane_cols(x + 2)] * own_bf16
            )
    second_part = matmul_lanes(shifted_ref[...], h9_ref[:, 2 * LANES : 14 * LANES])

    for a in range(3):
        for x in range(8):
            shifted_ref[C * a : C * (a + 1), plane_cols(x)] = grad2_ref[:, plane_cols(x + 4 - 2 * a)]
    for n in range(4):
        cols = slice(256 * n, 256 * (n + 1))
        back_ref[:, cols] = matmul(w2t_ref[...], shifted_ref[:, cols])
    grad1 = []
    for x in range(8):
        total = jnp.zeros((C, LANES), jnp.float32)
        for c in (-1, 0, 1):
            part = jnp.zeros((C, LANES), jnp.float32)
            for b in (-1, 0, 1):
                row = (3 * (b + 1) + c + 1) * C
                step = 16 * b + 2 * c
                piece = back_ref[row : row + C, plane_cols(x)]
                part += roll(piece, step) if step else piece
            if c:
                part = jnp.where(depth48 >= 2 if c == 1 else depth48 <= 5, part, 0.0)
            total += part
        grad1.append((total * slope1_ref[:, plane_cols(x)] * own_row).astype(jnp.bfloat16))

    shifted_ref[...] = jnp.zeros_like(shifted_ref)
    for a in range(3):
        for x in range(8):
            shifted_ref[C * a : C * (a + 1), plane_cols(x + a)] = grad1[x]
    first_part = matmul_lanes(
        shifted_ref[:, 0 : 10 * LANES], x9_ref[:, 4 * LANES : 14 * LANES]
    )

    head_part = jnp.concatenate([head_part, jnp.zeros((24, 16), jnp.float32)], axis=0)
    nothing = jnp.zeros((72, 16), jnp.float32)
    for base, part, extra in ((0, first_part, nothing), (HALF, second_part, head_part)):
        for q in range(3):
            packed_ref[base + 144 * q : base + 144 * (q + 1), :] = part[:, plane_cols(q)].astype(bf16)
        tail = [part[0:72, 384:], part[72:144, 384:], extra, nothing]
        tail = jnp.concatenate([jnp.concatenate(tail, axis=1), jnp.zeros((8, LANES))], axis=0)
        packed_ref[base + 432 : base + HALF, :] = tail.astype(bf16)


def sum_kernel(parts_ref, out_ref):
    total = parts_ref[0].astype(jnp.float32)
    for s in range(1, parts_ref.shape[0]):
        total += parts_ref[s].astype(jnp.float32)
    total = total.astype(jnp.bfloat16)
    for s in range(out_ref.shape[0]):
        out_ref[s] = total


def unpack_kernel(rows_ref, first_ref, second_ref, head_ref):
    for k, out in ((0, first_ref), (1, second_ref)):
        half = rows_ref[HALF * k : HALF * (k + 1), :].astype(jnp.float32)
        tail = jnp.concatenate([half[432:504, 0:C], half[432:504, C : 2 * C]], axis=0)
        tiles = [half[144 * q : 144 * (q + 1), :] for q in range(3)]
        whole = jnp.concatenate(tiles + [tail], axis=1)
        for a in range(3):
            for t in range(9):
                out[9 * a + t] = whole[C * a : C * (a + 1), C * t : C * (t + 1)]
        if k:
            head_ref[...] = half[432 : 432 + C, 96:112].T[0:3]


def on_device_flat(features, device_block, conv_first, conv_second, head_weight, targets):
    space_count = lax.axis_size("space")
    device_count = lax.axis_size("dp") * space_count
    bf16, f32 = jnp.bfloat16, jnp.float32
    small = pltpu.CompilerParams(vmem_limit_bytes=8 * 1024 * 1024)
    shape = jax.ShapeDtypeStruct
    vmem = pl.BlockSpec(memory_space=pltpu.VMEM)

    def swap(values, mask):
        return lax.ppermute(values, "space", [(s, s ^ mask) for s in range(space_count)])

    mate_features, mate_targets = swap(features, 1), swap(targets, 1)
    own, own_slabs = pl.pallas_call(
        pack_own_kernel,
        out_shape=(shape((13, 16, LANES), bf16), shape((3, 8, 16, LANES), bf16)),
        in_specs=[vmem] * 3,
        out_specs=(vmem,) * 2,
        scratch_shapes=[pltpu.VMEM((4, 8, 16, LANES), bf16)],
        compiler_params=small,
        cost_estimate=pl.CostEstimate(flops=1_000_000, bytes_accessed=2_000_000, transcendentals=0),
        name="pack_own",
    )(device_block, features[0, 0], targets[0].transpose(1, 0, 2))
    mate_slab, *pairs = pl.pallas_call(
        pack_mate_kernel,
        out_shape=(
            shape((8, 16, LANES), bf16),
            *[shape((2, 8, 16, LANES), bf16) for _ in PARTNERS],
        ),
        in_specs=[vmem] * 4,
        out_specs=(vmem,) * 4,
        scratch_shapes=[pltpu.VMEM((4, 8, 16, LANES), bf16)],
        compiler_params=small,
        name="pack_mate",
    )(device_block, mate_features[0, 0], mate_targets[0].transpose(1, 0, 2), own_slabs)
    pairs = [swap(pair, mask) for pair, mask in zip(pairs, PARTNERS)]

    w1, w2, w2t, head, head_t = pl.pallas_call(
        weights_kernel,
        out_shape=(
            shape((3 * C, 9 * C), bf16),
            shape((3 * C, 9 * C), bf16),
            shape((9 * C, 3 * C), bf16),
            shape((16, C), bf16),
            shape((C, 16), bf16),
        ),
        in_specs=[vmem] * 3,
        out_specs=(vmem,) * 5,
        compiler_params=small,
        cost_estimate=pl.CostEstimate(flops=2_000_000, bytes_accessed=4_000_000, transcendentals=0),
        name="lay_out_weights",
    )(conv_first.transpose(1, 0, 2), conv_second.transpose(1, 0, 2), head_weight)

    scale = (device_count * 3 * CELLS) ** (-0.5)
    logits, packed = pl.pallas_call(
        functools.partial(crop_kernel, scale),
        out_shape=(shape((3, 1, CELLS), f32), shape((2 * HALF, LANES), bf16)),
        in_specs=[vmem] * 11,
        out_specs=(vmem,) * 2,
        scratch_shapes=[
            pltpu.SMEM((2, 16), jnp.int32),
            pltpu.VMEM((space_count, 8, 16, LANES), bf16),
            pltpu.VMEM((2, 12, 16, LANES), bf16),
            pltpu.VMEM((9 * C, 18 * LANES), bf16),
            pltpu.VMEM((9 * C, 16 * LANES), bf16),
            pltpu.VMEM((3 * C, 18 * LANES), f32),
            pltpu.VMEM((C, 8 * LANES), f32),
            pltpu.VMEM((C, 12 * LANES), f32),
            pltpu.VMEM((C, 12 * LANES), bf16),
            pltpu.VMEM((C, 12 * LANES), bf16),
            pltpu.VMEM((3 * C, 12 * LANES), bf16),
            pltpu.VMEM((9 * C, 8 * LANES), f32),
        ],
        compiler_params=pltpu.CompilerParams(vmem_limit_bytes=20 * 1024 * 1024),
        name="forward_backward",
    )(device_block, own, mate_slab, *pairs, w1, w2, w2t, head, head_t)

    rows = HALF * 2 // device_count
    terms = lax.all_to_all(
        packed.reshape(device_count, rows, LANES), ("dp", "space"), 0, 0, tiled=True
    )
    summed = pl.pallas_call(
        sum_kernel,
        out_shape=shape((device_count, rows, LANES), bf16),
        in_specs=[vmem],
        out_specs=vmem,
        compiler_params=small,
        name="sum_terms",
    )(terms)
    total = lax.all_to_all(summed, ("dp", "space"), 0, 0, tiled=True)
    grad_first, grad_second, grad_head = pl.pallas_call(
        unpack_kernel,
        out_shape=(shape((27, C, C), f32), shape((27, C, C), f32), shape((3, C), f32)),
        in_specs=[vmem],
        out_specs=(vmem,) * 3,
        compiler_params=small,
        name="unpack_gradients",
    )(total.reshape(2 * HALF, LANES))
    return (
        logits.transpose(1, 0, 2)[None],
        grad_first.transpose(1, 0, 2),
        grad_second.transpose(1, 0, 2),
        grad_head,
    )


def solution(mesh):
    in_specs = (
        P("dp", "space", None, None),
        P("dp", None),
        P(),
        P(),
        P(),
        P("dp", "space", None, None),
    )
    out_specs = (P("dp", "space", None, None), P(), P(), P())
    flat = mesh.shape["space"] == 8 and mesh.shape["dp"] == 4
    return jax.shard_map(
        on_device_flat if flat else on_device_deep,
        mesh=mesh,
        in_specs=in_specs,
        out_specs=out_specs,
        check_vma=False,
    )
```

```python
import functools

import jax
import jax.numpy as jnp
from jax import lax
from jax.experimental import pallas as pl
from jax.experimental.pallas import tpu as pltpu
from jax.sharding import PartitionSpec as P

BS = 8


tap_offsets = [
    (tap_index // 9 - 1, tap_index // 3 % 3 - 1, tap_index % 3 - 1) for tap_index in range(27)
]


def elu_pair(values):
    negative = jnp.exp(jnp.minimum(values, 0.0))
    return (jnp.where(values > 0, values, negative - 1.0), jnp.where(values > 0, 1.0, negative))


def neighbor_tables(device_block):
    space_count = lax.axis_size("space")
    depth_z = space_count // 8
    self_index = lax.axis_index("space")
    blocks = device_block[0]
    coords = jnp.stack([blocks // (4 * depth_z), blocks // depth_z % 4, blocks % depth_z])
    own_coords = lax.dynamic_index_in_dim(coords, self_index, 1, keepdims=False)
    offsets = jnp.array(tap_offsets, jnp.int32)
    limits = jnp.array([4, 4, depth_z], jnp.int32)
    wanted = own_coords[None, :] + offsets
    inside = jnp.all((wanted >= 0) & (wanted < limits[None, :]), axis=1) & (jnp.arange(27) != 13)
    wanted_id = (wanted[:, 0] * 4 + wanted[:, 1]) * depth_z + wanted[:, 2]
    matches = (blocks[None, :] == wanted_id[:, None]) & inside[:, None]
    devices = jnp.arange(space_count, dtype=jnp.int32)
    owner_row = jnp.sum(jnp.where(matches, devices[None, :], 0), axis=1)
    present = jnp.any(matches, axis=1)
    relative = coords - own_coords[:, None]
    adjacent = jnp.all(jnp.abs(relative) <= 1, axis=0) & (devices != self_index)
    send_tap = jnp.where(
        adjacent, (relative[0] + 1) * 9 + (relative[1] + 1) * 3 + relative[2] + 1, 13
    )
    return (owner_row, present, send_tap)


def region_slice(block_data, offset, depth_cells):
    span_list = []
    for step_value in offset:
        if step_value == 1:
            span_list.append(slice(BS - depth_cells, BS))
        elif step_value == -1:
            span_list.append(slice(0, depth_cells))
        else:
            span_list.append(slice(0, BS))
    return block_data[:, span_list[0], span_list[1], span_list[2]]


def surround(block_data, depth_cells, tables):
    owner_row, present, send_tap = tables
    channels = block_data.shape[0]
    length = depth_cells * BS * BS
    pieces = []
    for tap_index in range(27):
        if tap_index == 13:
            pieces.append(jnp.zeros((channels, length), block_data.dtype))
        else:
            region = region_slice(block_data, tap_offsets[tap_index], depth_cells).reshape(
                channels, -1
            )
            pieces.append(jnp.pad(region, ((0, 0), (0, length - region.shape[1]))))
    outgoing = jnp.stack(pieces)
    sending = outgoing[send_tap]
    by_source = lax.all_to_all(sending, "space", split_axis=0, concat_axis=0, tiled=True)
    incoming = jnp.where(
        present[:, None, None], by_source[owner_row], jnp.zeros((), block_data.dtype)
    )
    rows_x = []
    for step_x in range(3):
        rows_y = []
        for step_y in range(3):
            rows_z = []
            for step_z in range(3):
                tap_index = step_x * 9 + step_y * 3 + step_z
                if tap_index == 13:
                    rows_z.append(block_data)
                else:
                    extent_list = [
                        BS if step_value == 1 else depth_cells
                        for step_value in (step_x, step_y, step_z)
                    ]
                    count_cells = extent_list[0] * extent_list[1] * extent_list[2]
                    rows_z.append(
                        incoming[tap_index][:, :count_cells].reshape(
                            channels, extent_list[0], extent_list[1], extent_list[2]
                        )
                    )
            rows_y.append(jnp.concatenate(rows_z, axis=3))
        rows_x.append(jnp.concatenate(rows_y, axis=2))
    return jnp.concatenate(rows_x, axis=1)


def conv_padded(padded, kernel, dilation):
    result = lax.conv_general_dilated(
        padded[None],
        kernel,
        (1, 1, 1),
        "VALID",
        rhs_dilation=(dilation, dilation, dilation),
        dimension_numbers=("NCDHW", "OIDHW", "NCDHW"),
        preferred_element_type=jnp.float32,
    )
    return result[0].reshape(kernel.shape[0], BS * BS * BS)


def kernel_grad(padded, grad_rows, dilation):
    channels = padded.shape[0]
    outputs = grad_rows.shape[0]
    grad_block = grad_rows.reshape(outputs, 1, BS, BS, BS)
    result = lax.conv_general_dilated(
        padded[None],
        grad_block,
        (dilation, dilation, dilation),
        "VALID",
        dimension_numbers=("CNDHW", "OIDHW", "NCDHW"),
        preferred_element_type=jnp.float32,
    )
    return result.reshape(channels, outputs, 27).transpose(1, 2, 0)


def on_device_deep(features, device_block, conv_first, conv_second, head_weight, targets):
    channels = features.shape[2]
    tables = neighbor_tables(device_block)
    kernel_first = conv_first.reshape(channels, 3, 3, 3, channels).transpose(0, 4, 1, 2, 3)
    kernel_second = conv_second.reshape(channels, 3, 3, 3, channels).transpose(0, 4, 1, 2, 3)
    block_in = features[0, 0].reshape(channels, BS, BS, BS)
    padded_in = surround(block_in, 1, tables)
    pre_first = conv_padded(padded_in, kernel_first, 1)
    act_first, slope_first = elu_pair(pre_first)
    hid_first = act_first.astype(jnp.bfloat16)
    padded_first = surround(hid_first.reshape(channels, BS, BS, BS), 2, tables)
    pre_second = conv_padded(padded_first, kernel_second, 2)
    act_second, slope_second = elu_pair(pre_second)
    hid_second = act_second.astype(jnp.bfloat16)
    logits = jnp.dot(head_weight, hid_second, preferred_element_type=jnp.float32)
    scale = (lax.axis_size("dp") * lax.axis_size("space") * 3 * BS * BS * BS) ** (-0.5)
    grad_logit = ((jax.nn.sigmoid(logits) - targets[0, 0].astype(jnp.float32)) * scale).astype(
        jnp.bfloat16
    )
    grad_head = lax.dot_general(
        grad_logit, hid_second, (((1,), (1,)), ((), ())), preferred_element_type=jnp.float32
    )
    back_second = lax.dot_general(
        head_weight, grad_logit, (((0,), (0,)), ((), ())), preferred_element_type=jnp.float32
    )
    grad_pre_second = (back_second * slope_second).astype(jnp.bfloat16)
    grad_second = kernel_grad(padded_first, grad_pre_second, 2)
    padded_grad = surround(grad_pre_second.reshape(channels, BS, BS, BS), 2, tables)
    kernel_back = jnp.transpose(kernel_second[:, :, ::-1, ::-1, ::-1], (1, 0, 2, 3, 4))
    back_first = conv_padded(padded_grad, kernel_back, 2)
    grad_pre_first = (back_first * slope_first).astype(jnp.bfloat16)
    grad_first = kernel_grad(padded_in, grad_pre_first, 1)
    grad_first, grad_second, grad_head = lax.psum(
        (grad_first, grad_second, grad_head), ("dp", "space")
    )
    return (logits[None, None], grad_first, grad_second, grad_head)


C = 48
CELLS = 512
HALF = 512
LANES = 128


def lanes(rows=1):
    return lax.broadcasted_iota(jnp.int32, (rows, LANES), 1)


def roll(values, shift):
    return pltpu.roll(values, shift % LANES, 1) if shift % LANES else values


def listed_blocks(block_ref, me):
    ids = block_ref[...].astype(jnp.float32)
    index = lax.broadcasted_iota(jnp.int32, ids.shape, 1)
    return [
        jnp.sum(jnp.where(index == (me ^ k), ids, 0.0)).astype(jnp.int32)
        for k in range(ids.shape[1])
    ]


def apart(source, target):
    return (target >> 2) - (source >> 2), (target & 3) - (source & 3)


PARTNERS = (6, 4, 2)


def block_tiles(features_ref, targets_ref):
    tiles = [
        [features_ref[16 * ct : 16 * (ct + 1), LANES * q : LANES * (q + 1)] for q in range(4)]
        for ct in range(3)
    ]
    targets = targets_ref[:, 0, :].astype(jnp.float32)
    targets = jnp.concatenate([targets, jnp.zeros((1, CELLS), jnp.float32)], axis=0)
    return tiles, [targets[:, LANES * q : LANES * (q + 1)] for q in range(4)]


def write_cases(tiles, rows, cases_ref):
    lane = lanes(16)
    left = lane < 64
    cell = lane & 63
    target_tile = jnp.concatenate(rows, axis=0)

    def write(case, pairs, halves, wanted):
        for ct in range(3):
            cases_ref[case, 2 * ct] = pairs[ct][0]
            cases_ref[case, 2 * ct + 1] = pairs[ct][1]
        cases_ref[case, 6] = jnp.where(left, halves[0], halves[1])
        cases_ref[case, 7] = jnp.where(left, halves[2], wanted.astype(jnp.bfloat16))

    for case, pair, single, q in ((0, (2, 3), 1, 3), (1, (0, 1), 2, 0)):
        turns = (64, 0, 64) if case == 0 else (0, 64, 0)
        halves = [roll(tiles[ct][single], turns[ct]) for ct in range(3)]
        both = [roll(rows[q], 64), rows[q], jnp.zeros((8, LANES), jnp.float32)]
        wanted = jnp.concatenate(both, axis=0)
        write(case, [(t[pair[0]], t[pair[1]]) for t in tiles], halves, wanted)
    for case, spare, turn, turns, target_turns in (
        (2, cell < 24, -24, (-48, -96, -16, -64), (16, -32)),
        (3, cell >= 40, 40, (-24, -72, 8, -40), (64, 16)),
    ):
        pairs, halves = [], []
        for ct, t in enumerate(tiles):
            pairs.append([jnp.where(spare, roll(t[q + 2], turn), t[q]) for q in range(2)])
            moved = [roll(t[2 + n // 2], turns[n] + (64 if ct == 1 else 0)) for n in range(4)]
            half = jnp.where(cell < 16, moved[0], jnp.where(cell < 32, moved[1], moved[2]))
            halves.append(jnp.where(cell < 48, half, moved[3]))
        wanted = [roll(target_tile, n) for n in target_turns]
        write(case, pairs, halves, jnp.where(lane < 80, wanted[0], wanted[1]))


def case_of(source, target):
    dx, dy = apart(source, target)
    return jnp.where(dx > 0, 0, jnp.where(dx < 0, 1, jnp.where(dy > 0, 2, 3)))


def pack_own_kernel(block_ref, features_ref, targets_ref, own_ref, slabs_ref, cases_ref):
    blocks = listed_blocks(block_ref, lax.axis_index("space"))
    tiles, rows = block_tiles(features_ref, targets_ref)
    for ct in range(3):
        for q in range(4):
            own_ref[4 * ct + q] = tiles[ct][q]
    own_ref[12] = jnp.concatenate(rows, axis=0).astype(jnp.bfloat16)
    write_cases(tiles, rows, cases_ref)
    for n, k in enumerate(PARTNERS):
        slabs_ref[n] = cases_ref[case_of(blocks[0], blocks[k])]


def pack_mate_kernel(block_ref, features_ref, targets_ref, slabs_ref, mate_ref, *refs):
    *pair_refs, cases_ref = refs
    blocks = listed_blocks(block_ref, lax.axis_index("space"))
    write_cases(*block_tiles(features_ref, targets_ref), cases_ref)
    mate_ref[...] = cases_ref[case_of(blocks[1], blocks[0])]
    for n, (k, ref) in enumerate(zip(PARTNERS, pair_refs)):
        ref[0] = slabs_ref[n]
        ref[1] = cases_ref[case_of(blocks[1], blocks[k])]


def stacked_taps(ref):
    rows = []
    for a in range(3):
        taps = [ref[9 * a + t] for t in range(9)]
        rows.append(jnp.concatenate(taps, axis=1))
    return jnp.concatenate(rows, axis=0)


def prepare_kernel(
    block_ref,
    first_ref,
    second_ref,
    head_ref,
    w1_ref,
    w2_ref,
    w2t_ref,
    h_ref,
    ht_ref,
    owners_ref,
    masks_ref,
    table_ref,
):
    w1_ref[...] = stacked_taps(first_ref)
    whole = stacked_taps(second_ref)
    w2_ref[...] = whole
    w2t_ref[...] = whole.T
    head = head_ref[...].astype(jnp.float32)
    head = jnp.concatenate([head, jnp.zeros((13, C), jnp.float32)], axis=0)
    h_ref[...] = head.astype(jnp.bfloat16)
    ht_ref[...] = head.T.astype(jnp.bfloat16)

    blocks = listed_blocks(block_ref, lax.axis_index("space"))
    for slot in range(10):
        table_ref[0, slot] = 1
        table_ref[1, slot] = 0
    table_ref[1, 4] = 1
    for k in range(1, len(blocks)):
        dx, dy = apart(blocks[0], blocks[k])
        near = (dx >= -1) & (dx <= 1) & (dy >= -1) & (dy <= 1)
        slot = jnp.where(near, dx * 3 + dy + 4, 9)
        table_ref[0, slot] = k
        table_ref[1, slot] = 1
    lane = lanes()
    there = [table_ref[1, q].astype(jnp.float32) for q in range(9)]
    owners = jnp.zeros((1, LANES), jnp.int32)
    for q in range(9):
        owners = jnp.where(lane == q, table_ref[0, q], owners)
    owners_ref[...] = owners
    for bx in range(3):
        before, middle, after = there[3 * bx : 3 * bx + 3]
        masks_ref[bx : bx + 1, :] = jnp.where(
            lane < 32, before, jnp.where(lane < 96, middle, after)
        )
        masks_ref[bx + 3 : bx + 4, :] = jnp.where(lane < 64, after, before)


def matmul(left, right):
    return lax.dot_general(
        left, right, (((1,), (0,)), ((), ())), preferred_element_type=jnp.float32
    )


def matmul_lanes(left, right):
    return lax.dot_general(
        left, right, (((1,), (1,)), ((), ())), preferred_element_type=jnp.float32
    )


def crop_kernel(scale, owners_ref, masks_ref, own_ref, mate_ref, *refs):
    crop_body(scale, owners_ref, masks_ref, own_ref, mate_ref, refs[:3], *refs[3:])


def crop_body(
    scale,
    owners_ref,
    masks_ref,
    own_ref,
    mate_ref,
    pairs,
    w1_ref,
    w2_ref,
    w2t_ref,
    h_ref,
    ht_ref,
    logits_ref,
    packed_ref,
    gathered_ref,
    sides_ref,
    ends_ref,
    x9_ref,
    h9_ref,
    product_ref,
    slope1_ref,
    slope2_ref,
    hid2_ref,
    grad2_ref,
    shifted_ref,
    back_ref,
):
    gathered_ref[1] = mate_ref[...]
    for k, pair in zip(PARTNERS, pairs):
        for j in range(2):
            gathered_ref[k + j] = pair[j]
    owners = owners_ref[...]
    owner = [owners[0, q] for q in range(9)]

    bf16 = jnp.bfloat16
    lane = lanes(16)
    depth = lane & 7
    depth48 = lanes(C) & 7
    low, mid, left_half = lane < 32, lane < 96, lane < 64
    masks = [masks_ref[bx : bx + 1, :] for bx in range(3)]
    main_masks = [jnp.broadcast_to(mask, (16, LANES)).astype(bf16) for mask in masks]
    edge_masks = [
        jnp.broadcast_to(masks_ref[bx + 3 : bx + 4, :], (16, LANES)).astype(bf16)
        for bx in range(3)
    ]
    own_row = jnp.where((lane >= 32) & mid, 1.0, 0.0)[0:1]

    cell = lane & 63
    for side, by, in_place, turn, turns in (
        (0, 0, cell < 48, 24, (48, 96, 16, 64)),
        (1, 2, cell < 24, -40, (24, 72, -8, 40)),
    ):
        slab = owner[3 + by]
        for ct in range(3):
            half = gathered_ref[slab, 6 + ct // 2]
            for q in range(2):
                sides_ref[side, 4 * ct + q] = gathered_ref[slab, 2 * ct + q]
                moved = [roll(half, turns[2 * q + n] - (64 if ct == 1 else 0)) for n in range(2)]
                sides_ref[side, 4 * ct + q + 2] = jnp.where(
                    in_place,
                    roll(gathered_ref[slab, 2 * ct + q], turn),
                    jnp.where(left_half, moved[0], moved[1]),
                )

    for bx in (0, 2):
        for by in range(3):
            for ct in range(3):
                tile = gathered_ref[owner[3 * bx + by], 6 + ct // 2]
                ends_ref[3 * bx // 2 + by, ct] = roll(tile, -64 * (ct % 2))

    def placed(ct, bx, i):
        if bx == 1:
            tile, half = 4 * ct + i // 2, i % 2
            parts = [sides_ref[0, tile], own_ref[tile], sides_ref[1, tile]]
        elif i == (3 if bx == 0 else 4):
            half = 0
            parts = [ends_ref[3 * bx // 2 + by, ct] for by in range(3)]
        else:
            tile, half = 2 * ct + (i // 2 - 2 if bx == 0 else i // 2), i % 2
            parts = [gathered_ref[owner[3 * bx + by], tile] for by in range(3)]
        outer = 96 - 64 * half
        return roll(parts[0], outer), roll(parts[1], 32 - 64 * half), roll(parts[2], outer)

    zero = jnp.zeros((16, LANES), bf16)

    @pl.loop(0, 3)
    def _(ct):
        for plane in range(18):
            bx, i = (plane + 3) // 8, (plane + 3) % 8
            before, middle, after = placed(ct, bx, i)
            main = jnp.where(low, before, jnp.where(mid, middle, after)) * main_masks[bx]
            edge = jnp.where(left_half, after, before) * edge_masks[bx]
            for c in (-1, 0, 1):
                if c == 0:
                    main_c, edge_c = main, edge
                else:
                    keep = depth >= 1 if c == 1 else depth <= 6
                    main_c, edge_c = jnp.where(keep, main, zero), jnp.where(keep, edge, zero)
                for b in (-1, 0, 1):
                    step = 8 * b + c
                    if b == 1:
                        source = jnp.where(lane < step, edge_c, main_c)
                    elif b == -1:
                        source = jnp.where(lane >= LANES + step, edge_c, main_c)
                    else:
                        source = main_c
                    row = pl.multiple_of((3 * (b + 1) + c + 1) * C + 16 * ct, 16)
                    x9_ref[pl.ds(row, 16), LANES * plane : LANES * (plane + 1)] = (
                        roll(source, -step) if step else source
                    )

    def plane_cols(plane):
        return slice(LANES * plane, LANES * (plane + 1))

    def summed(plane, stride):
        return (
            product_ref[0:C, plane_cols(plane)]
            + product_ref[C : 2 * C, plane_cols(plane + stride)]
            + product_ref[2 * C : 3 * C, plane_cols(plane + 2 * stride)]
        )

    for n in range(9):
        cols = slice(256 * n, 256 * (n + 1))
        product_ref[:, cols] = matmul(w1_ref[...], x9_ref[:, cols])

    for plane in range(16):
        bx = (plane + 4) // 8
        pre = summed(plane, 1)
        negative = jnp.exp(jnp.minimum(pre, 0.0))
        if 4 <= plane < 12:
            slope1_ref[:, plane_cols(plane - 4)] = jnp.where(pre > 0, 1.0, negative)
        hidden = jnp.where(pre > 0, pre, negative - 1.0) * masks[bx]
        hidden = hidden.astype(bf16)
        for c in (-1, 0, 1):
            if c == 0:
                source = hidden
            else:
                keep = depth48 >= 2 if c == 1 else depth48 <= 5
                source = jnp.where(keep, hidden, jnp.zeros((C, LANES), bf16))
            for b in (-1, 0, 1):
                step = 16 * b + 2 * c
                row = (3 * (b + 1) + c + 1) * C
                h9_ref[row : row + C, plane_cols(plane)] = roll(source, -step) if step else source

    for n in range(8):
        cols = slice(256 * n, 256 * (n + 1))
        product_ref[:, cols] = matmul(w2_ref[...], h9_ref[:, cols])

    for plane in range(12):
        bx = (plane + 6) // 8
        pre = summed(plane, 2)
        negative = jnp.exp(jnp.minimum(pre, 0.0))
        slope2_ref[:, plane_cols(plane)] = jnp.where(pre > 0, 1.0, negative) * masks[bx]
        hidden = jnp.where(pre > 0, pre, negative - 1.0) * masks[bx]
        hid2_ref[:, plane_cols(plane)] = hidden.astype(jnp.bfloat16)

    logits = matmul(h_ref[...], hid2_ref[...])
    targets = []
    for bx, half in ((0, 1), (1, 0), (1, 1), (2, 1)):
        if bx == 1:
            before = roll(gathered_ref[owner[3], 7], -48 - 16 * half)
            middle = roll(own_ref[12], 32 - 64 * half)
            after = roll(gathered_ref[owner[5], 7], 32 - 16 * half)
        else:
            parts = [gathered_ref[owner[3 * bx + by], 7] for by in range(3)]
            before, middle, after = roll(parts[0], 32), roll(parts[1], -32), roll(parts[2], 32)
        cells = jnp.where(low, before, jnp.where(mid, middle, after))
        targets.append(cells.astype(jnp.float32))
    grads = []
    for plane in range(12):
        bx, i = (plane + 6) // 8, (plane + 6) % 8
        value = logits[:, plane_cols(plane)]
        if bx == 1:
            wanted = targets[1 + i % 2][4 * (i // 2) : 4 * (i // 2) + 4]
        else:
            wanted = targets[0 if bx == 0 else 3][4 * (i % 2) : 4 * (i % 2) + 4]
        wanted = jnp.concatenate([wanted, jnp.zeros((12, LANES), jnp.float32)], axis=0)
        sigmoid = 1.0 / (1.0 + jnp.exp(-value))
        grads.append((sigmoid - wanted) * masks[bx] * scale)
    for q in range(4):
        first = roll(logits[:, plane_cols(2 + 2 * q)], -32)
        second = roll(logits[:, plane_cols(3 + 2 * q)], 32)
        logits_ref[:, plane_cols(q)] = jnp.where(left_half, first, second)[0:8]

    grad_logit = jnp.concatenate(grads, axis=1).astype(jnp.bfloat16)
    back = matmul(ht_ref[...], grad_logit)
    grad2_ref[...] = (back * slope2_ref[...]).astype(jnp.bfloat16)
    own_grads = jnp.concatenate([grads[2 + x] * own_row for x in range(8)], axis=1)
    head_part = matmul_lanes(hid2_ref[:, 2 * LANES : 10 * LANES], own_grads.astype(jnp.bfloat16))

    own_bf16 = jnp.broadcast_to(own_row, (C, LANES)).astype(bf16)
    shifted_ref[...] = jnp.zeros_like(shifted_ref)
    for a in range(3):
        for x in range(8):
            shifted_ref[C * a : C * (a + 1), plane_cols(x + 2 * a)] = (
                grad2_ref[:, plane_cols(x + 2)] * own_bf16
            )
    second_part = matmul_lanes(shifted_ref[...], h9_ref[:, 2 * LANES : 14 * LANES])

    for a in range(3):
        for x in range(8):
            shifted_ref[C * a : C * (a + 1), plane_cols(x)] = grad2_ref[:, plane_cols(x + 4 - 2 * a)]
    for n in range(4):
        cols = slice(256 * n, 256 * (n + 1))
        back_ref[:, cols] = matmul(w2t_ref[...], shifted_ref[:, cols])
    grad1 = []
    for x in range(8):
        total = jnp.zeros((C, LANES), jnp.float32)
        for c in (-1, 0, 1):
            part = jnp.zeros((C, LANES), jnp.float32)
            for b in (-1, 0, 1):
                row = (3 * (b + 1) + c + 1) * C
                step = 16 * b + 2 * c
                piece = back_ref[row : row + C, plane_cols(x)]
                part += roll(piece, step) if step else piece
            if c:
                part = jnp.where(depth48 >= 2 if c == 1 else depth48 <= 5, part, 0.0)
            total += part
        grad1.append((total * slope1_ref[:, plane_cols(x)] * own_row).astype(jnp.bfloat16))

    shifted_ref[...] = jnp.zeros_like(shifted_ref)
    for a in range(3):
        for x in range(8):
            shifted_ref[C * a : C * (a + 1), plane_cols(x + a)] = grad1[x]
    first_part = matmul_lanes(
        shifted_ref[:, 0 : 10 * LANES], x9_ref[:, 4 * LANES : 14 * LANES]
    )

    head_part = jnp.concatenate([head_part, jnp.zeros((24, 16), jnp.float32)], axis=0)
    nothing = jnp.zeros((72, 16), jnp.float32)
    for base, part, extra in ((0, first_part, nothing), (HALF, second_part, head_part)):
        for q in range(3):
            packed_ref[base + 144 * q : base + 144 * (q + 1), :] = part[:, plane_cols(q)].astype(bf16)
        tail = [part[0:72, 384:], part[72:144, 384:], extra, nothing]
        tail = jnp.concatenate([jnp.concatenate(tail, axis=1), jnp.zeros((8, LANES))], axis=0)
        packed_ref[base + 432 : base + HALF, :] = tail.astype(bf16)


def sum_kernel(parts_ref, out_ref):
    total = parts_ref[0].astype(jnp.float32)
    for s in range(1, parts_ref.shape[0]):
        total += parts_ref[s].astype(jnp.float32)
    total = total.astype(jnp.bfloat16)
    for s in range(out_ref.shape[0]):
        out_ref[s] = total


def unpack_kernel(rows_ref, logits_ref, first_ref, second_ref, head_ref, out_ref):
    out_ref[:, 0, :] = logits_ref[0:3, :]
    for k, out in ((0, first_ref), (1, second_ref)):
        half = rows_ref[HALF * k : HALF * (k + 1), :].astype(jnp.float32)
        tail = jnp.concatenate([half[432:504, 0:C], half[432:504, C : 2 * C]], axis=0)
        tiles = [half[144 * q : 144 * (q + 1), :] for q in range(3)]
        whole = jnp.concatenate(tiles + [tail], axis=1)
        for a in range(3):
            for t in range(9):
                out[9 * a + t] = whole[C * a : C * (a + 1), C * t : C * (t + 1)]
        if k:
            head_ref[...] = half[432 : 432 + C, 96:112].T[0:3]


def on_device_flat(features, device_block, conv_first, conv_second, head_weight, targets):
    space_count = lax.axis_size("space")
    device_count = lax.axis_size("dp") * space_count
    bf16, f32 = jnp.bfloat16, jnp.float32
    small = pltpu.CompilerParams(vmem_limit_bytes=8 * 1024 * 1024)
    shape = jax.ShapeDtypeStruct
    vmem = pl.BlockSpec(memory_space=pltpu.VMEM)

    def swap(values, mask):
        return lax.ppermute(values, "space", [(s, s ^ mask) for s in range(space_count)])

    mate_targets, mate_features = swap(targets, 1), swap(features, 1)
    own, own_slabs = pl.pallas_call(
        pack_own_kernel,
        out_shape=(shape((13, 16, LANES), bf16), shape((3, 8, 16, LANES), bf16)),
        in_specs=[vmem] * 3,
        out_specs=(vmem,) * 2,
        scratch_shapes=[pltpu.VMEM((4, 8, 16, LANES), bf16)],
        compiler_params=small,
        cost_estimate=pl.CostEstimate(flops=1_000_000, bytes_accessed=2_000_000, transcendentals=0),
        name="pack_own",
    )(device_block, features[0, 0], targets[0].transpose(1, 0, 2))
    mate_slab, *pairs = pl.pallas_call(
        pack_mate_kernel,
        out_shape=(
            shape((8, 16, LANES), bf16),
            *[shape((2, 8, 16, LANES), bf16) for _ in PARTNERS],
        ),
        in_specs=[vmem] * 4,
        out_specs=(vmem,) * 4,
        scratch_shapes=[pltpu.VMEM((4, 8, 16, LANES), bf16)],
        compiler_params=small,
        name="pack_mate",
    )(device_block, mate_features[0, 0], mate_targets[0].transpose(1, 0, 2), own_slabs)
    pairs = [swap(pair, mask) for pair, mask in zip(pairs, PARTNERS)]

    w1, w2, w2t, head, head_t, owners, masks = pl.pallas_call(
        prepare_kernel,
        out_shape=(
            shape((3 * C, 9 * C), bf16),
            shape((3 * C, 9 * C), bf16),
            shape((9 * C, 3 * C), bf16),
            shape((16, C), bf16),
            shape((C, 16), bf16),
            shape((1, LANES), jnp.int32),
            shape((8, LANES), f32),
        ),
        in_specs=[vmem] * 4,
        out_specs=(vmem,) * 7,
        scratch_shapes=[pltpu.SMEM((2, 16), jnp.int32)],
        compiler_params=small,
        cost_estimate=pl.CostEstimate(flops=2_000_000, bytes_accessed=4_000_000, transcendentals=0),
        name="prepare",
    )(device_block, conv_first.transpose(1, 0, 2), conv_second.transpose(1, 0, 2), head_weight)

    scale = (device_count * 3 * CELLS) ** (-0.5)
    logits, packed = pl.pallas_call(
        functools.partial(crop_kernel, scale),
        out_shape=(shape((8, CELLS), f32), shape((2 * HALF, LANES), bf16)),
        in_specs=[vmem] * 12,
        out_specs=(vmem,) * 2,
        scratch_shapes=[
            pltpu.VMEM((space_count, 8, 16, LANES), bf16),
            pltpu.VMEM((2, 12, 16, LANES), bf16),
            pltpu.VMEM((6, 3, 16, LANES), bf16),
            pltpu.VMEM((9 * C, 18 * LANES), bf16),
            pltpu.VMEM((9 * C, 16 * LANES), bf16),
            pltpu.VMEM((3 * C, 18 * LANES), f32),
            pltpu.VMEM((C, 8 * LANES), f32),
            pltpu.VMEM((C, 12 * LANES), f32),
            pltpu.VMEM((C, 12 * LANES), bf16),
            pltpu.VMEM((C, 12 * LANES), bf16),
            pltpu.VMEM((3 * C, 12 * LANES), bf16),
            pltpu.VMEM((9 * C, 8 * LANES), f32),
        ],
        compiler_params=pltpu.CompilerParams(vmem_limit_bytes=20 * 1024 * 1024),
        name="forward_backward",
    )(owners, masks, own, mate_slab, *pairs, w1, w2, w2t, head, head_t)

    rows = HALF * 2 // device_count
    terms = lax.all_to_all(
        packed.reshape(device_count, rows, LANES), ("dp", "space"), 0, 0, tiled=True
    )
    summed = pl.pallas_call(
        sum_kernel,
        out_shape=shape((device_count, rows, LANES), bf16),
        in_specs=[vmem],
        out_specs=vmem,
        compiler_params=small,
        name="sum_terms",
    )(terms)
    total = lax.all_to_all(summed, ("dp", "space"), 0, 0, tiled=True)
    grad_first, grad_second, grad_head, logits = pl.pallas_call(
        unpack_kernel,
        out_shape=(
            shape((27, C, C), f32),
            shape((27, C, C), f32),
            shape((3, C), f32),
            shape((3, 1, CELLS), f32),
        ),
        in_specs=[vmem] * 2,
        out_specs=(vmem,) * 4,
        compiler_params=small,
        name="unpack_gradients",
    )(total.reshape(2 * HALF, LANES), logits)
    return (
        logits.transpose(1, 0, 2)[None],
        grad_first.transpose(1, 0, 2),
        grad_second.transpose(1, 0, 2),
        grad_head,
    )


def solution(mesh):
    in_specs = (
        P("dp", "space", None, None),
        P("dp", None),
        P(),
        P(),
        P(),
        P("dp", "space", None, None),
    )
    out_specs = (P("dp", "space", None, None), P(), P(), P())
    flat = mesh.shape["space"] == 8 and mesh.shape["dp"] == 4
    return jax.shard_map(
        on_device_flat if flat else on_device_deep,
        mesh=mesh,
        in_specs=in_specs,
        out_specs=out_specs,
        check_vma=False,
    )
```

```python
import functools

import jax
import jax.numpy as jnp
from jax import lax
from jax.experimental import pallas as pl
from jax.experimental.pallas import tpu as pltpu
from jax.sharding import PartitionSpec as P

BS = 8


tap_offsets = [
    (tap_index // 9 - 1, tap_index // 3 % 3 - 1, tap_index % 3 - 1) for tap_index in range(27)
]


def elu_pair(values):
    negative = jnp.exp(jnp.minimum(values, 0.0))
    return (jnp.where(values > 0, values, negative - 1.0), jnp.where(values > 0, 1.0, negative))


def neighbor_tables(device_block):
    space_count = lax.axis_size("space")
    depth_z = space_count // 8
    self_index = lax.axis_index("space")
    blocks = device_block[0]
    coords = jnp.stack([blocks // (4 * depth_z), blocks // depth_z % 4, blocks % depth_z])
    own_coords = lax.dynamic_index_in_dim(coords, self_index, 1, keepdims=False)
    offsets = jnp.array(tap_offsets, jnp.int32)
    limits = jnp.array([4, 4, depth_z], jnp.int32)
    wanted = own_coords[None, :] + offsets
    inside = jnp.all((wanted >= 0) & (wanted < limits[None, :]), axis=1) & (jnp.arange(27) != 13)
    wanted_id = (wanted[:, 0] * 4 + wanted[:, 1]) * depth_z + wanted[:, 2]
    matches = (blocks[None, :] == wanted_id[:, None]) & inside[:, None]
    devices = jnp.arange(space_count, dtype=jnp.int32)
    owner_row = jnp.sum(jnp.where(matches, devices[None, :], 0), axis=1)
    present = jnp.any(matches, axis=1)
    relative = coords - own_coords[:, None]
    adjacent = jnp.all(jnp.abs(relative) <= 1, axis=0) & (devices != self_index)
    send_tap = jnp.where(
        adjacent, (relative[0] + 1) * 9 + (relative[1] + 1) * 3 + relative[2] + 1, 13
    )
    return (owner_row, present, send_tap)


def region_slice(block_data, offset, depth_cells):
    span_list = []
    for step_value in offset:
        if step_value == 1:
            span_list.append(slice(BS - depth_cells, BS))
        elif step_value == -1:
            span_list.append(slice(0, depth_cells))
        else:
            span_list.append(slice(0, BS))
    return block_data[:, span_list[0], span_list[1], span_list[2]]


def surround(block_data, depth_cells, tables):
    owner_row, present, send_tap = tables
    channels = block_data.shape[0]
    length = depth_cells * BS * BS
    pieces = []
    for tap_index in range(27):
        if tap_index == 13:
            pieces.append(jnp.zeros((channels, length), block_data.dtype))
        else:
            region = region_slice(block_data, tap_offsets[tap_index], depth_cells).reshape(
                channels, -1
            )
            pieces.append(jnp.pad(region, ((0, 0), (0, length - region.shape[1]))))
    outgoing = jnp.stack(pieces)
    sending = outgoing[send_tap]
    by_source = lax.all_to_all(sending, "space", split_axis=0, concat_axis=0, tiled=True)
    incoming = jnp.where(
        present[:, None, None], by_source[owner_row], jnp.zeros((), block_data.dtype)
    )
    rows_x = []
    for step_x in range(3):
        rows_y = []
        for step_y in range(3):
            rows_z = []
            for step_z in range(3):
                tap_index = step_x * 9 + step_y * 3 + step_z
                if tap_index == 13:
                    rows_z.append(block_data)
                else:
                    extent_list = [
                        BS if step_value == 1 else depth_cells
                        for step_value in (step_x, step_y, step_z)
                    ]
                    count_cells = extent_list[0] * extent_list[1] * extent_list[2]
                    rows_z.append(
                        incoming[tap_index][:, :count_cells].reshape(
                            channels, extent_list[0], extent_list[1], extent_list[2]
                        )
                    )
            rows_y.append(jnp.concatenate(rows_z, axis=3))
        rows_x.append(jnp.concatenate(rows_y, axis=2))
    return jnp.concatenate(rows_x, axis=1)


def conv_padded(padded, kernel, dilation):
    result = lax.conv_general_dilated(
        padded[None],
        kernel,
        (1, 1, 1),
        "VALID",
        rhs_dilation=(dilation, dilation, dilation),
        dimension_numbers=("NCDHW", "OIDHW", "NCDHW"),
        preferred_element_type=jnp.float32,
    )
    return result[0].reshape(kernel.shape[0], BS * BS * BS)


def kernel_grad(padded, grad_rows, dilation):
    channels = padded.shape[0]
    outputs = grad_rows.shape[0]
    grad_block = grad_rows.reshape(outputs, 1, BS, BS, BS)
    result = lax.conv_general_dilated(
        padded[None],
        grad_block,
        (dilation, dilation, dilation),
        "VALID",
        dimension_numbers=("CNDHW", "OIDHW", "NCDHW"),
        preferred_element_type=jnp.float32,
    )
    return result.reshape(channels, outputs, 27).transpose(1, 2, 0)


def on_device_deep(features, device_block, conv_first, conv_second, head_weight, targets):
    channels = features.shape[2]
    tables = neighbor_tables(device_block)
    kernel_first = conv_first.reshape(channels, 3, 3, 3, channels).transpose(0, 4, 1, 2, 3)
    kernel_second = conv_second.reshape(channels, 3, 3, 3, channels).transpose(0, 4, 1, 2, 3)
    block_in = features[0, 0].reshape(channels, BS, BS, BS)
    padded_in = surround(block_in, 1, tables)
    pre_first = conv_padded(padded_in, kernel_first, 1)
    act_first, slope_first = elu_pair(pre_first)
    hid_first = act_first.astype(jnp.bfloat16)
    padded_first = surround(hid_first.reshape(channels, BS, BS, BS), 2, tables)
    pre_second = conv_padded(padded_first, kernel_second, 2)
    act_second, slope_second = elu_pair(pre_second)
    hid_second = act_second.astype(jnp.bfloat16)
    logits = jnp.dot(head_weight, hid_second, preferred_element_type=jnp.float32)
    scale = (lax.axis_size("dp") * lax.axis_size("space") * 3 * BS * BS * BS) ** (-0.5)
    grad_logit = ((jax.nn.sigmoid(logits) - targets[0, 0].astype(jnp.float32)) * scale).astype(
        jnp.bfloat16
    )
    grad_head = lax.dot_general(
        grad_logit, hid_second, (((1,), (1,)), ((), ())), preferred_element_type=jnp.float32
    )
    back_second = lax.dot_general(
        head_weight, grad_logit, (((0,), (0,)), ((), ())), preferred_element_type=jnp.float32
    )
    grad_pre_second = (back_second * slope_second).astype(jnp.bfloat16)
    grad_second = kernel_grad(padded_first, grad_pre_second, 2)
    padded_grad = surround(grad_pre_second.reshape(channels, BS, BS, BS), 2, tables)
    kernel_back = jnp.transpose(kernel_second[:, :, ::-1, ::-1, ::-1], (1, 0, 2, 3, 4))
    back_first = conv_padded(padded_grad, kernel_back, 2)
    grad_pre_first = (back_first * slope_first).astype(jnp.bfloat16)
    grad_first = kernel_grad(padded_in, grad_pre_first, 1)
    grad_first, grad_second, grad_head = lax.psum(
        (grad_first, grad_second, grad_head), ("dp", "space")
    )
    return (logits[None, None], grad_first, grad_second, grad_head)


C = 48
CELLS = 512
HALF = 512
LANES = 128


def lanes(rows=1):
    return lax.broadcasted_iota(jnp.int32, (rows, LANES), 1)


def roll(values, shift):
    return pltpu.roll(values, shift % LANES, 1) if shift % LANES else values


def listed_blocks(block_ref, me):
    ids = block_ref[...].astype(jnp.float32)
    index = lax.broadcasted_iota(jnp.int32, ids.shape, 1)
    return [
        jnp.sum(jnp.where(index == (me ^ k), ids, 0.0)).astype(jnp.int32)
        for k in range(ids.shape[1])
    ]


def apart(source, target):
    return (target >> 2) - (source >> 2), (target & 3) - (source & 3)


PARTNERS = (6, 4, 2)


def block_tiles(features_ref, targets_ref):
    tiles = [
        [features_ref[16 * ct : 16 * (ct + 1), LANES * q : LANES * (q + 1)] for q in range(4)]
        for ct in range(3)
    ]
    targets = targets_ref[:, 0, :].astype(jnp.float32)
    targets = jnp.concatenate([targets, jnp.zeros((1, CELLS), jnp.float32)], axis=0)
    return tiles, [targets[:, LANES * q : LANES * (q + 1)] for q in range(4)]


def write_cases(tiles, rows, cases_ref):
    lane = lanes(16)
    left = lane < 64
    cell = lane & 63
    target_tile = jnp.concatenate(rows, axis=0)

    def write(case, pairs, halves, wanted):
        for ct in range(3):
            cases_ref[case, 2 * ct] = pairs[ct][0]
            cases_ref[case, 2 * ct + 1] = pairs[ct][1]
        cases_ref[case, 6] = jnp.where(left, halves[0], halves[1])
        cases_ref[case, 7] = jnp.where(left, halves[2], wanted.astype(jnp.bfloat16))

    for case, pair, single, q in ((0, (2, 3), 1, 3), (1, (0, 1), 2, 0)):
        turns = (64, 0, 64) if case == 0 else (0, 64, 0)
        halves = [roll(tiles[ct][single], turns[ct]) for ct in range(3)]
        both = [roll(rows[q], 64), rows[q], jnp.zeros((8, LANES), jnp.float32)]
        wanted = jnp.concatenate(both, axis=0)
        write(case, [(t[pair[0]], t[pair[1]]) for t in tiles], halves, wanted)
    for case, spare, turn, turns, target_turns in (
        (2, cell < 24, -24, (-48, -96, -16, -64), (16, -32)),
        (3, cell >= 40, 40, (-24, -72, 8, -40), (64, 16)),
    ):
        pairs, halves = [], []
        for ct, t in enumerate(tiles):
            pairs.append([jnp.where(spare, roll(t[q + 2], turn), t[q]) for q in range(2)])
            moved = [roll(t[2 + n // 2], turns[n] + (64 if ct == 1 else 0)) for n in range(4)]
            half = jnp.where(cell < 16, moved[0], jnp.where(cell < 32, moved[1], moved[2]))
            halves.append(jnp.where(cell < 48, half, moved[3]))
        wanted = [roll(target_tile, n) for n in target_turns]
        write(case, pairs, halves, jnp.where(lane < 80, wanted[0], wanted[1]))


def case_of(source, target):
    dx, dy = apart(source, target)
    return jnp.where(dx > 0, 0, jnp.where(dx < 0, 1, jnp.where(dy > 0, 2, 3)))


def pack_own_kernel(block_ref, features_ref, targets_ref, own_ref, slabs_ref, cases_ref):
    blocks = listed_blocks(block_ref, lax.axis_index("space"))
    tiles, rows = block_tiles(features_ref, targets_ref)
    for ct in range(3):
        for q in range(4):
            own_ref[4 * ct + q] = tiles[ct][q]
    own_ref[12] = jnp.concatenate(rows, axis=0).astype(jnp.bfloat16)
    write_cases(tiles, rows, cases_ref)
    for n, k in enumerate(PARTNERS):
        slabs_ref[n] = cases_ref[case_of(blocks[0], blocks[k])]


def pack_mate_kernel(block_ref, features_ref, targets_ref, slabs_ref, mate_ref, *refs):
    *pair_refs, cases_ref = refs
    blocks = listed_blocks(block_ref, lax.axis_index("space"))
    write_cases(*block_tiles(features_ref, targets_ref), cases_ref)
    mate_ref[...] = cases_ref[case_of(blocks[1], blocks[0])]
    for n, (k, ref) in enumerate(zip(PARTNERS, pair_refs)):
        ref[0] = slabs_ref[n]
        ref[1] = cases_ref[case_of(blocks[1], blocks[k])]


def stacked_taps(ref):
    rows = []
    for a in range(3):
        taps = [ref[9 * a + t] for t in range(9)]
        rows.append(jnp.concatenate(taps, axis=1))
    return jnp.concatenate(rows, axis=0)


def prepare_kernel(
    block_ref,
    first_ref,
    second_ref,
    head_ref,
    w1_ref,
    w2_ref,
    w2t_ref,
    h_ref,
    ht_ref,
    owners_ref,
    masks_ref,
    table_ref,
):
    w1_ref[...] = stacked_taps(first_ref)
    whole = stacked_taps(second_ref)
    w2_ref[...] = whole
    w2t_ref[...] = whole.T
    head = head_ref[...].astype(jnp.float32)
    head = jnp.concatenate([head, jnp.zeros((13, C), jnp.float32)], axis=0)
    h_ref[...] = head.astype(jnp.bfloat16)
    ht_ref[...] = head.T.astype(jnp.bfloat16)

    blocks = listed_blocks(block_ref, lax.axis_index("space"))
    for slot in range(10):
        table_ref[0, slot] = 1
        table_ref[1, slot] = 0
    table_ref[1, 4] = 1
    for k in range(1, len(blocks)):
        dx, dy = apart(blocks[0], blocks[k])
        near = (dx >= -1) & (dx <= 1) & (dy >= -1) & (dy <= 1)
        slot = jnp.where(near, dx * 3 + dy + 4, 9)
        table_ref[0, slot] = k
        table_ref[1, slot] = 1
    lane = lanes()
    there = [table_ref[1, q].astype(jnp.float32) for q in range(9)]
    owners = jnp.zeros((1, LANES), jnp.int32)
    for q in range(9):
        owners = jnp.where(lane == q, table_ref[0, q], owners)
    owners_ref[...] = owners
    for bx in range(3):
        before, middle, after = there[3 * bx : 3 * bx + 3]
        masks_ref[bx : bx + 1, :] = jnp.where(
            lane < 32, before, jnp.where(lane < 96, middle, after)
        )
        masks_ref[bx + 3 : bx + 4, :] = jnp.where(lane < 64, after, before)


def matmul(left, right):
    return lax.dot_general(
        left, right, (((1,), (0,)), ((), ())), preferred_element_type=jnp.float32
    )


def matmul_lanes(left, right):
    return lax.dot_general(
        left, right, (((1,), (1,)), ((), ())), preferred_element_type=jnp.float32
    )


def crop_kernel(scale, owners_ref, masks_ref, own_ref, mate_ref, *refs):
    crop_body(scale, owners_ref, masks_ref, own_ref, mate_ref, refs[:3], *refs[3:])


def crop_body(
    scale,
    owners_ref,
    masks_ref,
    own_ref,
    mate_ref,
    pairs,
    w1_ref,
    w2_ref,
    w2t_ref,
    h_ref,
    ht_ref,
    logits_ref,
    keep_ref,
    send_ref,
    gathered_ref,
    sides_ref,
    ends_ref,
    x9_ref,
    h9_ref,
    product_ref,
    slope1_ref,
    slope2_ref,
    hid2_ref,
    grad2_ref,
    shifted_ref,
    back_ref,
):
    gathered_ref[1] = mate_ref[...]
    for k, pair in zip(PARTNERS, pairs):
        for j in range(2):
            gathered_ref[k + j] = pair[j]
    owners = owners_ref[...]
    owner = [owners[0, q] for q in range(9)]

    bf16 = jnp.bfloat16
    lane = lanes(16)
    depth = lane & 7
    depth48 = lanes(C) & 7
    low, mid, left_half = lane < 32, lane < 96, lane < 64
    masks = [masks_ref[bx : bx + 1, :] for bx in range(3)]
    main_masks = [jnp.broadcast_to(mask, (16, LANES)).astype(bf16) for mask in masks]
    edge_masks = [
        jnp.broadcast_to(masks_ref[bx + 3 : bx + 4, :], (16, LANES)).astype(bf16)
        for bx in range(3)
    ]
    own_row = jnp.where((lane >= 32) & mid, 1.0, 0.0)[0:1]

    cell = lane & 63
    for side, by, in_place, turn, turns in (
        (0, 0, cell < 48, 24, (48, 96, 16, 64)),
        (1, 2, cell < 24, -40, (24, 72, -8, 40)),
    ):
        slab = owner[3 + by]
        for ct in range(3):
            half = gathered_ref[slab, 6 + ct // 2]
            for q in range(2):
                sides_ref[side, 4 * ct + q] = gathered_ref[slab, 2 * ct + q]
                moved = [roll(half, turns[2 * q + n] - (64 if ct == 1 else 0)) for n in range(2)]
                sides_ref[side, 4 * ct + q + 2] = jnp.where(
                    in_place,
                    roll(gathered_ref[slab, 2 * ct + q], turn),
                    jnp.where(left_half, moved[0], moved[1]),
                )

    for bx in (0, 2):
        for by in range(3):
            for ct in range(3):
                tile = gathered_ref[owner[3 * bx + by], 6 + ct // 2]
                ends_ref[3 * bx // 2 + by, ct] = roll(tile, -64 * (ct % 2))

    def placed(ct, bx, i):
        if bx == 1:
            tile, half = 4 * ct + i // 2, i % 2
            parts = [sides_ref[0, tile], own_ref[tile], sides_ref[1, tile]]
        elif i == (3 if bx == 0 else 4):
            half = 0
            parts = [ends_ref[3 * bx // 2 + by, ct] for by in range(3)]
        else:
            tile, half = 2 * ct + (i // 2 - 2 if bx == 0 else i // 2), i % 2
            parts = [gathered_ref[owner[3 * bx + by], tile] for by in range(3)]
        outer = 96 - 64 * half
        return roll(parts[0], outer), roll(parts[1], 32 - 64 * half), roll(parts[2], outer)

    zero = jnp.zeros((16, LANES), bf16)

    for plane in range(18):
        bx, i = (plane + 3) // 8, (plane + 3) % 8
        for ct in range(3):
            before, middle, after = placed(ct, bx, i)
            main = jnp.where(low, before, jnp.where(mid, middle, after)) * main_masks[bx]
            edge = jnp.where(left_half, after, before) * edge_masks[bx]
            for c in (-1, 0, 1):
                if c == 0:
                    main_c, edge_c = main, edge
                else:
                    keep = depth >= 1 if c == 1 else depth <= 6
                    main_c, edge_c = jnp.where(keep, main, zero), jnp.where(keep, edge, zero)
                for b in (-1, 0, 1):
                    step = 8 * b + c
                    if b == 1:
                        source = jnp.where(lane < step, edge_c, main_c)
                    elif b == -1:
                        source = jnp.where(lane >= LANES + step, edge_c, main_c)
                    else:
                        source = main_c
                    row = (3 * (b + 1) + c + 1) * C + 16 * ct
                    x9_ref[row : row + 16, LANES * plane : LANES * (plane + 1)] = (
                        roll(source, -step) if step else source
                    )

    def plane_cols(plane):
        return slice(LANES * plane, LANES * (plane + 1))

    def summed(plane, stride):
        return (
            product_ref[0:C, plane_cols(plane)]
            + product_ref[C : 2 * C, plane_cols(plane + stride)]
            + product_ref[2 * C : 3 * C, plane_cols(plane + 2 * stride)]
        )

    for n in range(9):
        cols = slice(256 * n, 256 * (n + 1))
        product_ref[:, cols] = matmul(w1_ref[...], x9_ref[:, cols])

    for plane in range(16):
        bx = (plane + 4) // 8
        pre = summed(plane, 1)
        negative = jnp.exp(jnp.minimum(pre, 0.0))
        if 4 <= plane < 12:
            slope1_ref[:, plane_cols(plane - 4)] = jnp.where(pre > 0, 1.0, negative)
        hidden = jnp.where(pre > 0, pre, negative - 1.0) * masks[bx]
        hidden = hidden.astype(bf16)
        for c in (-1, 0, 1):
            if c == 0:
                source = hidden
            else:
                keep = depth48 >= 2 if c == 1 else depth48 <= 5
                source = jnp.where(keep, hidden, jnp.zeros((C, LANES), bf16))
            for b in (-1, 0, 1):
                step = 16 * b + 2 * c
                row = (3 * (b + 1) + c + 1) * C
                h9_ref[row : row + C, plane_cols(plane)] = roll(source, -step) if step else source

    for n in range(8):
        cols = slice(256 * n, 256 * (n + 1))
        product_ref[:, cols] = matmul(w2_ref[...], h9_ref[:, cols])

    for plane in range(12):
        bx = (plane + 6) // 8
        pre = summed(plane, 2)
        negative = jnp.exp(jnp.minimum(pre, 0.0))
        slope2_ref[:, plane_cols(plane)] = jnp.where(pre > 0, 1.0, negative) * masks[bx]
        hidden = jnp.where(pre > 0, pre, negative - 1.0) * masks[bx]
        hid2_ref[:, plane_cols(plane)] = hidden.astype(jnp.bfloat16)

    logits = matmul(h_ref[...], hid2_ref[...])
    targets = []
    for bx, half in ((0, 1), (1, 0), (1, 1), (2, 1)):
        if bx == 1:
            before = roll(gathered_ref[owner[3], 7], -48 - 16 * half)
            middle = roll(own_ref[12], 32 - 64 * half)
            after = roll(gathered_ref[owner[5], 7], 32 - 16 * half)
        else:
            parts = [gathered_ref[owner[3 * bx + by], 7] for by in range(3)]
            before, middle, after = roll(parts[0], 32), roll(parts[1], -32), roll(parts[2], 32)
        cells = jnp.where(low, before, jnp.where(mid, middle, after))
        targets.append(cells.astype(jnp.float32))
    grads = []
    for plane in range(12):
        bx, i = (plane + 6) // 8, (plane + 6) % 8
        value = logits[:, plane_cols(plane)]
        if bx == 1:
            wanted = targets[1 + i % 2][4 * (i // 2) : 4 * (i // 2) + 4]
        else:
            wanted = targets[0 if bx == 0 else 3][4 * (i % 2) : 4 * (i % 2) + 4]
        wanted = jnp.concatenate([wanted, jnp.zeros((12, LANES), jnp.float32)], axis=0)
        sigmoid = 1.0 / (1.0 + jnp.exp(-value))
        grads.append((sigmoid - wanted) * masks[bx] * scale)
    for q in range(4):
        first = roll(logits[:, plane_cols(2 + 2 * q)], -32)
        second = roll(logits[:, plane_cols(3 + 2 * q)], 32)
        logits_ref[:, plane_cols(q)] = jnp.where(left_half, first, second)[0:8]

    grad_logit = jnp.concatenate(grads, axis=1).astype(jnp.bfloat16)
    back = matmul(ht_ref[...], grad_logit)
    grad2_ref[...] = (back * slope2_ref[...]).astype(jnp.bfloat16)
    own_grads = jnp.concatenate([grads[2 + x] * own_row for x in range(8)], axis=1)
    head_part = matmul_lanes(hid2_ref[:, 2 * LANES : 10 * LANES], own_grads.astype(jnp.bfloat16))

    own_bf16 = jnp.broadcast_to(own_row, (C, LANES)).astype(bf16)
    shifted_ref[...] = jnp.zeros_like(shifted_ref)
    for a in range(3):
        for x in range(8):
            shifted_ref[C * a : C * (a + 1), plane_cols(x + 2 * a)] = (
                grad2_ref[:, plane_cols(x + 2)] * own_bf16
            )
    second_part = matmul_lanes(shifted_ref[...], h9_ref[:, 2 * LANES : 14 * LANES])

    for a in range(3):
        for x in range(8):
            shifted_ref[C * a : C * (a + 1), plane_cols(x)] = grad2_ref[:, plane_cols(x + 4 - 2 * a)]
    for n in range(4):
        cols = slice(256 * n, 256 * (n + 1))
        back_ref[:, cols] = matmul(w2t_ref[...], shifted_ref[:, cols])
    grad1 = []
    for x in range(8):
        total = jnp.zeros((C, LANES), jnp.float32)
        for c in (-1, 0, 1):
            part = jnp.zeros((C, LANES), jnp.float32)
            for b in (-1, 0, 1):
                row = (3 * (b + 1) + c + 1) * C
                step = 16 * b + 2 * c
                piece = back_ref[row : row + C, plane_cols(x)]
                part += roll(piece, step) if step else piece
            if c:
                part = jnp.where(depth48 >= 2 if c == 1 else depth48 <= 5, part, 0.0)
            total += part
        grad1.append((total * slope1_ref[:, plane_cols(x)] * own_row).astype(jnp.bfloat16))

    shifted_ref[...] = jnp.zeros_like(shifted_ref)
    for a in range(3):
        for x in range(8):
            shifted_ref[C * a : C * (a + 1), plane_cols(x + a)] = grad1[x]
    first_part = matmul_lanes(
        shifted_ref[:, 0 : 10 * LANES], x9_ref[:, 4 * LANES : 14 * LANES]
    )

    first_core = (lax.axis_index("dp") & 1) == 0
    head_part = jnp.concatenate([head_part, jnp.zeros((24, 16), jnp.float32)], axis=0)
    nothing = jnp.zeros((72, 16), jnp.float32)
    ends = []
    for part, extra in ((first_part, nothing), (second_part, head_part)):
        tail = jnp.concatenate([part[0:72, 384:], part[72:144, 384:], extra, nothing], axis=1)
        ends.append(jnp.concatenate([tail, jnp.zeros((8, LANES), jnp.float32)], axis=0))
    pieces = [(first_part[:, plane_cols(q)], second_part[:, plane_cols(q)]) for q in range(3)]
    row = 0
    for first, second in pieces + [tuple(ends)]:
        rows = slice(row, row + first.shape[0])
        keep_ref[rows, :] = jnp.where(first_core, first, second)
        send_ref[rows, :] = jnp.where(first_core, second, first)
        row += first.shape[0]


def add_kernel(mine_ref, other_ref, out_ref):
    out_ref[...] = (mine_ref[...] + other_ref[...]).astype(jnp.bfloat16)


def sum_kernel(parts_ref, out_ref):
    total = parts_ref[0].astype(jnp.float32)
    for s in range(1, parts_ref.shape[0]):
        total += parts_ref[s].astype(jnp.float32)
    total = total.astype(jnp.bfloat16)
    for s in range(out_ref.shape[0]):
        out_ref[s] = total


def unpack_kernel(mine_ref, other_ref, logits_ref, first_ref, second_ref, head_ref, out_ref):
    out_ref[:, 0, :] = logits_ref[0:3, :]
    first_core = (lax.axis_index("dp") & 1) == 0
    mine, other = mine_ref[...], other_ref[...]
    for k, out in ((0, first_ref), (1, second_ref)):
        half = jnp.where(first_core, other if k else mine, mine if k else other)
        half = half.astype(jnp.float32)
        tail = jnp.concatenate([half[432:504, 0:C], half[432:504, C : 2 * C]], axis=0)
        tiles = [half[144 * q : 144 * (q + 1), :] for q in range(3)]
        whole = jnp.concatenate(tiles + [tail], axis=1)
        for a in range(3):
            for t in range(9):
                out[9 * a + t] = whole[C * a : C * (a + 1), C * t : C * (t + 1)]
        if k:
            head_ref[...] = half[432 : 432 + C, 96:112].T[0:3]


def on_device_flat(features, device_block, conv_first, conv_second, head_weight, targets):
    space_count = lax.axis_size("space")
    device_count = lax.axis_size("dp") * space_count
    bf16, f32 = jnp.bfloat16, jnp.float32
    small = pltpu.CompilerParams(vmem_limit_bytes=8 * 1024 * 1024)
    shape = jax.ShapeDtypeStruct
    vmem = pl.BlockSpec(memory_space=pltpu.VMEM)

    def swap(values, mask):
        return lax.ppermute(values, "space", [(s, s ^ mask) for s in range(space_count)])

    mate_targets, mate_features = swap(targets, 1), swap(features, 1)
    own, own_slabs = pl.pallas_call(
        pack_own_kernel,
        out_shape=(shape((13, 16, LANES), bf16), shape((3, 8, 16, LANES), bf16)),
        in_specs=[vmem] * 3,
        out_specs=(vmem,) * 2,
        scratch_shapes=[pltpu.VMEM((4, 8, 16, LANES), bf16)],
        compiler_params=small,
        cost_estimate=pl.CostEstimate(flops=1_000_000, bytes_accessed=2_000_000, transcendentals=0),
        name="pack_own",
    )(device_block, features[0, 0], targets[0].transpose(1, 0, 2))
    mate_slab, *pairs = pl.pallas_call(
        pack_mate_kernel,
        out_shape=(
            shape((8, 16, LANES), bf16),
            *[shape((2, 8, 16, LANES), bf16) for _ in PARTNERS],
        ),
        in_specs=[vmem] * 4,
        out_specs=(vmem,) * 4,
        scratch_shapes=[pltpu.VMEM((4, 8, 16, LANES), bf16)],
        compiler_params=small,
        name="pack_mate",
    )(device_block, mate_features[0, 0], mate_targets[0].transpose(1, 0, 2), own_slabs)
    pairs = [swap(pair, mask) for pair, mask in zip(pairs, PARTNERS)]

    w1, w2, w2t, head, head_t, owners, masks = pl.pallas_call(
        prepare_kernel,
        out_shape=(
            shape((3 * C, 9 * C), bf16),
            shape((3 * C, 9 * C), bf16),
            shape((9 * C, 3 * C), bf16),
            shape((16, C), bf16),
            shape((C, 16), bf16),
            shape((1, LANES), jnp.int32),
            shape((8, LANES), f32),
        ),
        in_specs=[vmem] * 4,
        out_specs=(vmem,) * 7,
        scratch_shapes=[pltpu.SMEM((2, 16), jnp.int32)],
        compiler_params=small,
        cost_estimate=pl.CostEstimate(flops=2_000_000, bytes_accessed=4_000_000, transcendentals=0),
        name="prepare",
    )(device_block, conv_first.transpose(1, 0, 2), conv_second.transpose(1, 0, 2), head_weight)

    scale = (device_count * 3 * CELLS) ** (-0.5)
    logits, keep, send = pl.pallas_call(
        functools.partial(crop_kernel, scale),
        out_shape=(shape((8, CELLS), f32), shape((HALF, LANES), f32), shape((HALF, LANES), f32)),
        in_specs=[vmem] * 12,
        out_specs=(vmem,) * 3,
        scratch_shapes=[
            pltpu.VMEM((space_count, 8, 16, LANES), bf16),
            pltpu.VMEM((2, 12, 16, LANES), bf16),
            pltpu.VMEM((6, 3, 16, LANES), bf16),
            pltpu.VMEM((9 * C, 18 * LANES), bf16),
            pltpu.VMEM((9 * C, 16 * LANES), bf16),
            pltpu.VMEM((3 * C, 18 * LANES), f32),
            pltpu.VMEM((C, 8 * LANES), f32),
            pltpu.VMEM((C, 12 * LANES), f32),
            pltpu.VMEM((C, 12 * LANES), bf16),
            pltpu.VMEM((C, 12 * LANES), bf16),
            pltpu.VMEM((3 * C, 12 * LANES), bf16),
            pltpu.VMEM((9 * C, 8 * LANES), f32),
        ],
        compiler_params=pltpu.CompilerParams(vmem_limit_bytes=20 * 1024 * 1024),
        name="forward_backward",
    )(owners, masks, own, mate_slab, *pairs, w1, w2, w2t, head, head_t)

    dp_count = lax.axis_size("dp")

    def swap_cores(values):
        return lax.ppermute(values, "dp", [(d, d ^ 1) for d in range(dp_count)])

    peers = device_count // 2
    groups = [
        [d * space_count + s for d in range(core, dp_count, 2) for s in range(space_count)]
        for core in range(2)
    ]

    def exchange(values):
        return lax.all_to_all(
            values, ("dp", "space"), 0, 0, axis_index_groups=groups, tiled=True
        )

    def step(kernel, out, *operands):
        return pl.pallas_call(
            kernel,
            out_shape=out,
            in_specs=[vmem] * len(operands),
            out_specs=vmem,
            compiler_params=small,
            name="gradient_sum",
        )(*operands)

    term = step(add_kernel, shape((HALF, LANES), bf16), keep, swap_cores(send))
    pieces = shape((peers, HALF // peers, LANES), bf16)
    total = exchange(step(sum_kernel, pieces, exchange(term.reshape(pieces.shape))))
    total = total.reshape(HALF, LANES)
    grad_first, grad_second, grad_head, logits = pl.pallas_call(
        unpack_kernel,
        out_shape=(
            shape((27, C, C), f32),
            shape((27, C, C), f32),
            shape((3, C), f32),
            shape((3, 1, CELLS), f32),
        ),
        in_specs=[vmem] * 3,
        out_specs=(vmem,) * 4,
        compiler_params=small,
        name="unpack_gradients",
    )(total, swap_cores(total), logits)
    return (
        logits.transpose(1, 0, 2)[None],
        grad_first.transpose(1, 0, 2),
        grad_second.transpose(1, 0, 2),
        grad_head,
    )


def solution(mesh):
    in_specs = (
        P("dp", "space", None, None),
        P("dp", None),
        P(),
        P(),
        P(),
        P("dp", "space", None, None),
    )
    out_specs = (P("dp", "space", None, None), P(), P(), P())
    flat = mesh.shape["space"] == 8 and mesh.shape["dp"] in (2, 4)
    return jax.shard_map(
        on_device_flat if flat else on_device_deep,
        mesh=mesh,
        in_specs=in_specs,
        out_specs=out_specs,
        check_vma=False,
    )
```

```python
import functools

import jax
import jax.numpy as jnp
from jax import lax
from jax.experimental import pallas as pl
from jax.experimental.pallas import tpu as pltpu
from jax.sharding import PartitionSpec as P

BS = 8


tap_offsets = [
    (tap_index // 9 - 1, tap_index // 3 % 3 - 1, tap_index % 3 - 1) for tap_index in range(27)
]


def elu_pair(values):
    negative = jnp.exp(jnp.minimum(values, 0.0))
    return (jnp.where(values > 0, values, negative - 1.0), jnp.where(values > 0, 1.0, negative))


def neighbor_tables(device_block):
    space_count = lax.axis_size("space")
    depth_z = space_count // 8
    self_index = lax.axis_index("space")
    blocks = device_block[0]
    coords = jnp.stack([blocks // (4 * depth_z), blocks // depth_z % 4, blocks % depth_z])
    own_coords = lax.dynamic_index_in_dim(coords, self_index, 1, keepdims=False)
    offsets = jnp.array(tap_offsets, jnp.int32)
    limits = jnp.array([4, 4, depth_z], jnp.int32)
    wanted = own_coords[None, :] + offsets
    inside = jnp.all((wanted >= 0) & (wanted < limits[None, :]), axis=1) & (jnp.arange(27) != 13)
    wanted_id = (wanted[:, 0] * 4 + wanted[:, 1]) * depth_z + wanted[:, 2]
    matches = (blocks[None, :] == wanted_id[:, None]) & inside[:, None]
    devices = jnp.arange(space_count, dtype=jnp.int32)
    owner_row = jnp.sum(jnp.where(matches, devices[None, :], 0), axis=1)
    present = jnp.any(matches, axis=1)
    relative = coords - own_coords[:, None]
    adjacent = jnp.all(jnp.abs(relative) <= 1, axis=0) & (devices != self_index)
    send_tap = jnp.where(
        adjacent, (relative[0] + 1) * 9 + (relative[1] + 1) * 3 + relative[2] + 1, 13
    )
    return (owner_row, present, send_tap)


def region_slice(block_data, offset, depth_cells):
    span_list = []
    for step_value in offset:
        if step_value == 1:
            span_list.append(slice(BS - depth_cells, BS))
        elif step_value == -1:
            span_list.append(slice(0, depth_cells))
        else:
            span_list.append(slice(0, BS))
    return block_data[:, span_list[0], span_list[1], span_list[2]]


def surround(block_data, depth_cells, tables):
    owner_row, present, send_tap = tables
    channels = block_data.shape[0]
    length = depth_cells * BS * BS
    pieces = []
    for tap_index in range(27):
        if tap_index == 13:
            pieces.append(jnp.zeros((channels, length), block_data.dtype))
        else:
            region = region_slice(block_data, tap_offsets[tap_index], depth_cells).reshape(
                channels, -1
            )
            pieces.append(jnp.pad(region, ((0, 0), (0, length - region.shape[1]))))
    outgoing = jnp.stack(pieces)
    sending = outgoing[send_tap]
    by_source = lax.all_to_all(sending, "space", split_axis=0, concat_axis=0, tiled=True)
    incoming = jnp.where(
        present[:, None, None], by_source[owner_row], jnp.zeros((), block_data.dtype)
    )
    rows_x = []
    for step_x in range(3):
        rows_y = []
        for step_y in range(3):
            rows_z = []
            for step_z in range(3):
                tap_index = step_x * 9 + step_y * 3 + step_z
                if tap_index == 13:
                    rows_z.append(block_data)
                else:
                    extent_list = [
                        BS if step_value == 1 else depth_cells
                        for step_value in (step_x, step_y, step_z)
                    ]
                    count_cells = extent_list[0] * extent_list[1] * extent_list[2]
                    rows_z.append(
                        incoming[tap_index][:, :count_cells].reshape(
                            channels, extent_list[0], extent_list[1], extent_list[2]
                        )
                    )
            rows_y.append(jnp.concatenate(rows_z, axis=3))
        rows_x.append(jnp.concatenate(rows_y, axis=2))
    return jnp.concatenate(rows_x, axis=1)


def conv_padded(padded, kernel, dilation):
    result = lax.conv_general_dilated(
        padded[None],
        kernel,
        (1, 1, 1),
        "VALID",
        rhs_dilation=(dilation, dilation, dilation),
        dimension_numbers=("NCDHW", "OIDHW", "NCDHW"),
        preferred_element_type=jnp.float32,
    )
    return result[0].reshape(kernel.shape[0], BS * BS * BS)


def kernel_grad(padded, grad_rows, dilation):
    channels = padded.shape[0]
    outputs = grad_rows.shape[0]
    grad_block = grad_rows.reshape(outputs, 1, BS, BS, BS)
    result = lax.conv_general_dilated(
        padded[None],
        grad_block,
        (dilation, dilation, dilation),
        "VALID",
        dimension_numbers=("CNDHW", "OIDHW", "NCDHW"),
        preferred_element_type=jnp.float32,
    )
    return result.reshape(channels, outputs, 27).transpose(1, 2, 0)


def on_device_deep(features, device_block, conv_first, conv_second, head_weight, targets):
    channels = features.shape[2]
    tables = neighbor_tables(device_block)
    kernel_first = conv_first.reshape(channels, 3, 3, 3, channels).transpose(0, 4, 1, 2, 3)
    kernel_second = conv_second.reshape(channels, 3, 3, 3, channels).transpose(0, 4, 1, 2, 3)
    block_in = features[0, 0].reshape(channels, BS, BS, BS)
    padded_in = surround(block_in, 1, tables)
    pre_first = conv_padded(padded_in, kernel_first, 1)
    act_first, slope_first = elu_pair(pre_first)
    hid_first = act_first.astype(jnp.bfloat16)
    padded_first = surround(hid_first.reshape(channels, BS, BS, BS), 2, tables)
    pre_second = conv_padded(padded_first, kernel_second, 2)
    act_second, slope_second = elu_pair(pre_second)
    hid_second = act_second.astype(jnp.bfloat16)
    logits = jnp.dot(head_weight, hid_second, preferred_element_type=jnp.float32)
    scale = (lax.axis_size("dp") * lax.axis_size("space") * 3 * BS * BS * BS) ** (-0.5)
    grad_logit = ((jax.nn.sigmoid(logits) - targets[0, 0].astype(jnp.float32)) * scale).astype(
        jnp.bfloat16
    )
    grad_head = lax.dot_general(
        grad_logit, hid_second, (((1,), (1,)), ((), ())), preferred_element_type=jnp.float32
    )
    back_second = lax.dot_general(
        head_weight, grad_logit, (((0,), (0,)), ((), ())), preferred_element_type=jnp.float32
    )
    grad_pre_second = (back_second * slope_second).astype(jnp.bfloat16)
    grad_second = kernel_grad(padded_first, grad_pre_second, 2)
    padded_grad = surround(grad_pre_second.reshape(channels, BS, BS, BS), 2, tables)
    kernel_back = jnp.transpose(kernel_second[:, :, ::-1, ::-1, ::-1], (1, 0, 2, 3, 4))
    back_first = conv_padded(padded_grad, kernel_back, 2)
    grad_pre_first = (back_first * slope_first).astype(jnp.bfloat16)
    grad_first = kernel_grad(padded_in, grad_pre_first, 1)
    grad_first, grad_second, grad_head = lax.psum(
        (grad_first, grad_second, grad_head), ("dp", "space")
    )
    return (logits[None, None], grad_first, grad_second, grad_head)


C = 48
CELLS = 512
HALF = 512
LANES = 128


def lanes(rows=1):
    return lax.broadcasted_iota(jnp.int32, (rows, LANES), 1)


def roll(values, shift):
    return pltpu.roll(values, shift % LANES, 1) if shift % LANES else values


def listed_blocks(block_ref, me):
    ids = block_ref[...].astype(jnp.float32)
    index = lax.broadcasted_iota(jnp.int32, ids.shape, 1)
    return [
        jnp.sum(jnp.where(index == (me ^ k), ids, 0.0)).astype(jnp.int32)
        for k in range(ids.shape[1])
    ]


def apart(source, target):
    return (target >> 2) - (source >> 2), (target & 3) - (source & 3)


PARTNERS = (6, 4, 2)


def block_tiles(features_ref, targets_ref):
    tiles = [
        [features_ref[16 * ct : 16 * (ct + 1), LANES * q : LANES * (q + 1)] for q in range(4)]
        for ct in range(3)
    ]
    targets = targets_ref[:, 0, :].astype(jnp.float32)
    targets = jnp.concatenate([targets, jnp.zeros((1, CELLS), jnp.float32)], axis=0)
    return tiles, [targets[:, LANES * q : LANES * (q + 1)] for q in range(4)]


def write_cases(tiles, rows, cases_ref):
    lane = lanes(16)
    left = lane < 64
    cell = lane & 63
    target_tile = jnp.concatenate(rows, axis=0)

    def write(case, pairs, halves, wanted):
        for ct in range(3):
            cases_ref[case, 2 * ct] = pairs[ct][0]
            cases_ref[case, 2 * ct + 1] = pairs[ct][1]
        cases_ref[case, 6] = jnp.where(left, halves[0], halves[1])
        cases_ref[case, 7] = jnp.where(left, halves[2], wanted.astype(jnp.bfloat16))

    for case, pair, single, q in ((0, (2, 3), 1, 3), (1, (0, 1), 2, 0)):
        turns = (64, 0, 64) if case == 0 else (0, 64, 0)
        halves = [roll(tiles[ct][single], turns[ct]) for ct in range(3)]
        both = [roll(rows[q], 64), rows[q], jnp.zeros((8, LANES), jnp.float32)]
        wanted = jnp.concatenate(both, axis=0)
        write(case, [(t[pair[0]], t[pair[1]]) for t in tiles], halves, wanted)
    for case, spare, turn, turns, target_turns in (
        (2, cell < 24, -24, (-48, -96, -16, -64), (16, -32)),
        (3, cell >= 40, 40, (-24, -72, 8, -40), (64, 16)),
    ):
        pairs, halves = [], []
        for ct, t in enumerate(tiles):
            pairs.append([jnp.where(spare, roll(t[q + 2], turn), t[q]) for q in range(2)])
            moved = [roll(t[2 + n // 2], turns[n] + (64 if ct == 1 else 0)) for n in range(4)]
            half = jnp.where(cell < 16, moved[0], jnp.where(cell < 32, moved[1], moved[2]))
            halves.append(jnp.where(cell < 48, half, moved[3]))
        wanted = [roll(target_tile, n) for n in target_turns]
        write(case, pairs, halves, jnp.where(lane < 80, wanted[0], wanted[1]))


def case_of(source, target):
    dx, dy = apart(source, target)
    return jnp.where(dx > 0, 0, jnp.where(dx < 0, 1, jnp.where(dy > 0, 2, 3)))


def pack_own_kernel(block_ref, features_ref, targets_ref, own_ref, slabs_ref, cases_ref):
    blocks = listed_blocks(block_ref, lax.axis_index("space"))
    tiles, rows = block_tiles(features_ref, targets_ref)
    for ct in range(3):
        for q in range(4):
            own_ref[4 * ct + q] = tiles[ct][q]
    own_ref[12] = jnp.concatenate(rows, axis=0).astype(jnp.bfloat16)
    write_cases(tiles, rows, cases_ref)
    for n, k in enumerate(PARTNERS):
        slabs_ref[n] = cases_ref[case_of(blocks[0], blocks[k])]


def pack_mate_kernel(block_ref, features_ref, targets_ref, slabs_ref, mate_ref, *refs):
    *pair_refs, cases_ref = refs
    blocks = listed_blocks(block_ref, lax.axis_index("space"))
    write_cases(*block_tiles(features_ref, targets_ref), cases_ref)
    mate_ref[...] = cases_ref[case_of(blocks[1], blocks[0])]
    for n, (k, ref) in enumerate(zip(PARTNERS, pair_refs)):
        ref[0] = slabs_ref[n]
        ref[1] = cases_ref[case_of(blocks[1], blocks[k])]


def stacked_taps(ref):
    rows = []
    for a in range(3):
        taps = [ref[9 * a + t] for t in range(9)]
        rows.append(jnp.concatenate(taps, axis=1))
    return jnp.concatenate(rows, axis=0)


def prepare_kernel(
    block_ref,
    first_ref,
    second_ref,
    head_ref,
    w1_ref,
    w2_ref,
    w2t_ref,
    h_ref,
    ht_ref,
    owners_ref,
    masks_ref,
    table_ref,
):
    w1_ref[...] = stacked_taps(first_ref)
    whole = stacked_taps(second_ref)
    w2_ref[...] = whole
    w2t_ref[...] = whole.T
    head = head_ref[...].astype(jnp.float32)
    head = jnp.concatenate([head, jnp.zeros((13, C), jnp.float32)], axis=0)
    h_ref[...] = head.astype(jnp.bfloat16)
    ht_ref[...] = head.T.astype(jnp.bfloat16)

    blocks = listed_blocks(block_ref, lax.axis_index("space"))
    for slot in range(10):
        table_ref[0, slot] = 1
        table_ref[1, slot] = 0
    table_ref[1, 4] = 1
    for k in range(1, len(blocks)):
        dx, dy = apart(blocks[0], blocks[k])
        near = (dx >= -1) & (dx <= 1) & (dy >= -1) & (dy <= 1)
        slot = jnp.where(near, dx * 3 + dy + 4, 9)
        table_ref[0, slot] = k
        table_ref[1, slot] = 1
    lane = lanes()
    there = [table_ref[1, q].astype(jnp.float32) for q in range(9)]
    owners = jnp.zeros((1, LANES), jnp.int32)
    for q in range(9):
        owners = jnp.where(lane == q, table_ref[0, q], owners)
    owners_ref[...] = owners
    for bx in range(3):
        before, middle, after = there[3 * bx : 3 * bx + 3]
        masks_ref[bx : bx + 1, :] = jnp.where(
            lane < 32, before, jnp.where(lane < 96, middle, after)
        )
        masks_ref[bx + 3 : bx + 4, :] = jnp.where(lane < 64, after, before)


def matmul(left, right):
    return lax.dot_general(
        left, right, (((1,), (0,)), ((), ())), preferred_element_type=jnp.float32
    )


def matmul_lanes(left, right):
    return lax.dot_general(
        left, right, (((1,), (1,)), ((), ())), preferred_element_type=jnp.float32
    )


def crop_kernel(scale, owners_ref, masks_ref, own_ref, mate_ref, *refs):
    crop_body(scale, owners_ref, masks_ref, own_ref, mate_ref, refs[:3], *refs[3:])


def crop_body(
    scale,
    owners_ref,
    masks_ref,
    own_ref,
    mate_ref,
    pairs,
    w1_ref,
    w2_ref,
    w2t_ref,
    h_ref,
    ht_ref,
    logits_ref,
    keep_ref,
    send_ref,
    gathered_ref,
    sides_ref,
    ends_ref,
    x9_ref,
    h9_ref,
    product_ref,
    slope1_ref,
    slope2_ref,
    hid2_ref,
    grad2_ref,
    shifted_ref,
    back_ref,
):
    gathered_ref[1] = mate_ref[...]
    for k, pair in zip(PARTNERS, pairs):
        for j in range(2):
            gathered_ref[k + j] = pair[j]
    owners = owners_ref[...]
    owner = [owners[0, q] for q in range(9)]

    bf16 = jnp.bfloat16
    lane = lanes(16)
    depth = lane & 7
    depth48 = lanes(C) & 7
    low, mid, left_half = lane < 32, lane < 96, lane < 64
    masks = [masks_ref[bx : bx + 1, :] for bx in range(3)]
    main_masks = [jnp.broadcast_to(mask, (16, LANES)).astype(bf16) for mask in masks]
    edge_masks = [
        jnp.broadcast_to(masks_ref[bx + 3 : bx + 4, :], (16, LANES)).astype(bf16)
        for bx in range(3)
    ]
    own_row = jnp.where((lane >= 32) & mid, 1.0, 0.0)[0:1]

    cell = lane & 63
    for side, by, in_place, turn, turns in (
        (0, 0, cell < 48, 24, (48, 96, 16, 64)),
        (1, 2, cell < 24, -40, (24, 72, -8, 40)),
    ):
        slab = owner[3 + by]
        for ct in range(3):
            half = gathered_ref[slab, 6 + ct // 2]
            for q in range(2):
                sides_ref[side, 4 * ct + q] = gathered_ref[slab, 2 * ct + q]
                moved = [roll(half, turns[2 * q + n] - (64 if ct == 1 else 0)) for n in range(2)]
                sides_ref[side, 4 * ct + q + 2] = jnp.where(
                    in_place,
                    roll(gathered_ref[slab, 2 * ct + q], turn),
                    jnp.where(left_half, moved[0], moved[1]),
                )

    for bx in (0, 2):
        for by in range(3):
            for ct in range(3):
                tile = gathered_ref[owner[3 * bx + by], 6 + ct // 2]
                ends_ref[3 * bx // 2 + by, ct] = roll(tile, -64 * (ct % 2))

    def placed(ct, bx, i):
        if bx == 1:
            tile, half = 4 * ct + i // 2, i % 2
            parts = [sides_ref[0, tile], own_ref[tile], sides_ref[1, tile]]
        elif i == (3 if bx == 0 else 4):
            half = 0
            parts = [ends_ref[3 * bx // 2 + by, ct] for by in range(3)]
        else:
            tile, half = 2 * ct + (i // 2 - 2 if bx == 0 else i // 2), i % 2
            parts = [gathered_ref[owner[3 * bx + by], tile] for by in range(3)]
        outer = 96 - 64 * half
        return roll(parts[0], outer), roll(parts[1], 32 - 64 * half), roll(parts[2], outer)

    zero = jnp.zeros((16, LANES), bf16)

    for plane in range(18):
        bx, i = (plane + 3) // 8, (plane + 3) % 8
        for ct in range(3):
            before, middle, after = placed(ct, bx, i)
            main = jnp.where(low, before, jnp.where(mid, middle, after)) * main_masks[bx]
            edge = jnp.where(left_half, after, before) * edge_masks[bx]
            for c in (-1, 0, 1):
                if c == 0:
                    main_c, edge_c = main, edge
                else:
                    keep = depth >= 1 if c == 1 else depth <= 6
                    main_c, edge_c = jnp.where(keep, main, zero), jnp.where(keep, edge, zero)
                for b in (-1, 0, 1):
                    step = 8 * b + c
                    if b == 1:
                        source = jnp.where(lane < step, edge_c, main_c)
                    elif b == -1:
                        source = jnp.where(lane >= LANES + step, edge_c, main_c)
                    else:
                        source = main_c
                    row = (3 * (b + 1) + c + 1) * C + 16 * ct
                    x9_ref[row : row + 16, LANES * plane : LANES * (plane + 1)] = (
                        roll(source, -step) if step else source
                    )

    def plane_cols(plane):
        return slice(LANES * plane, LANES * (plane + 1))

    def summed(plane, stride):
        return (
            product_ref[0:C, plane_cols(plane)]
            + product_ref[C : 2 * C, plane_cols(plane + stride)]
            + product_ref[2 * C : 3 * C, plane_cols(plane + 2 * stride)]
        )

    for n in range(9):
        cols = slice(256 * n, 256 * (n + 1))
        product_ref[:, cols] = matmul(w1_ref[...], x9_ref[:, cols])

    for plane in range(16):
        bx = (plane + 4) // 8
        pre = summed(plane, 1)
        negative = jnp.exp(jnp.minimum(pre, 0.0))
        if 4 <= plane < 12:
            slope1_ref[:, plane_cols(plane - 4)] = jnp.where(pre > 0, 1.0, negative)
        hidden = jnp.where(pre > 0, pre, negative - 1.0) * masks[bx]
        hidden = hidden.astype(bf16)
        for c in (-1, 0, 1):
            if c == 0:
                source = hidden
            else:
                keep = depth48 >= 2 if c == 1 else depth48 <= 5
                source = jnp.where(keep, hidden, jnp.zeros((C, LANES), bf16))
            for b in (-1, 0, 1):
                step = 16 * b + 2 * c
                row = (3 * (b + 1) + c + 1) * C
                h9_ref[row : row + C, plane_cols(plane)] = roll(source, -step) if step else source

    for n in range(8):
        cols = slice(256 * n, 256 * (n + 1))
        product_ref[:, cols] = matmul(w2_ref[...], h9_ref[:, cols])

    for plane in range(12):
        bx = (plane + 6) // 8
        pre = summed(plane, 2)
        negative = jnp.exp(jnp.minimum(pre, 0.0))
        slope2_ref[:, plane_cols(plane)] = jnp.where(pre > 0, 1.0, negative) * masks[bx]
        hidden = jnp.where(pre > 0, pre, negative - 1.0) * masks[bx]
        hid2_ref[:, plane_cols(plane)] = hidden.astype(jnp.bfloat16)

    logits = matmul(h_ref[...], hid2_ref[...])
    targets = []
    for bx, half in ((0, 1), (1, 0), (1, 1), (2, 1)):
        if bx == 1:
            before = roll(gathered_ref[owner[3], 7], -48 - 16 * half)
            middle = roll(own_ref[12], 32 - 64 * half)
            after = roll(gathered_ref[owner[5], 7], 32 - 16 * half)
        else:
            parts = [gathered_ref[owner[3 * bx + by], 7] for by in range(3)]
            before, middle, after = roll(parts[0], 32), roll(parts[1], -32), roll(parts[2], 32)
        cells = jnp.where(low, before, jnp.where(mid, middle, after))
        targets.append(cells.astype(jnp.float32))
    grads = []
    for plane in range(12):
        bx, i = (plane + 6) // 8, (plane + 6) % 8
        value = logits[:, plane_cols(plane)]
        if bx == 1:
            wanted = targets[1 + i % 2][4 * (i // 2) : 4 * (i // 2) + 4]
        else:
            wanted = targets[0 if bx == 0 else 3][4 * (i % 2) : 4 * (i % 2) + 4]
        wanted = jnp.concatenate([wanted, jnp.zeros((12, LANES), jnp.float32)], axis=0)
        sigmoid = 1.0 / (1.0 + jnp.exp(-value))
        grads.append((sigmoid - wanted) * masks[bx] * scale)
    for q in range(4):
        first = roll(logits[:, plane_cols(2 + 2 * q)], -32)
        second = roll(logits[:, plane_cols(3 + 2 * q)], 32)
        logits_ref[:, plane_cols(q)] = jnp.where(left_half, first, second)[0:8]

    grad_logit = jnp.concatenate(grads, axis=1).astype(jnp.bfloat16)
    back = matmul(ht_ref[...], grad_logit)
    grad2_ref[...] = (back * slope2_ref[...]).astype(jnp.bfloat16)
    own_grads = jnp.concatenate([grads[2 + x] * own_row for x in range(8)], axis=1)
    head_part = matmul_lanes(hid2_ref[:, 2 * LANES : 10 * LANES], own_grads.astype(jnp.bfloat16))

    own_bf16 = jnp.broadcast_to(own_row, (C, LANES)).astype(bf16)
    shifted_ref[...] = jnp.zeros_like(shifted_ref)
    for a in range(3):
        for x in range(8):
            shifted_ref[C * a : C * (a + 1), plane_cols(x + 2 * a)] = (
                grad2_ref[:, plane_cols(x + 2)] * own_bf16
            )
    second_part = matmul_lanes(shifted_ref[...], h9_ref[:, 2 * LANES : 14 * LANES])

    for a in range(3):
        for x in range(8):
            shifted_ref[C * a : C * (a + 1), plane_cols(x)] = grad2_ref[:, plane_cols(x + 4 - 2 * a)]
    for n in range(4):
        cols = slice(256 * n, 256 * (n + 1))
        back_ref[:, cols] = matmul(w2t_ref[...], shifted_ref[:, cols])
    grad1 = []
    for x in range(8):
        total = jnp.zeros((C, LANES), jnp.float32)
        for c in (-1, 0, 1):
            part = jnp.zeros((C, LANES), jnp.float32)
            for b in (-1, 0, 1):
                row = (3 * (b + 1) + c + 1) * C
                step = 16 * b + 2 * c
                piece = back_ref[row : row + C, plane_cols(x)]
                part += roll(piece, step) if step else piece
            if c:
                part = jnp.where(depth48 >= 2 if c == 1 else depth48 <= 5, part, 0.0)
            total += part
        grad1.append((total * slope1_ref[:, plane_cols(x)] * own_row).astype(jnp.bfloat16))

    shifted_ref[...] = jnp.zeros_like(shifted_ref)
    for a in range(3):
        for x in range(8):
            shifted_ref[C * a : C * (a + 1), plane_cols(x + a)] = grad1[x]
    first_part = matmul_lanes(
        shifted_ref[:, 0 : 10 * LANES], x9_ref[:, 4 * LANES : 14 * LANES]
    )

    first_core = core_bit() == 0
    head_part = jnp.concatenate([head_part, jnp.zeros((24, 16), jnp.float32)], axis=0)
    nothing = jnp.zeros((72, 16), jnp.float32)
    ends = []
    for part, extra in ((first_part, nothing), (second_part, head_part)):
        tail = jnp.concatenate([part[0:72, 384:], part[72:144, 384:], extra, nothing], axis=1)
        ends.append(jnp.concatenate([tail, jnp.zeros((8, LANES), jnp.float32)], axis=0))
    pieces = [(first_part[:, plane_cols(q)], second_part[:, plane_cols(q)]) for q in range(3)]
    row = 0
    for first, second in pieces + [tuple(ends)]:
        rows = slice(row, row + first.shape[0])
        keep_ref[rows, :] = jnp.where(first_core, first, second)
        send_ref[rows, :] = jnp.where(first_core, second, first)
        row += first.shape[0]


def core_bit():
    return lax.axis_index("dp") & 1


def y_bit():
    return lax.axis_index("dp") >> 1


def x_bit():
    return lax.axis_index("space") & 1


def near_z_bit():
    return (lax.axis_index("space") >> 1) & 1


def far_z_bit():
    return lax.axis_index("space") >> 2


def halve_kernel(bit, mine_ref, other_ref, keep_ref, send_ref):
    rows = keep_ref.shape[0]
    for side, out_ref in ((bit(), keep_ref), (1 - bit(), send_ref)):
        half = pl.ds(pl.multiple_of(side * rows, rows), rows)
        total = mine_ref[half, :].astype(jnp.float32) + other_ref[half, :].astype(jnp.float32)
        out_ref[...] = total.astype(out_ref.dtype)


def add_kernel(mine_ref, other_ref, out_ref):
    out_ref[...] = (mine_ref[...] + other_ref[...]).astype(jnp.bfloat16)


def join_kernel(bit, mine_ref, other_ref, out_ref):
    rows = mine_ref.shape[0]
    for side, ref in ((bit(), mine_ref), (1 - bit(), other_ref)):
        out_ref[pl.ds(pl.multiple_of(side * rows, rows), rows), :] = ref[...]


def unpack_kernel(mine_ref, other_ref, logits_ref, first_ref, second_ref, head_ref, out_ref):
    out_ref[:, 0, :] = logits_ref[0:3, :]
    first_core = core_bit() == 0
    mine, other = mine_ref[...], other_ref[...]
    for k, out in ((0, first_ref), (1, second_ref)):
        half = jnp.where(first_core, other if k else mine, mine if k else other)
        half = half.astype(jnp.float32)
        tail = jnp.concatenate([half[432:504, 0:C], half[432:504, C : 2 * C]], axis=0)
        tiles = [half[144 * q : 144 * (q + 1), :] for q in range(3)]
        whole = jnp.concatenate(tiles + [tail], axis=1)
        for a in range(3):
            for t in range(9):
                out[9 * a + t] = whole[C * a : C * (a + 1), C * t : C * (t + 1)]
        if k:
            head_ref[...] = half[432 : 432 + C, 96:112].T[0:3]


def on_device_flat(features, device_block, conv_first, conv_second, head_weight, targets):
    space_count = lax.axis_size("space")
    device_count = lax.axis_size("dp") * space_count
    bf16, f32 = jnp.bfloat16, jnp.float32
    small = pltpu.CompilerParams(vmem_limit_bytes=8 * 1024 * 1024)
    shape = jax.ShapeDtypeStruct
    vmem = pl.BlockSpec(memory_space=pltpu.VMEM)

    def swap(values, mask):
        return lax.ppermute(values, "space", [(s, s ^ mask) for s in range(space_count)])

    mate_targets, mate_features = swap(targets, 1), swap(features, 1)
    own, own_slabs = pl.pallas_call(
        pack_own_kernel,
        out_shape=(shape((13, 16, LANES), bf16), shape((3, 8, 16, LANES), bf16)),
        in_specs=[vmem] * 3,
        out_specs=(vmem,) * 2,
        scratch_shapes=[pltpu.VMEM((4, 8, 16, LANES), bf16)],
        compiler_params=small,
        cost_estimate=pl.CostEstimate(flops=1_000_000, bytes_accessed=2_000_000, transcendentals=0),
        name="pack_own",
    )(device_block, features[0, 0], targets[0].transpose(1, 0, 2))
    mate_slab, *pairs = pl.pallas_call(
        pack_mate_kernel,
        out_shape=(
            shape((8, 16, LANES), bf16),
            *[shape((2, 8, 16, LANES), bf16) for _ in PARTNERS],
        ),
        in_specs=[vmem] * 4,
        out_specs=(vmem,) * 4,
        scratch_shapes=[pltpu.VMEM((4, 8, 16, LANES), bf16)],
        compiler_params=small,
        name="pack_mate",
    )(device_block, mate_features[0, 0], mate_targets[0].transpose(1, 0, 2), own_slabs)
    pairs = [swap(pair, mask) for pair, mask in zip(pairs, PARTNERS)]

    w1, w2, w2t, head, head_t, owners, masks = pl.pallas_call(
        prepare_kernel,
        out_shape=(
            shape((3 * C, 9 * C), bf16),
            shape((3 * C, 9 * C), bf16),
            shape((9 * C, 3 * C), bf16),
            shape((16, C), bf16),
            shape((C, 16), bf16),
            shape((1, LANES), jnp.int32),
            shape((8, LANES), f32),
        ),
        in_specs=[vmem] * 4,
        out_specs=(vmem,) * 7,
        scratch_shapes=[pltpu.SMEM((2, 16), jnp.int32)],
        compiler_params=small,
        cost_estimate=pl.CostEstimate(flops=2_000_000, bytes_accessed=4_000_000, transcendentals=0),
        name="prepare",
    )(device_block, conv_first.transpose(1, 0, 2), conv_second.transpose(1, 0, 2), head_weight)

    scale = (device_count * 3 * CELLS) ** (-0.5)
    logits, keep, send = pl.pallas_call(
        functools.partial(crop_kernel, scale),
        out_shape=(shape((8, CELLS), f32), shape((HALF, LANES), f32), shape((HALF, LANES), f32)),
        in_specs=[vmem] * 12,
        out_specs=(vmem,) * 3,
        scratch_shapes=[
            pltpu.VMEM((space_count, 8, 16, LANES), bf16),
            pltpu.VMEM((2, 12, 16, LANES), bf16),
            pltpu.VMEM((6, 3, 16, LANES), bf16),
            pltpu.VMEM((9 * C, 18 * LANES), bf16),
            pltpu.VMEM((9 * C, 16 * LANES), bf16),
            pltpu.VMEM((3 * C, 18 * LANES), f32),
            pltpu.VMEM((C, 8 * LANES), f32),
            pltpu.VMEM((C, 12 * LANES), f32),
            pltpu.VMEM((C, 12 * LANES), bf16),
            pltpu.VMEM((C, 12 * LANES), bf16),
            pltpu.VMEM((3 * C, 12 * LANES), bf16),
            pltpu.VMEM((9 * C, 8 * LANES), f32),
        ],
        compiler_params=pltpu.CompilerParams(vmem_limit_bytes=20 * 1024 * 1024),
        name="forward_backward",
    )(owners, masks, own, mate_slab, *pairs, w1, w2, w2t, head, head_t)

    def swapper(axis, mask):
        pairs = [(d, d ^ mask) for d in range(lax.axis_size(axis))]
        return lambda values: lax.ppermute(values, axis, pairs)

    swap_cores = swapper("dp", 1)
    swaps = (
        (y_bit, swapper("dp", 2), bf16),
        (x_bit, swapper("space", 1), bf16),
        (near_z_bit, swapper("space", 2), f32),
        (far_z_bit, swapper("space", 4), f32),
    )

    def step(kernel, outs, *operands):
        return pl.pallas_call(
            kernel,
            out_shape=outs,
            in_specs=[vmem] * len(operands),
            out_specs=jax.tree.map(lambda _: vmem, outs),
            compiler_params=small,
            name="gradient_sum",
        )(*operands)

    rows, other = HALF, swap_cores(send)
    for bit, swap_rows, sent_as in swaps:
        rows //= 2
        keep, send = step(
            functools.partial(halve_kernel, bit),
            (shape((rows, LANES), f32), shape((rows, LANES), sent_as)),
            keep,
            other,
        )
        other = swap_rows(send)
    total = step(add_kernel, shape((rows, LANES), bf16), keep, other)
    for bit, swap_rows, _ in reversed(swaps):
        rows *= 2
        total = step(
            functools.partial(join_kernel, bit),
            shape((rows, LANES), bf16),
            total,
            swap_rows(total),
        )
    grad_first, grad_second, grad_head, logits = pl.pallas_call(
        unpack_kernel,
        out_shape=(
            shape((27, C, C), f32),
            shape((27, C, C), f32),
            shape((3, C), f32),
            shape((3, 1, CELLS), f32),
        ),
        in_specs=[vmem] * 3,
        out_specs=(vmem,) * 4,
        compiler_params=small,
        name="unpack_gradients",
    )(total, swap_cores(total), logits)
    return (
        logits.transpose(1, 0, 2)[None],
        grad_first.transpose(1, 0, 2),
        grad_second.transpose(1, 0, 2),
        grad_head,
    )


def solution(mesh):
    in_specs = (
        P("dp", "space", None, None),
        P("dp", None),
        P(),
        P(),
        P(),
        P("dp", "space", None, None),
    )
    out_specs = (P("dp", "space", None, None), P(), P(), P())
    flat = mesh.shape["space"] == 8 and mesh.shape["dp"] == 4
    return jax.shard_map(
        on_device_flat if flat else on_device_deep,
        mesh=mesh,
        in_specs=in_specs,
        out_specs=out_specs,
        check_vma=False,
    )
```

```python
import functools

import jax
import jax.numpy as jnp
from jax import lax
from jax.experimental import pallas as pl
from jax.experimental.pallas import tpu as pltpu
from jax.sharding import PartitionSpec as P

BS = 8


tap_offsets = [
    (tap_index // 9 - 1, tap_index // 3 % 3 - 1, tap_index % 3 - 1) for tap_index in range(27)
]


def elu_pair(values):
    negative = jnp.exp(jnp.minimum(values, 0.0))
    return (jnp.where(values > 0, values, negative - 1.0), jnp.where(values > 0, 1.0, negative))


def neighbor_tables(device_block):
    space_count = lax.axis_size("space")
    depth_z = space_count // 8
    self_index = lax.axis_index("space")
    blocks = device_block[0]
    coords = jnp.stack([blocks // (4 * depth_z), blocks // depth_z % 4, blocks % depth_z])
    own_coords = lax.dynamic_index_in_dim(coords, self_index, 1, keepdims=False)
    offsets = jnp.array(tap_offsets, jnp.int32)
    limits = jnp.array([4, 4, depth_z], jnp.int32)
    wanted = own_coords[None, :] + offsets
    inside = jnp.all((wanted >= 0) & (wanted < limits[None, :]), axis=1) & (jnp.arange(27) != 13)
    wanted_id = (wanted[:, 0] * 4 + wanted[:, 1]) * depth_z + wanted[:, 2]
    matches = (blocks[None, :] == wanted_id[:, None]) & inside[:, None]
    devices = jnp.arange(space_count, dtype=jnp.int32)
    owner_row = jnp.sum(jnp.where(matches, devices[None, :], 0), axis=1)
    present = jnp.any(matches, axis=1)
    relative = coords - own_coords[:, None]
    adjacent = jnp.all(jnp.abs(relative) <= 1, axis=0) & (devices != self_index)
    send_tap = jnp.where(
        adjacent, (relative[0] + 1) * 9 + (relative[1] + 1) * 3 + relative[2] + 1, 13
    )
    return (owner_row, present, send_tap)


def region_slice(block_data, offset, depth_cells):
    span_list = []
    for step_value in offset:
        if step_value == 1:
            span_list.append(slice(BS - depth_cells, BS))
        elif step_value == -1:
            span_list.append(slice(0, depth_cells))
        else:
            span_list.append(slice(0, BS))
    return block_data[:, span_list[0], span_list[1], span_list[2]]


def surround(block_data, depth_cells, tables):
    owner_row, present, send_tap = tables
    channels = block_data.shape[0]
    length = depth_cells * BS * BS
    pieces = []
    for tap_index in range(27):
        if tap_index == 13:
            pieces.append(jnp.zeros((channels, length), block_data.dtype))
        else:
            region = region_slice(block_data, tap_offsets[tap_index], depth_cells).reshape(
                channels, -1
            )
            pieces.append(jnp.pad(region, ((0, 0), (0, length - region.shape[1]))))
    outgoing = jnp.stack(pieces)
    sending = outgoing[send_tap]
    by_source = lax.all_to_all(sending, "space", split_axis=0, concat_axis=0, tiled=True)
    incoming = jnp.where(
        present[:, None, None], by_source[owner_row], jnp.zeros((), block_data.dtype)
    )
    rows_x = []
    for step_x in range(3):
        rows_y = []
        for step_y in range(3):
            rows_z = []
            for step_z in range(3):
                tap_index = step_x * 9 + step_y * 3 + step_z
                if tap_index == 13:
                    rows_z.append(block_data)
                else:
                    extent_list = [
                        BS if step_value == 1 else depth_cells
                        for step_value in (step_x, step_y, step_z)
                    ]
                    count_cells = extent_list[0] * extent_list[1] * extent_list[2]
                    rows_z.append(
                        incoming[tap_index][:, :count_cells].reshape(
                            channels, extent_list[0], extent_list[1], extent_list[2]
                        )
                    )
            rows_y.append(jnp.concatenate(rows_z, axis=3))
        rows_x.append(jnp.concatenate(rows_y, axis=2))
    return jnp.concatenate(rows_x, axis=1)


def conv_padded(padded, kernel, dilation):
    result = lax.conv_general_dilated(
        padded[None],
        kernel,
        (1, 1, 1),
        "VALID",
        rhs_dilation=(dilation, dilation, dilation),
        dimension_numbers=("NCDHW", "OIDHW", "NCDHW"),
        preferred_element_type=jnp.float32,
    )
    return result[0].reshape(kernel.shape[0], BS * BS * BS)


def kernel_grad(padded, grad_rows, dilation):
    channels = padded.shape[0]
    outputs = grad_rows.shape[0]
    grad_block = grad_rows.reshape(outputs, 1, BS, BS, BS)
    result = lax.conv_general_dilated(
        padded[None],
        grad_block,
        (dilation, dilation, dilation),
        "VALID",
        dimension_numbers=("CNDHW", "OIDHW", "NCDHW"),
        preferred_element_type=jnp.float32,
    )
    return result.reshape(channels, outputs, 27).transpose(1, 2, 0)


def on_device_deep(features, device_block, conv_first, conv_second, head_weight, targets):
    channels = features.shape[2]
    tables = neighbor_tables(device_block)
    kernel_first = conv_first.reshape(channels, 3, 3, 3, channels).transpose(0, 4, 1, 2, 3)
    kernel_second = conv_second.reshape(channels, 3, 3, 3, channels).transpose(0, 4, 1, 2, 3)
    block_in = features[0, 0].reshape(channels, BS, BS, BS)
    padded_in = surround(block_in, 1, tables)
    pre_first = conv_padded(padded_in, kernel_first, 1)
    act_first, slope_first = elu_pair(pre_first)
    hid_first = act_first.astype(jnp.bfloat16)
    padded_first = surround(hid_first.reshape(channels, BS, BS, BS), 2, tables)
    pre_second = conv_padded(padded_first, kernel_second, 2)
    act_second, slope_second = elu_pair(pre_second)
    hid_second = act_second.astype(jnp.bfloat16)
    logits = jnp.dot(head_weight, hid_second, preferred_element_type=jnp.float32)
    scale = (lax.axis_size("dp") * lax.axis_size("space") * 3 * BS * BS * BS) ** (-0.5)
    grad_logit = ((jax.nn.sigmoid(logits) - targets[0, 0].astype(jnp.float32)) * scale).astype(
        jnp.bfloat16
    )
    grad_head = lax.dot_general(
        grad_logit, hid_second, (((1,), (1,)), ((), ())), preferred_element_type=jnp.float32
    )
    back_second = lax.dot_general(
        head_weight, grad_logit, (((0,), (0,)), ((), ())), preferred_element_type=jnp.float32
    )
    grad_pre_second = (back_second * slope_second).astype(jnp.bfloat16)
    grad_second = kernel_grad(padded_first, grad_pre_second, 2)
    padded_grad = surround(grad_pre_second.reshape(channels, BS, BS, BS), 2, tables)
    kernel_back = jnp.transpose(kernel_second[:, :, ::-1, ::-1, ::-1], (1, 0, 2, 3, 4))
    back_first = conv_padded(padded_grad, kernel_back, 2)
    grad_pre_first = (back_first * slope_first).astype(jnp.bfloat16)
    grad_first = kernel_grad(padded_in, grad_pre_first, 1)
    grad_first, grad_second, grad_head = lax.psum(
        (grad_first, grad_second, grad_head), ("dp", "space")
    )
    return (logits[None, None], grad_first, grad_second, grad_head)


C = 48
CELLS = 512
HALF = 512
LANES = 128


def lanes(rows=1):
    return lax.broadcasted_iota(jnp.int32, (rows, LANES), 1)


def roll(values, shift):
    return pltpu.roll(values, shift % LANES, 1) if shift % LANES else values


def listed_blocks(block_ref, me):
    ids = block_ref[...].astype(jnp.float32)
    index = lax.broadcasted_iota(jnp.int32, ids.shape, 1)
    return [
        jnp.sum(jnp.where(index == (me ^ k), ids, 0.0)).astype(jnp.int32)
        for k in range(ids.shape[1])
    ]


def apart(source, target):
    return (target >> 2) - (source >> 2), (target & 3) - (source & 3)


PARTNERS = (6, 4, 2)


def block_tiles(features_ref, targets_ref):
    tiles = [
        [features_ref[16 * ct : 16 * (ct + 1), LANES * q : LANES * (q + 1)] for q in range(4)]
        for ct in range(3)
    ]
    targets = targets_ref[:, 0, :].astype(jnp.float32)
    targets = jnp.concatenate([targets, jnp.zeros((1, CELLS), jnp.float32)], axis=0)
    return tiles, [targets[:, LANES * q : LANES * (q + 1)] for q in range(4)]


def write_cases(tiles, rows, cases_ref):
    lane = lanes(16)
    left = lane < 64
    cell = lane & 63
    target_tile = jnp.concatenate(rows, axis=0)

    def write(case, pairs, halves, wanted):
        for ct in range(3):
            cases_ref[case, 2 * ct] = pairs[ct][0]
            cases_ref[case, 2 * ct + 1] = pairs[ct][1]
        cases_ref[case, 6] = jnp.where(left, halves[0], halves[1])
        cases_ref[case, 7] = jnp.where(left, halves[2], wanted.astype(jnp.bfloat16))

    for case, pair, single, q in ((0, (2, 3), 1, 3), (1, (0, 1), 2, 0)):
        turns = (64, 0, 64) if case == 0 else (0, 64, 0)
        halves = [roll(tiles[ct][single], turns[ct]) for ct in range(3)]
        both = [roll(rows[q], 64), rows[q], jnp.zeros((8, LANES), jnp.float32)]
        wanted = jnp.concatenate(both, axis=0)
        write(case, [(t[pair[0]], t[pair[1]]) for t in tiles], halves, wanted)
    for case, spare, turn, turns, target_turns in (
        (2, cell < 24, -24, (-48, -96, -16, -64), (16, -32)),
        (3, cell >= 40, 40, (-24, -72, 8, -40), (64, 16)),
    ):
        pairs, halves = [], []
        for ct, t in enumerate(tiles):
            pairs.append([jnp.where(spare, roll(t[q + 2], turn), t[q]) for q in range(2)])
            moved = [roll(t[2 + n // 2], turns[n] + (64 if ct == 1 else 0)) for n in range(4)]
            half = jnp.where(cell < 16, moved[0], jnp.where(cell < 32, moved[1], moved[2]))
            halves.append(jnp.where(cell < 48, half, moved[3]))
        wanted = [roll(target_tile, n) for n in target_turns]
        write(case, pairs, halves, jnp.where(lane < 80, wanted[0], wanted[1]))


def case_of(source, target):
    dx, dy = apart(source, target)
    return jnp.where(dx > 0, 0, jnp.where(dx < 0, 1, jnp.where(dy > 0, 2, 3)))


def pack_own_kernel(block_ref, features_ref, targets_ref, own_ref, slabs_ref, cases_ref):
    blocks = listed_blocks(block_ref, lax.axis_index("space"))
    tiles, rows = block_tiles(features_ref, targets_ref)
    for ct in range(3):
        for q in range(4):
            own_ref[4 * ct + q] = tiles[ct][q]
    own_ref[12] = jnp.concatenate(rows, axis=0).astype(jnp.bfloat16)
    write_cases(tiles, rows, cases_ref)
    for n, k in enumerate(PARTNERS):
        slabs_ref[n] = cases_ref[case_of(blocks[0], blocks[k])]


def pack_mate_kernel(block_ref, features_ref, targets_ref, slabs_ref, mate_ref, *refs):
    *pair_refs, cases_ref = refs
    blocks = listed_blocks(block_ref, lax.axis_index("space"))
    write_cases(*block_tiles(features_ref, targets_ref), cases_ref)
    mate_ref[...] = cases_ref[case_of(blocks[1], blocks[0])]
    for n, (k, ref) in enumerate(zip(PARTNERS, pair_refs)):
        ref[0] = slabs_ref[n]
        ref[1] = cases_ref[case_of(blocks[1], blocks[k])]


def stacked_taps(ref):
    rows = []
    for a in range(3):
        taps = [ref[9 * a + t] for t in range(9)]
        rows.append(jnp.concatenate(taps, axis=1))
    return jnp.concatenate(rows, axis=0)


def prepare_kernel(
    block_ref,
    first_ref,
    second_ref,
    head_ref,
    w1_ref,
    w2_ref,
    w2t_ref,
    h_ref,
    ht_ref,
    owners_ref,
    masks_ref,
    table_ref,
):
    w1_ref[...] = stacked_taps(first_ref)
    whole = stacked_taps(second_ref)
    w2_ref[...] = whole
    w2t_ref[...] = whole.T
    head = head_ref[...].astype(jnp.float32)
    head = jnp.concatenate([head, jnp.zeros((13, C), jnp.float32)], axis=0)
    h_ref[...] = head.astype(jnp.bfloat16)
    ht_ref[...] = head.T.astype(jnp.bfloat16)

    blocks = listed_blocks(block_ref, lax.axis_index("space"))
    for slot in range(10):
        table_ref[0, slot] = 1
        table_ref[1, slot] = 0
    table_ref[1, 4] = 1
    for k in range(1, len(blocks)):
        dx, dy = apart(blocks[0], blocks[k])
        near = (dx >= -1) & (dx <= 1) & (dy >= -1) & (dy <= 1)
        slot = jnp.where(near, dx * 3 + dy + 4, 9)
        table_ref[0, slot] = k
        table_ref[1, slot] = 1
    lane = lanes()
    there = [table_ref[1, q].astype(jnp.float32) for q in range(9)]
    owners = jnp.zeros((1, LANES), jnp.int32)
    for q in range(9):
        owners = jnp.where(lane == q, table_ref[0, q], owners)
    owners_ref[...] = owners
    for bx in range(3):
        before, middle, after = there[3 * bx : 3 * bx + 3]
        masks_ref[bx : bx + 1, :] = jnp.where(
            lane < 32, before, jnp.where(lane < 96, middle, after)
        )
        masks_ref[bx + 3 : bx + 4, :] = jnp.where(lane < 64, after, before)


def matmul(left, right):
    return lax.dot_general(
        left, right, (((1,), (0,)), ((), ())), preferred_element_type=jnp.float32
    )


def matmul_lanes(left, right):
    return lax.dot_general(
        left, right, (((1,), (1,)), ((), ())), preferred_element_type=jnp.float32
    )


def crop_kernel(scale, owners_ref, masks_ref, own_ref, mate_ref, *refs):
    crop_body(scale, owners_ref, masks_ref, own_ref, mate_ref, refs[:3], *refs[3:])


def crop_body(
    scale,
    owners_ref,
    masks_ref,
    own_ref,
    mate_ref,
    pairs,
    w1_ref,
    w2_ref,
    w2t_ref,
    h_ref,
    ht_ref,
    logits_ref,
    keep_ref,
    send_ref,
    gathered_ref,
    sides_ref,
    ends_ref,
    x9_ref,
    h9_ref,
    product_ref,
    slope1_ref,
    hid2_ref,
    grad2_ref,
    shifted_ref,
    spread_ref,
    back_ref,
):
    gathered_ref[1] = mate_ref[...]
    for k, pair in zip(PARTNERS, pairs):
        for j in range(2):
            gathered_ref[k + j] = pair[j]
    owners = owners_ref[...]
    owner = [owners[0, q] for q in range(9)]

    bf16 = jnp.bfloat16
    lane = lanes(16)
    depth = lane & 7
    depth48 = lanes(C) & 7
    low, mid, left_half = lane < 32, lane < 96, lane < 64
    masks = [masks_ref[bx : bx + 1, :] for bx in range(3)]
    main_masks = [jnp.broadcast_to(mask, (16, LANES)).astype(bf16) for mask in masks]
    edge_masks = [
        jnp.broadcast_to(masks_ref[bx + 3 : bx + 4, :], (16, LANES)).astype(bf16)
        for bx in range(3)
    ]
    own_row = jnp.where((lane >= 32) & mid, 1.0, 0.0)[0:1]

    cell = lane & 63
    for side, by, in_place, turn, turns in (
        (0, 0, cell < 48, 24, (48, 96, 16, 64)),
        (1, 2, cell < 24, -40, (24, 72, -8, 40)),
    ):
        slab = owner[3 + by]
        for ct in range(3):
            half = gathered_ref[slab, 6 + ct // 2]
            for q in range(2):
                sides_ref[side, 4 * ct + q] = gathered_ref[slab, 2 * ct + q]
                moved = [roll(half, turns[2 * q + n] - (64 if ct == 1 else 0)) for n in range(2)]
                sides_ref[side, 4 * ct + q + 2] = jnp.where(
                    in_place,
                    roll(gathered_ref[slab, 2 * ct + q], turn),
                    jnp.where(left_half, moved[0], moved[1]),
                )

    for bx in (0, 2):
        for by in range(3):
            for ct in range(3):
                tile = gathered_ref[owner[3 * bx + by], 6 + ct // 2]
                ends_ref[3 * bx // 2 + by, ct] = roll(tile, -64 * (ct % 2))

    def placed(ct, bx, i):
        if bx == 1:
            tile, half = 4 * ct + i // 2, i % 2
            parts = [sides_ref[0, tile], own_ref[tile], sides_ref[1, tile]]
        elif i == (3 if bx == 0 else 4):
            half = 0
            parts = [ends_ref[3 * bx // 2 + by, ct] for by in range(3)]
        else:
            tile, half = 2 * ct + (i // 2 - 2 if bx == 0 else i // 2), i % 2
            parts = [gathered_ref[owner[3 * bx + by], tile] for by in range(3)]
        outer = 96 - 64 * half
        return roll(parts[0], outer), roll(parts[1], 32 - 64 * half), roll(parts[2], outer)

    zero = jnp.zeros((16, LANES), bf16)

    for plane in range(18):
        bx, i = (plane + 3) // 8, (plane + 3) % 8
        for ct in range(3):
            before, middle, after = placed(ct, bx, i)
            main = jnp.where(low, before, jnp.where(mid, middle, after)) * main_masks[bx]
            edge = jnp.where(left_half, after, before) * edge_masks[bx]
            for c in (-1, 0, 1):
                if c == 0:
                    main_c, edge_c = main, edge
                else:
                    keep = depth >= 1 if c == 1 else depth <= 6
                    main_c, edge_c = jnp.where(keep, main, zero), jnp.where(keep, edge, zero)
                for b in (-1, 0, 1):
                    step = 8 * b + c
                    if b == 1:
                        source = jnp.where(lane < step, edge_c, main_c)
                    elif b == -1:
                        source = jnp.where(lane >= LANES + step, edge_c, main_c)
                    else:
                        source = main_c
                    row = (3 * (b + 1) + c + 1) * C + 16 * ct
                    x9_ref[row : row + 16, LANES * plane : LANES * (plane + 1)] = (
                        roll(source, -step) if step else source
                    )

    def plane_cols(plane):
        return slice(LANES * plane, LANES * (plane + 1))

    def summed(plane, stride):
        return (
            product_ref[0:C, plane_cols(plane)]
            + product_ref[C : 2 * C, plane_cols(plane + stride)]
            + product_ref[2 * C : 3 * C, plane_cols(plane + 2 * stride)]
        )

    for n in range(9):
        cols = slice(256 * n, 256 * (n + 1))
        product_ref[:, cols] = matmul(w1_ref[...], x9_ref[:, cols])

    for plane in range(16):
        bx = (plane + 4) // 8
        pre = summed(plane, 1)
        negative = jnp.exp(jnp.minimum(pre, 0.0))
        if 4 <= plane < 12:
            slope1_ref[:, plane_cols(plane - 4)] = jnp.where(pre > 0, 1.0, negative)
        hidden = jnp.where(pre > 0, pre, negative - 1.0) * masks[bx]
        hidden = hidden.astype(bf16)
        for c in (-1, 0, 1):
            if c == 0:
                source = hidden
            else:
                keep = depth48 >= 2 if c == 1 else depth48 <= 5
                source = jnp.where(keep, hidden, jnp.zeros((C, LANES), bf16))
            for b in (-1, 0, 1):
                step = 16 * b + 2 * c
                row = (3 * (b + 1) + c + 1) * C
                h9_ref[row : row + C, plane_cols(plane)] = roll(source, -step) if step else source

    for n in range(8):
        cols = slice(256 * n, 256 * (n + 1))
        product_ref[:, cols] = matmul(w2_ref[...], h9_ref[:, cols])

    targets = []
    for bx, half in ((0, 1), (1, 0), (1, 1), (2, 1)):
        if bx == 1:
            before = roll(gathered_ref[owner[3], 7], -48 - 16 * half)
            middle = roll(own_ref[12], 32 - 64 * half)
            after = roll(gathered_ref[owner[5], 7], 32 - 16 * half)
        else:
            parts = [gathered_ref[owner[3 * bx + by], 7] for by in range(3)]
            before, middle, after = roll(parts[0], 32), roll(parts[1], -32), roll(parts[2], 32)
        cells = jnp.where(low, before, jnp.where(mid, middle, after))
        targets.append(cells.astype(jnp.float32))
    own_grads = []
    for pair in range(6):
        cols = slice(256 * pair, 256 * (pair + 1))
        slopes = []
        for plane in (2 * pair, 2 * pair + 1):
            bx = (plane + 6) // 8
            pre = summed(plane, 2)
            negative = jnp.exp(jnp.minimum(pre, 0.0))
            slopes.append(jnp.where(pre > 0, 1.0, negative) * masks[bx])
            hidden = jnp.where(pre > 0, pre, negative - 1.0) * masks[bx]
            hid2_ref[:, plane_cols(plane)] = hidden.astype(bf16)
        logits = matmul(h_ref[...], hid2_ref[:, cols])
        grads = []
        for side in range(2):
            plane = 2 * pair + side
            bx, i = (plane + 6) // 8, (plane + 6) % 8
            value = logits[:, plane_cols(side)]
            if bx == 1:
                wanted = targets[1 + i % 2][4 * (i // 2) : 4 * (i // 2) + 4]
            else:
                wanted = targets[0 if bx == 0 else 3][4 * (i % 2) : 4 * (i % 2) + 4]
            wanted = jnp.concatenate([wanted, jnp.zeros((12, LANES), jnp.float32)], axis=0)
            sigmoid = 1.0 / (1.0 + jnp.exp(-value))
            grads.append((sigmoid - wanted) * masks[bx] * scale)
        if 1 <= pair <= 4:
            first = roll(logits[:, plane_cols(0)], -32)
            second = roll(logits[:, plane_cols(1)], 32)
            logits_ref[:, plane_cols(pair - 1)] = jnp.where(left_half, first, second)[0:8]
            own_grads += [(grad * own_row).astype(bf16) for grad in grads]
        back = matmul(ht_ref[...], jnp.concatenate(grads, axis=1).astype(bf16))
        for side in range(2):
            grad2_ref[:, plane_cols(2 * pair + side)] = (
                back[:, plane_cols(side)] * slopes[side]
            ).astype(bf16)
    head_part = matmul_lanes(
        hid2_ref[:, 2 * LANES : 10 * LANES], jnp.concatenate(own_grads, axis=1)
    )

    for a in range(3):
        for x in range(8):
            shifted_ref[C * a : C * (a + 1), plane_cols(x)] = grad2_ref[:, plane_cols(x + 4 - 2 * a)]
    for n in range(4):
        cols = slice(256 * n, 256 * (n + 1))
        back_ref[:, cols] = matmul(w2t_ref[...], shifted_ref[:, cols])
    own_bf16 = jnp.broadcast_to(own_row, (C, LANES)).astype(bf16)
    empty = jnp.zeros((C, LANES), bf16)
    for a in range(3):
        for x in [*range(2 * a), *range(2 * a + 8, 12)]:
            spread_ref[C * a : C * (a + 1), plane_cols(x)] = empty
        for x in range(8):
            spread_ref[C * a : C * (a + 1), plane_cols(x + 2 * a)] = (
                grad2_ref[:, plane_cols(x + 2)] * own_bf16
            )
    second_part = matmul_lanes(spread_ref[...], h9_ref[:, 2 * LANES : 14 * LANES])

    grad1 = []
    for x in range(8):
        total = jnp.zeros((C, LANES), jnp.float32)
        for c in (-1, 0, 1):
            part = jnp.zeros((C, LANES), jnp.float32)
            for b in (-1, 0, 1):
                row = (3 * (b + 1) + c + 1) * C
                step = 16 * b + 2 * c
                piece = back_ref[row : row + C, plane_cols(x)]
                part += roll(piece, step) if step else piece
            if c:
                part = jnp.where(depth48 >= 2 if c == 1 else depth48 <= 5, part, 0.0)
            total += part
        grad1.append((total * slope1_ref[:, plane_cols(x)] * own_row).astype(jnp.bfloat16))

    for a in range(3):
        for x in [*range(a), *range(a + 8, 10)]:
            shifted_ref[C * a : C * (a + 1), plane_cols(x)] = empty
        for x in range(8):
            shifted_ref[C * a : C * (a + 1), plane_cols(x + a)] = grad1[x]
    first_part = matmul_lanes(
        shifted_ref[:, 0 : 10 * LANES], x9_ref[:, 4 * LANES : 14 * LANES]
    )

    first_core = (lax.axis_index("dp") & 1) == 0
    head_part = jnp.concatenate([head_part, jnp.zeros((24, 16), jnp.float32)], axis=0)
    nothing = jnp.zeros((72, 16), jnp.float32)
    ends = []
    for part, extra in ((first_part, nothing), (second_part, head_part)):
        tail = jnp.concatenate([part[0:72, 384:], part[72:144, 384:], extra, nothing], axis=1)
        ends.append(jnp.concatenate([tail, jnp.zeros((8, LANES), jnp.float32)], axis=0))
    pieces = [(first_part[:, plane_cols(q)], second_part[:, plane_cols(q)]) for q in range(3)]
    row = 0
    for first, second in pieces + [tuple(ends)]:
        rows = slice(row, row + first.shape[0])
        keep_ref[rows, :] = jnp.where(first_core, first, second)
        send_ref[rows, :] = jnp.where(first_core, second, first)
        row += first.shape[0]


def add_kernel(mine_ref, other_ref, out_ref):
    out_ref[...] = (mine_ref[...] + other_ref[...]).astype(jnp.bfloat16)


def sum_kernel(parts_ref, out_ref):
    total = parts_ref[0].astype(jnp.float32)
    for s in range(1, parts_ref.shape[0]):
        total += parts_ref[s].astype(jnp.float32)
    total = total.astype(jnp.bfloat16)
    for s in range(out_ref.shape[0]):
        out_ref[s] = total


def unpack_kernel(mine_ref, other_ref, logits_ref, first_ref, second_ref, head_ref, out_ref):
    out_ref[:, 0, :] = logits_ref[0:3, :]
    first_core = (lax.axis_index("dp") & 1) == 0
    mine, other = mine_ref[...], other_ref[...]
    for k, out in ((0, first_ref), (1, second_ref)):
        half = jnp.where(first_core, other if k else mine, mine if k else other)
        half = half.astype(jnp.float32)
        tail = jnp.concatenate([half[432:504, 0:C], half[432:504, C : 2 * C]], axis=0)
        tiles = [half[144 * q : 144 * (q + 1), :] for q in range(3)]
        whole = jnp.concatenate(tiles + [tail], axis=1)
        for a in range(3):
            for t in range(9):
                out[9 * a + t] = whole[C * a : C * (a + 1), C * t : C * (t + 1)]
        if k:
            head_ref[...] = half[432 : 432 + C, 96:112].T[0:3]


def on_device_flat(features, device_block, conv_first, conv_second, head_weight, targets):
    space_count = lax.axis_size("space")
    device_count = lax.axis_size("dp") * space_count
    bf16, f32 = jnp.bfloat16, jnp.float32
    small = pltpu.CompilerParams(vmem_limit_bytes=8 * 1024 * 1024)
    shape = jax.ShapeDtypeStruct
    vmem = pl.BlockSpec(memory_space=pltpu.VMEM)

    def swap(values, mask):
        return lax.ppermute(values, "space", [(s, s ^ mask) for s in range(space_count)])

    mate_targets, mate_features = swap(targets, 1), swap(features, 1)
    own, own_slabs = pl.pallas_call(
        pack_own_kernel,
        out_shape=(shape((13, 16, LANES), bf16), shape((3, 8, 16, LANES), bf16)),
        in_specs=[vmem] * 3,
        out_specs=(vmem,) * 2,
        scratch_shapes=[pltpu.VMEM((4, 8, 16, LANES), bf16)],
        compiler_params=small,
        cost_estimate=pl.CostEstimate(flops=1_000_000, bytes_accessed=2_000_000, transcendentals=0),
        name="pack_own",
    )(device_block, features[0, 0], targets[0].transpose(1, 0, 2))
    mate_slab, *pairs = pl.pallas_call(
        pack_mate_kernel,
        out_shape=(
            shape((8, 16, LANES), bf16),
            *[shape((2, 8, 16, LANES), bf16) for _ in PARTNERS],
        ),
        in_specs=[vmem] * 4,
        out_specs=(vmem,) * 4,
        scratch_shapes=[pltpu.VMEM((4, 8, 16, LANES), bf16)],
        compiler_params=small,
        name="pack_mate",
    )(device_block, mate_features[0, 0], mate_targets[0].transpose(1, 0, 2), own_slabs)
    pairs = [swap(pair, mask) for pair, mask in zip(pairs, PARTNERS)]

    w1, w2, w2t, head, head_t, owners, masks = pl.pallas_call(
        prepare_kernel,
        out_shape=(
            shape((3 * C, 9 * C), bf16),
            shape((3 * C, 9 * C), bf16),
            shape((9 * C, 3 * C), bf16),
            shape((16, C), bf16),
            shape((C, 16), bf16),
            shape((1, LANES), jnp.int32),
            shape((8, LANES), f32),
        ),
        in_specs=[vmem] * 4,
        out_specs=(vmem,) * 7,
        scratch_shapes=[pltpu.SMEM((2, 16), jnp.int32)],
        compiler_params=small,
        cost_estimate=pl.CostEstimate(flops=2_000_000, bytes_accessed=4_000_000, transcendentals=0),
        name="prepare",
    )(device_block, conv_first.transpose(1, 0, 2), conv_second.transpose(1, 0, 2), head_weight)

    scale = (device_count * 3 * CELLS) ** (-0.5)
    logits, keep, send = pl.pallas_call(
        functools.partial(crop_kernel, scale),
        out_shape=(shape((8, CELLS), f32), shape((HALF, LANES), f32), shape((HALF, LANES), f32)),
        in_specs=[vmem] * 12,
        out_specs=(vmem,) * 3,
        scratch_shapes=[
            pltpu.VMEM((space_count, 8, 16, LANES), bf16),
            pltpu.VMEM((2, 12, 16, LANES), bf16),
            pltpu.VMEM((6, 3, 16, LANES), bf16),
            pltpu.VMEM((9 * C, 18 * LANES), bf16),
            pltpu.VMEM((9 * C, 16 * LANES), bf16),
            pltpu.VMEM((3 * C, 18 * LANES), f32),
            pltpu.VMEM((C, 8 * LANES), f32),
            pltpu.VMEM((C, 12 * LANES), bf16),
            pltpu.VMEM((C, 12 * LANES), bf16),
            pltpu.VMEM((3 * C, 12 * LANES), bf16),
            pltpu.VMEM((3 * C, 12 * LANES), bf16),
            pltpu.VMEM((9 * C, 8 * LANES), f32),
        ],
        compiler_params=pltpu.CompilerParams(vmem_limit_bytes=20 * 1024 * 1024),
        name="forward_backward",
    )(owners, masks, own, mate_slab, *pairs, w1, w2, w2t, head, head_t)

    dp_count = lax.axis_size("dp")

    def swap_cores(values):
        return lax.ppermute(values, "dp", [(d, d ^ 1) for d in range(dp_count)])

    peers = device_count // 2
    groups = [
        [d * space_count + s for d in range(core, dp_count, 2) for s in range(space_count)]
        for core in range(2)
    ]

    def exchange(values):
        return lax.all_to_all(
            values, ("dp", "space"), 0, 0, axis_index_groups=groups, tiled=True
        )

    def step(kernel, out, *operands):
        return pl.pallas_call(
            kernel,
            out_shape=out,
            in_specs=[vmem] * len(operands),
            out_specs=vmem,
            compiler_params=small,
            name="gradient_sum",
        )(*operands)

    term = step(add_kernel, shape((HALF, LANES), bf16), keep, swap_cores(send))
    pieces = shape((peers, HALF // peers, LANES), bf16)
    total = exchange(step(sum_kernel, pieces, exchange(term.reshape(pieces.shape))))
    total = total.reshape(HALF, LANES)
    grad_first, grad_second, grad_head, logits = pl.pallas_call(
        unpack_kernel,
        out_shape=(
            shape((27, C, C), f32),
            shape((27, C, C), f32),
            shape((3, C), f32),
            shape((3, 1, CELLS), f32),
        ),
        in_specs=[vmem] * 3,
        out_specs=(vmem,) * 4,
        compiler_params=small,
        name="unpack_gradients",
    )(total, swap_cores(total), logits)
    return (
        logits.transpose(1, 0, 2)[None],
        grad_first.transpose(1, 0, 2),
        grad_second.transpose(1, 0, 2),
        grad_head,
    )


def solution(mesh):
    in_specs = (
        P("dp", "space", None, None),
        P("dp", None),
        P(),
        P(),
        P(),
        P("dp", "space", None, None),
    )
    out_specs = (P("dp", "space", None, None), P(), P(), P())
    flat = mesh.shape["space"] == 8 and mesh.shape["dp"] in (2, 4)
    return jax.shard_map(
        on_device_flat if flat else on_device_deep,
        mesh=mesh,
        in_specs=in_specs,
        out_specs=out_specs,
        check_vma=False,
    )
```

```python
import functools

import jax
import jax.numpy as jnp
from jax import lax
from jax.experimental import pallas as pl
from jax.experimental.pallas import tpu as pltpu
from jax.sharding import PartitionSpec as P

BS = 8


tap_offsets = [
    (tap_index // 9 - 1, tap_index // 3 % 3 - 1, tap_index % 3 - 1) for tap_index in range(27)
]


def elu_pair(values):
    negative = jnp.exp(jnp.minimum(values, 0.0))
    return (jnp.where(values > 0, values, negative - 1.0), jnp.where(values > 0, 1.0, negative))


def neighbor_tables(device_block):
    space_count = lax.axis_size("space")
    depth_z = space_count // 8
    self_index = lax.axis_index("space")
    blocks = device_block[0]
    coords = jnp.stack([blocks // (4 * depth_z), blocks // depth_z % 4, blocks % depth_z])
    own_coords = lax.dynamic_index_in_dim(coords, self_index, 1, keepdims=False)
    offsets = jnp.array(tap_offsets, jnp.int32)
    limits = jnp.array([4, 4, depth_z], jnp.int32)
    wanted = own_coords[None, :] + offsets
    inside = jnp.all((wanted >= 0) & (wanted < limits[None, :]), axis=1) & (jnp.arange(27) != 13)
    wanted_id = (wanted[:, 0] * 4 + wanted[:, 1]) * depth_z + wanted[:, 2]
    matches = (blocks[None, :] == wanted_id[:, None]) & inside[:, None]
    devices = jnp.arange(space_count, dtype=jnp.int32)
    owner_row = jnp.sum(jnp.where(matches, devices[None, :], 0), axis=1)
    present = jnp.any(matches, axis=1)
    relative = coords - own_coords[:, None]
    adjacent = jnp.all(jnp.abs(relative) <= 1, axis=0) & (devices != self_index)
    send_tap = jnp.where(
        adjacent, (relative[0] + 1) * 9 + (relative[1] + 1) * 3 + relative[2] + 1, 13
    )
    return (owner_row, present, send_tap)


def region_slice(block_data, offset, depth_cells):
    span_list = []
    for step_value in offset:
        if step_value == 1:
            span_list.append(slice(BS - depth_cells, BS))
        elif step_value == -1:
            span_list.append(slice(0, depth_cells))
        else:
            span_list.append(slice(0, BS))
    return block_data[:, span_list[0], span_list[1], span_list[2]]


def surround(block_data, depth_cells, tables):
    owner_row, present, send_tap = tables
    channels = block_data.shape[0]
    length = depth_cells * BS * BS
    pieces = []
    for tap_index in range(27):
        if tap_index == 13:
            pieces.append(jnp.zeros((channels, length), block_data.dtype))
        else:
            region = region_slice(block_data, tap_offsets[tap_index], depth_cells).reshape(
                channels, -1
            )
            pieces.append(jnp.pad(region, ((0, 0), (0, length - region.shape[1]))))
    outgoing = jnp.stack(pieces)
    sending = outgoing[send_tap]
    by_source = lax.all_to_all(sending, "space", split_axis=0, concat_axis=0, tiled=True)
    incoming = jnp.where(
        present[:, None, None], by_source[owner_row], jnp.zeros((), block_data.dtype)
    )
    rows_x = []
    for step_x in range(3):
        rows_y = []
        for step_y in range(3):
            rows_z = []
            for step_z in range(3):
                tap_index = step_x * 9 + step_y * 3 + step_z
                if tap_index == 13:
                    rows_z.append(block_data)
                else:
                    extent_list = [
                        BS if step_value == 1 else depth_cells
                        for step_value in (step_x, step_y, step_z)
                    ]
                    count_cells = extent_list[0] * extent_list[1] * extent_list[2]
                    rows_z.append(
                        incoming[tap_index][:, :count_cells].reshape(
                            channels, extent_list[0], extent_list[1], extent_list[2]
                        )
                    )
            rows_y.append(jnp.concatenate(rows_z, axis=3))
        rows_x.append(jnp.concatenate(rows_y, axis=2))
    return jnp.concatenate(rows_x, axis=1)


def conv_padded(padded, kernel, dilation):
    result = lax.conv_general_dilated(
        padded[None],
        kernel,
        (1, 1, 1),
        "VALID",
        rhs_dilation=(dilation, dilation, dilation),
        dimension_numbers=("NCDHW", "OIDHW", "NCDHW"),
        preferred_element_type=jnp.float32,
    )
    return result[0].reshape(kernel.shape[0], BS * BS * BS)


def kernel_grad(padded, grad_rows, dilation):
    channels = padded.shape[0]
    outputs = grad_rows.shape[0]
    grad_block = grad_rows.reshape(outputs, 1, BS, BS, BS)
    result = lax.conv_general_dilated(
        padded[None],
        grad_block,
        (dilation, dilation, dilation),
        "VALID",
        dimension_numbers=("CNDHW", "OIDHW", "NCDHW"),
        preferred_element_type=jnp.float32,
    )
    return result.reshape(channels, outputs, 27).transpose(1, 2, 0)


def on_device_deep(features, device_block, conv_first, conv_second, head_weight, targets):
    channels = features.shape[2]
    tables = neighbor_tables(device_block)
    kernel_first = conv_first.reshape(channels, 3, 3, 3, channels).transpose(0, 4, 1, 2, 3)
    kernel_second = conv_second.reshape(channels, 3, 3, 3, channels).transpose(0, 4, 1, 2, 3)
    block_in = features[0, 0].reshape(channels, BS, BS, BS)
    padded_in = surround(block_in, 1, tables)
    pre_first = conv_padded(padded_in, kernel_first, 1)
    act_first, slope_first = elu_pair(pre_first)
    hid_first = act_first.astype(jnp.bfloat16)
    padded_first = surround(hid_first.reshape(channels, BS, BS, BS), 2, tables)
    pre_second = conv_padded(padded_first, kernel_second, 2)
    act_second, slope_second = elu_pair(pre_second)
    hid_second = act_second.astype(jnp.bfloat16)
    logits = jnp.dot(head_weight, hid_second, preferred_element_type=jnp.float32)
    scale = (lax.axis_size("dp") * lax.axis_size("space") * 3 * BS * BS * BS) ** (-0.5)
    grad_logit = ((jax.nn.sigmoid(logits) - targets[0, 0].astype(jnp.float32)) * scale).astype(
        jnp.bfloat16
    )
    grad_head = lax.dot_general(
        grad_logit, hid_second, (((1,), (1,)), ((), ())), preferred_element_type=jnp.float32
    )
    back_second = lax.dot_general(
        head_weight, grad_logit, (((0,), (0,)), ((), ())), preferred_element_type=jnp.float32
    )
    grad_pre_second = (back_second * slope_second).astype(jnp.bfloat16)
    grad_second = kernel_grad(padded_first, grad_pre_second, 2)
    padded_grad = surround(grad_pre_second.reshape(channels, BS, BS, BS), 2, tables)
    kernel_back = jnp.transpose(kernel_second[:, :, ::-1, ::-1, ::-1], (1, 0, 2, 3, 4))
    back_first = conv_padded(padded_grad, kernel_back, 2)
    grad_pre_first = (back_first * slope_first).astype(jnp.bfloat16)
    grad_first = kernel_grad(padded_in, grad_pre_first, 1)
    grad_first, grad_second, grad_head = lax.psum(
        (grad_first, grad_second, grad_head), ("dp", "space")
    )
    return (logits[None, None], grad_first, grad_second, grad_head)


C = 48
CELLS = 512
HALF = 512
LANES = 128


def lanes(rows=1):
    return lax.broadcasted_iota(jnp.int32, (rows, LANES), 1)


def roll(values, shift):
    return pltpu.roll(values, shift % LANES, 1) if shift % LANES else values


def listed_blocks(block_ref, me):
    ids = block_ref[...].astype(jnp.float32)
    index = lax.broadcasted_iota(jnp.int32, ids.shape, 1)
    return [
        jnp.sum(jnp.where(index == (me ^ k), ids, 0.0)).astype(jnp.int32)
        for k in range(ids.shape[1])
    ]


def apart(source, target):
    return (target >> 2) - (source >> 2), (target & 3) - (source & 3)


PARTNERS = (6, 2, 4)


def block_tiles(features_ref, targets_ref):
    tiles = [
        [features_ref[16 * ct : 16 * (ct + 1), LANES * q : LANES * (q + 1)] for q in range(4)]
        for ct in range(3)
    ]
    targets = targets_ref[:, 0, :].astype(jnp.float32)
    targets = jnp.concatenate([targets, jnp.zeros((1, CELLS), jnp.float32)], axis=0)
    return tiles, [targets[:, LANES * q : LANES * (q + 1)] for q in range(4)]


def write_cases(tiles, rows, cases_ref):
    lane = lanes(16)
    left = lane < 64
    cell = lane & 63
    target_tile = jnp.concatenate(rows, axis=0)

    def write(case, pairs, halves, wanted):
        for ct in range(3):
            cases_ref[case, 2 * ct] = pairs[ct][0]
            cases_ref[case, 2 * ct + 1] = pairs[ct][1]
        cases_ref[case, 6] = jnp.where(left, halves[0], halves[1])
        cases_ref[case, 7] = jnp.where(left, halves[2], wanted.astype(jnp.bfloat16))

    for case, pair, single, q in ((0, (2, 3), 1, 3), (1, (0, 1), 2, 0)):
        turns = (64, 0, 64) if case == 0 else (0, 64, 0)
        halves = [roll(tiles[ct][single], turns[ct]) for ct in range(3)]
        both = [roll(rows[q], 64), rows[q], jnp.zeros((8, LANES), jnp.float32)]
        wanted = jnp.concatenate(both, axis=0)
        write(case, [(t[pair[0]], t[pair[1]]) for t in tiles], halves, wanted)
    for case, spare, turn, turns, target_turns in (
        (2, cell < 24, -24, (-48, -96, -16, -64), (16, -32)),
        (3, cell >= 40, 40, (-24, -72, 8, -40), (64, 16)),
    ):
        pairs, halves = [], []
        for ct, t in enumerate(tiles):
            pairs.append([jnp.where(spare, roll(t[q + 2], turn), t[q]) for q in range(2)])
            moved = [roll(t[2 + n // 2], turns[n] + (64 if ct == 1 else 0)) for n in range(4)]
            half = jnp.where(cell < 16, moved[0], jnp.where(cell < 32, moved[1], moved[2]))
            halves.append(jnp.where(cell < 48, half, moved[3]))
        wanted = [roll(target_tile, n) for n in target_turns]
        write(case, pairs, halves, jnp.where(lane < 80, wanted[0], wanted[1]))


def case_of(source, target):
    dx, dy = apart(source, target)
    return jnp.where(dx > 0, 0, jnp.where(dx < 0, 1, jnp.where(dy > 0, 2, 3)))


def pack_own_kernel(
    block_ref, features_ref, targets_ref, head_ref, own_ref, slabs_ref, h_ref, ht_ref, cases_ref
):
    blocks = listed_blocks(block_ref, lax.axis_index("space"))
    tiles, rows = block_tiles(features_ref, targets_ref)
    for ct in range(3):
        for q in range(4):
            own_ref[4 * ct + q] = tiles[ct][q]
    own_ref[12] = jnp.concatenate(rows, axis=0).astype(jnp.bfloat16)
    write_cases(tiles, rows, cases_ref)
    for n, k in enumerate(PARTNERS):
        slabs_ref[n] = cases_ref[case_of(blocks[0], blocks[k])]
    head = head_ref[...].astype(jnp.float32)
    head = jnp.concatenate([head, jnp.zeros((13, C), jnp.float32)], axis=0)
    h_ref[...] = head.astype(jnp.bfloat16)
    ht_ref[...] = head.T.astype(jnp.bfloat16)


def pack_mate_kernel(block_ref, features_ref, targets_ref, slabs_ref, mate_ref, *refs):
    *pair_refs, cases_ref = refs
    blocks = listed_blocks(block_ref, lax.axis_index("space"))
    write_cases(*block_tiles(features_ref, targets_ref), cases_ref)
    mate_ref[...] = cases_ref[case_of(blocks[1], blocks[0])]
    for n, (k, ref) in enumerate(zip(PARTNERS, pair_refs)):
        ref[0] = slabs_ref[n]
        ref[1] = cases_ref[case_of(blocks[1], blocks[k])]


def stacked_taps(ref):
    rows = []
    for a in range(3):
        taps = [ref[9 * a + t] for t in range(9)]
        rows.append(jnp.concatenate(taps, axis=1))
    return jnp.concatenate(rows, axis=0)


def prepare_kernel(
    block_ref,
    first_ref,
    second_ref,
    w1_ref,
    w2_ref,
    w2t_ref,
    owners_ref,
    masks_ref,
    table_ref,
):
    w1_ref[...] = stacked_taps(first_ref)
    whole = stacked_taps(second_ref)
    w2_ref[...] = whole
    w2t_ref[...] = whole.T

    blocks = listed_blocks(block_ref, lax.axis_index("space"))
    for slot in range(10):
        table_ref[0, slot] = 1
        table_ref[1, slot] = 0
    table_ref[1, 4] = 1
    for k in range(1, len(blocks)):
        dx, dy = apart(blocks[0], blocks[k])
        near = (dx >= -1) & (dx <= 1) & (dy >= -1) & (dy <= 1)
        slot = jnp.where(near, dx * 3 + dy + 4, 9)
        table_ref[0, slot] = k
        table_ref[1, slot] = 1
    lane = lanes()
    there = [table_ref[1, q].astype(jnp.float32) for q in range(9)]
    owners = jnp.zeros((1, LANES), jnp.int32)
    for q in range(9):
        owners = jnp.where(lane == q, table_ref[0, q], owners)
    owners_ref[...] = owners
    for bx in range(3):
        before, middle, after = there[3 * bx : 3 * bx + 3]
        masks_ref[bx : bx + 1, :] = jnp.where(
            lane < 32, before, jnp.where(lane < 96, middle, after)
        )
        masks_ref[bx + 3 : bx + 4, :] = jnp.where(lane < 64, after, before)


def matmul(left, right):
    return lax.dot_general(
        left, right, (((1,), (0,)), ((), ())), preferred_element_type=jnp.float32
    )


def matmul_lanes(left, right):
    return lax.dot_general(
        left, right, (((1,), (1,)), ((), ())), preferred_element_type=jnp.float32
    )


def crop_kernel(scale, owners_ref, masks_ref, own_ref, mate_ref, *refs):
    crop_body(scale, owners_ref, masks_ref, own_ref, mate_ref, refs[:3], *refs[3:])


def crop_body(
    scale,
    owners_ref,
    masks_ref,
    own_ref,
    mate_ref,
    pairs,
    w1_ref,
    w2_ref,
    w2t_ref,
    h_ref,
    ht_ref,
    logits_ref,
    keep_ref,
    send_ref,
    gathered_ref,
    sides_ref,
    ends_ref,
    x9_ref,
    h9_ref,
    product_ref,
    slope1_ref,
    slope2_ref,
    hid2_ref,
    grad2_ref,
    shifted_ref,
    back_ref,
):
    gathered_ref[1] = mate_ref[...]
    for k, pair in zip(PARTNERS, pairs):
        for j in range(2):
            gathered_ref[k + j] = pair[j]
    owners = owners_ref[...]
    owner = [owners[0, q] for q in range(9)]

    bf16 = jnp.bfloat16
    lane = lanes(16)
    depth = lane & 7
    depth48 = lanes(C) & 7
    low, mid, left_half = lane < 32, lane < 96, lane < 64
    masks = [masks_ref[bx : bx + 1, :] for bx in range(3)]
    main_masks = [jnp.broadcast_to(mask, (16, LANES)).astype(bf16) for mask in masks]
    edge_masks = [
        jnp.broadcast_to(masks_ref[bx + 3 : bx + 4, :], (16, LANES)).astype(bf16)
        for bx in range(3)
    ]
    own_row = jnp.where((lane >= 32) & mid, 1.0, 0.0)[0:1]

    cell = lane & 63
    for side, by, in_place, turn, turns in (
        (0, 0, cell < 48, 24, (48, 96, 16, 64)),
        (1, 2, cell < 24, -40, (24, 72, -8, 40)),
    ):
        slab = owner[3 + by]
        for ct in range(3):
            half = gathered_ref[slab, 6 + ct // 2]
            for q in range(2):
                sides_ref[side, 4 * ct + q] = gathered_ref[slab, 2 * ct + q]
                moved = [roll(half, turns[2 * q + n] - (64 if ct == 1 else 0)) for n in range(2)]
                sides_ref[side, 4 * ct + q + 2] = jnp.where(
                    in_place,
                    roll(gathered_ref[slab, 2 * ct + q], turn),
                    jnp.where(left_half, moved[0], moved[1]),
                )

    for bx in (0, 2):
        for by in range(3):
            for ct in range(3):
                tile = gathered_ref[owner[3 * bx + by], 6 + ct // 2]
                ends_ref[3 * bx // 2 + by, ct] = roll(tile, -64 * (ct % 2))

    def placed(ct, bx, i):
        if bx == 1:
            tile, half = 4 * ct + i // 2, i % 2
            parts = [sides_ref[0, tile], own_ref[tile], sides_ref[1, tile]]
        elif i == (3 if bx == 0 else 4):
            half = 0
            parts = [ends_ref[3 * bx // 2 + by, ct] for by in range(3)]
        else:
            tile, half = 2 * ct + (i // 2 - 2 if bx == 0 else i // 2), i % 2
            parts = [gathered_ref[owner[3 * bx + by], tile] for by in range(3)]
        outer = 96 - 64 * half
        return roll(parts[0], outer), roll(parts[1], 32 - 64 * half), roll(parts[2], outer)

    zero = jnp.zeros((16, LANES), bf16)

    for plane in range(18):
        bx, i = (plane + 3) // 8, (plane + 3) % 8
        for ct in range(3):
            before, middle, after = placed(ct, bx, i)
            main = jnp.where(low, before, jnp.where(mid, middle, after)) * main_masks[bx]
            edge = jnp.where(left_half, after, before) * edge_masks[bx]
            for c in (-1, 0, 1):
                if c == 0:
                    main_c, edge_c = main, edge
                else:
                    keep = depth >= 1 if c == 1 else depth <= 6
                    main_c, edge_c = jnp.where(keep, main, zero), jnp.where(keep, edge, zero)
                for b in (-1, 0, 1):
                    step = 8 * b + c
                    if b == 1:
                        source = jnp.where(lane < step, edge_c, main_c)
                    elif b == -1:
                        source = jnp.where(lane >= LANES + step, edge_c, main_c)
                    else:
                        source = main_c
                    row = (3 * (b + 1) + c + 1) * C + 16 * ct
                    x9_ref[row : row + 16, LANES * plane : LANES * (plane + 1)] = (
                        roll(source, -step) if step else source
                    )

    def plane_cols(plane):
        return slice(LANES * plane, LANES * (plane + 1))

    def summed(plane, stride):
        return (
            product_ref[0:C, plane_cols(plane)]
            + product_ref[C : 2 * C, plane_cols(plane + stride)]
            + product_ref[2 * C : 3 * C, plane_cols(plane + 2 * stride)]
        )

    for n in range(9):
        cols = slice(256 * n, 256 * (n + 1))
        product_ref[:, cols] = matmul(w1_ref[...], x9_ref[:, cols])

    for plane in range(16):
        bx = (plane + 4) // 8
        pre = summed(plane, 1)
        negative = jnp.exp(jnp.minimum(pre, 0.0))
        if 4 <= plane < 12:
            slope1_ref[:, plane_cols(plane - 4)] = jnp.where(pre > 0, 1.0, negative)
        hidden = jnp.where(pre > 0, pre, negative - 1.0) * masks[bx]
        hidden = hidden.astype(bf16)
        for c in (-1, 0, 1):
            if c == 0:
                source = hidden
            else:
                keep = depth48 >= 2 if c == 1 else depth48 <= 5
                source = jnp.where(keep, hidden, jnp.zeros((C, LANES), bf16))
            for b in (-1, 0, 1):
                step = 16 * b + 2 * c
                row = (3 * (b + 1) + c + 1) * C
                h9_ref[row : row + C, plane_cols(plane)] = roll(source, -step) if step else source

    for n in range(8):
        cols = slice(256 * n, 256 * (n + 1))
        product_ref[:, cols] = matmul(w2_ref[...], h9_ref[:, cols])

    for plane in range(12):
        bx = (plane + 6) // 8
        pre = summed(plane, 2)
        negative = jnp.exp(jnp.minimum(pre, 0.0))
        slope2_ref[:, plane_cols(plane)] = jnp.where(pre > 0, 1.0, negative) * masks[bx]
        hidden = jnp.where(pre > 0, pre, negative - 1.0) * masks[bx]
        hid2_ref[:, plane_cols(plane)] = hidden.astype(jnp.bfloat16)

    logits = matmul(h_ref[...], hid2_ref[...])
    targets = []
    for bx, half in ((0, 1), (1, 0), (1, 1), (2, 1)):
        if bx == 1:
            before = roll(gathered_ref[owner[3], 7], -48 - 16 * half)
            middle = roll(own_ref[12], 32 - 64 * half)
            after = roll(gathered_ref[owner[5], 7], 32 - 16 * half)
        else:
            parts = [gathered_ref[owner[3 * bx + by], 7] for by in range(3)]
            before, middle, after = roll(parts[0], 32), roll(parts[1], -32), roll(parts[2], 32)
        cells = jnp.where(low, before, jnp.where(mid, middle, after))
        targets.append(cells.astype(jnp.float32))
    grads = []
    for plane in range(12):
        bx, i = (plane + 6) // 8, (plane + 6) % 8
        value = logits[:, plane_cols(plane)]
        if bx == 1:
            wanted = targets[1 + i % 2][4 * (i // 2) : 4 * (i // 2) + 4]
        else:
            wanted = targets[0 if bx == 0 else 3][4 * (i % 2) : 4 * (i % 2) + 4]
        wanted = jnp.concatenate([wanted, jnp.zeros((12, LANES), jnp.float32)], axis=0)
        sigmoid = 1.0 / (1.0 + jnp.exp(-value))
        grads.append((sigmoid - wanted) * masks[bx] * scale)
    for q in range(4):
        first = roll(logits[:, plane_cols(2 + 2 * q)], -32)
        second = roll(logits[:, plane_cols(3 + 2 * q)], 32)
        logits_ref[:, plane_cols(q)] = jnp.where(left_half, first, second)[0:8]

    grad_logit = jnp.concatenate(grads, axis=1).astype(jnp.bfloat16)
    back = matmul(ht_ref[...], grad_logit)
    grad2_ref[...] = (back * slope2_ref[...]).astype(jnp.bfloat16)
    own_grads = jnp.concatenate([grads[2 + x] * own_row for x in range(8)], axis=1)
    head_part = matmul_lanes(hid2_ref[:, 2 * LANES : 10 * LANES], own_grads.astype(jnp.bfloat16))

    own_bf16 = jnp.broadcast_to(own_row, (C, LANES)).astype(bf16)
    shifted_ref[...] = jnp.zeros_like(shifted_ref)
    for a in range(3):
        for x in range(8):
            shifted_ref[C * a : C * (a + 1), plane_cols(x + 2 * a)] = (
                grad2_ref[:, plane_cols(x + 2)] * own_bf16
            )
    second_part = matmul_lanes(shifted_ref[...], h9_ref[:, 2 * LANES : 14 * LANES])

    for a in range(3):
        for x in range(8):
            shifted_ref[C * a : C * (a + 1), plane_cols(x)] = grad2_ref[:, plane_cols(x + 4 - 2 * a)]
    for n in range(4):
        cols = slice(256 * n, 256 * (n + 1))
        back_ref[:, cols] = matmul(w2t_ref[...], shifted_ref[:, cols])
    grad1 = []
    for x in range(8):
        total = jnp.zeros((C, LANES), jnp.float32)
        for c in (-1, 0, 1):
            part = jnp.zeros((C, LANES), jnp.float32)
            for b in (-1, 0, 1):
                row = (3 * (b + 1) + c + 1) * C
                step = 16 * b + 2 * c
                piece = back_ref[row : row + C, plane_cols(x)]
                part += roll(piece, step) if step else piece
            if c:
                part = jnp.where(depth48 >= 2 if c == 1 else depth48 <= 5, part, 0.0)
            total += part
        grad1.append((total * slope1_ref[:, plane_cols(x)] * own_row).astype(jnp.bfloat16))

    shifted_ref[...] = jnp.zeros_like(shifted_ref)
    for a in range(3):
        for x in range(8):
            shifted_ref[C * a : C * (a + 1), plane_cols(x + a)] = grad1[x]
    first_part = matmul_lanes(
        shifted_ref[:, 0 : 10 * LANES], x9_ref[:, 4 * LANES : 14 * LANES]
    )

    first_core = (lax.axis_index("dp") & 1) == 0
    head_part = jnp.concatenate([head_part, jnp.zeros((24, 16), jnp.float32)], axis=0)
    nothing = jnp.zeros((72, 16), jnp.float32)
    ends = []
    for part, extra in ((first_part, nothing), (second_part, head_part)):
        tail = jnp.concatenate([part[0:72, 384:], part[72:144, 384:], extra, nothing], axis=1)
        ends.append(jnp.concatenate([tail, jnp.zeros((8, LANES), jnp.float32)], axis=0))
    pieces = [(first_part[:, plane_cols(q)], second_part[:, plane_cols(q)]) for q in range(3)]
    row = 0
    for first, second in pieces + [tuple(ends)]:
        rows = slice(row, row + first.shape[0])
        keep_ref[rows, :] = jnp.where(first_core, first, second)
        send_ref[rows, :] = jnp.where(first_core, second, first)
        row += first.shape[0]


def add_kernel(mine_ref, other_ref, out_ref):
    out_ref[...] = (mine_ref[...] + other_ref[...]).astype(jnp.bfloat16)


def sum_kernel(parts_ref, out_ref):
    total = parts_ref[0].astype(jnp.float32)
    for s in range(1, parts_ref.shape[0]):
        total += parts_ref[s].astype(jnp.float32)
    total = total.astype(jnp.bfloat16)
    for s in range(out_ref.shape[0]):
        out_ref[s] = total


def unpack_kernel(mine_ref, other_ref, logits_ref, first_ref, second_ref, head_ref, out_ref):
    out_ref[:, 0, :] = logits_ref[0:3, :]
    first_core = (lax.axis_index("dp") & 1) == 0
    mine, other = mine_ref[...], other_ref[...]
    for k, out in ((0, first_ref), (1, second_ref)):
        half = jnp.where(first_core, other if k else mine, mine if k else other)
        half = half.astype(jnp.float32)
        tail = jnp.concatenate([half[432:504, 0:C], half[432:504, C : 2 * C]], axis=0)
        tiles = [half[144 * q : 144 * (q + 1), :] for q in range(3)]
        whole = jnp.concatenate(tiles + [tail], axis=1)
        for a in range(3):
            for t in range(9):
                out[9 * a + t] = whole[C * a : C * (a + 1), C * t : C * (t + 1)]
        if k:
            head_ref[...] = half[432 : 432 + C, 96:112].T[0:3]


def on_device_flat(features, device_block, conv_first, conv_second, head_weight, targets):
    space_count = lax.axis_size("space")
    device_count = lax.axis_size("dp") * space_count
    bf16, f32 = jnp.bfloat16, jnp.float32
    small = pltpu.CompilerParams(vmem_limit_bytes=8 * 1024 * 1024)
    shape = jax.ShapeDtypeStruct
    vmem = pl.BlockSpec(memory_space=pltpu.VMEM)

    def swap(values, mask):
        return lax.ppermute(values, "space", [(s, s ^ mask) for s in range(space_count)])

    mate_targets, mate_features = swap(targets, 1), swap(features, 1)
    own, own_slabs, head, head_t = pl.pallas_call(
        pack_own_kernel,
        out_shape=(
            shape((13, 16, LANES), bf16),
            shape((3, 8, 16, LANES), bf16),
            shape((16, C), bf16),
            shape((C, 16), bf16),
        ),
        in_specs=[vmem] * 4,
        out_specs=(vmem,) * 4,
        scratch_shapes=[pltpu.VMEM((4, 8, 16, LANES), bf16)],
        compiler_params=small,
        cost_estimate=pl.CostEstimate(flops=1_000_000, bytes_accessed=2_000_000, transcendentals=0),
        name="pack_own",
    )(device_block, features[0, 0], targets[0].transpose(1, 0, 2), head_weight)
    mate_slab, *pairs = pl.pallas_call(
        pack_mate_kernel,
        out_shape=(
            shape((8, 16, LANES), bf16),
            *[shape((2, 8, 16, LANES), bf16) for _ in PARTNERS],
        ),
        in_specs=[vmem] * 4,
        out_specs=(vmem,) * 4,
        scratch_shapes=[pltpu.VMEM((4, 8, 16, LANES), bf16)],
        compiler_params=small,
        name="pack_mate",
    )(device_block, mate_features[0, 0], mate_targets[0].transpose(1, 0, 2), own_slabs)
    pairs = [swap(pair, mask) for pair, mask in zip(pairs, PARTNERS)]

    w1, w2, w2t, owners, masks = pl.pallas_call(
        prepare_kernel,
        out_shape=(
            shape((3 * C, 9 * C), bf16),
            shape((3 * C, 9 * C), bf16),
            shape((9 * C, 3 * C), bf16),
            shape((1, LANES), jnp.int32),
            shape((8, LANES), f32),
        ),
        in_specs=[vmem] * 3,
        out_specs=(vmem,) * 5,
        scratch_shapes=[pltpu.SMEM((2, 16), jnp.int32)],
        compiler_params=small,
        cost_estimate=pl.CostEstimate(flops=2_000_000, bytes_accessed=4_000_000, transcendentals=0),
        name="prepare",
    )(device_block, conv_first.transpose(1, 0, 2), conv_second.transpose(1, 0, 2))

    scale = (device_count * 3 * CELLS) ** (-0.5)
    logits, keep, send = pl.pallas_call(
        functools.partial(crop_kernel, scale),
        out_shape=(shape((8, CELLS), f32), shape((HALF, LANES), f32), shape((HALF, LANES), f32)),
        in_specs=[vmem] * 12,
        out_specs=(vmem,) * 3,
        scratch_shapes=[
            pltpu.VMEM((space_count, 8, 16, LANES), bf16),
            pltpu.VMEM((2, 12, 16, LANES), bf16),
            pltpu.VMEM((6, 3, 16, LANES), bf16),
            pltpu.VMEM((9 * C, 18 * LANES), bf16),
            pltpu.VMEM((9 * C, 16 * LANES), bf16),
            pltpu.VMEM((3 * C, 18 * LANES), f32),
            pltpu.VMEM((C, 8 * LANES), f32),
            pltpu.VMEM((C, 12 * LANES), f32),
            pltpu.VMEM((C, 12 * LANES), bf16),
            pltpu.VMEM((C, 12 * LANES), bf16),
            pltpu.VMEM((3 * C, 12 * LANES), bf16),
            pltpu.VMEM((9 * C, 8 * LANES), f32),
        ],
        compiler_params=pltpu.CompilerParams(vmem_limit_bytes=20 * 1024 * 1024),
        name="forward_backward",
    )(owners, masks, own, mate_slab, *pairs, w1, w2, w2t, head, head_t)

    dp_count = lax.axis_size("dp")

    def swap_cores(values):
        return lax.ppermute(values, "dp", [(d, d ^ 1) for d in range(dp_count)])

    peers = device_count // 2
    groups = [
        [d * space_count + s for d in range(core, dp_count, 2) for s in range(space_count)]
        for core in range(2)
    ]

    def exchange(values):
        return lax.all_to_all(
            values, ("dp", "space"), 0, 0, axis_index_groups=groups, tiled=True
        )

    def step(kernel, out, *operands):
        return pl.pallas_call(
            kernel,
            out_shape=out,
            in_specs=[vmem] * len(operands),
            out_specs=vmem,
            compiler_params=small,
            name="gradient_sum",
        )(*operands)

    term = step(add_kernel, shape((HALF, LANES), bf16), keep, swap_cores(send))
    pieces = shape((peers, HALF // peers, LANES), bf16)
    total = exchange(step(sum_kernel, pieces, exchange(term.reshape(pieces.shape))))
    total = total.reshape(HALF, LANES)
    grad_first, grad_second, grad_head, logits = pl.pallas_call(
        unpack_kernel,
        out_shape=(
            shape((27, C, C), f32),
            shape((27, C, C), f32),
            shape((3, C), f32),
            shape((3, 1, CELLS), f32),
        ),
        in_specs=[vmem] * 3,
        out_specs=(vmem,) * 4,
        compiler_params=small,
        name="unpack_gradients",
    )(total, swap_cores(total), logits)
    return (
        logits.transpose(1, 0, 2)[None],
        grad_first.transpose(1, 0, 2),
        grad_second.transpose(1, 0, 2),
        grad_head,
    )


def solution(mesh):
    in_specs = (
        P("dp", "space", None, None),
        P("dp", None),
        P(),
        P(),
        P(),
        P("dp", "space", None, None),
    )
    out_specs = (P("dp", "space", None, None), P(), P(), P())
    flat = mesh.shape["space"] == 8 and mesh.shape["dp"] in (2, 4)
    return jax.shard_map(
        on_device_flat if flat else on_device_deep,
        mesh=mesh,
        in_specs=in_specs,
        out_specs=out_specs,
        check_vma=False,
    )
```

```python
import functools

import jax
import jax.numpy as jnp
from jax import lax
from jax.experimental import pallas as pl
from jax.experimental.pallas import tpu as pltpu
from jax.sharding import PartitionSpec as P

BS = 8


tap_offsets = [
    (tap_index // 9 - 1, tap_index // 3 % 3 - 1, tap_index % 3 - 1) for tap_index in range(27)
]


def elu_pair(values):
    negative = jnp.exp(jnp.minimum(values, 0.0))
    return (jnp.where(values > 0, values, negative - 1.0), jnp.where(values > 0, 1.0, negative))


def neighbor_tables(device_block):
    space_count = lax.axis_size("space")
    depth_z = space_count // 8
    self_index = lax.axis_index("space")
    blocks = device_block[0]
    coords = jnp.stack([blocks // (4 * depth_z), blocks // depth_z % 4, blocks % depth_z])
    own_coords = lax.dynamic_index_in_dim(coords, self_index, 1, keepdims=False)
    offsets = jnp.array(tap_offsets, jnp.int32)
    limits = jnp.array([4, 4, depth_z], jnp.int32)
    wanted = own_coords[None, :] + offsets
    inside = jnp.all((wanted >= 0) & (wanted < limits[None, :]), axis=1) & (jnp.arange(27) != 13)
    wanted_id = (wanted[:, 0] * 4 + wanted[:, 1]) * depth_z + wanted[:, 2]
    matches = (blocks[None, :] == wanted_id[:, None]) & inside[:, None]
    devices = jnp.arange(space_count, dtype=jnp.int32)
    owner_row = jnp.sum(jnp.where(matches, devices[None, :], 0), axis=1)
    present = jnp.any(matches, axis=1)
    relative = coords - own_coords[:, None]
    adjacent = jnp.all(jnp.abs(relative) <= 1, axis=0) & (devices != self_index)
    send_tap = jnp.where(
        adjacent, (relative[0] + 1) * 9 + (relative[1] + 1) * 3 + relative[2] + 1, 13
    )
    return (owner_row, present, send_tap)


def region_slice(block_data, offset, depth_cells):
    span_list = []
    for step_value in offset:
        if step_value == 1:
            span_list.append(slice(BS - depth_cells, BS))
        elif step_value == -1:
            span_list.append(slice(0, depth_cells))
        else:
            span_list.append(slice(0, BS))
    return block_data[:, span_list[0], span_list[1], span_list[2]]


def surround(block_data, depth_cells, tables):
    owner_row, present, send_tap = tables
    channels = block_data.shape[0]
    length = depth_cells * BS * BS
    pieces = []
    for tap_index in range(27):
        if tap_index == 13:
            pieces.append(jnp.zeros((channels, length), block_data.dtype))
        else:
            region = region_slice(block_data, tap_offsets[tap_index], depth_cells).reshape(
                channels, -1
            )
            pieces.append(jnp.pad(region, ((0, 0), (0, length - region.shape[1]))))
    outgoing = jnp.stack(pieces)
    sending = outgoing[send_tap]
    by_source = lax.all_to_all(sending, "space", split_axis=0, concat_axis=0, tiled=True)
    incoming = jnp.where(
        present[:, None, None], by_source[owner_row], jnp.zeros((), block_data.dtype)
    )
    rows_x = []
    for step_x in range(3):
        rows_y = []
        for step_y in range(3):
            rows_z = []
            for step_z in range(3):
                tap_index = step_x * 9 + step_y * 3 + step_z
                if tap_index == 13:
                    rows_z.append(block_data)
                else:
                    extent_list = [
                        BS if step_value == 1 else depth_cells
                        for step_value in (step_x, step_y, step_z)
                    ]
                    count_cells = extent_list[0] * extent_list[1] * extent_list[2]
                    rows_z.append(
                        incoming[tap_index][:, :count_cells].reshape(
                            channels, extent_list[0], extent_list[1], extent_list[2]
                        )
                    )
            rows_y.append(jnp.concatenate(rows_z, axis=3))
        rows_x.append(jnp.concatenate(rows_y, axis=2))
    return jnp.concatenate(rows_x, axis=1)


def conv_padded(padded, kernel, dilation):
    result = lax.conv_general_dilated(
        padded[None],
        kernel,
        (1, 1, 1),
        "VALID",
        rhs_dilation=(dilation, dilation, dilation),
        dimension_numbers=("NCDHW", "OIDHW", "NCDHW"),
        preferred_element_type=jnp.float32,
    )
    return result[0].reshape(kernel.shape[0], BS * BS * BS)


def kernel_grad(padded, grad_rows, dilation):
    channels = padded.shape[0]
    outputs = grad_rows.shape[0]
    grad_block = grad_rows.reshape(outputs, 1, BS, BS, BS)
    result = lax.conv_general_dilated(
        padded[None],
        grad_block,
        (dilation, dilation, dilation),
        "VALID",
        dimension_numbers=("CNDHW", "OIDHW", "NCDHW"),
        preferred_element_type=jnp.float32,
    )
    return result.reshape(channels, outputs, 27).transpose(1, 2, 0)


def on_device_deep(features, device_block, conv_first, conv_second, head_weight, targets):
    channels = features.shape[2]
    tables = neighbor_tables(device_block)
    kernel_first = conv_first.reshape(channels, 3, 3, 3, channels).transpose(0, 4, 1, 2, 3)
    kernel_second = conv_second.reshape(channels, 3, 3, 3, channels).transpose(0, 4, 1, 2, 3)
    block_in = features[0, 0].reshape(channels, BS, BS, BS)
    padded_in = surround(block_in, 1, tables)
    pre_first = conv_padded(padded_in, kernel_first, 1)
    act_first, slope_first = elu_pair(pre_first)
    hid_first = act_first.astype(jnp.bfloat16)
    padded_first = surround(hid_first.reshape(channels, BS, BS, BS), 2, tables)
    pre_second = conv_padded(padded_first, kernel_second, 2)
    act_second, slope_second = elu_pair(pre_second)
    hid_second = act_second.astype(jnp.bfloat16)
    logits = jnp.dot(head_weight, hid_second, preferred_element_type=jnp.float32)
    scale = (lax.axis_size("dp") * lax.axis_size("space") * 3 * BS * BS * BS) ** (-0.5)
    grad_logit = ((jax.nn.sigmoid(logits) - targets[0, 0].astype(jnp.float32)) * scale).astype(
        jnp.bfloat16
    )
    grad_head = lax.dot_general(
        grad_logit, hid_second, (((1,), (1,)), ((), ())), preferred_element_type=jnp.float32
    )
    back_second = lax.dot_general(
        head_weight, grad_logit, (((0,), (0,)), ((), ())), preferred_element_type=jnp.float32
    )
    grad_pre_second = (back_second * slope_second).astype(jnp.bfloat16)
    grad_second = kernel_grad(padded_first, grad_pre_second, 2)
    padded_grad = surround(grad_pre_second.reshape(channels, BS, BS, BS), 2, tables)
    kernel_back = jnp.transpose(kernel_second[:, :, ::-1, ::-1, ::-1], (1, 0, 2, 3, 4))
    back_first = conv_padded(padded_grad, kernel_back, 2)
    grad_pre_first = (back_first * slope_first).astype(jnp.bfloat16)
    grad_first = kernel_grad(padded_in, grad_pre_first, 1)
    grad_first, grad_second, grad_head = lax.psum(
        (grad_first, grad_second, grad_head), ("dp", "space")
    )
    return (logits[None, None], grad_first, grad_second, grad_head)


C = 48
CELLS = 512
HALF = 512
LANES = 128


def lanes(rows=1):
    return lax.broadcasted_iota(jnp.int32, (rows, LANES), 1)


def roll(values, shift):
    return pltpu.roll(values, shift % LANES, 1) if shift % LANES else values


def listed_blocks(block_ref, me):
    ids = block_ref[...].astype(jnp.float32)
    index = lax.broadcasted_iota(jnp.int32, ids.shape, 1)
    return [
        jnp.sum(jnp.where(index == (me ^ k), ids, 0.0)).astype(jnp.int32)
        for k in range(ids.shape[1])
    ]


def apart(source, target):
    return (target >> 2) - (source >> 2), (target & 3) - (source & 3)


PARTNERS = (4, 6, 2)


def block_tiles(features_ref, targets_ref):
    tiles = [
        [features_ref[16 * ct : 16 * (ct + 1), LANES * q : LANES * (q + 1)] for q in range(4)]
        for ct in range(3)
    ]
    targets = targets_ref[:, 0, :].astype(jnp.float32)
    targets = jnp.concatenate([targets, jnp.zeros((1, CELLS), jnp.float32)], axis=0)
    return tiles, [targets[:, LANES * q : LANES * (q + 1)] for q in range(4)]


def write_cases(tiles, rows, cases_ref):
    lane = lanes(16)
    left = lane < 64
    cell = lane & 63
    target_tile = jnp.concatenate(rows, axis=0)

    def write(case, pairs, halves, wanted):
        for ct in range(3):
            cases_ref[case, 2 * ct] = pairs[ct][0]
            cases_ref[case, 2 * ct + 1] = pairs[ct][1]
        cases_ref[case, 6] = jnp.where(left, halves[0], halves[1])
        cases_ref[case, 7] = jnp.where(left, halves[2], wanted.astype(jnp.bfloat16))

    for case, pair, single, q in ((0, (2, 3), 1, 3), (1, (0, 1), 2, 0)):
        turns = (64, 0, 64) if case == 0 else (0, 64, 0)
        halves = [roll(tiles[ct][single], turns[ct]) for ct in range(3)]
        both = [roll(rows[q], 64), rows[q], jnp.zeros((8, LANES), jnp.float32)]
        wanted = jnp.concatenate(both, axis=0)
        write(case, [(t[pair[0]], t[pair[1]]) for t in tiles], halves, wanted)
    for case, spare, turn, turns, target_turns in (
        (2, cell < 24, -24, (-48, -96, -16, -64), (16, -32)),
        (3, cell >= 40, 40, (-24, -72, 8, -40), (64, 16)),
    ):
        pairs, halves = [], []
        for ct, t in enumerate(tiles):
            pairs.append([jnp.where(spare, roll(t[q + 2], turn), t[q]) for q in range(2)])
            moved = [roll(t[2 + n // 2], turns[n] + (64 if ct == 1 else 0)) for n in range(4)]
            half = jnp.where(cell < 16, moved[0], jnp.where(cell < 32, moved[1], moved[2]))
            halves.append(jnp.where(cell < 48, half, moved[3]))
        wanted = [roll(target_tile, n) for n in target_turns]
        write(case, pairs, halves, jnp.where(lane < 80, wanted[0], wanted[1]))


def case_of(source, target):
    dx, dy = apart(source, target)
    return jnp.where(dx > 0, 0, jnp.where(dx < 0, 1, jnp.where(dy > 0, 2, 3)))


def head_kernel(head_ref, h_ref, ht_ref):
    head = head_ref[...].astype(jnp.float32)
    head = jnp.concatenate([head, jnp.zeros((13, C), jnp.float32)], axis=0)
    h_ref[...] = head.astype(jnp.bfloat16)
    ht_ref[...] = head.T.astype(jnp.bfloat16)


def pack_own_kernel(block_ref, features_ref, targets_ref, own_ref, slabs_ref, cases_ref):
    blocks = listed_blocks(block_ref, lax.axis_index("space"))
    tiles, rows = block_tiles(features_ref, targets_ref)
    for ct in range(3):
        for q in range(4):
            own_ref[4 * ct + q] = tiles[ct][q]
    own_ref[12] = jnp.concatenate(rows, axis=0).astype(jnp.bfloat16)
    write_cases(tiles, rows, cases_ref)
    for n, k in enumerate(PARTNERS):
        slabs_ref[n] = cases_ref[case_of(blocks[0], blocks[k])]


def pack_mate_kernel(block_ref, features_ref, targets_ref, slabs_ref, mate_ref, *refs):
    *pair_refs, cases_ref = refs
    blocks = listed_blocks(block_ref, lax.axis_index("space"))
    write_cases(*block_tiles(features_ref, targets_ref), cases_ref)
    mate_ref[...] = cases_ref[case_of(blocks[1], blocks[0])]
    for n, (k, ref) in enumerate(zip(PARTNERS, pair_refs)):
        ref[0] = slabs_ref[n]
        ref[1] = cases_ref[case_of(blocks[1], blocks[k])]


def stacked_taps(ref):
    rows = []
    for a in range(3):
        taps = [ref[9 * a + t] for t in range(9)]
        rows.append(jnp.concatenate(taps, axis=1))
    return jnp.concatenate(rows, axis=0)


def second_kernel(second_ref, w2_ref, w2t_ref):
    whole = stacked_taps(second_ref)
    w2_ref[...] = whole
    w2t_ref[...] = whole.T


def prepare_kernel(block_ref, first_ref, w1_ref, owners_ref, masks_ref, table_ref):
    w1_ref[...] = stacked_taps(first_ref)

    blocks = listed_blocks(block_ref, lax.axis_index("space"))
    for slot in range(10):
        table_ref[0, slot] = 1
        table_ref[1, slot] = 0
    table_ref[1, 4] = 1
    for k in range(1, len(blocks)):
        dx, dy = apart(blocks[0], blocks[k])
        near = (dx >= -1) & (dx <= 1) & (dy >= -1) & (dy <= 1)
        slot = jnp.where(near, dx * 3 + dy + 4, 9)
        table_ref[0, slot] = k
        table_ref[1, slot] = 1
    lane = lanes()
    there = [table_ref[1, q].astype(jnp.float32) for q in range(9)]
    owners = jnp.zeros((1, LANES), jnp.int32)
    for q in range(9):
        owners = jnp.where(lane == q, table_ref[0, q], owners)
    owners_ref[...] = owners
    for bx in range(3):
        before, middle, after = there[3 * bx : 3 * bx + 3]
        masks_ref[bx : bx + 1, :] = jnp.where(
            lane < 32, before, jnp.where(lane < 96, middle, after)
        )
        masks_ref[bx + 3 : bx + 4, :] = jnp.where(lane < 64, after, before)


def matmul(left, right):
    return lax.dot_general(
        left, right, (((1,), (0,)), ((), ())), preferred_element_type=jnp.float32
    )


def matmul_lanes(left, right):
    return lax.dot_general(
        left, right, (((1,), (1,)), ((), ())), preferred_element_type=jnp.float32
    )


def crop_kernel(scale, owners_ref, masks_ref, own_ref, mate_ref, *refs):
    crop_body(scale, owners_ref, masks_ref, own_ref, mate_ref, refs[:3], *refs[3:])


def crop_body(
    scale,
    owners_ref,
    masks_ref,
    own_ref,
    mate_ref,
    pairs,
    w1_ref,
    w2_ref,
    w2t_ref,
    h_ref,
    ht_ref,
    logits_ref,
    keep_ref,
    send_ref,
    gathered_ref,
    sides_ref,
    ends_ref,
    x9_ref,
    h9_ref,
    product_ref,
    slope1_ref,
    slope2_ref,
    hid2_ref,
    grad2_ref,
    shifted_ref,
    back_ref,
):
    gathered_ref[1] = mate_ref[...]
    for k, pair in zip(PARTNERS, pairs):
        for j in range(2):
            gathered_ref[k + j] = pair[j]
    owners = owners_ref[...]
    owner = [owners[0, q] for q in range(9)]

    bf16 = jnp.bfloat16
    lane = lanes(16)
    depth = lane & 7
    depth48 = lanes(C) & 7
    low, mid, left_half = lane < 32, lane < 96, lane < 64
    masks = [masks_ref[bx : bx + 1, :] for bx in range(3)]
    main_masks = [jnp.broadcast_to(mask, (16, LANES)).astype(bf16) for mask in masks]
    edge_masks = [
        jnp.broadcast_to(masks_ref[bx + 3 : bx + 4, :], (16, LANES)).astype(bf16)
        for bx in range(3)
    ]
    own_row = jnp.where((lane >= 32) & mid, 1.0, 0.0)[0:1]

    cell = lane & 63
    for side, by, in_place, turn, turns in (
        (0, 0, cell < 48, 24, (48, 96, 16, 64)),
        (1, 2, cell < 24, -40, (24, 72, -8, 40)),
    ):
        slab = owner[3 + by]
        for ct in range(3):
            half = gathered_ref[slab, 6 + ct // 2]
            for q in range(2):
                sides_ref[side, 4 * ct + q] = gathered_ref[slab, 2 * ct + q]
                moved = [roll(half, turns[2 * q + n] - (64 if ct == 1 else 0)) for n in range(2)]
                sides_ref[side, 4 * ct + q + 2] = jnp.where(
                    in_place,
                    roll(gathered_ref[slab, 2 * ct + q], turn),
                    jnp.where(left_half, moved[0], moved[1]),
                )

    for bx in (0, 2):
        for by in range(3):
            for ct in range(3):
                tile = gathered_ref[owner[3 * bx + by], 6 + ct // 2]
                ends_ref[3 * bx // 2 + by, ct] = roll(tile, -64 * (ct % 2))

    def placed(ct, bx, i):
        if bx == 1:
            tile, half = 4 * ct + i // 2, i % 2
            parts = [sides_ref[0, tile], own_ref[tile], sides_ref[1, tile]]
        elif i == (3 if bx == 0 else 4):
            half = 0
            parts = [ends_ref[3 * bx // 2 + by, ct] for by in range(3)]
        else:
            tile, half = 2 * ct + (i // 2 - 2 if bx == 0 else i // 2), i % 2
            parts = [gathered_ref[owner[3 * bx + by], tile] for by in range(3)]
        outer = 96 - 64 * half
        return roll(parts[0], outer), roll(parts[1], 32 - 64 * half), roll(parts[2], outer)

    zero = jnp.zeros((16, LANES), bf16)

    for plane in range(18):
        bx, i = (plane + 3) // 8, (plane + 3) % 8
        for ct in range(3):
            before, middle, after = placed(ct, bx, i)
            main = jnp.where(low, before, jnp.where(mid, middle, after)) * main_masks[bx]
            edge = jnp.where(left_half, after, before) * edge_masks[bx]
            for c in (-1, 0, 1):
                if c == 0:
                    main_c, edge_c = main, edge
                else:
                    keep = depth >= 1 if c == 1 else depth <= 6
                    main_c, edge_c = jnp.where(keep, main, zero), jnp.where(keep, edge, zero)
                for b in (-1, 0, 1):
                    step = 8 * b + c
                    if b == 1:
                        source = jnp.where(lane < step, edge_c, main_c)
                    elif b == -1:
                        source = jnp.where(lane >= LANES + step, edge_c, main_c)
                    else:
                        source = main_c
                    row = (3 * (b + 1) + c + 1) * C + 16 * ct
                    x9_ref[row : row + 16, LANES * plane : LANES * (plane + 1)] = (
                        roll(source, -step) if step else source
                    )

    def plane_cols(plane):
        return slice(LANES * plane, LANES * (plane + 1))

    def summed(plane, stride):
        return (
            product_ref[0:C, plane_cols(plane)]
            + product_ref[C : 2 * C, plane_cols(plane + stride)]
            + product_ref[2 * C : 3 * C, plane_cols(plane + 2 * stride)]
        )

    for n in range(9):
        cols = slice(256 * n, 256 * (n + 1))
        product_ref[:, cols] = matmul(w1_ref[...], x9_ref[:, cols])

    for plane in range(16):
        bx = (plane + 4) // 8
        pre = summed(plane, 1)
        negative = jnp.exp(jnp.minimum(pre, 0.0))
        if 4 <= plane < 12:
            slope1_ref[:, plane_cols(plane - 4)] = jnp.where(pre > 0, 1.0, negative)
        hidden = jnp.where(pre > 0, pre, negative - 1.0) * masks[bx]
        hidden = hidden.astype(bf16)
        for c in (-1, 0, 1):
            if c == 0:
                source = hidden
            else:
                keep = depth48 >= 2 if c == 1 else depth48 <= 5
                source = jnp.where(keep, hidden, jnp.zeros((C, LANES), bf16))
            for b in (-1, 0, 1):
                step = 16 * b + 2 * c
                row = (3 * (b + 1) + c + 1) * C
                h9_ref[row : row + C, plane_cols(plane)] = roll(source, -step) if step else source

    for n in range(8):
        cols = slice(256 * n, 256 * (n + 1))
        product_ref[:, cols] = matmul(w2_ref[...], h9_ref[:, cols])

    for plane in range(12):
        bx = (plane + 6) // 8
        pre = summed(plane, 2)
        negative = jnp.exp(jnp.minimum(pre, 0.0))
        slope2_ref[:, plane_cols(plane)] = jnp.where(pre > 0, 1.0, negative) * masks[bx]
        hidden = jnp.where(pre > 0, pre, negative - 1.0) * masks[bx]
        hid2_ref[:, plane_cols(plane)] = hidden.astype(jnp.bfloat16)

    logits = matmul(h_ref[...], hid2_ref[...])
    targets = []
    for bx, half in ((0, 1), (1, 0), (1, 1), (2, 1)):
        if bx == 1:
            before = roll(gathered_ref[owner[3], 7], -48 - 16 * half)
            middle = roll(own_ref[12], 32 - 64 * half)
            after = roll(gathered_ref[owner[5], 7], 32 - 16 * half)
        else:
            parts = [gathered_ref[owner[3 * bx + by], 7] for by in range(3)]
            before, middle, after = roll(parts[0], 32), roll(parts[1], -32), roll(parts[2], 32)
        cells = jnp.where(low, before, jnp.where(mid, middle, after))
        targets.append(cells.astype(jnp.float32))
    grads = []
    for plane in range(12):
        bx, i = (plane + 6) // 8, (plane + 6) % 8
        value = logits[:, plane_cols(plane)]
        if bx == 1:
            wanted = targets[1 + i % 2][4 * (i // 2) : 4 * (i // 2) + 4]
        else:
            wanted = targets[0 if bx == 0 else 3][4 * (i % 2) : 4 * (i % 2) + 4]
        wanted = jnp.concatenate([wanted, jnp.zeros((12, LANES), jnp.float32)], axis=0)
        sigmoid = 1.0 / (1.0 + jnp.exp(-value))
        grads.append((sigmoid - wanted) * masks[bx] * scale)
    for q in range(4):
        first = roll(logits[:, plane_cols(2 + 2 * q)], -32)
        second = roll(logits[:, plane_cols(3 + 2 * q)], 32)
        logits_ref[:, plane_cols(q)] = jnp.where(left_half, first, second)[0:8]

    grad_logit = jnp.concatenate(grads, axis=1).astype(jnp.bfloat16)
    back = matmul(ht_ref[...], grad_logit)
    grad2_ref[...] = (back * slope2_ref[...]).astype(jnp.bfloat16)
    own_grads = jnp.concatenate([grads[2 + x] * own_row for x in range(8)], axis=1)
    head_part = matmul_lanes(hid2_ref[:, 2 * LANES : 10 * LANES], own_grads.astype(jnp.bfloat16))

    own_bf16 = jnp.broadcast_to(own_row, (C, LANES)).astype(bf16)
    shifted_ref[...] = jnp.zeros_like(shifted_ref)
    for a in range(3):
        for x in range(8):
            shifted_ref[C * a : C * (a + 1), plane_cols(x + 2 * a)] = (
                grad2_ref[:, plane_cols(x + 2)] * own_bf16
            )
    second_part = matmul_lanes(shifted_ref[...], h9_ref[:, 2 * LANES : 14 * LANES])

    for a in range(3):
        for x in range(8):
            shifted_ref[C * a : C * (a + 1), plane_cols(x)] = grad2_ref[:, plane_cols(x + 4 - 2 * a)]
    for n in range(4):
        cols = slice(256 * n, 256 * (n + 1))
        back_ref[:, cols] = matmul(w2t_ref[...], shifted_ref[:, cols])
    grad1 = []
    for x in range(8):
        total = jnp.zeros((C, LANES), jnp.float32)
        for c in (-1, 0, 1):
            part = jnp.zeros((C, LANES), jnp.float32)
            for b in (-1, 0, 1):
                row = (3 * (b + 1) + c + 1) * C
                step = 16 * b + 2 * c
                piece = back_ref[row : row + C, plane_cols(x)]
                part += roll(piece, step) if step else piece
            if c:
                part = jnp.where(depth48 >= 2 if c == 1 else depth48 <= 5, part, 0.0)
            total += part
        grad1.append((total * slope1_ref[:, plane_cols(x)] * own_row).astype(jnp.bfloat16))

    shifted_ref[...] = jnp.zeros_like(shifted_ref)
    for a in range(3):
        for x in range(8):
            shifted_ref[C * a : C * (a + 1), plane_cols(x + a)] = grad1[x]
    first_part = matmul_lanes(
        shifted_ref[:, 0 : 10 * LANES], x9_ref[:, 4 * LANES : 14 * LANES]
    )

    first_core = (lax.axis_index("dp") & 1) == 0
    head_part = jnp.concatenate([head_part, jnp.zeros((24, 16), jnp.float32)], axis=0)
    nothing = jnp.zeros((72, 16), jnp.float32)
    ends = []
    for part, extra in ((first_part, nothing), (second_part, head_part)):
        tail = jnp.concatenate([part[0:72, 384:], part[72:144, 384:], extra, nothing], axis=1)
        ends.append(jnp.concatenate([tail, jnp.zeros((8, LANES), jnp.float32)], axis=0))
    pieces = [(first_part[:, plane_cols(q)], second_part[:, plane_cols(q)]) for q in range(3)]
    row = 0
    for first, second in pieces + [tuple(ends)]:
        rows = slice(row, row + first.shape[0])
        keep_ref[rows, :] = jnp.where(first_core, first, second)
        send_ref[rows, :] = jnp.where(first_core, second, first)
        row += first.shape[0]


def add_kernel(mine_ref, other_ref, out_ref):
    out_ref[...] = (mine_ref[...] + other_ref[...]).astype(jnp.bfloat16)


def sum_kernel(parts_ref, out_ref):
    total = parts_ref[0].astype(jnp.float32)
    for s in range(1, parts_ref.shape[0]):
        total += parts_ref[s].astype(jnp.float32)
    total = total.astype(jnp.bfloat16)
    for s in range(out_ref.shape[0]):
        out_ref[s] = total


def unpack_kernel(mine_ref, other_ref, logits_ref, first_ref, second_ref, head_ref, out_ref):
    out_ref[:, 0, :] = logits_ref[0:3, :]
    first_core = (lax.axis_index("dp") & 1) == 0
    mine, other = mine_ref[...], other_ref[...]
    for k, out in ((0, first_ref), (1, second_ref)):
        half = jnp.where(first_core, other if k else mine, mine if k else other)
        half = half.astype(jnp.float32)
        tail = jnp.concatenate([half[432:504, 0:C], half[432:504, C : 2 * C]], axis=0)
        tiles = [half[144 * q : 144 * (q + 1), :] for q in range(3)]
        whole = jnp.concatenate(tiles + [tail], axis=1)
        for a in range(3):
            for t in range(9):
                out[9 * a + t] = whole[C * a : C * (a + 1), C * t : C * (t + 1)]
        if k:
            head_ref[...] = half[432 : 432 + C, 96:112].T[0:3]


def on_device_flat(features, device_block, conv_first, conv_second, head_weight, targets):
    space_count = lax.axis_size("space")
    device_count = lax.axis_size("dp") * space_count
    bf16, f32 = jnp.bfloat16, jnp.float32
    small = pltpu.CompilerParams(vmem_limit_bytes=8 * 1024 * 1024)
    shape = jax.ShapeDtypeStruct
    vmem = pl.BlockSpec(memory_space=pltpu.VMEM)

    def swap(values, mask):
        return lax.ppermute(values, "space", [(s, s ^ mask) for s in range(space_count)])

    mate_targets, mate_features = swap(targets, 1), swap(features, 1)
    head, head_t = pl.pallas_call(
        head_kernel,
        out_shape=(shape((16, C), bf16), shape((C, 16), bf16)),
        in_specs=[vmem],
        out_specs=(vmem,) * 2,
        compiler_params=small,
        cost_estimate=pl.CostEstimate(flops=1_000_000, bytes_accessed=2_000_000, transcendentals=0),
        name="lay_out_head",
    )(head_weight)
    own, own_slabs = pl.pallas_call(
        pack_own_kernel,
        out_shape=(shape((13, 16, LANES), bf16), shape((3, 8, 16, LANES), bf16)),
        in_specs=[vmem] * 3,
        out_specs=(vmem,) * 2,
        scratch_shapes=[pltpu.VMEM((4, 8, 16, LANES), bf16)],
        compiler_params=small,
        cost_estimate=pl.CostEstimate(flops=1_000_000, bytes_accessed=2_000_000, transcendentals=0),
        name="pack_own",
    )(device_block, features[0, 0], targets[0].transpose(1, 0, 2))
    mate_slab, *pairs = pl.pallas_call(
        pack_mate_kernel,
        out_shape=(
            shape((8, 16, LANES), bf16),
            *[shape((2, 8, 16, LANES), bf16) for _ in PARTNERS],
        ),
        in_specs=[vmem] * 4,
        out_specs=(vmem,) * 4,
        scratch_shapes=[pltpu.VMEM((4, 8, 16, LANES), bf16)],
        compiler_params=small,
        cost_estimate=pl.CostEstimate(flops=1_000_000, bytes_accessed=2_000_000, transcendentals=0),
        name="pack_mate",
    )(device_block, mate_features[0, 0], mate_targets[0].transpose(1, 0, 2), own_slabs)
    pairs = [swap(pair, mask) for pair, mask in zip(pairs, PARTNERS)]

    w1, owners, masks = pl.pallas_call(
        prepare_kernel,
        out_shape=(
            shape((3 * C, 9 * C), bf16),
            shape((1, LANES), jnp.int32),
            shape((8, LANES), f32),
        ),
        in_specs=[vmem] * 2,
        out_specs=(vmem,) * 3,
        scratch_shapes=[pltpu.SMEM((2, 16), jnp.int32)],
        compiler_params=small,
        cost_estimate=pl.CostEstimate(flops=2_000_000, bytes_accessed=4_000_000, transcendentals=0),
        name="prepare",
    )(device_block, conv_first.transpose(1, 0, 2))
    w2, w2t = pl.pallas_call(
        second_kernel,
        out_shape=(shape((3 * C, 9 * C), bf16), shape((9 * C, 3 * C), bf16)),
        in_specs=[vmem],
        out_specs=(vmem,) * 2,
        compiler_params=small,
        cost_estimate=pl.CostEstimate(flops=2_000_000, bytes_accessed=4_000_000, transcendentals=0),
        name="second_weights",
    )(conv_second.transpose(1, 0, 2))

    scale = (device_count * 3 * CELLS) ** (-0.5)
    logits, keep, send = pl.pallas_call(
        functools.partial(crop_kernel, scale),
        out_shape=(shape((8, CELLS), f32), shape((HALF, LANES), f32), shape((HALF, LANES), f32)),
        in_specs=[vmem] * 12,
        out_specs=(vmem,) * 3,
        scratch_shapes=[
            pltpu.VMEM((space_count, 8, 16, LANES), bf16),
            pltpu.VMEM((2, 12, 16, LANES), bf16),
            pltpu.VMEM((6, 3, 16, LANES), bf16),
            pltpu.VMEM((9 * C, 18 * LANES), bf16),
            pltpu.VMEM((9 * C, 16 * LANES), bf16),
            pltpu.VMEM((3 * C, 18 * LANES), f32),
            pltpu.VMEM((C, 8 * LANES), f32),
            pltpu.VMEM((C, 12 * LANES), f32),
            pltpu.VMEM((C, 12 * LANES), bf16),
            pltpu.VMEM((C, 12 * LANES), bf16),
            pltpu.VMEM((3 * C, 12 * LANES), bf16),
            pltpu.VMEM((9 * C, 8 * LANES), f32),
        ],
        compiler_params=pltpu.CompilerParams(vmem_limit_bytes=20 * 1024 * 1024),
        name="forward_backward",
    )(owners, masks, own, mate_slab, *pairs, w1, w2, w2t, head, head_t)

    dp_count = lax.axis_size("dp")

    def swap_cores(values):
        return lax.ppermute(values, "dp", [(d, d ^ 1) for d in range(dp_count)])

    peers = device_count // 2
    groups = [
        [d * space_count + s for d in range(core, dp_count, 2) for s in range(space_count)]
        for core in range(2)
    ]

    def exchange(values):
        return lax.all_to_all(
            values, ("dp", "space"), 0, 0, axis_index_groups=groups, tiled=True
        )

    def step(kernel, out, *operands):
        return pl.pallas_call(
            kernel,
            out_shape=out,
            in_specs=[vmem] * len(operands),
            out_specs=vmem,
            compiler_params=small,
            name="gradient_sum",
        )(*operands)

    term = step(add_kernel, shape((HALF, LANES), bf16), keep, swap_cores(send))
    pieces = shape((peers, HALF // peers, LANES), bf16)
    total = exchange(step(sum_kernel, pieces, exchange(term.reshape(pieces.shape))))
    total = total.reshape(HALF, LANES)
    grad_first, grad_second, grad_head, logits = pl.pallas_call(
        unpack_kernel,
        out_shape=(
            shape((27, C, C), f32),
            shape((27, C, C), f32),
            shape((3, C), f32),
            shape((3, 1, CELLS), f32),
        ),
        in_specs=[vmem] * 3,
        out_specs=(vmem,) * 4,
        compiler_params=small,
        name="unpack_gradients",
    )(total, swap_cores(total), logits)
    return (
        logits.transpose(1, 0, 2)[None],
        grad_first.transpose(1, 0, 2),
        grad_second.transpose(1, 0, 2),
        grad_head,
    )


def solution(mesh):
    in_specs = (
        P("dp", "space", None, None),
        P("dp", None),
        P(),
        P(),
        P(),
        P("dp", "space", None, None),
    )
    out_specs = (P("dp", "space", None, None), P(), P(), P())
    flat = mesh.shape["space"] == 8 and mesh.shape["dp"] in (2, 4)
    return jax.shard_map(
        on_device_flat if flat else on_device_deep,
        mesh=mesh,
        in_specs=in_specs,
        out_specs=out_specs,
        check_vma=False,
    )
```

```python
import functools

import jax
import jax.numpy as jnp
from jax import lax
from jax.experimental import pallas as pl
from jax.experimental.pallas import tpu as pltpu
from jax.sharding import PartitionSpec as P

BS = 8


tap_offsets = [
    (tap_index // 9 - 1, tap_index // 3 % 3 - 1, tap_index % 3 - 1) for tap_index in range(27)
]


def elu_pair(values):
    negative = jnp.exp(jnp.minimum(values, 0.0))
    return (jnp.where(values > 0, values, negative - 1.0), jnp.where(values > 0, 1.0, negative))


def neighbor_tables(device_block):
    space_count = lax.axis_size("space")
    depth_z = space_count // 8
    self_index = lax.axis_index("space")
    blocks = device_block[0]
    coords = jnp.stack([blocks // (4 * depth_z), blocks // depth_z % 4, blocks % depth_z])
    own_coords = lax.dynamic_index_in_dim(coords, self_index, 1, keepdims=False)
    offsets = jnp.array(tap_offsets, jnp.int32)
    limits = jnp.array([4, 4, depth_z], jnp.int32)
    wanted = own_coords[None, :] + offsets
    inside = jnp.all((wanted >= 0) & (wanted < limits[None, :]), axis=1) & (jnp.arange(27) != 13)
    wanted_id = (wanted[:, 0] * 4 + wanted[:, 1]) * depth_z + wanted[:, 2]
    matches = (blocks[None, :] == wanted_id[:, None]) & inside[:, None]
    devices = jnp.arange(space_count, dtype=jnp.int32)
    owner_row = jnp.sum(jnp.where(matches, devices[None, :], 0), axis=1)
    present = jnp.any(matches, axis=1)
    relative = coords - own_coords[:, None]
    adjacent = jnp.all(jnp.abs(relative) <= 1, axis=0) & (devices != self_index)
    send_tap = jnp.where(
        adjacent, (relative[0] + 1) * 9 + (relative[1] + 1) * 3 + relative[2] + 1, 13
    )
    return (owner_row, present, send_tap)


def region_slice(block_data, offset, depth_cells):
    span_list = []
    for step_value in offset:
        if step_value == 1:
            span_list.append(slice(BS - depth_cells, BS))
        elif step_value == -1:
            span_list.append(slice(0, depth_cells))
        else:
            span_list.append(slice(0, BS))
    return block_data[:, span_list[0], span_list[1], span_list[2]]


def surround(block_data, depth_cells, tables):
    owner_row, present, send_tap = tables
    channels = block_data.shape[0]
    length = depth_cells * BS * BS
    pieces = []
    for tap_index in range(27):
        if tap_index == 13:
            pieces.append(jnp.zeros((channels, length), block_data.dtype))
        else:
            region = region_slice(block_data, tap_offsets[tap_index], depth_cells).reshape(
                channels, -1
            )
            pieces.append(jnp.pad(region, ((0, 0), (0, length - region.shape[1]))))
    outgoing = jnp.stack(pieces)
    sending = outgoing[send_tap]
    by_source = lax.all_to_all(sending, "space", split_axis=0, concat_axis=0, tiled=True)
    incoming = jnp.where(
        present[:, None, None], by_source[owner_row], jnp.zeros((), block_data.dtype)
    )
    rows_x = []
    for step_x in range(3):
        rows_y = []
        for step_y in range(3):
            rows_z = []
            for step_z in range(3):
                tap_index = step_x * 9 + step_y * 3 + step_z
                if tap_index == 13:
                    rows_z.append(block_data)
                else:
                    extent_list = [
                        BS if step_value == 1 else depth_cells
                        for step_value in (step_x, step_y, step_z)
                    ]
                    count_cells = extent_list[0] * extent_list[1] * extent_list[2]
                    rows_z.append(
                        incoming[tap_index][:, :count_cells].reshape(
                            channels, extent_list[0], extent_list[1], extent_list[2]
                        )
                    )
            rows_y.append(jnp.concatenate(rows_z, axis=3))
        rows_x.append(jnp.concatenate(rows_y, axis=2))
    return jnp.concatenate(rows_x, axis=1)


def conv_padded(padded, kernel, dilation):
    result = lax.conv_general_dilated(
        padded[None],
        kernel,
        (1, 1, 1),
        "VALID",
        rhs_dilation=(dilation, dilation, dilation),
        dimension_numbers=("NCDHW", "OIDHW", "NCDHW"),
        preferred_element_type=jnp.float32,
    )
    return result[0].reshape(kernel.shape[0], BS * BS * BS)


def kernel_grad(padded, grad_rows, dilation):
    channels = padded.shape[0]
    outputs = grad_rows.shape[0]
    grad_block = grad_rows.reshape(outputs, 1, BS, BS, BS)
    result = lax.conv_general_dilated(
        padded[None],
        grad_block,
        (dilation, dilation, dilation),
        "VALID",
        dimension_numbers=("CNDHW", "OIDHW", "NCDHW"),
        preferred_element_type=jnp.float32,
    )
    return result.reshape(channels, outputs, 27).transpose(1, 2, 0)


def on_device_deep(features, device_block, conv_first, conv_second, head_weight, targets):
    channels = features.shape[2]
    tables = neighbor_tables(device_block)
    kernel_first = conv_first.reshape(channels, 3, 3, 3, channels).transpose(0, 4, 1, 2, 3)
    kernel_second = conv_second.reshape(channels, 3, 3, 3, channels).transpose(0, 4, 1, 2, 3)
    block_in = features[0, 0].reshape(channels, BS, BS, BS)
    padded_in = surround(block_in, 1, tables)
    pre_first = conv_padded(padded_in, kernel_first, 1)
    act_first, slope_first = elu_pair(pre_first)
    hid_first = act_first.astype(jnp.bfloat16)
    padded_first = surround(hid_first.reshape(channels, BS, BS, BS), 2, tables)
    pre_second = conv_padded(padded_first, kernel_second, 2)
    act_second, slope_second = elu_pair(pre_second)
    hid_second = act_second.astype(jnp.bfloat16)
    logits = jnp.dot(head_weight, hid_second, preferred_element_type=jnp.float32)
    scale = (lax.axis_size("dp") * lax.axis_size("space") * 3 * BS * BS * BS) ** (-0.5)
    grad_logit = ((jax.nn.sigmoid(logits) - targets[0, 0].astype(jnp.float32)) * scale).astype(
        jnp.bfloat16
    )
    grad_head = lax.dot_general(
        grad_logit, hid_second, (((1,), (1,)), ((), ())), preferred_element_type=jnp.float32
    )
    back_second = lax.dot_general(
        head_weight, grad_logit, (((0,), (0,)), ((), ())), preferred_element_type=jnp.float32
    )
    grad_pre_second = (back_second * slope_second).astype(jnp.bfloat16)
    grad_second = kernel_grad(padded_first, grad_pre_second, 2)
    padded_grad = surround(grad_pre_second.reshape(channels, BS, BS, BS), 2, tables)
    kernel_back = jnp.transpose(kernel_second[:, :, ::-1, ::-1, ::-1], (1, 0, 2, 3, 4))
    back_first = conv_padded(padded_grad, kernel_back, 2)
    grad_pre_first = (back_first * slope_first).astype(jnp.bfloat16)
    grad_first = kernel_grad(padded_in, grad_pre_first, 1)
    grad_first, grad_second, grad_head = lax.psum(
        (grad_first, grad_second, grad_head), ("dp", "space")
    )
    return (logits[None, None], grad_first, grad_second, grad_head)


C = 48
CELLS = 512
HALF = 512
LANES = 128


def lanes(rows=1):
    return lax.broadcasted_iota(jnp.int32, (rows, LANES), 1)


def roll(values, shift):
    return pltpu.roll(values, shift % LANES, 1) if shift % LANES else values


def listed_blocks(block_ref, me):
    ids = block_ref[...].astype(jnp.float32)
    index = lax.broadcasted_iota(jnp.int32, ids.shape, 1)
    return [
        jnp.sum(jnp.where(index == (me ^ k), ids, 0.0)).astype(jnp.int32)
        for k in range(ids.shape[1])
    ]


def apart(source, target):
    return (target >> 2) - (source >> 2), (target & 3) - (source & 3)


PARTNERS = (4, 6, 2)


def block_tiles(features_ref, targets_ref):
    tiles = [
        [features_ref[16 * ct : 16 * (ct + 1), LANES * q : LANES * (q + 1)] for q in range(4)]
        for ct in range(3)
    ]
    targets = targets_ref[:, 0, :].astype(jnp.float32)
    targets = jnp.concatenate([targets, jnp.zeros((1, CELLS), jnp.float32)], axis=0)
    return tiles, [targets[:, LANES * q : LANES * (q + 1)] for q in range(4)]


def write_cases(tiles, rows, cases_ref, lane):
    left = lane < 64
    cell = lane & 63
    target_tile = jnp.concatenate(rows, axis=0)

    def write(case, pairs, halves, wanted):
        for ct in range(3):
            cases_ref[case, 2 * ct] = pairs[ct][0]
            cases_ref[case, 2 * ct + 1] = pairs[ct][1]
        cases_ref[case, 6] = jnp.where(left, halves[0], halves[1])
        cases_ref[case, 7] = jnp.where(left, halves[2], wanted.astype(jnp.bfloat16))

    for case, pair, single, q in ((0, (2, 3), 1, 3), (1, (0, 1), 2, 0)):
        turns = (64, 0, 64) if case == 0 else (0, 64, 0)
        halves = [roll(tiles[ct][single], turns[ct]) for ct in range(3)]
        both = [roll(rows[q], 64), rows[q], jnp.zeros((8, LANES), jnp.float32)]
        wanted = jnp.concatenate(both, axis=0)
        write(case, [(t[pair[0]], t[pair[1]]) for t in tiles], halves, wanted)
    for case, spare, turn, turns, target_turns in (
        (2, cell < 24, -24, (-48, -96, -16, -64), (16, -32)),
        (3, cell >= 40, 40, (-24, -72, 8, -40), (64, 16)),
    ):
        pairs, halves = [], []
        for ct, t in enumerate(tiles):
            pairs.append([jnp.where(spare, roll(t[q + 2], turn), t[q]) for q in range(2)])
            moved = [roll(t[2 + n // 2], turns[n] + (64 if ct == 1 else 0)) for n in range(4)]
            half = jnp.where(cell < 16, moved[0], jnp.where(cell < 32, moved[1], moved[2]))
            halves.append(jnp.where(cell < 48, half, moved[3]))
        wanted = [roll(target_tile, n) for n in target_turns]
        write(case, pairs, halves, jnp.where(lane < 80, wanted[0], wanted[1]))


def case_of(source, target):
    dx, dy = apart(source, target)
    return jnp.where(dx > 0, 0, jnp.where(dx < 0, 1, jnp.where(dy > 0, 2, 3)))


def head_kernel(head_ref, h_ref, ht_ref):
    head = head_ref[...].astype(jnp.float32)
    head = jnp.concatenate([head, jnp.zeros((13, C), jnp.float32)], axis=0)
    h_ref[...] = head.astype(jnp.bfloat16)
    ht_ref[...] = head.T.astype(jnp.bfloat16)


def lanes_kernel(out_ref):
    out_ref[...] = lanes(16)


def pack_own_kernel(
    block_ref, features_ref, targets_ref, lane_ref, own_ref, slabs_ref, cases_ref
):
    blocks = listed_blocks(block_ref, lax.axis_index("space"))
    tiles, rows = block_tiles(features_ref, targets_ref)
    for ct in range(3):
        for q in range(4):
            own_ref[4 * ct + q] = tiles[ct][q]
    own_ref[12] = jnp.concatenate(rows, axis=0).astype(jnp.bfloat16)
    write_cases(tiles, rows, cases_ref, lane_ref[...])
    for n, k in enumerate(PARTNERS):
        slabs_ref[n] = cases_ref[case_of(blocks[0], blocks[k])]


def pack_mate_kernel(block_ref, features_ref, targets_ref, slabs_ref, mate_ref, *refs):
    *pair_refs, cases_ref = refs
    blocks = listed_blocks(block_ref, lax.axis_index("space"))
    write_cases(*block_tiles(features_ref, targets_ref), cases_ref, lanes(16))
    mate_ref[...] = cases_ref[case_of(blocks[1], blocks[0])]
    for n, (k, ref) in enumerate(zip(PARTNERS, pair_refs)):
        ref[0] = slabs_ref[n]
        ref[1] = cases_ref[case_of(blocks[1], blocks[k])]


def stacked_taps(ref):
    rows = []
    for a in range(3):
        taps = [ref[9 * a + t] for t in range(9)]
        rows.append(jnp.concatenate(taps, axis=1))
    return jnp.concatenate(rows, axis=0)


def second_kernel(second_ref, w2_ref, w2t_ref):
    whole = stacked_taps(second_ref)
    w2_ref[...] = whole
    w2t_ref[...] = whole.T


def prepare_kernel(block_ref, first_ref, w1_ref, owners_ref, masks_ref, table_ref):
    w1_ref[...] = stacked_taps(first_ref)

    blocks = listed_blocks(block_ref, lax.axis_index("space"))
    for slot in range(10):
        table_ref[0, slot] = 1
        table_ref[1, slot] = 0
    table_ref[1, 4] = 1
    for k in range(1, len(blocks)):
        dx, dy = apart(blocks[0], blocks[k])
        near = (dx >= -1) & (dx <= 1) & (dy >= -1) & (dy <= 1)
        slot = jnp.where(near, dx * 3 + dy + 4, 9)
        table_ref[0, slot] = k
        table_ref[1, slot] = 1
    lane = lanes()
    there = [table_ref[1, q].astype(jnp.float32) for q in range(9)]
    owners = jnp.zeros((1, LANES), jnp.int32)
    for q in range(9):
        owners = jnp.where(lane == q, table_ref[0, q], owners)
    owners_ref[...] = owners
    for bx in range(3):
        before, middle, after = there[3 * bx : 3 * bx + 3]
        masks_ref[bx : bx + 1, :] = jnp.where(
            lane < 32, before, jnp.where(lane < 96, middle, after)
        )
        masks_ref[bx + 3 : bx + 4, :] = jnp.where(lane < 64, after, before)


def matmul(left, right):
    return lax.dot_general(
        left, right, (((1,), (0,)), ((), ())), preferred_element_type=jnp.float32
    )


def matmul_lanes(left, right):
    return lax.dot_general(
        left, right, (((1,), (1,)), ((), ())), preferred_element_type=jnp.float32
    )


def crop_kernel(scale, owners_ref, masks_ref, own_ref, mate_ref, *refs):
    crop_body(scale, owners_ref, masks_ref, own_ref, mate_ref, refs[:3], *refs[3:])


def crop_body(
    scale,
    owners_ref,
    masks_ref,
    own_ref,
    mate_ref,
    pairs,
    w1_ref,
    w2_ref,
    w2t_ref,
    h_ref,
    ht_ref,
    logits_ref,
    keep_ref,
    send_ref,
    gathered_ref,
    sides_ref,
    ends_ref,
    x9_ref,
    h9_ref,
    product_ref,
    slope1_ref,
    slope2_ref,
    hid2_ref,
    grad2_ref,
    shifted_ref,
    back_ref,
):
    gathered_ref[1] = mate_ref[...]
    for k, pair in zip(PARTNERS, pairs):
        for j in range(2):
            gathered_ref[k + j] = pair[j]
    owners = owners_ref[...]
    owner = [owners[0, q] for q in range(9)]

    bf16 = jnp.bfloat16
    lane = lanes(16)
    depth = lane & 7
    depth48 = lanes(C) & 7
    low, mid, left_half = lane < 32, lane < 96, lane < 64
    masks = [masks_ref[bx : bx + 1, :] for bx in range(3)]
    main_masks = [jnp.broadcast_to(mask, (16, LANES)).astype(bf16) for mask in masks]
    edge_masks = [
        jnp.broadcast_to(masks_ref[bx + 3 : bx + 4, :], (16, LANES)).astype(bf16)
        for bx in range(3)
    ]
    own_row = jnp.where((lane >= 32) & mid, 1.0, 0.0)[0:1]

    cell = lane & 63
    for side, by, in_place, turn, turns in (
        (0, 0, cell < 48, 24, (48, 96, 16, 64)),
        (1, 2, cell < 24, -40, (24, 72, -8, 40)),
    ):
        slab = owner[3 + by]
        for ct in range(3):
            half = gathered_ref[slab, 6 + ct // 2]
            for q in range(2):
                sides_ref[side, 4 * ct + q] = gathered_ref[slab, 2 * ct + q]
                moved = [roll(half, turns[2 * q + n] - (64 if ct == 1 else 0)) for n in range(2)]
                sides_ref[side, 4 * ct + q + 2] = jnp.where(
                    in_place,
                    roll(gathered_ref[slab, 2 * ct + q], turn),
                    jnp.where(left_half, moved[0], moved[1]),
                )

    for bx in (0, 2):
        for by in range(3):
            for ct in range(3):
                tile = gathered_ref[owner[3 * bx + by], 6 + ct // 2]
                ends_ref[3 * bx // 2 + by, ct] = roll(tile, -64 * (ct % 2))

    def placed(ct, bx, i):
        if bx == 1:
            tile, half = 4 * ct + i // 2, i % 2
            parts = [sides_ref[0, tile], own_ref[tile], sides_ref[1, tile]]
        elif i == (3 if bx == 0 else 4):
            half = 0
            parts = [ends_ref[3 * bx // 2 + by, ct] for by in range(3)]
        else:
            tile, half = 2 * ct + (i // 2 - 2 if bx == 0 else i // 2), i % 2
            parts = [gathered_ref[owner[3 * bx + by], tile] for by in range(3)]
        outer = 96 - 64 * half
        return roll(parts[0], outer), roll(parts[1], 32 - 64 * half), roll(parts[2], outer)

    zero = jnp.zeros((16, LANES), bf16)

    for plane in range(18):
        bx, i = (plane + 3) // 8, (plane + 3) % 8
        for ct in range(3):
            before, middle, after = placed(ct, bx, i)
            main = jnp.where(low, before, jnp.where(mid, middle, after)) * main_masks[bx]
            edge = jnp.where(left_half, after, before) * edge_masks[bx]
            for c in (-1, 0, 1):
                if c == 0:
                    main_c, edge_c = main, edge
                else:
                    keep = depth >= 1 if c == 1 else depth <= 6
                    main_c, edge_c = jnp.where(keep, main, zero), jnp.where(keep, edge, zero)
                for b in (-1, 0, 1):
                    step = 8 * b + c
                    if b == 1:
                        source = jnp.where(lane < step, edge_c, main_c)
                    elif b == -1:
                        source = jnp.where(lane >= LANES + step, edge_c, main_c)
                    else:
                        source = main_c
                    row = (3 * (b + 1) + c + 1) * C + 16 * ct
                    x9_ref[row : row + 16, LANES * plane : LANES * (plane + 1)] = (
                        roll(source, -step) if step else source
                    )

    def plane_cols(plane):
        return slice(LANES * plane, LANES * (plane + 1))

    def summed(plane, stride):
        return (
            product_ref[0:C, plane_cols(plane)]
            + product_ref[C : 2 * C, plane_cols(plane + stride)]
            + product_ref[2 * C : 3 * C, plane_cols(plane + 2 * stride)]
        )

    for n in range(9):
        cols = slice(256 * n, 256 * (n + 1))
        product_ref[:, cols] = matmul(w1_ref[...], x9_ref[:, cols])

    for plane in range(16):
        bx = (plane + 4) // 8
        pre = summed(plane, 1)
        negative = jnp.exp(jnp.minimum(pre, 0.0))
        if 4 <= plane < 12:
            slope1_ref[:, plane_cols(plane - 4)] = jnp.where(pre > 0, 1.0, negative)
        hidden = jnp.where(pre > 0, pre, negative - 1.0) * masks[bx]
        hidden = hidden.astype(bf16)
        for c in (-1, 0, 1):
            if c == 0:
                source = hidden
            else:
                keep = depth48 >= 2 if c == 1 else depth48 <= 5
                source = jnp.where(keep, hidden, jnp.zeros((C, LANES), bf16))
            for b in (-1, 0, 1):
                step = 16 * b + 2 * c
                row = (3 * (b + 1) + c + 1) * C
                h9_ref[row : row + C, plane_cols(plane)] = roll(source, -step) if step else source

    for n in range(8):
        cols = slice(256 * n, 256 * (n + 1))
        product_ref[:, cols] = matmul(w2_ref[...], h9_ref[:, cols])

    for plane in range(12):
        bx = (plane + 6) // 8
        pre = summed(plane, 2)
        negative = jnp.exp(jnp.minimum(pre, 0.0))
        slope2_ref[:, plane_cols(plane)] = jnp.where(pre > 0, 1.0, negative) * masks[bx]
        hidden = jnp.where(pre > 0, pre, negative - 1.0) * masks[bx]
        hid2_ref[:, plane_cols(plane)] = hidden.astype(jnp.bfloat16)

    logits = matmul(h_ref[...], hid2_ref[...])
    targets = []
    for bx, half in ((0, 1), (1, 0), (1, 1), (2, 1)):
        if bx == 1:
            before = roll(gathered_ref[owner[3], 7], -48 - 16 * half)
            middle = roll(own_ref[12], 32 - 64 * half)
            after = roll(gathered_ref[owner[5], 7], 32 - 16 * half)
        else:
            parts = [gathered_ref[owner[3 * bx + by], 7] for by in range(3)]
            before, middle, after = roll(parts[0], 32), roll(parts[1], -32), roll(parts[2], 32)
        cells = jnp.where(low, before, jnp.where(mid, middle, after))
        targets.append(cells.astype(jnp.float32))
    grads = []
    for plane in range(12):
        bx, i = (plane + 6) // 8, (plane + 6) % 8
        value = logits[:, plane_cols(plane)]
        if bx == 1:
            wanted = targets[1 + i % 2][4 * (i // 2) : 4 * (i // 2) + 4]
        else:
            wanted = targets[0 if bx == 0 else 3][4 * (i % 2) : 4 * (i % 2) + 4]
        wanted = jnp.concatenate([wanted, jnp.zeros((12, LANES), jnp.float32)], axis=0)
        sigmoid = 1.0 / (1.0 + jnp.exp(-value))
        grads.append((sigmoid - wanted) * masks[bx] * scale)
    for q in range(4):
        first = roll(logits[:, plane_cols(2 + 2 * q)], -32)
        second = roll(logits[:, plane_cols(3 + 2 * q)], 32)
        logits_ref[:, plane_cols(q)] = jnp.where(left_half, first, second)[0:8]

    grad_logit = jnp.concatenate(grads, axis=1).astype(jnp.bfloat16)
    back = matmul(ht_ref[...], grad_logit)
    grad2_ref[...] = (back * slope2_ref[...]).astype(jnp.bfloat16)
    own_grads = jnp.concatenate([grads[2 + x] * own_row for x in range(8)], axis=1)
    head_part = matmul_lanes(hid2_ref[:, 2 * LANES : 10 * LANES], own_grads.astype(jnp.bfloat16))

    own_bf16 = jnp.broadcast_to(own_row, (C, LANES)).astype(bf16)
    shifted_ref[...] = jnp.zeros_like(shifted_ref)
    for a in range(3):
        for x in range(8):
            shifted_ref[C * a : C * (a + 1), plane_cols(x + 2 * a)] = (
                grad2_ref[:, plane_cols(x + 2)] * own_bf16
            )
    second_part = matmul_lanes(shifted_ref[...], h9_ref[:, 2 * LANES : 14 * LANES])

    for a in range(3):
        for x in range(8):
            shifted_ref[C * a : C * (a + 1), plane_cols(x)] = grad2_ref[:, plane_cols(x + 4 - 2 * a)]
    for n in range(4):
        cols = slice(256 * n, 256 * (n + 1))
        back_ref[:, cols] = matmul(w2t_ref[...], shifted_ref[:, cols])
    grad1 = []
    for x in range(8):
        total = jnp.zeros((C, LANES), jnp.float32)
        for c in (-1, 0, 1):
            part = jnp.zeros((C, LANES), jnp.float32)
            for b in (-1, 0, 1):
                row = (3 * (b + 1) + c + 1) * C
                step = 16 * b + 2 * c
                piece = back_ref[row : row + C, plane_cols(x)]
                part += roll(piece, step) if step else piece
            if c:
                part = jnp.where(depth48 >= 2 if c == 1 else depth48 <= 5, part, 0.0)
            total += part
        grad1.append((total * slope1_ref[:, plane_cols(x)] * own_row).astype(jnp.bfloat16))

    shifted_ref[...] = jnp.zeros_like(shifted_ref)
    for a in range(3):
        for x in range(8):
            shifted_ref[C * a : C * (a + 1), plane_cols(x + a)] = grad1[x]
    first_part = matmul_lanes(
        shifted_ref[:, 0 : 10 * LANES], x9_ref[:, 4 * LANES : 14 * LANES]
    )

    first_core = (lax.axis_index("dp") & 1) == 0
    head_part = jnp.concatenate([head_part, jnp.zeros((24, 16), jnp.float32)], axis=0)
    nothing = jnp.zeros((72, 16), jnp.float32)
    ends = []
    for part, extra in ((first_part, nothing), (second_part, head_part)):
        tail = jnp.concatenate([part[0:72, 384:], part[72:144, 384:], extra, nothing], axis=1)
        ends.append(jnp.concatenate([tail, jnp.zeros((8, LANES), jnp.float32)], axis=0))
    pieces = [(first_part[:, plane_cols(q)], second_part[:, plane_cols(q)]) for q in range(3)]
    row = 0
    for first, second in pieces + [tuple(ends)]:
        rows = slice(row, row + first.shape[0])
        keep_ref[rows, :] = jnp.where(first_core, first, second)
        send_ref[rows, :] = jnp.where(first_core, second, first)
        row += first.shape[0]


def add_kernel(mine_ref, other_ref, out_ref):
    out_ref[...] = (mine_ref[...] + other_ref[...]).astype(jnp.bfloat16)


def sum_kernel(parts_ref, out_ref):
    total = parts_ref[0].astype(jnp.float32)
    for s in range(1, parts_ref.shape[0]):
        total += parts_ref[s].astype(jnp.float32)
    total = total.astype(jnp.bfloat16)
    for s in range(out_ref.shape[0]):
        out_ref[s] = total


def unpack_kernel(mine_ref, other_ref, logits_ref, first_ref, second_ref, head_ref, out_ref):
    out_ref[:, 0, :] = logits_ref[0:3, :]
    first_core = (lax.axis_index("dp") & 1) == 0
    mine, other = mine_ref[...], other_ref[...]
    for k, out in ((0, first_ref), (1, second_ref)):
        half = jnp.where(first_core, other if k else mine, mine if k else other)
        half = half.astype(jnp.float32)
        tail = jnp.concatenate([half[432:504, 0:C], half[432:504, C : 2 * C]], axis=0)
        tiles = [half[144 * q : 144 * (q + 1), :] for q in range(3)]
        whole = jnp.concatenate(tiles + [tail], axis=1)
        for a in range(3):
            for t in range(9):
                out[9 * a + t] = whole[C * a : C * (a + 1), C * t : C * (t + 1)]
        if k:
            head_ref[...] = half[432 : 432 + C, 96:112].T[0:3]


def on_device_flat(features, device_block, conv_first, conv_second, head_weight, targets):
    space_count = lax.axis_size("space")
    device_count = lax.axis_size("dp") * space_count
    bf16, f32 = jnp.bfloat16, jnp.float32
    small = pltpu.CompilerParams(vmem_limit_bytes=8 * 1024 * 1024)
    shape = jax.ShapeDtypeStruct
    vmem = pl.BlockSpec(memory_space=pltpu.VMEM)

    def swap(values, mask):
        return lax.ppermute(values, "space", [(s, s ^ mask) for s in range(space_count)])

    mate_targets, mate_features = swap(targets, 1), swap(features, 1)
    head, head_t = pl.pallas_call(
        head_kernel,
        out_shape=(shape((16, C), bf16), shape((C, 16), bf16)),
        in_specs=[vmem],
        out_specs=(vmem,) * 2,
        compiler_params=small,
        cost_estimate=pl.CostEstimate(flops=1_000_000, bytes_accessed=2_000_000, transcendentals=0),
        name="lay_out_head",
    )(head_weight)
    lane = pl.pallas_call(
        lanes_kernel,
        out_shape=shape((16, LANES), jnp.int32),
        out_specs=vmem,
        compiler_params=small,
        cost_estimate=pl.CostEstimate(flops=0, bytes_accessed=2_000_000, transcendentals=0),
        name="lane_indices",
    )()
    own, own_slabs = pl.pallas_call(
        pack_own_kernel,
        out_shape=(shape((13, 16, LANES), bf16), shape((3, 8, 16, LANES), bf16)),
        in_specs=[vmem] * 4,
        out_specs=(vmem,) * 2,
        scratch_shapes=[pltpu.VMEM((4, 8, 16, LANES), bf16)],
        compiler_params=small,
        cost_estimate=pl.CostEstimate(flops=1_000_000, bytes_accessed=2_000_000, transcendentals=0),
        name="pack_own",
    )(device_block, features[0, 0], targets[0].transpose(1, 0, 2), lane)
    mate_slab, *pairs = pl.pallas_call(
        pack_mate_kernel,
        out_shape=(
            shape((8, 16, LANES), bf16),
            *[shape((2, 8, 16, LANES), bf16) for _ in PARTNERS],
        ),
        in_specs=[vmem] * 4,
        out_specs=(vmem,) * 4,
        scratch_shapes=[pltpu.VMEM((4, 8, 16, LANES), bf16)],
        compiler_params=small,
        cost_estimate=pl.CostEstimate(flops=1_000_000, bytes_accessed=2_000_000, transcendentals=0),
        name="pack_mate",
    )(device_block, mate_features[0, 0], mate_targets[0].transpose(1, 0, 2), own_slabs)
    pairs = [swap(pair, mask) for pair, mask in zip(pairs, PARTNERS)]

    w1, owners, masks = pl.pallas_call(
        prepare_kernel,
        out_shape=(
            shape((3 * C, 9 * C), bf16),
            shape((1, LANES), jnp.int32),
            shape((8, LANES), f32),
        ),
        in_specs=[vmem] * 2,
        out_specs=(vmem,) * 3,
        scratch_shapes=[pltpu.SMEM((2, 16), jnp.int32)],
        compiler_params=small,
        cost_estimate=pl.CostEstimate(flops=2_000_000, bytes_accessed=4_000_000, transcendentals=0),
        name="prepare",
    )(device_block, conv_first.transpose(1, 0, 2))
    w2, w2t = pl.pallas_call(
        second_kernel,
        out_shape=(shape((3 * C, 9 * C), bf16), shape((9 * C, 3 * C), bf16)),
        in_specs=[vmem],
        out_specs=(vmem,) * 2,
        compiler_params=small,
        cost_estimate=pl.CostEstimate(flops=2_000_000, bytes_accessed=4_000_000, transcendentals=0),
        name="second_weights",
    )(conv_second.transpose(1, 0, 2))

    scale = (device_count * 3 * CELLS) ** (-0.5)
    logits, keep, send = pl.pallas_call(
        functools.partial(crop_kernel, scale),
        out_shape=(shape((8, CELLS), f32), shape((HALF, LANES), f32), shape((HALF, LANES), f32)),
        in_specs=[vmem] * 12,
        out_specs=(vmem,) * 3,
        scratch_shapes=[
            pltpu.VMEM((space_count, 8, 16, LANES), bf16),
            pltpu.VMEM((2, 12, 16, LANES), bf16),
            pltpu.VMEM((6, 3, 16, LANES), bf16),
            pltpu.VMEM((9 * C, 18 * LANES), bf16),
            pltpu.VMEM((9 * C, 16 * LANES), bf16),
            pltpu.VMEM((3 * C, 18 * LANES), f32),
            pltpu.VMEM((C, 8 * LANES), f32),
            pltpu.VMEM((C, 12 * LANES), f32),
            pltpu.VMEM((C, 12 * LANES), bf16),
            pltpu.VMEM((C, 12 * LANES), bf16),
            pltpu.VMEM((3 * C, 12 * LANES), bf16),
            pltpu.VMEM((9 * C, 8 * LANES), f32),
        ],
        compiler_params=pltpu.CompilerParams(vmem_limit_bytes=20 * 1024 * 1024),
        name="forward_backward",
    )(owners, masks, own, mate_slab, *pairs, w1, w2, w2t, head, head_t)

    dp_count = lax.axis_size("dp")

    def swap_cores(values):
        return lax.ppermute(values, "dp", [(d, d ^ 1) for d in range(dp_count)])

    peers = device_count // 2
    groups = [
        [d * space_count + s for d in range(core, dp_count, 2) for s in range(space_count)]
        for core in range(2)
    ]

    def exchange(values):
        return lax.all_to_all(
            values, ("dp", "space"), 0, 0, axis_index_groups=groups, tiled=True
        )

    def step(kernel, out, *operands):
        return pl.pallas_call(
            kernel,
            out_shape=out,
            in_specs=[vmem] * len(operands),
            out_specs=vmem,
            compiler_params=small,
            name="gradient_sum",
        )(*operands)

    term = step(add_kernel, shape((HALF, LANES), bf16), keep, swap_cores(send))
    pieces = shape((peers, HALF // peers, LANES), bf16)
    total = exchange(step(sum_kernel, pieces, exchange(term.reshape(pieces.shape))))
    total = total.reshape(HALF, LANES)
    grad_first, grad_second, grad_head, logits = pl.pallas_call(
        unpack_kernel,
        out_shape=(
            shape((27, C, C), f32),
            shape((27, C, C), f32),
            shape((3, C), f32),
            shape((3, 1, CELLS), f32),
        ),
        in_specs=[vmem] * 3,
        out_specs=(vmem,) * 4,
        compiler_params=small,
        name="unpack_gradients",
    )(total, swap_cores(total), logits)
    return (
        logits.transpose(1, 0, 2)[None],
        grad_first.transpose(1, 0, 2),
        grad_second.transpose(1, 0, 2),
        grad_head,
    )


def solution(mesh):
    in_specs = (
        P("dp", "space", None, None),
        P("dp", None),
        P(),
        P(),
        P(),
        P("dp", "space", None, None),
    )
    out_specs = (P("dp", "space", None, None), P(), P(), P())
    flat = mesh.shape["space"] == 8 and mesh.shape["dp"] in (2, 4)
    return jax.shard_map(
        on_device_flat if flat else on_device_deep,
        mesh=mesh,
        in_specs=in_specs,
        out_specs=out_specs,
        check_vma=False,
    )
```

```python
import functools

import jax
import jax.numpy as jnp
from jax import lax
from jax.experimental import pallas as pl
from jax.experimental.pallas import tpu as pltpu
from jax.sharding import PartitionSpec as P

BS = 8


tap_offsets = [
    (tap_index // 9 - 1, tap_index // 3 % 3 - 1, tap_index % 3 - 1) for tap_index in range(27)
]


def elu_pair(values):
    negative = jnp.exp(jnp.minimum(values, 0.0))
    return (jnp.where(values > 0, values, negative - 1.0), jnp.where(values > 0, 1.0, negative))


def neighbor_tables(device_block):
    space_count = lax.axis_size("space")
    depth_z = space_count // 8
    self_index = lax.axis_index("space")
    blocks = device_block[0]
    coords = jnp.stack([blocks // (4 * depth_z), blocks // depth_z % 4, blocks % depth_z])
    own_coords = lax.dynamic_index_in_dim(coords, self_index, 1, keepdims=False)
    offsets = jnp.array(tap_offsets, jnp.int32)
    limits = jnp.array([4, 4, depth_z], jnp.int32)
    wanted = own_coords[None, :] + offsets
    inside = jnp.all((wanted >= 0) & (wanted < limits[None, :]), axis=1) & (jnp.arange(27) != 13)
    wanted_id = (wanted[:, 0] * 4 + wanted[:, 1]) * depth_z + wanted[:, 2]
    matches = (blocks[None, :] == wanted_id[:, None]) & inside[:, None]
    devices = jnp.arange(space_count, dtype=jnp.int32)
    owner_row = jnp.sum(jnp.where(matches, devices[None, :], 0), axis=1)
    present = jnp.any(matches, axis=1)
    relative = coords - own_coords[:, None]
    adjacent = jnp.all(jnp.abs(relative) <= 1, axis=0) & (devices != self_index)
    send_tap = jnp.where(
        adjacent, (relative[0] + 1) * 9 + (relative[1] + 1) * 3 + relative[2] + 1, 13
    )
    return (owner_row, present, send_tap)


def region_slice(block_data, offset, depth_cells):
    span_list = []
    for step_value in offset:
        if step_value == 1:
            span_list.append(slice(BS - depth_cells, BS))
        elif step_value == -1:
            span_list.append(slice(0, depth_cells))
        else:
            span_list.append(slice(0, BS))
    return block_data[:, span_list[0], span_list[1], span_list[2]]


def surround(block_data, depth_cells, tables):
    owner_row, present, send_tap = tables
    channels = block_data.shape[0]
    length = depth_cells * BS * BS
    pieces = []
    for tap_index in range(27):
        if tap_index == 13:
            pieces.append(jnp.zeros((channels, length), block_data.dtype))
        else:
            region = region_slice(block_data, tap_offsets[tap_index], depth_cells).reshape(
                channels, -1
            )
            pieces.append(jnp.pad(region, ((0, 0), (0, length - region.shape[1]))))
    outgoing = jnp.stack(pieces)
    sending = outgoing[send_tap]
    by_source = lax.all_to_all(sending, "space", split_axis=0, concat_axis=0, tiled=True)
    incoming = jnp.where(
        present[:, None, None], by_source[owner_row], jnp.zeros((), block_data.dtype)
    )
    rows_x = []
    for step_x in range(3):
        rows_y = []
        for step_y in range(3):
            rows_z = []
            for step_z in range(3):
                tap_index = step_x * 9 + step_y * 3 + step_z
                if tap_index == 13:
                    rows_z.append(block_data)
                else:
                    extent_list = [
                        BS if step_value == 1 else depth_cells
                        for step_value in (step_x, step_y, step_z)
                    ]
                    count_cells = extent_list[0] * extent_list[1] * extent_list[2]
                    rows_z.append(
                        incoming[tap_index][:, :count_cells].reshape(
                            channels, extent_list[0], extent_list[1], extent_list[2]
                        )
                    )
            rows_y.append(jnp.concatenate(rows_z, axis=3))
        rows_x.append(jnp.concatenate(rows_y, axis=2))
    return jnp.concatenate(rows_x, axis=1)


def conv_padded(padded, kernel, dilation):
    result = lax.conv_general_dilated(
        padded[None],
        kernel,
        (1, 1, 1),
        "VALID",
        rhs_dilation=(dilation, dilation, dilation),
        dimension_numbers=("NCDHW", "OIDHW", "NCDHW"),
        preferred_element_type=jnp.float32,
    )
    return result[0].reshape(kernel.shape[0], BS * BS * BS)


def kernel_grad(padded, grad_rows, dilation):
    channels = padded.shape[0]
    outputs = grad_rows.shape[0]
    grad_block = grad_rows.reshape(outputs, 1, BS, BS, BS)
    result = lax.conv_general_dilated(
        padded[None],
        grad_block,
        (dilation, dilation, dilation),
        "VALID",
        dimension_numbers=("CNDHW", "OIDHW", "NCDHW"),
        preferred_element_type=jnp.float32,
    )
    return result.reshape(channels, outputs, 27).transpose(1, 2, 0)


def on_device_deep(features, device_block, conv_first, conv_second, head_weight, targets):
    channels = features.shape[2]
    tables = neighbor_tables(device_block)
    kernel_first = conv_first.reshape(channels, 3, 3, 3, channels).transpose(0, 4, 1, 2, 3)
    kernel_second = conv_second.reshape(channels, 3, 3, 3, channels).transpose(0, 4, 1, 2, 3)
    block_in = features[0, 0].reshape(channels, BS, BS, BS)
    padded_in = surround(block_in, 1, tables)
    pre_first = conv_padded(padded_in, kernel_first, 1)
    act_first, slope_first = elu_pair(pre_first)
    hid_first = act_first.astype(jnp.bfloat16)
    padded_first = surround(hid_first.reshape(channels, BS, BS, BS), 2, tables)
    pre_second = conv_padded(padded_first, kernel_second, 2)
    act_second, slope_second = elu_pair(pre_second)
    hid_second = act_second.astype(jnp.bfloat16)
    logits = jnp.dot(head_weight, hid_second, preferred_element_type=jnp.float32)
    scale = (lax.axis_size("dp") * lax.axis_size("space") * 3 * BS * BS * BS) ** (-0.5)
    grad_logit = ((jax.nn.sigmoid(logits) - targets[0, 0].astype(jnp.float32)) * scale).astype(
        jnp.bfloat16
    )
    grad_head = lax.dot_general(
        grad_logit, hid_second, (((1,), (1,)), ((), ())), preferred_element_type=jnp.float32
    )
    back_second = lax.dot_general(
        head_weight, grad_logit, (((0,), (0,)), ((), ())), preferred_element_type=jnp.float32
    )
    grad_pre_second = (back_second * slope_second).astype(jnp.bfloat16)
    grad_second = kernel_grad(padded_first, grad_pre_second, 2)
    padded_grad = surround(grad_pre_second.reshape(channels, BS, BS, BS), 2, tables)
    kernel_back = jnp.transpose(kernel_second[:, :, ::-1, ::-1, ::-1], (1, 0, 2, 3, 4))
    back_first = conv_padded(padded_grad, kernel_back, 2)
    grad_pre_first = (back_first * slope_first).astype(jnp.bfloat16)
    grad_first = kernel_grad(padded_in, grad_pre_first, 1)
    grad_first, grad_second, grad_head = lax.psum(
        (grad_first, grad_second, grad_head), ("dp", "space")
    )
    return (logits[None, None], grad_first, grad_second, grad_head)


C = 48
CELLS = 512
HALF = 512
LANES = 128


def lanes(rows=1):
    return lax.broadcasted_iota(jnp.int32, (rows, LANES), 1)


def roll(values, shift):
    return pltpu.roll(values, shift % LANES, 1) if shift % LANES else values


def listed_blocks(block_ref, me):
    ids = block_ref[...].astype(jnp.float32)
    index = lax.broadcasted_iota(jnp.int32, ids.shape, 1)
    return [
        jnp.sum(jnp.where(index == (me ^ k), ids, 0.0)).astype(jnp.int32)
        for k in range(ids.shape[1])
    ]


def apart(source, target):
    return (target >> 2) - (source >> 2), (target & 3) - (source & 3)


PARTNERS = (4, 6, 2)


def block_tiles(features_ref, targets_ref):
    tiles = [
        [features_ref[16 * ct : 16 * (ct + 1), LANES * q : LANES * (q + 1)] for q in range(4)]
        for ct in range(3)
    ]
    targets = targets_ref[:, 0, :].astype(jnp.float32)
    targets = jnp.concatenate([targets, jnp.zeros((1, CELLS), jnp.float32)], axis=0)
    return tiles, [targets[:, LANES * q : LANES * (q + 1)] for q in range(4)]


def write_cases(tiles, rows, cases_ref, lane):
    left = lane < 64
    cell = lane & 63
    target_tile = jnp.concatenate(rows, axis=0)

    def write(case, pairs, halves, wanted):
        for ct in range(3):
            cases_ref[case, 2 * ct] = pairs[ct][0]
            cases_ref[case, 2 * ct + 1] = pairs[ct][1]
        cases_ref[case, 6] = jnp.where(left, halves[0], halves[1])
        cases_ref[case, 7] = jnp.where(left, halves[2], wanted.astype(jnp.bfloat16))

    for case, pair, single, q in ((0, (2, 3), 1, 3), (1, (0, 1), 2, 0)):
        turns = (64, 0, 64) if case == 0 else (0, 64, 0)
        halves = [roll(tiles[ct][single], turns[ct]) for ct in range(3)]
        both = [roll(rows[q], 64), rows[q], jnp.zeros((8, LANES), jnp.float32)]
        wanted = jnp.concatenate(both, axis=0)
        write(case, [(t[pair[0]], t[pair[1]]) for t in tiles], halves, wanted)
    for case, spare, turn, turns, target_turns in (
        (2, cell < 24, -24, (-48, -96, -16, -64), (16, -32)),
        (3, cell >= 40, 40, (-24, -72, 8, -40), (64, 16)),
    ):
        pairs, halves = [], []
        for ct, t in enumerate(tiles):
            pairs.append([jnp.where(spare, roll(t[q + 2], turn), t[q]) for q in range(2)])
            moved = [roll(t[2 + n // 2], turns[n] + (64 if ct == 1 else 0)) for n in range(4)]
            half = jnp.where(cell < 16, moved[0], jnp.where(cell < 32, moved[1], moved[2]))
            halves.append(jnp.where(cell < 48, half, moved[3]))
        wanted = [roll(target_tile, n) for n in target_turns]
        write(case, pairs, halves, jnp.where(lane < 80, wanted[0], wanted[1]))


def case_of(source, target):
    dx, dy = apart(source, target)
    return jnp.where(dx > 0, 0, jnp.where(dx < 0, 1, jnp.where(dy > 0, 2, 3)))


def head_kernel(head_ref, h_ref, ht_ref):
    head = head_ref[...].astype(jnp.float32)
    head = jnp.concatenate([head, jnp.zeros((13, C), jnp.float32)], axis=0)
    h_ref[...] = head.astype(jnp.bfloat16)
    ht_ref[...] = head.T.astype(jnp.bfloat16)


def lanes_kernel(out_ref):
    out_ref[...] = lanes(16)


def pack_own_kernel(
    block_ref, features_ref, targets_ref, lane_ref, own_ref, slabs_ref, cases_ref
):
    blocks = listed_blocks(block_ref, lax.axis_index("space"))
    tiles, rows = block_tiles(features_ref, targets_ref)
    for ct in range(3):
        for q in range(4):
            own_ref[4 * ct + q] = tiles[ct][q]
    own_ref[12] = jnp.concatenate(rows, axis=0).astype(jnp.bfloat16)
    write_cases(tiles, rows, cases_ref, lane_ref[...])
    for n, k in enumerate(PARTNERS):
        slabs_ref[n] = cases_ref[case_of(blocks[0], blocks[k])]


def pack_mate_kernel(block_ref, features_ref, targets_ref, slabs_ref, mate_ref, *refs):
    *pair_refs, cases_ref = refs
    blocks = listed_blocks(block_ref, lax.axis_index("space"))
    write_cases(*block_tiles(features_ref, targets_ref), cases_ref, lanes(16))
    mate_ref[...] = cases_ref[case_of(blocks[1], blocks[0])]
    for n, (k, ref) in enumerate(zip(PARTNERS, pair_refs)):
        ref[0] = slabs_ref[n]
        ref[1] = cases_ref[case_of(blocks[1], blocks[k])]


def stacked_taps(ref):
    rows = []
    for a in range(3):
        taps = [ref[9 * a + t] for t in range(9)]
        rows.append(jnp.concatenate(taps, axis=1))
    return jnp.concatenate(rows, axis=0)


def second_kernel(second_ref, w2_ref, w2t_ref):
    whole = stacked_taps(second_ref)
    w2_ref[...] = whole
    w2t_ref[...] = whole.T


def prepare_kernel(block_ref, first_ref, w1_ref, owners_ref, masks_ref, table_ref):
    w1_ref[...] = stacked_taps(first_ref)

    blocks = listed_blocks(block_ref, lax.axis_index("space"))
    for slot in range(10):
        table_ref[0, slot] = 1
        table_ref[1, slot] = 0
    table_ref[1, 4] = 1
    for k in range(1, len(blocks)):
        dx, dy = apart(blocks[0], blocks[k])
        near = (dx >= -1) & (dx <= 1) & (dy >= -1) & (dy <= 1)
        slot = jnp.where(near, dx * 3 + dy + 4, 9)
        table_ref[0, slot] = k
        table_ref[1, slot] = 1
    lane = lanes()
    there = [table_ref[1, q].astype(jnp.float32) for q in range(9)]
    owners = jnp.zeros((1, LANES), jnp.int32)
    for q in range(9):
        owners = jnp.where(lane == q, table_ref[0, q], owners)
    owners_ref[...] = owners
    for bx in range(3):
        before, middle, after = there[3 * bx : 3 * bx + 3]
        masks_ref[bx : bx + 1, :] = jnp.where(
            lane < 32, before, jnp.where(lane < 96, middle, after)
        )
        masks_ref[bx + 3 : bx + 4, :] = jnp.where(lane < 64, after, before)


def matmul(left, right):
    return lax.dot_general(
        left, right, (((1,), (0,)), ((), ())), preferred_element_type=jnp.float32
    )


def matmul_lanes(left, right):
    return lax.dot_general(
        left, right, (((1,), (1,)), ((), ())), preferred_element_type=jnp.float32
    )


def crop_kernel(scale, owners_ref, masks_ref, own_ref, mate_ref, *refs):
    crop_body(scale, owners_ref, masks_ref, own_ref, mate_ref, refs[:3], *refs[3:])


def crop_body(
    scale,
    owners_ref,
    masks_ref,
    own_ref,
    mate_ref,
    pairs,
    w1_ref,
    w2_ref,
    w2t_ref,
    h_ref,
    ht_ref,
    logits_ref,
    keep_ref,
    send_ref,
    gathered_ref,
    sides_ref,
    ends_ref,
    x9_ref,
    h9_ref,
    product_ref,
    slope1_ref,
    slope2_ref,
    hid2_ref,
    grad2_ref,
    shifted_ref,
    back_ref,
):
    gathered_ref[1] = mate_ref[...]
    for k, pair in zip(PARTNERS, pairs):
        for j in range(2):
            gathered_ref[k + j] = pair[j]
    owners = owners_ref[...]
    owner = [owners[0, q] for q in range(9)]

    bf16 = jnp.bfloat16
    lane = lanes(16)
    depth = lane & 7
    depth48 = lanes(C) & 7
    low, mid, left_half = lane < 32, lane < 96, lane < 64
    masks = [masks_ref[bx : bx + 1, :] for bx in range(3)]
    main_masks = [jnp.broadcast_to(mask, (16, LANES)).astype(bf16) for mask in masks]
    edge_masks = [
        jnp.broadcast_to(masks_ref[bx + 3 : bx + 4, :], (16, LANES)).astype(bf16)
        for bx in range(3)
    ]
    own_row = jnp.where((lane >= 32) & mid, 1.0, 0.0)[0:1]

    cell = lane & 63
    for side, by, in_place, turn, turns in (
        (0, 0, cell < 48, 24, (48, 96, 16, 64)),
        (1, 2, cell < 24, -40, (24, 72, -8, 40)),
    ):
        slab = owner[3 + by]
        for ct in range(3):
            half = gathered_ref[slab, 6 + ct // 2]
            for q in range(2):
                sides_ref[side, 4 * ct + q] = gathered_ref[slab, 2 * ct + q]
                moved = [roll(half, turns[2 * q + n] - (64 if ct == 1 else 0)) for n in range(2)]
                sides_ref[side, 4 * ct + q + 2] = jnp.where(
                    in_place,
                    roll(gathered_ref[slab, 2 * ct + q], turn),
                    jnp.where(left_half, moved[0], moved[1]),
                )

    for bx in (0, 2):
        for by in range(3):
            for ct in range(3):
                tile = gathered_ref[owner[3 * bx + by], 6 + ct // 2]
                ends_ref[3 * bx // 2 + by, ct] = roll(tile, -64 * (ct % 2))

    def placed(ct, bx, i):
        if bx == 1:
            tile, half = 4 * ct + i // 2, i % 2
            parts = [sides_ref[0, tile], own_ref[tile], sides_ref[1, tile]]
        elif i == (3 if bx == 0 else 4):
            half = 0
            parts = [ends_ref[3 * bx // 2 + by, ct] for by in range(3)]
        else:
            tile, half = 2 * ct + (i // 2 - 2 if bx == 0 else i // 2), i % 2
            parts = [gathered_ref[owner[3 * bx + by], tile] for by in range(3)]
        outer = 96 - 64 * half
        return roll(parts[0], outer), roll(parts[1], 32 - 64 * half), roll(parts[2], outer)

    zero = jnp.zeros((16, LANES), bf16)

    for plane in range(18):
        bx, i = (plane + 3) // 8, (plane + 3) % 8
        for ct in range(3):
            before, middle, after = placed(ct, bx, i)
            main = jnp.where(low, before, jnp.where(mid, middle, after)) * main_masks[bx]
            edge = jnp.where(left_half, after, before) * edge_masks[bx]
            for c in (-1, 0, 1):
                if c == 0:
                    main_c, edge_c = main, edge
                else:
                    keep = depth >= 1 if c == 1 else depth <= 6
                    main_c, edge_c = jnp.where(keep, main, zero), jnp.where(keep, edge, zero)
                for b in (-1, 0, 1):
                    step = 8 * b + c
                    if b == 1:
                        source = jnp.where(lane < step, edge_c, main_c)
                    elif b == -1:
                        source = jnp.where(lane >= LANES + step, edge_c, main_c)
                    else:
                        source = main_c
                    row = (3 * (b + 1) + c + 1) * C + 16 * ct
                    x9_ref[row : row + 16, LANES * plane : LANES * (plane + 1)] = (
                        roll(source, -step) if step else source
                    )

    def plane_cols(plane):
        return slice(LANES * plane, LANES * (plane + 1))

    def summed(plane, stride):
        return (
            product_ref[0:C, plane_cols(plane)]
            + product_ref[C : 2 * C, plane_cols(plane + stride)]
            + product_ref[2 * C : 3 * C, plane_cols(plane + 2 * stride)]
        )

    for n in range(9):
        cols = slice(256 * n, 256 * (n + 1))
        product_ref[:, cols] = matmul(w1_ref[...], x9_ref[:, cols])

    for plane in range(16):
        bx = (plane + 4) // 8
        pre = summed(plane, 1)
        negative = jnp.exp(jnp.minimum(pre, 0.0))
        if 4 <= plane < 12:
            slope1_ref[:, plane_cols(plane - 4)] = jnp.where(pre > 0, 1.0, negative)
        hidden = jnp.where(pre > 0, pre, negative - 1.0) * masks[bx]
        hidden = hidden.astype(bf16)
        for c in (-1, 0, 1):
            if c == 0:
                source = hidden
            else:
                keep = depth48 >= 2 if c == 1 else depth48 <= 5
                source = jnp.where(keep, hidden, jnp.zeros((C, LANES), bf16))
            for b in (-1, 0, 1):
                step = 16 * b + 2 * c
                row = (3 * (b + 1) + c + 1) * C
                h9_ref[row : row + C, plane_cols(plane)] = roll(source, -step) if step else source

    for n in range(8):
        cols = slice(256 * n, 256 * (n + 1))
        product_ref[:, cols] = matmul(w2_ref[...], h9_ref[:, cols])

    for plane in range(12):
        bx = (plane + 6) // 8
        pre = summed(plane, 2)
        negative = jnp.exp(jnp.minimum(pre, 0.0))
        slope2_ref[:, plane_cols(plane)] = jnp.where(pre > 0, 1.0, negative) * masks[bx]
        hidden = jnp.where(pre > 0, pre, negative - 1.0) * masks[bx]
        hid2_ref[:, plane_cols(plane)] = hidden.astype(jnp.bfloat16)

    logits = matmul(h_ref[...], hid2_ref[...])
    targets = []
    for bx, half in ((0, 1), (1, 0), (1, 1), (2, 1)):
        if bx == 1:
            before = roll(gathered_ref[owner[3], 7], -48 - 16 * half)
            middle = roll(own_ref[12], 32 - 64 * half)
            after = roll(gathered_ref[owner[5], 7], 32 - 16 * half)
        else:
            parts = [gathered_ref[owner[3 * bx + by], 7] for by in range(3)]
            before, middle, after = roll(parts[0], 32), roll(parts[1], -32), roll(parts[2], 32)
        cells = jnp.where(low, before, jnp.where(mid, middle, after))
        targets.append(cells.astype(jnp.float32))
    grads = []
    for plane in range(12):
        bx, i = (plane + 6) // 8, (plane + 6) % 8
        value = logits[:, plane_cols(plane)]
        if bx == 1:
            wanted = targets[1 + i % 2][4 * (i // 2) : 4 * (i // 2) + 4]
        else:
            wanted = targets[0 if bx == 0 else 3][4 * (i % 2) : 4 * (i % 2) + 4]
        wanted = jnp.concatenate([wanted, jnp.zeros((12, LANES), jnp.float32)], axis=0)
        sigmoid = 1.0 / (1.0 + jnp.exp(-value))
        grads.append((sigmoid - wanted) * masks[bx] * scale)
    for q in range(4):
        first = roll(logits[:, plane_cols(2 + 2 * q)], -32)
        second = roll(logits[:, plane_cols(3 + 2 * q)], 32)
        logits_ref[:, plane_cols(q)] = jnp.where(left_half, first, second)[0:8]

    grad_logit = jnp.concatenate(grads, axis=1).astype(jnp.bfloat16)
    back = matmul(ht_ref[...], grad_logit)
    grad2_ref[...] = (back * slope2_ref[...]).astype(jnp.bfloat16)
    own_grads = jnp.concatenate([grads[2 + x] * own_row for x in range(8)], axis=1)
    head_part = matmul_lanes(hid2_ref[:, 2 * LANES : 10 * LANES], own_grads.astype(jnp.bfloat16))

    own_bf16 = jnp.broadcast_to(own_row, (C, LANES)).astype(bf16)
    shifted_ref[...] = jnp.zeros_like(shifted_ref)
    for a in range(3):
        for x in range(8):
            shifted_ref[C * a : C * (a + 1), plane_cols(x + 2 * a)] = (
                grad2_ref[:, plane_cols(x + 2)] * own_bf16
            )
    second_part = matmul_lanes(shifted_ref[...], h9_ref[:, 2 * LANES : 14 * LANES])

    for a in range(3):
        for x in range(8):
            shifted_ref[C * a : C * (a + 1), plane_cols(x)] = grad2_ref[:, plane_cols(x + 4 - 2 * a)]
    for n in range(4):
        cols = slice(256 * n, 256 * (n + 1))
        back_ref[:, cols] = matmul(w2t_ref[...], shifted_ref[:, cols])
    grad1 = []
    for x in range(8):
        total = jnp.zeros((C, LANES), jnp.float32)
        for c in (-1, 0, 1):
            part = jnp.zeros((C, LANES), jnp.float32)
            for b in (-1, 0, 1):
                row = (3 * (b + 1) + c + 1) * C
                step = 16 * b + 2 * c
                piece = back_ref[row : row + C, plane_cols(x)]
                part += roll(piece, step) if step else piece
            if c:
                part = jnp.where(depth48 >= 2 if c == 1 else depth48 <= 5, part, 0.0)
            total += part
        grad1.append((total * slope1_ref[:, plane_cols(x)] * own_row).astype(jnp.bfloat16))

    shifted_ref[...] = jnp.zeros_like(shifted_ref)
    for a in range(3):
        for x in range(8):
            shifted_ref[C * a : C * (a + 1), plane_cols(x + a)] = grad1[x]
    first_part = matmul_lanes(
        shifted_ref[:, 0 : 10 * LANES], x9_ref[:, 4 * LANES : 14 * LANES]
    )

    first_core = (lax.axis_index("dp") & 1) == 0

    def halves(part):
        blocks = [part[24 * n : 24 * (n + 1)] for n in range(6)]
        return [jnp.concatenate(blocks[side::2], axis=0) for side in range(2)]

    pieces = [
        halves(part[:, plane_cols(q)]) for part in (first_part, second_part) for q in range(3)
    ]
    ends = []
    for side, first, second in zip(
        range(2), halves(first_part[:, 384:]), halves(second_part[:, 384:])
    ):
        head = jnp.concatenate(
            [head_part[24 * side : 24 * (side + 1)], jnp.zeros((48, 16), jnp.float32)], axis=0
        )
        nothing = jnp.zeros((72, 16), jnp.float32)
        tail = jnp.concatenate([first, second, head, nothing], axis=1)
        ends.append(jnp.concatenate([tail, jnp.zeros((8, LANES), jnp.float32)], axis=0))
    row = 0
    for low_half, high_half in pieces + [ends]:
        rows = slice(row, row + low_half.shape[0])
        keep_ref[rows, :] = jnp.where(first_core, low_half, high_half)
        send_ref[rows, :] = jnp.where(first_core, high_half, low_half)
        row += low_half.shape[0]


def add_kernel(mine_ref, other_ref, out_ref):
    out_ref[...] = (mine_ref[...] + other_ref[...]).astype(jnp.bfloat16)


def sum_kernel(parts_ref, out_ref):
    total = parts_ref[0].astype(jnp.float32)
    for s in range(1, parts_ref.shape[0]):
        total += parts_ref[s].astype(jnp.float32)
    total = total.astype(jnp.bfloat16)
    for s in range(out_ref.shape[0]):
        out_ref[s] = total


def unpack_half(side, rows_ref, outs, whole_ref, sems):
    rows = rows_ref[...].astype(jnp.float32)
    copies = []
    for m, out in enumerate(outs):
        tiles = [rows[72 * (3 * m + q) : 72 * (3 * m + q + 1)] for q in range(3)]
        whole = jnp.concatenate(tiles + [rows[432:504, C * m : C * (m + 1)]], axis=1)
        for a in range(3):
            for t in range(9):
                whole_ref[m, 9 * a + t] = whole[24 * a : 24 * (a + 1), C * t : C * (t + 1)]
        channels = pl.ds(pl.multiple_of(24 * side, 8), 24)
        copy = pltpu.make_async_copy(whole_ref.at[m], out.at[:, channels, :], sems.at[m])
        copy.start()
        copies.append(copy)
    for copy in copies:
        copy.wait()


def unpack_own_kernel(mine_ref, logits_ref, first_ref, second_ref, out_ref, whole_ref, sems):
    out_ref[:, 0, :] = logits_ref[0:3, :]
    core = lax.axis_index("dp") & 1
    unpack_half(core, mine_ref, (first_ref, second_ref), whole_ref, sems)


def unpack_other_kernel(
    mine_ref, other_ref, _first, _second, first_ref, second_ref, head_ref, whole_ref, sems
):
    core = lax.axis_index("dp") & 1
    mine, other = (ref[432:504, :].astype(jnp.float32)[0:24, 96:112] for ref in (mine_ref, other_ref))
    low_half = jnp.where(core == 0, mine, other)
    high_half = jnp.where(core == 0, other, mine)
    head_ref[...] = jnp.concatenate([low_half, high_half], axis=0).T[0:3]
    unpack_half(1 - core, other_ref, (first_ref, second_ref), whole_ref, sems)


def on_device_flat(features, device_block, conv_first, conv_second, head_weight, targets):
    space_count = lax.axis_size("space")
    device_count = lax.axis_size("dp") * space_count
    bf16, f32 = jnp.bfloat16, jnp.float32
    small = pltpu.CompilerParams(vmem_limit_bytes=8 * 1024 * 1024)
    shape = jax.ShapeDtypeStruct
    vmem = pl.BlockSpec(memory_space=pltpu.VMEM)

    def swap(values, mask):
        return lax.ppermute(values, "space", [(s, s ^ mask) for s in range(space_count)])

    mate_targets, mate_features = swap(targets, 1), swap(features, 1)
    head, head_t = pl.pallas_call(
        head_kernel,
        out_shape=(shape((16, C), bf16), shape((C, 16), bf16)),
        in_specs=[vmem],
        out_specs=(vmem,) * 2,
        compiler_params=small,
        cost_estimate=pl.CostEstimate(flops=1_000_000, bytes_accessed=2_000_000, transcendentals=0),
        name="lay_out_head",
    )(head_weight)
    lane = pl.pallas_call(
        lanes_kernel,
        out_shape=shape((16, LANES), jnp.int32),
        out_specs=vmem,
        compiler_params=small,
        cost_estimate=pl.CostEstimate(flops=0, bytes_accessed=2_000_000, transcendentals=0),
        name="lane_indices",
    )()
    own, own_slabs = pl.pallas_call(
        pack_own_kernel,
        out_shape=(shape((13, 16, LANES), bf16), shape((3, 8, 16, LANES), bf16)),
        in_specs=[vmem] * 4,
        out_specs=(vmem,) * 2,
        scratch_shapes=[pltpu.VMEM((4, 8, 16, LANES), bf16)],
        compiler_params=small,
        cost_estimate=pl.CostEstimate(flops=1_000_000, bytes_accessed=2_000_000, transcendentals=0),
        name="pack_own",
    )(device_block, features[0, 0], targets[0].transpose(1, 0, 2), lane)
    mate_slab, *pairs = pl.pallas_call(
        pack_mate_kernel,
        out_shape=(
            shape((8, 16, LANES), bf16),
            *[shape((2, 8, 16, LANES), bf16) for _ in PARTNERS],
        ),
        in_specs=[vmem] * 4,
        out_specs=(vmem,) * 4,
        scratch_shapes=[pltpu.VMEM((4, 8, 16, LANES), bf16)],
        compiler_params=small,
        cost_estimate=pl.CostEstimate(flops=1_000_000, bytes_accessed=2_000_000, transcendentals=0),
        name="pack_mate",
    )(device_block, mate_features[0, 0], mate_targets[0].transpose(1, 0, 2), own_slabs)
    pairs = [swap(pair, mask) for pair, mask in zip(pairs, PARTNERS)]

    w1, owners, masks = pl.pallas_call(
        prepare_kernel,
        out_shape=(
            shape((3 * C, 9 * C), bf16),
            shape((1, LANES), jnp.int32),
            shape((8, LANES), f32),
        ),
        in_specs=[vmem] * 2,
        out_specs=(vmem,) * 3,
        scratch_shapes=[pltpu.SMEM((2, 16), jnp.int32)],
        compiler_params=small,
        cost_estimate=pl.CostEstimate(flops=2_000_000, bytes_accessed=4_000_000, transcendentals=0),
        name="prepare",
    )(device_block, conv_first.transpose(1, 0, 2))
    w2, w2t = pl.pallas_call(
        second_kernel,
        out_shape=(shape((3 * C, 9 * C), bf16), shape((9 * C, 3 * C), bf16)),
        in_specs=[vmem],
        out_specs=(vmem,) * 2,
        compiler_params=small,
        cost_estimate=pl.CostEstimate(flops=2_000_000, bytes_accessed=4_000_000, transcendentals=0),
        name="second_weights",
    )(conv_second.transpose(1, 0, 2))

    scale = (device_count * 3 * CELLS) ** (-0.5)
    logits, keep, send = pl.pallas_call(
        functools.partial(crop_kernel, scale),
        out_shape=(shape((8, CELLS), f32), shape((HALF, LANES), f32), shape((HALF, LANES), f32)),
        in_specs=[vmem] * 12,
        out_specs=(vmem,) * 3,
        scratch_shapes=[
            pltpu.VMEM((space_count, 8, 16, LANES), bf16),
            pltpu.VMEM((2, 12, 16, LANES), bf16),
            pltpu.VMEM((6, 3, 16, LANES), bf16),
            pltpu.VMEM((9 * C, 18 * LANES), bf16),
            pltpu.VMEM((9 * C, 16 * LANES), bf16),
            pltpu.VMEM((3 * C, 18 * LANES), f32),
            pltpu.VMEM((C, 8 * LANES), f32),
            pltpu.VMEM((C, 12 * LANES), f32),
            pltpu.VMEM((C, 12 * LANES), bf16),
            pltpu.VMEM((C, 12 * LANES), bf16),
            pltpu.VMEM((3 * C, 12 * LANES), bf16),
            pltpu.VMEM((9 * C, 8 * LANES), f32),
        ],
        compiler_params=pltpu.CompilerParams(vmem_limit_bytes=20 * 1024 * 1024),
        name="forward_backward",
    )(owners, masks, own, mate_slab, *pairs, w1, w2, w2t, head, head_t)

    dp_count = lax.axis_size("dp")

    def swap_cores(values):
        return lax.ppermute(values, "dp", [(d, d ^ 1) for d in range(dp_count)])

    peers = device_count // 2
    groups = [
        [d * space_count + s for d in range(core, dp_count, 2) for s in range(space_count)]
        for core in range(2)
    ]

    def exchange(values):
        return lax.all_to_all(
            values, ("dp", "space"), 0, 0, axis_index_groups=groups, tiled=True
        )

    def step(kernel, out, *operands):
        return pl.pallas_call(
            kernel,
            out_shape=out,
            in_specs=[vmem] * len(operands),
            out_specs=vmem,
            compiler_params=small,
            name="gradient_sum",
        )(*operands)

    term = step(add_kernel, shape((HALF, LANES), bf16), keep, swap_cores(send))
    pieces = shape((peers, HALF // peers, LANES), bf16)
    total = exchange(step(sum_kernel, pieces, exchange(term.reshape(pieces.shape))))
    total = total.reshape(HALF, LANES)
    other = swap_cores(total)
    gradient = shape((27, C, C), f32)
    anywhere = pl.BlockSpec(memory_space=pl.ANY)
    scratch = [pltpu.VMEM((2, 27, 24, C), f32), pltpu.SemaphoreType.DMA((2,))]
    grad_first, grad_second, logits = pl.pallas_call(
        unpack_own_kernel,
        out_shape=(gradient, gradient, shape((3, 1, CELLS), f32)),
        in_specs=[vmem] * 2,
        out_specs=(anywhere, anywhere, vmem),
        scratch_shapes=scratch,
        compiler_params=small,
        cost_estimate=pl.CostEstimate(flops=1_000_000, bytes_accessed=2_000_000, transcendentals=0),
        name="unpack_own",
    )(total, logits)
    grad_first, grad_second, grad_head = pl.pallas_call(
        unpack_other_kernel,
        out_shape=(gradient, gradient, shape((3, C), f32)),
        in_specs=[vmem, vmem, anywhere, anywhere],
        out_specs=(anywhere, anywhere, vmem),
        input_output_aliases={2: 0, 3: 1},
        scratch_shapes=scratch,
        compiler_params=small,
        name="unpack_other",
    )(total, other, grad_first, grad_second)
    return (
        logits.transpose(1, 0, 2)[None],
        grad_first.transpose(1, 0, 2),
        grad_second.transpose(1, 0, 2),
        grad_head,
    )


def solution(mesh):
    in_specs = (
        P("dp", "space", None, None),
        P("dp", None),
        P(),
        P(),
        P(),
        P("dp", "space", None, None),
    )
    out_specs = (P("dp", "space", None, None), P(), P(), P())
    flat = mesh.shape["space"] == 8 and mesh.shape["dp"] in (2, 4)
    return jax.shard_map(
        on_device_flat if flat else on_device_deep,
        mesh=mesh,
        in_specs=in_specs,
        out_specs=out_specs,
        check_vma=False,
    )
```

```python
import functools

import jax
import jax.numpy as jnp
from jax import lax
from jax.experimental import pallas as pl
from jax.experimental.pallas import tpu as pltpu
from jax.sharding import PartitionSpec as P

BS = 8


tap_offsets = [
    (tap_index // 9 - 1, tap_index // 3 % 3 - 1, tap_index % 3 - 1) for tap_index in range(27)
]


def elu_pair(values):
    negative = jnp.exp(jnp.minimum(values, 0.0))
    return (jnp.where(values > 0, values, negative - 1.0), jnp.where(values > 0, 1.0, negative))


def neighbor_tables(device_block):
    space_count = lax.axis_size("space")
    depth_z = space_count // 8
    self_index = lax.axis_index("space")
    blocks = device_block[0]
    coords = jnp.stack([blocks // (4 * depth_z), blocks // depth_z % 4, blocks % depth_z])
    own_coords = lax.dynamic_index_in_dim(coords, self_index, 1, keepdims=False)
    offsets = jnp.array(tap_offsets, jnp.int32)
    limits = jnp.array([4, 4, depth_z], jnp.int32)
    wanted = own_coords[None, :] + offsets
    inside = jnp.all((wanted >= 0) & (wanted < limits[None, :]), axis=1) & (jnp.arange(27) != 13)
    wanted_id = (wanted[:, 0] * 4 + wanted[:, 1]) * depth_z + wanted[:, 2]
    matches = (blocks[None, :] == wanted_id[:, None]) & inside[:, None]
    devices = jnp.arange(space_count, dtype=jnp.int32)
    owner_row = jnp.sum(jnp.where(matches, devices[None, :], 0), axis=1)
    present = jnp.any(matches, axis=1)
    relative = coords - own_coords[:, None]
    adjacent = jnp.all(jnp.abs(relative) <= 1, axis=0) & (devices != self_index)
    send_tap = jnp.where(
        adjacent, (relative[0] + 1) * 9 + (relative[1] + 1) * 3 + relative[2] + 1, 13
    )
    return (owner_row, present, send_tap)


def region_slice(block_data, offset, depth_cells):
    span_list = []
    for step_value in offset:
        if step_value == 1:
            span_list.append(slice(BS - depth_cells, BS))
        elif step_value == -1:
            span_list.append(slice(0, depth_cells))
        else:
            span_list.append(slice(0, BS))
    return block_data[:, span_list[0], span_list[1], span_list[2]]


def surround(block_data, depth_cells, tables):
    owner_row, present, send_tap = tables
    channels = block_data.shape[0]
    length = depth_cells * BS * BS
    pieces = []
    for tap_index in range(27):
        if tap_index == 13:
            pieces.append(jnp.zeros((channels, length), block_data.dtype))
        else:
            region = region_slice(block_data, tap_offsets[tap_index], depth_cells).reshape(
                channels, -1
            )
            pieces.append(jnp.pad(region, ((0, 0), (0, length - region.shape[1]))))
    outgoing = jnp.stack(pieces)
    sending = outgoing[send_tap]
    by_source = lax.all_to_all(sending, "space", split_axis=0, concat_axis=0, tiled=True)
    incoming = jnp.where(
        present[:, None, None], by_source[owner_row], jnp.zeros((), block_data.dtype)
    )
    rows_x = []
    for step_x in range(3):
        rows_y = []
        for step_y in range(3):
            rows_z = []
            for step_z in range(3):
                tap_index = step_x * 9 + step_y * 3 + step_z
                if tap_index == 13:
                    rows_z.append(block_data)
                else:
                    extent_list = [
                        BS if step_value == 1 else depth_cells
                        for step_value in (step_x, step_y, step_z)
                    ]
                    count_cells = extent_list[0] * extent_list[1] * extent_list[2]
                    rows_z.append(
                        incoming[tap_index][:, :count_cells].reshape(
                            channels, extent_list[0], extent_list[1], extent_list[2]
                        )
                    )
            rows_y.append(jnp.concatenate(rows_z, axis=3))
        rows_x.append(jnp.concatenate(rows_y, axis=2))
    return jnp.concatenate(rows_x, axis=1)


def conv_padded(padded, kernel, dilation):
    result = lax.conv_general_dilated(
        padded[None],
        kernel,
        (1, 1, 1),
        "VALID",
        rhs_dilation=(dilation, dilation, dilation),
        dimension_numbers=("NCDHW", "OIDHW", "NCDHW"),
        preferred_element_type=jnp.float32,
    )
    return result[0].reshape(kernel.shape[0], BS * BS * BS)


def kernel_grad(padded, grad_rows, dilation):
    channels = padded.shape[0]
    outputs = grad_rows.shape[0]
    grad_block = grad_rows.reshape(outputs, 1, BS, BS, BS)
    result = lax.conv_general_dilated(
        padded[None],
        grad_block,
        (dilation, dilation, dilation),
        "VALID",
        dimension_numbers=("CNDHW", "OIDHW", "NCDHW"),
        preferred_element_type=jnp.float32,
    )
    return result.reshape(channels, outputs, 27).transpose(1, 2, 0)


def on_device_deep(features, device_block, conv_first, conv_second, head_weight, targets):
    channels = features.shape[2]
    tables = neighbor_tables(device_block)
    kernel_first = conv_first.reshape(channels, 3, 3, 3, channels).transpose(0, 4, 1, 2, 3)
    kernel_second = conv_second.reshape(channels, 3, 3, 3, channels).transpose(0, 4, 1, 2, 3)
    block_in = features[0, 0].reshape(channels, BS, BS, BS)
    padded_in = surround(block_in, 1, tables)
    pre_first = conv_padded(padded_in, kernel_first, 1)
    act_first, slope_first = elu_pair(pre_first)
    hid_first = act_first.astype(jnp.bfloat16)
    padded_first = surround(hid_first.reshape(channels, BS, BS, BS), 2, tables)
    pre_second = conv_padded(padded_first, kernel_second, 2)
    act_second, slope_second = elu_pair(pre_second)
    hid_second = act_second.astype(jnp.bfloat16)
    logits = jnp.dot(head_weight, hid_second, preferred_element_type=jnp.float32)
    scale = (lax.axis_size("dp") * lax.axis_size("space") * 3 * BS * BS * BS) ** (-0.5)
    grad_logit = ((jax.nn.sigmoid(logits) - targets[0, 0].astype(jnp.float32)) * scale).astype(
        jnp.bfloat16
    )
    grad_head = lax.dot_general(
        grad_logit, hid_second, (((1,), (1,)), ((), ())), preferred_element_type=jnp.float32
    )
    back_second = lax.dot_general(
        head_weight, grad_logit, (((0,), (0,)), ((), ())), preferred_element_type=jnp.float32
    )
    grad_pre_second = (back_second * slope_second).astype(jnp.bfloat16)
    grad_second = kernel_grad(padded_first, grad_pre_second, 2)
    padded_grad = surround(grad_pre_second.reshape(channels, BS, BS, BS), 2, tables)
    kernel_back = jnp.transpose(kernel_second[:, :, ::-1, ::-1, ::-1], (1, 0, 2, 3, 4))
    back_first = conv_padded(padded_grad, kernel_back, 2)
    grad_pre_first = (back_first * slope_first).astype(jnp.bfloat16)
    grad_first = kernel_grad(padded_in, grad_pre_first, 1)
    grad_first, grad_second, grad_head = lax.psum(
        (grad_first, grad_second, grad_head), ("dp", "space")
    )
    return (logits[None, None], grad_first, grad_second, grad_head)


C = 48
CELLS = 512
HALF = 512
LANES = 128


def lanes(rows=1):
    return lax.broadcasted_iota(jnp.int32, (rows, LANES), 1)


def roll(values, shift):
    return pltpu.roll(values, shift % LANES, 1) if shift % LANES else values


def listed_blocks(block_ref, me):
    ids = block_ref[...].astype(jnp.float32)
    index = lax.broadcasted_iota(jnp.int32, ids.shape, 1)
    return [
        jnp.sum(jnp.where(index == (me ^ k), ids, 0.0)).astype(jnp.int32)
        for k in range(ids.shape[1])
    ]


def apart(source, target):
    return (target >> 2) - (source >> 2), (target & 3) - (source & 3)


PARTNERS = (4, 6, 2)


def block_tiles(features_ref, targets_ref):
    tiles = [
        [features_ref[16 * ct : 16 * (ct + 1), LANES * q : LANES * (q + 1)] for q in range(4)]
        for ct in range(3)
    ]
    targets = targets_ref[:, 0, :].astype(jnp.float32)
    targets = jnp.concatenate([targets, jnp.zeros((1, CELLS), jnp.float32)], axis=0)
    return tiles, [targets[:, LANES * q : LANES * (q + 1)] for q in range(4)]


def write_cases(tiles, rows, cases_ref, lane):
    left = lane < 64
    cell = lane & 63
    target_tile = jnp.concatenate(rows, axis=0)

    def write(case, pairs, halves, wanted):
        for ct in range(3):
            cases_ref[case, 2 * ct] = pairs[ct][0]
            cases_ref[case, 2 * ct + 1] = pairs[ct][1]
        cases_ref[case, 6] = jnp.where(left, halves[0], halves[1])
        cases_ref[case, 7] = jnp.where(left, halves[2], wanted.astype(jnp.bfloat16))

    for case, pair, single, q in ((0, (2, 3), 1, 3), (1, (0, 1), 2, 0)):
        turns = (64, 0, 64) if case == 0 else (0, 64, 0)
        halves = [roll(tiles[ct][single], turns[ct]) for ct in range(3)]
        both = [roll(rows[q], 64), rows[q], jnp.zeros((8, LANES), jnp.float32)]
        wanted = jnp.concatenate(both, axis=0)
        write(case, [(t[pair[0]], t[pair[1]]) for t in tiles], halves, wanted)
    for case, spare, turn, turns, target_turns in (
        (2, cell < 24, -24, (-48, -96, -16, -64), (16, -32)),
        (3, cell >= 40, 40, (-24, -72, 8, -40), (64, 16)),
    ):
        pairs, halves = [], []
        for ct, t in enumerate(tiles):
            pairs.append([jnp.where(spare, roll(t[q + 2], turn), t[q]) for q in range(2)])
            moved = [roll(t[2 + n // 2], turns[n] + (64 if ct == 1 else 0)) for n in range(4)]
            half = jnp.where(cell < 16, moved[0], jnp.where(cell < 32, moved[1], moved[2]))
            halves.append(jnp.where(cell < 48, half, moved[3]))
        wanted = [roll(target_tile, n) for n in target_turns]
        write(case, pairs, halves, jnp.where(lane < 80, wanted[0], wanted[1]))


def case_of(source, target):
    dx, dy = apart(source, target)
    return jnp.where(dx > 0, 0, jnp.where(dx < 0, 1, jnp.where(dy > 0, 2, 3)))


def head_kernel(head_ref, h_ref, ht_ref):
    head = head_ref[...].astype(jnp.float32)
    head = jnp.concatenate([head, jnp.zeros((13, C), jnp.float32)], axis=0)
    h_ref[...] = head.astype(jnp.bfloat16)
    ht_ref[...] = head.T.astype(jnp.bfloat16)


def lanes_kernel(out_ref):
    out_ref[...] = lanes(16)


def pack_own_kernel(block_ref, features_ref, targets_ref, lane_ref, own_ref, *refs):
    *slab_refs, cases_ref = refs
    blocks = listed_blocks(block_ref, lax.axis_index("space"))
    tiles, rows = block_tiles(features_ref, targets_ref)
    for ct in range(3):
        for q in range(4):
            own_ref[4 * ct + q] = tiles[ct][q]
    own_ref[12] = jnp.concatenate(rows, axis=0).astype(jnp.bfloat16)
    write_cases(tiles, rows, cases_ref, lane_ref[...])
    for k, ref in zip(PARTNERS, slab_refs):
        ref[...] = cases_ref[case_of(blocks[0], blocks[k])]


def pack_mate_kernel(block_ref, features_ref, targets_ref, mate_ref, *refs):
    *slab_refs, cases_ref = refs
    blocks = listed_blocks(block_ref, lax.axis_index("space"))
    write_cases(*block_tiles(features_ref, targets_ref), cases_ref, lanes(16))
    mate_ref[...] = cases_ref[case_of(blocks[1], blocks[0])]
    for k, ref in zip(PARTNERS, slab_refs):
        ref[...] = cases_ref[case_of(blocks[1], blocks[k])]


def stacked_taps(ref):
    rows = []
    for a in range(3):
        taps = [ref[9 * a + t] for t in range(9)]
        rows.append(jnp.concatenate(taps, axis=1))
    return jnp.concatenate(rows, axis=0)


def second_kernel(second_ref, w2_ref, w2t_ref):
    whole = stacked_taps(second_ref)
    w2_ref[...] = whole
    w2t_ref[...] = whole.T


def prepare_kernel(block_ref, first_ref, w1_ref, owners_ref, masks_ref, table_ref):
    w1_ref[...] = stacked_taps(first_ref)

    blocks = listed_blocks(block_ref, lax.axis_index("space"))
    for slot in range(10):
        table_ref[0, slot] = 1
        table_ref[1, slot] = 0
    table_ref[1, 4] = 1
    for k in range(1, len(blocks)):
        dx, dy = apart(blocks[0], blocks[k])
        near = (dx >= -1) & (dx <= 1) & (dy >= -1) & (dy <= 1)
        slot = jnp.where(near, dx * 3 + dy + 4, 9)
        table_ref[0, slot] = k
        table_ref[1, slot] = 1
    lane = lanes()
    there = [table_ref[1, q].astype(jnp.float32) for q in range(9)]
    owners = jnp.zeros((1, LANES), jnp.int32)
    for q in range(9):
        owners = jnp.where(lane == q, table_ref[0, q], owners)
    owners_ref[...] = owners
    for bx in range(3):
        before, middle, after = there[3 * bx : 3 * bx + 3]
        masks_ref[bx : bx + 1, :] = jnp.where(
            lane < 32, before, jnp.where(lane < 96, middle, after)
        )
        masks_ref[bx + 3 : bx + 4, :] = jnp.where(lane < 64, after, before)


def matmul(left, right):
    return lax.dot_general(
        left, right, (((1,), (0,)), ((), ())), preferred_element_type=jnp.float32
    )


def matmul_lanes(left, right):
    return lax.dot_general(
        left, right, (((1,), (1,)), ((), ())), preferred_element_type=jnp.float32
    )


def crop_kernel(scale, owners_ref, masks_ref, own_ref, mate_ref, *refs):
    crop_body(scale, owners_ref, masks_ref, own_ref, mate_ref, refs[:6], *refs[6:])


def crop_body(
    scale,
    owners_ref,
    masks_ref,
    own_ref,
    mate_ref,
    slabs,
    w1_ref,
    w2_ref,
    w2t_ref,
    h_ref,
    ht_ref,
    logits_ref,
    keep_ref,
    send_ref,
    gathered_ref,
    sides_ref,
    ends_ref,
    x9_ref,
    h9_ref,
    product_ref,
    slope1_ref,
    slope2_ref,
    hid2_ref,
    grad2_ref,
    shifted_ref,
    back_ref,
):
    gathered_ref[1] = mate_ref[...]
    for n, k in enumerate(PARTNERS):
        for j in range(2):
            gathered_ref[k + j] = slabs[3 * j + n][...]
    owners = owners_ref[...]
    owner = [owners[0, q] for q in range(9)]

    bf16 = jnp.bfloat16
    lane = lanes(16)
    depth = lane & 7
    depth48 = lanes(C) & 7
    low, mid, left_half = lane < 32, lane < 96, lane < 64
    masks = [masks_ref[bx : bx + 1, :] for bx in range(3)]
    main_masks = [jnp.broadcast_to(mask, (16, LANES)).astype(bf16) for mask in masks]
    edge_masks = [
        jnp.broadcast_to(masks_ref[bx + 3 : bx + 4, :], (16, LANES)).astype(bf16)
        for bx in range(3)
    ]
    own_row = jnp.where((lane >= 32) & mid, 1.0, 0.0)[0:1]

    cell = lane & 63
    for side, by, in_place, turn, turns in (
        (0, 0, cell < 48, 24, (48, 96, 16, 64)),
        (1, 2, cell < 24, -40, (24, 72, -8, 40)),
    ):
        slab = owner[3 + by]
        for ct in range(3):
            half = gathered_ref[slab, 6 + ct // 2]
            for q in range(2):
                sides_ref[side, 4 * ct + q] = gathered_ref[slab, 2 * ct + q]
                moved = [roll(half, turns[2 * q + n] - (64 if ct == 1 else 0)) for n in range(2)]
                sides_ref[side, 4 * ct + q + 2] = jnp.where(
                    in_place,
                    roll(gathered_ref[slab, 2 * ct + q], turn),
                    jnp.where(left_half, moved[0], moved[1]),
                )

    for bx in (0, 2):
        for by in range(3):
            for ct in range(3):
                tile = gathered_ref[owner[3 * bx + by], 6 + ct // 2]
                ends_ref[3 * bx // 2 + by, ct] = roll(tile, -64 * (ct % 2))

    def placed(ct, bx, i):
        if bx == 1:
            tile, half = 4 * ct + i // 2, i % 2
            parts = [sides_ref[0, tile], own_ref[tile], sides_ref[1, tile]]
        elif i == (3 if bx == 0 else 4):
            half = 0
            parts = [ends_ref[3 * bx // 2 + by, ct] for by in range(3)]
        else:
            tile, half = 2 * ct + (i // 2 - 2 if bx == 0 else i // 2), i % 2
            parts = [gathered_ref[owner[3 * bx + by], tile] for by in range(3)]
        outer = 96 - 64 * half
        return roll(parts[0], outer), roll(parts[1], 32 - 64 * half), roll(parts[2], outer)

    zero = jnp.zeros((16, LANES), bf16)

    for plane in range(18):
        bx, i = (plane + 3) // 8, (plane + 3) % 8
        for ct in range(3):
            before, middle, after = placed(ct, bx, i)
            main = jnp.where(low, before, jnp.where(mid, middle, after)) * main_masks[bx]
            edge = jnp.where(left_half, after, before) * edge_masks[bx]
            for c in (-1, 0, 1):
                if c == 0:
                    main_c, edge_c = main, edge
                else:
                    keep = depth >= 1 if c == 1 else depth <= 6
                    main_c, edge_c = jnp.where(keep, main, zero), jnp.where(keep, edge, zero)
                for b in (-1, 0, 1):
                    step = 8 * b + c
                    if b == 1:
                        source = jnp.where(lane < step, edge_c, main_c)
                    elif b == -1:
                        source = jnp.where(lane >= LANES + step, edge_c, main_c)
                    else:
                        source = main_c
                    row = (3 * (b + 1) + c + 1) * C + 16 * ct
                    x9_ref[row : row + 16, LANES * plane : LANES * (plane + 1)] = (
                        roll(source, -step) if step else source
                    )

    def plane_cols(plane):
        return slice(LANES * plane, LANES * (plane + 1))

    def summed(plane, stride):
        return (
            product_ref[0:C, plane_cols(plane)]
            + product_ref[C : 2 * C, plane_cols(plane + stride)]
            + product_ref[2 * C : 3 * C, plane_cols(plane + 2 * stride)]
        )

    for n in range(9):
        cols = slice(256 * n, 256 * (n + 1))
        product_ref[:, cols] = matmul(w1_ref[...], x9_ref[:, cols])

    for plane in range(16):
        bx = (plane + 4) // 8
        pre = summed(plane, 1)
        negative = jnp.exp(jnp.minimum(pre, 0.0))
        if 4 <= plane < 12:
            slope1_ref[:, plane_cols(plane - 4)] = negative
        hidden = (jnp.maximum(pre, 0.0) + (negative - 1.0)) * masks[bx]
        hidden = hidden.astype(bf16)
        for c in (-1, 0, 1):
            if c == 0:
                source = hidden
            else:
                keep = depth48 >= 2 if c == 1 else depth48 <= 5
                source = jnp.where(keep, hidden, jnp.zeros((C, LANES), bf16))
            for b in (-1, 0, 1):
                step = 16 * b + 2 * c
                row = (3 * (b + 1) + c + 1) * C
                h9_ref[row : row + C, plane_cols(plane)] = roll(source, -step) if step else source

    for n in range(8):
        cols = slice(256 * n, 256 * (n + 1))
        product_ref[:, cols] = matmul(w2_ref[...], h9_ref[:, cols])

    for plane in range(12):
        bx = (plane + 6) // 8
        pre = summed(plane, 2)
        negative = jnp.exp(jnp.minimum(pre, 0.0))
        slope2_ref[:, plane_cols(plane)] = negative * masks[bx]
        hidden = (jnp.maximum(pre, 0.0) + (negative - 1.0)) * masks[bx]
        hid2_ref[:, plane_cols(plane)] = hidden.astype(jnp.bfloat16)

    logits = matmul(h_ref[...], hid2_ref[...])
    targets = []
    for bx, half in ((0, 1), (1, 0), (1, 1), (2, 1)):
        if bx == 1:
            before = roll(gathered_ref[owner[3], 7], -48 - 16 * half)
            middle = roll(own_ref[12], 32 - 64 * half)
            after = roll(gathered_ref[owner[5], 7], 32 - 16 * half)
        else:
            parts = [gathered_ref[owner[3 * bx + by], 7] for by in range(3)]
            before, middle, after = roll(parts[0], 32), roll(parts[1], -32), roll(parts[2], 32)
        cells = jnp.where(low, before, jnp.where(mid, middle, after))
        targets.append(cells.astype(jnp.float32))
    grads = []
    for plane in range(12):
        bx, i = (plane + 6) // 8, (plane + 6) % 8
        value = logits[:, plane_cols(plane)]
        if bx == 1:
            wanted = targets[1 + i % 2][4 * (i // 2) : 4 * (i // 2) + 4]
        else:
            wanted = targets[0 if bx == 0 else 3][4 * (i % 2) : 4 * (i % 2) + 4]
        wanted = jnp.concatenate([wanted, jnp.zeros((12, LANES), jnp.float32)], axis=0)
        sigmoid = 1.0 / (1.0 + jnp.exp(-value))
        grads.append((sigmoid - wanted) * masks[bx] * scale)
    for q in range(4):
        first = roll(logits[:, plane_cols(2 + 2 * q)], -32)
        second = roll(logits[:, plane_cols(3 + 2 * q)], 32)
        logits_ref[:, plane_cols(q)] = jnp.where(left_half, first, second)[0:8]

    grad_logit = jnp.concatenate(grads, axis=1).astype(jnp.bfloat16)
    back = matmul(ht_ref[...], grad_logit)
    grad2_ref[...] = (back * slope2_ref[...]).astype(jnp.bfloat16)
    own_grads = jnp.concatenate([grads[2 + x] * own_row for x in range(8)], axis=1)
    head_part = matmul_lanes(hid2_ref[:, 2 * LANES : 10 * LANES], own_grads.astype(jnp.bfloat16))

    own_bf16 = jnp.broadcast_to(own_row, (C, LANES)).astype(bf16)
    shifted_ref[...] = jnp.zeros_like(shifted_ref)
    for a in range(3):
        for x in range(8):
            shifted_ref[C * a : C * (a + 1), plane_cols(x + 2 * a)] = (
                grad2_ref[:, plane_cols(x + 2)] * own_bf16
            )
    second_part = matmul_lanes(shifted_ref[...], h9_ref[:, 2 * LANES : 14 * LANES])

    for a in range(3):
        for x in range(8):
            shifted_ref[C * a : C * (a + 1), plane_cols(x)] = grad2_ref[:, plane_cols(x + 4 - 2 * a)]
    for n in range(4):
        cols = slice(256 * n, 256 * (n + 1))
        back_ref[:, cols] = matmul(w2t_ref[...], shifted_ref[:, cols])
    grad1 = []
    for x in range(8):
        total = jnp.zeros((C, LANES), jnp.float32)
        for c in (-1, 0, 1):
            part = jnp.zeros((C, LANES), jnp.float32)
            for b in (-1, 0, 1):
                row = (3 * (b + 1) + c + 1) * C
                step = 16 * b + 2 * c
                piece = back_ref[row : row + C, plane_cols(x)]
                part += roll(piece, step) if step else piece
            if c:
                part = jnp.where(depth48 >= 2 if c == 1 else depth48 <= 5, part, 0.0)
            total += part
        grad1.append((total * slope1_ref[:, plane_cols(x)] * own_row).astype(jnp.bfloat16))

    shifted_ref[...] = jnp.zeros_like(shifted_ref)
    for a in range(3):
        for x in range(8):
            shifted_ref[C * a : C * (a + 1), plane_cols(x + a)] = grad1[x]
    first_part = matmul_lanes(
        shifted_ref[:, 0 : 10 * LANES], x9_ref[:, 4 * LANES : 14 * LANES]
    )

    first_core = (lax.axis_index("dp") & 1) == 0
    head_part = jnp.concatenate([head_part, jnp.zeros((24, 16), jnp.float32)], axis=0)
    nothing = jnp.zeros((72, 16), jnp.float32)
    ends = []
    for part, extra in ((first_part, nothing), (second_part, head_part)):
        tail = jnp.concatenate([part[0:72, 384:], part[72:144, 384:], extra, nothing], axis=1)
        ends.append(jnp.concatenate([tail, jnp.zeros((8, LANES), jnp.float32)], axis=0))
    pieces = [(first_part[:, plane_cols(q)], second_part[:, plane_cols(q)]) for q in range(3)]
    row = 0
    for first, second in pieces + [tuple(ends)]:
        rows = slice(row, row + first.shape[0])
        keep_ref[rows, :] = jnp.where(first_core, first, second)
        send_ref[rows, :] = jnp.where(first_core, second, first)
        row += first.shape[0]


def add_kernel(mine_ref, other_ref, out_ref):
    out_ref[...] = (mine_ref[...] + other_ref[...]).astype(jnp.bfloat16)


def sum_kernel(parts_ref, out_ref):
    total = parts_ref[0].astype(jnp.float32)
    for s in range(1, parts_ref.shape[0]):
        total += parts_ref[s].astype(jnp.float32)
    total = total.astype(jnp.bfloat16)
    for s in range(out_ref.shape[0]):
        out_ref[s] = total


def unpack_kernel(mine_ref, other_ref, logits_ref, first_ref, second_ref, head_ref, out_ref):
    out_ref[:, 0, :] = logits_ref[0:3, :]
    first_core = (lax.axis_index("dp") & 1) == 0
    mine, other = mine_ref[...], other_ref[...]
    for k, out in ((0, first_ref), (1, second_ref)):
        half = jnp.where(first_core, other if k else mine, mine if k else other)
        half = half.astype(jnp.float32)
        tail = jnp.concatenate([half[432:504, 0:C], half[432:504, C : 2 * C]], axis=0)
        tiles = [half[144 * q : 144 * (q + 1), :] for q in range(3)]
        whole = jnp.concatenate(tiles + [tail], axis=1)
        for a in range(3):
            for t in range(9):
                out[9 * a + t] = whole[C * a : C * (a + 1), C * t : C * (t + 1)]
        if k:
            head_ref[...] = half[432 : 432 + C, 96:112].T[0:3]


def on_device_flat(features, device_block, conv_first, conv_second, head_weight, targets):
    space_count = lax.axis_size("space")
    device_count = lax.axis_size("dp") * space_count
    bf16, f32 = jnp.bfloat16, jnp.float32
    small = pltpu.CompilerParams(vmem_limit_bytes=8 * 1024 * 1024)
    shape = jax.ShapeDtypeStruct
    vmem = pl.BlockSpec(memory_space=pltpu.VMEM)

    def swap(values, mask):
        return lax.ppermute(values, "space", [(s, s ^ mask) for s in range(space_count)])

    mate_targets, mate_features = swap(targets, 1), swap(features, 1)
    head, head_t = pl.pallas_call(
        head_kernel,
        out_shape=(shape((16, C), bf16), shape((C, 16), bf16)),
        in_specs=[vmem],
        out_specs=(vmem,) * 2,
        compiler_params=small,
        cost_estimate=pl.CostEstimate(flops=1_000_000, bytes_accessed=2_000_000, transcendentals=0),
        name="lay_out_head",
    )(head_weight)
    lane = pl.pallas_call(
        lanes_kernel,
        out_shape=shape((16, LANES), jnp.int32),
        out_specs=vmem,
        compiler_params=small,
        cost_estimate=pl.CostEstimate(flops=0, bytes_accessed=2_000_000, transcendentals=0),
        name="lane_indices",
    )()
    slab = shape((8, 16, LANES), bf16)
    own, *own_slabs = pl.pallas_call(
        pack_own_kernel,
        out_shape=(shape((13, 16, LANES), bf16), slab, slab, slab),
        in_specs=[vmem] * 4,
        out_specs=(vmem,) * 4,
        scratch_shapes=[pltpu.VMEM((4, 8, 16, LANES), bf16)],
        compiler_params=small,
        cost_estimate=pl.CostEstimate(flops=1_000_000, bytes_accessed=2_000_000, transcendentals=0),
        name="pack_own",
    )(device_block, features[0, 0], targets[0].transpose(1, 0, 2), lane)
    slabs = [swap(own_slab, mask) for own_slab, mask in zip(own_slabs, PARTNERS)]
    mate_slab, *mate_slabs = pl.pallas_call(
        pack_mate_kernel,
        out_shape=(slab,) * 4,
        in_specs=[vmem] * 3,
        out_specs=(vmem,) * 4,
        scratch_shapes=[pltpu.VMEM((4, 8, 16, LANES), bf16)],
        compiler_params=small,
        name="pack_mate",
    )(device_block, mate_features[0, 0], mate_targets[0].transpose(1, 0, 2))
    slabs += [swap(mate_part, mask) for mate_part, mask in zip(mate_slabs, PARTNERS)]

    w1, owners, masks = pl.pallas_call(
        prepare_kernel,
        out_shape=(
            shape((3 * C, 9 * C), bf16),
            shape((1, LANES), jnp.int32),
            shape((8, LANES), f32),
        ),
        in_specs=[vmem] * 2,
        out_specs=(vmem,) * 3,
        scratch_shapes=[pltpu.SMEM((2, 16), jnp.int32)],
        compiler_params=small,
        cost_estimate=pl.CostEstimate(flops=2_000_000, bytes_accessed=4_000_000, transcendentals=0),
        name="prepare",
    )(device_block, conv_first.transpose(1, 0, 2))
    w2, w2t = pl.pallas_call(
        second_kernel,
        out_shape=(shape((3 * C, 9 * C), bf16), shape((9 * C, 3 * C), bf16)),
        in_specs=[vmem],
        out_specs=(vmem,) * 2,
        compiler_params=small,
        cost_estimate=pl.CostEstimate(flops=2_000_000, bytes_accessed=4_000_000, transcendentals=0),
        name="second_weights",
    )(conv_second.transpose(1, 0, 2))

    scale = (device_count * 3 * CELLS) ** (-0.5)
    logits, keep, send = pl.pallas_call(
        functools.partial(crop_kernel, scale),
        out_shape=(shape((8, CELLS), f32), shape((HALF, LANES), f32), shape((HALF, LANES), f32)),
        in_specs=[vmem] * 15,
        out_specs=(vmem,) * 3,
        scratch_shapes=[
            pltpu.VMEM((space_count, 8, 16, LANES), bf16),
            pltpu.VMEM((2, 12, 16, LANES), bf16),
            pltpu.VMEM((6, 3, 16, LANES), bf16),
            pltpu.VMEM((9 * C, 18 * LANES), bf16),
            pltpu.VMEM((9 * C, 16 * LANES), bf16),
            pltpu.VMEM((3 * C, 18 * LANES), f32),
            pltpu.VMEM((C, 8 * LANES), f32),
            pltpu.VMEM((C, 12 * LANES), f32),
            pltpu.VMEM((C, 12 * LANES), bf16),
            pltpu.VMEM((C, 12 * LANES), bf16),
            pltpu.VMEM((3 * C, 12 * LANES), bf16),
            pltpu.VMEM((9 * C, 8 * LANES), f32),
        ],
        compiler_params=pltpu.CompilerParams(vmem_limit_bytes=20 * 1024 * 1024),
        name="forward_backward",
    )(owners, masks, own, mate_slab, *slabs, w1, w2, w2t, head, head_t)

    dp_count = lax.axis_size("dp")

    def swap_cores(values):
        return lax.ppermute(values, "dp", [(d, d ^ 1) for d in range(dp_count)])

    peers = device_count // 2
    groups = [
        [d * space_count + s for d in range(core, dp_count, 2) for s in range(space_count)]
        for core in range(2)
    ]

    def exchange(values):
        return lax.all_to_all(
            values, ("dp", "space"), 0, 0, axis_index_groups=groups, tiled=True
        )

    def step(kernel, out, *operands):
        return pl.pallas_call(
            kernel,
            out_shape=out,
            in_specs=[vmem] * len(operands),
            out_specs=vmem,
            compiler_params=small,
            name="gradient_sum",
        )(*operands)

    term = step(add_kernel, shape((HALF, LANES), bf16), keep, swap_cores(send))
    pieces = shape((peers, HALF // peers, LANES), bf16)
    total = exchange(step(sum_kernel, pieces, exchange(term.reshape(pieces.shape))))
    total = total.reshape(HALF, LANES)
    grad_first, grad_second, grad_head, logits = pl.pallas_call(
        unpack_kernel,
        out_shape=(
            shape((27, C, C), f32),
            shape((27, C, C), f32),
            shape((3, C), f32),
            shape((3, 1, CELLS), f32),
        ),
        in_specs=[vmem] * 3,
        out_specs=(vmem,) * 4,
        compiler_params=small,
        name="unpack_gradients",
    )(total, swap_cores(total), logits)
    return (
        logits.transpose(1, 0, 2)[None],
        grad_first.transpose(1, 0, 2),
        grad_second.transpose(1, 0, 2),
        grad_head,
    )


def solution(mesh):
    in_specs = (
        P("dp", "space", None, None),
        P("dp", None),
        P(),
        P(),
        P(),
        P("dp", "space", None, None),
    )
    out_specs = (P("dp", "space", None, None), P(), P(), P())
    flat = mesh.shape["space"] == 8 and mesh.shape["dp"] in (2, 4)
    return jax.shard_map(
        on_device_flat if flat else on_device_deep,
        mesh=mesh,
        in_specs=in_specs,
        out_specs=out_specs,
        check_vma=False,
    )
```

```python
import functools

import jax
import jax.numpy as jnp
from jax import lax
from jax.experimental import pallas as pl
from jax.experimental.pallas import tpu as pltpu
from jax.sharding import PartitionSpec as P

BS = 8


tap_offsets = [
    (tap_index // 9 - 1, tap_index // 3 % 3 - 1, tap_index % 3 - 1) for tap_index in range(27)
]


def elu_pair(values):
    negative = jnp.exp(jnp.minimum(values, 0.0))
    return (jnp.where(values > 0, values, negative - 1.0), jnp.where(values > 0, 1.0, negative))


def neighbor_tables(device_block):
    space_count = lax.axis_size("space")
    depth_z = space_count // 8
    self_index = lax.axis_index("space")
    blocks = device_block[0]
    coords = jnp.stack([blocks // (4 * depth_z), blocks // depth_z % 4, blocks % depth_z])
    own_coords = lax.dynamic_index_in_dim(coords, self_index, 1, keepdims=False)
    offsets = jnp.array(tap_offsets, jnp.int32)
    limits = jnp.array([4, 4, depth_z], jnp.int32)
    wanted = own_coords[None, :] + offsets
    inside = jnp.all((wanted >= 0) & (wanted < limits[None, :]), axis=1) & (jnp.arange(27) != 13)
    wanted_id = (wanted[:, 0] * 4 + wanted[:, 1]) * depth_z + wanted[:, 2]
    matches = (blocks[None, :] == wanted_id[:, None]) & inside[:, None]
    devices = jnp.arange(space_count, dtype=jnp.int32)
    owner_row = jnp.sum(jnp.where(matches, devices[None, :], 0), axis=1)
    present = jnp.any(matches, axis=1)
    relative = coords - own_coords[:, None]
    adjacent = jnp.all(jnp.abs(relative) <= 1, axis=0) & (devices != self_index)
    send_tap = jnp.where(
        adjacent, (relative[0] + 1) * 9 + (relative[1] + 1) * 3 + relative[2] + 1, 13
    )
    return (owner_row, present, send_tap)


def region_slice(block_data, offset, depth_cells):
    span_list = []
    for step_value in offset:
        if step_value == 1:
            span_list.append(slice(BS - depth_cells, BS))
        elif step_value == -1:
            span_list.append(slice(0, depth_cells))
        else:
            span_list.append(slice(0, BS))
    return block_data[:, span_list[0], span_list[1], span_list[2]]


def surround(block_data, depth_cells, tables):
    owner_row, present, send_tap = tables
    channels = block_data.shape[0]
    length = depth_cells * BS * BS
    pieces = []
    for tap_index in range(27):
        if tap_index == 13:
            pieces.append(jnp.zeros((channels, length), block_data.dtype))
        else:
            region = region_slice(block_data, tap_offsets[tap_index], depth_cells).reshape(
                channels, -1
            )
            pieces.append(jnp.pad(region, ((0, 0), (0, length - region.shape[1]))))
    outgoing = jnp.stack(pieces)
    sending = outgoing[send_tap]
    by_source = lax.all_to_all(sending, "space", split_axis=0, concat_axis=0, tiled=True)
    incoming = jnp.where(
        present[:, None, None], by_source[owner_row], jnp.zeros((), block_data.dtype)
    )
    rows_x = []
    for step_x in range(3):
        rows_y = []
        for step_y in range(3):
            rows_z = []
            for step_z in range(3):
                tap_index = step_x * 9 + step_y * 3 + step_z
                if tap_index == 13:
                    rows_z.append(block_data)
                else:
                    extent_list = [
                        BS if step_value == 1 else depth_cells
                        for step_value in (step_x, step_y, step_z)
                    ]
                    count_cells = extent_list[0] * extent_list[1] * extent_list[2]
                    rows_z.append(
                        incoming[tap_index][:, :count_cells].reshape(
                            channels, extent_list[0], extent_list[1], extent_list[2]
                        )
                    )
            rows_y.append(jnp.concatenate(rows_z, axis=3))
        rows_x.append(jnp.concatenate(rows_y, axis=2))
    return jnp.concatenate(rows_x, axis=1)


def conv_padded(padded, kernel, dilation):
    result = lax.conv_general_dilated(
        padded[None],
        kernel,
        (1, 1, 1),
        "VALID",
        rhs_dilation=(dilation, dilation, dilation),
        dimension_numbers=("NCDHW", "OIDHW", "NCDHW"),
        preferred_element_type=jnp.float32,
    )
    return result[0].reshape(kernel.shape[0], BS * BS * BS)


def kernel_grad(padded, grad_rows, dilation):
    channels = padded.shape[0]
    outputs = grad_rows.shape[0]
    grad_block = grad_rows.reshape(outputs, 1, BS, BS, BS)
    result = lax.conv_general_dilated(
        padded[None],
        grad_block,
        (dilation, dilation, dilation),
        "VALID",
        dimension_numbers=("CNDHW", "OIDHW", "NCDHW"),
        preferred_element_type=jnp.float32,
    )
    return result.reshape(channels, outputs, 27).transpose(1, 2, 0)


def on_device_deep(features, device_block, conv_first, conv_second, head_weight, targets):
    channels = features.shape[2]
    tables = neighbor_tables(device_block)
    kernel_first = conv_first.reshape(channels, 3, 3, 3, channels).transpose(0, 4, 1, 2, 3)
    kernel_second = conv_second.reshape(channels, 3, 3, 3, channels).transpose(0, 4, 1, 2, 3)
    block_in = features[0, 0].reshape(channels, BS, BS, BS)
    padded_in = surround(block_in, 1, tables)
    pre_first = conv_padded(padded_in, kernel_first, 1)
    act_first, slope_first = elu_pair(pre_first)
    hid_first = act_first.astype(jnp.bfloat16)
    padded_first = surround(hid_first.reshape(channels, BS, BS, BS), 2, tables)
    pre_second = conv_padded(padded_first, kernel_second, 2)
    act_second, slope_second = elu_pair(pre_second)
    hid_second = act_second.astype(jnp.bfloat16)
    logits = jnp.dot(head_weight, hid_second, preferred_element_type=jnp.float32)
    scale = (lax.axis_size("dp") * lax.axis_size("space") * 3 * BS * BS * BS) ** (-0.5)
    grad_logit = ((jax.nn.sigmoid(logits) - targets[0, 0].astype(jnp.float32)) * scale).astype(
        jnp.bfloat16
    )
    grad_head = lax.dot_general(
        grad_logit, hid_second, (((1,), (1,)), ((), ())), preferred_element_type=jnp.float32
    )
    back_second = lax.dot_general(
        head_weight, grad_logit, (((0,), (0,)), ((), ())), preferred_element_type=jnp.float32
    )
    grad_pre_second = (back_second * slope_second).astype(jnp.bfloat16)
    grad_second = kernel_grad(padded_first, grad_pre_second, 2)
    padded_grad = surround(grad_pre_second.reshape(channels, BS, BS, BS), 2, tables)
    kernel_back = jnp.transpose(kernel_second[:, :, ::-1, ::-1, ::-1], (1, 0, 2, 3, 4))
    back_first = conv_padded(padded_grad, kernel_back, 2)
    grad_pre_first = (back_first * slope_first).astype(jnp.bfloat16)
    grad_first = kernel_grad(padded_in, grad_pre_first, 1)
    grad_first, grad_second, grad_head = lax.psum(
        (grad_first, grad_second, grad_head), ("dp", "space")
    )
    return (logits[None, None], grad_first, grad_second, grad_head)


C = 48
CELLS = 512
HALF = 512
LANES = 128


def lanes(rows=1):
    return lax.broadcasted_iota(jnp.int32, (rows, LANES), 1)


def roll(values, shift):
    return pltpu.roll(values, shift % LANES, 1) if shift % LANES else values


def listed_blocks(block_ref, me):
    ids = block_ref[...].astype(jnp.float32)
    index = lax.broadcasted_iota(jnp.int32, ids.shape, 1)
    return [
        jnp.sum(jnp.where(index == (me ^ k), ids, 0.0)).astype(jnp.int32)
        for k in range(ids.shape[1])
    ]


def apart(source, target):
    return (target >> 2) - (source >> 2), (target & 3) - (source & 3)


PARTNERS = (4, 6, 2)


def block_tiles(features_ref, targets_ref):
    tiles = [
        [features_ref[16 * ct : 16 * (ct + 1), LANES * q : LANES * (q + 1)] for q in range(4)]
        for ct in range(3)
    ]
    targets = targets_ref[:, 0, :].astype(jnp.float32)
    targets = jnp.concatenate([targets, jnp.zeros((1, CELLS), jnp.float32)], axis=0)
    return tiles, [targets[:, LANES * q : LANES * (q + 1)] for q in range(4)]


def write_cases(tiles, rows, cases_ref, lane):
    left = lane < 64
    cell = lane & 63
    target_tile = jnp.concatenate(rows, axis=0)

    def write(case, pairs, halves, wanted):
        for ct in range(3):
            cases_ref[case, 2 * ct] = pairs[ct][0]
            cases_ref[case, 2 * ct + 1] = pairs[ct][1]
        cases_ref[case, 6] = jnp.where(left, halves[0], halves[1])
        cases_ref[case, 7] = jnp.where(left, halves[2], wanted.astype(jnp.bfloat16))

    for case, pair, single, q in ((0, (2, 3), 1, 3), (1, (0, 1), 2, 0)):
        turns = (64, 0, 64) if case == 0 else (0, 64, 0)
        halves = [roll(tiles[ct][single], turns[ct]) for ct in range(3)]
        both = [roll(rows[q], 64), rows[q], jnp.zeros((8, LANES), jnp.float32)]
        wanted = jnp.concatenate(both, axis=0)
        write(case, [(t[pair[0]], t[pair[1]]) for t in tiles], halves, wanted)
    for case, spare, turn, turns, target_turns in (
        (2, cell < 24, -24, (-48, -96, -16, -64), (16, -32)),
        (3, cell >= 40, 40, (-24, -72, 8, -40), (64, 16)),
    ):
        pairs, halves = [], []
        for ct, t in enumerate(tiles):
            pairs.append([jnp.where(spare, roll(t[q + 2], turn), t[q]) for q in range(2)])
            moved = [roll(t[2 + n // 2], turns[n] + (64 if ct == 1 else 0)) for n in range(4)]
            half = jnp.where(cell < 16, moved[0], jnp.where(cell < 32, moved[1], moved[2]))
            halves.append(jnp.where(cell < 48, half, moved[3]))
        wanted = [roll(target_tile, n) for n in target_turns]
        write(case, pairs, halves, jnp.where(lane < 80, wanted[0], wanted[1]))


def case_of(source, target):
    dx, dy = apart(source, target)
    return jnp.where(dx > 0, 0, jnp.where(dx < 0, 1, jnp.where(dy > 0, 2, 3)))


def head_kernel(head_ref, h_ref, ht_ref):
    head = head_ref[...].astype(jnp.float32)
    head = jnp.concatenate([head, jnp.zeros((13, C), jnp.float32)], axis=0)
    h_ref[...] = head.astype(jnp.bfloat16)
    ht_ref[...] = head.T.astype(jnp.bfloat16)


def lanes_kernel(out_ref):
    out_ref[...] = lanes(16)


def pack_own_kernel(
    block_ref, features_ref, targets_ref, lane_ref, own_ref, slabs_ref, cases_ref
):
    blocks = listed_blocks(block_ref, lax.axis_index("space"))
    tiles, rows = block_tiles(features_ref, targets_ref)
    for ct in range(3):
        for q in range(4):
            own_ref[4 * ct + q] = tiles[ct][q]
    own_ref[12] = jnp.concatenate(rows, axis=0).astype(jnp.bfloat16)
    write_cases(tiles, rows, cases_ref, lane_ref[...])
    for n, k in enumerate(PARTNERS):
        slabs_ref[n] = cases_ref[case_of(blocks[0], blocks[k])]


def pack_mate_kernel(block_ref, features_ref, targets_ref, slabs_ref, mate_ref, *refs):
    *pair_refs, cases_ref = refs
    blocks = listed_blocks(block_ref, lax.axis_index("space"))
    write_cases(*block_tiles(features_ref, targets_ref), cases_ref, lanes(16))
    mate_ref[...] = cases_ref[case_of(blocks[1], blocks[0])]
    for n, (k, ref) in enumerate(zip(PARTNERS, pair_refs)):
        ref[0] = slabs_ref[n]
        ref[1] = cases_ref[case_of(blocks[1], blocks[k])]


def stacked_taps(ref):
    rows = []
    for a in range(3):
        taps = [ref[9 * a + t] for t in range(9)]
        rows.append(jnp.concatenate(taps, axis=1))
    return jnp.concatenate(rows, axis=0)


def second_kernel(second_ref, w2_ref, w2t_ref):
    whole = stacked_taps(second_ref)
    w2_ref[...] = whole
    w2t_ref[...] = whole.T


def prepare_kernel(block_ref, first_ref, w1_ref, owners_ref, masks_ref, table_ref):
    w1_ref[...] = stacked_taps(first_ref)

    blocks = listed_blocks(block_ref, lax.axis_index("space"))
    for slot in range(10):
        table_ref[0, slot] = 1
        table_ref[1, slot] = 0
    table_ref[1, 4] = 1
    for k in range(1, len(blocks)):
        dx, dy = apart(blocks[0], blocks[k])
        near = (dx >= -1) & (dx <= 1) & (dy >= -1) & (dy <= 1)
        slot = jnp.where(near, dx * 3 + dy + 4, 9)
        table_ref[0, slot] = k
        table_ref[1, slot] = 1
    lane = lanes()
    there = [table_ref[1, q].astype(jnp.float32) for q in range(9)]
    owners = jnp.zeros((1, LANES), jnp.int32)
    for q in range(9):
        owners = jnp.where(lane == q, table_ref[0, q], owners)
    owners_ref[...] = owners
    for bx in range(3):
        before, middle, after = there[3 * bx : 3 * bx + 3]
        masks_ref[bx : bx + 1, :] = jnp.where(
            lane < 32, before, jnp.where(lane < 96, middle, after)
        )
        masks_ref[bx + 3 : bx + 4, :] = jnp.where(lane < 64, after, before)


def matmul(left, right):
    return lax.dot_general(
        left, right, (((1,), (0,)), ((), ())), preferred_element_type=jnp.float32
    )


def matmul_lanes(left, right):
    return lax.dot_general(
        left, right, (((1,), (1,)), ((), ())), preferred_element_type=jnp.float32
    )


def crop_kernel(scale, owners_ref, masks_ref, own_ref, mate_ref, *refs):
    crop_body(scale, owners_ref, masks_ref, own_ref, mate_ref, refs[:3], *refs[3:])


def crop_body(
    scale,
    owners_ref,
    masks_ref,
    own_ref,
    mate_ref,
    pairs,
    w1_ref,
    w2_ref,
    w2t_ref,
    h_ref,
    ht_ref,
    logits_ref,
    keep_ref,
    send_ref,
    gathered_ref,
    sides_ref,
    ends_ref,
    x9_ref,
    h9_ref,
    product_ref,
    slope1_ref,
    slope2_ref,
    hid2_ref,
    grad2_ref,
    shifted_ref,
    back_ref,
):
    gathered_ref[1] = mate_ref[...]
    for k, pair in zip(PARTNERS, pairs):
        for j in range(2):
            gathered_ref[k + j] = pair[j]
    owners = owners_ref[...]
    owner = [owners[0, q] for q in range(9)]

    bf16 = jnp.bfloat16
    lane = lanes(16)
    depth = lane & 7
    depth48 = lanes(C) & 7
    low, mid, left_half = lane < 32, lane < 96, lane < 64
    masks = [masks_ref[bx : bx + 1, :] for bx in range(3)]
    main_masks = [jnp.broadcast_to(mask, (16, LANES)).astype(bf16) for mask in masks]
    edge_masks = [
        jnp.broadcast_to(masks_ref[bx + 3 : bx + 4, :], (16, LANES)).astype(bf16)
        for bx in range(3)
    ]
    own_row = jnp.where((lane >= 32) & mid, 1.0, 0.0)[0:1]

    cell = lane & 63
    for side, by, in_place, turn, turns in (
        (0, 0, cell < 48, 24, (48, 96, 16, 64)),
        (1, 2, cell < 24, -40, (24, 72, -8, 40)),
    ):
        slab = owner[3 + by]
        for ct in range(3):
            half = gathered_ref[slab, 6 + ct // 2]
            for q in range(2):
                sides_ref[side, 4 * ct + q] = gathered_ref[slab, 2 * ct + q]
                moved = [roll(half, turns[2 * q + n] - (64 if ct == 1 else 0)) for n in range(2)]
                sides_ref[side, 4 * ct + q + 2] = jnp.where(
                    in_place,
                    roll(gathered_ref[slab, 2 * ct + q], turn),
                    jnp.where(left_half, moved[0], moved[1]),
                )

    for bx in (0, 2):
        for by in range(3):
            for ct in range(3):
                tile = gathered_ref[owner[3 * bx + by], 6 + ct // 2]
                ends_ref[3 * bx // 2 + by, ct] = roll(tile, -64 * (ct % 2))

    def placed(ct, bx, i):
        if bx == 1:
            tile, half = 4 * ct + i // 2, i % 2
            parts = [sides_ref[0, tile], own_ref[tile], sides_ref[1, tile]]
        elif i == (3 if bx == 0 else 4):
            half = 0
            parts = [ends_ref[3 * bx // 2 + by, ct] for by in range(3)]
        else:
            tile, half = 2 * ct + (i // 2 - 2 if bx == 0 else i // 2), i % 2
            parts = [gathered_ref[owner[3 * bx + by], tile] for by in range(3)]
        outer = 96 - 64 * half
        return roll(parts[0], outer), roll(parts[1], 32 - 64 * half), roll(parts[2], outer)

    zero = jnp.zeros((16, LANES), bf16)

    for plane in range(18):
        bx, i = (plane + 3) // 8, (plane + 3) % 8
        for ct in range(3):
            before, middle, after = placed(ct, bx, i)
            main = jnp.where(low, before, jnp.where(mid, middle, after)) * main_masks[bx]
            edge = jnp.where(left_half, after, before) * edge_masks[bx]
            for c in (-1, 0, 1):
                if c == 0:
                    main_c, edge_c = main, edge
                else:
                    keep = depth >= 1 if c == 1 else depth <= 6
                    main_c, edge_c = jnp.where(keep, main, zero), jnp.where(keep, edge, zero)
                for b in (-1, 0, 1):
                    step = 8 * b + c
                    if b == 1:
                        source = jnp.where(lane < step, edge_c, main_c)
                    elif b == -1:
                        source = jnp.where(lane >= LANES + step, edge_c, main_c)
                    else:
                        source = main_c
                    row = (3 * (b + 1) + c + 1) * C + 16 * ct
                    x9_ref[row : row + 16, LANES * plane : LANES * (plane + 1)] = (
                        roll(source, -step) if step else source
                    )

    def plane_cols(plane):
        return slice(LANES * plane, LANES * (plane + 1))

    def summed(plane, stride):
        return (
            product_ref[0:C, plane_cols(plane)]
            + product_ref[C : 2 * C, plane_cols(plane + stride)]
            + product_ref[2 * C : 3 * C, plane_cols(plane + 2 * stride)]
        )

    for n in range(3):
        cols = slice(768 * n, 768 * (n + 1))
        product_ref[:, cols] = matmul(w1_ref[...], x9_ref[:, cols])

    for plane in range(16):
        bx = (plane + 4) // 8
        pre = summed(plane, 1)
        negative = jnp.exp(jnp.minimum(pre, 0.0))
        if 4 <= plane < 12:
            slope1_ref[:, plane_cols(plane - 4)] = negative
        hidden = (jnp.maximum(pre, 0.0) + (negative - 1.0)) * masks[bx]
        hidden = hidden.astype(bf16)
        for c in (-1, 0, 1):
            if c == 0:
                source = hidden
            else:
                keep = depth48 >= 2 if c == 1 else depth48 <= 5
                source = jnp.where(keep, hidden, jnp.zeros((C, LANES), bf16))
            for b in (-1, 0, 1):
                step = 16 * b + 2 * c
                row = (3 * (b + 1) + c + 1) * C
                h9_ref[row : row + C, plane_cols(plane)] = roll(source, -step) if step else source

    for n in range(4):
        cols = slice(512 * n, 512 * (n + 1))
        product_ref[:, cols] = matmul(w2_ref[...], h9_ref[:, cols])

    for plane in range(12):
        bx = (plane + 6) // 8
        pre = summed(plane, 2)
        negative = jnp.exp(jnp.minimum(pre, 0.0))
        slope2_ref[:, plane_cols(plane)] = negative * masks[bx]
        hidden = (jnp.maximum(pre, 0.0) + (negative - 1.0)) * masks[bx]
        hid2_ref[:, plane_cols(plane)] = hidden.astype(jnp.bfloat16)

    logits = matmul(h_ref[...], hid2_ref[...])
    targets = []
    for bx, half in ((0, 1), (1, 0), (1, 1), (2, 1)):
        if bx == 1:
            before = roll(gathered_ref[owner[3], 7], -48 - 16 * half)
            middle = roll(own_ref[12], 32 - 64 * half)
            after = roll(gathered_ref[owner[5], 7], 32 - 16 * half)
        else:
            parts = [gathered_ref[owner[3 * bx + by], 7] for by in range(3)]
            before, middle, after = roll(parts[0], 32), roll(parts[1], -32), roll(parts[2], 32)
        cells = jnp.where(low, before, jnp.where(mid, middle, after))
        targets.append(cells.astype(jnp.float32))
    grads = []
    for plane in range(12):
        bx, i = (plane + 6) // 8, (plane + 6) % 8
        value = logits[:, plane_cols(plane)]
        if bx == 1:
            wanted = targets[1 + i % 2][4 * (i // 2) : 4 * (i // 2) + 4]
        else:
            wanted = targets[0 if bx == 0 else 3][4 * (i % 2) : 4 * (i % 2) + 4]
        wanted = jnp.concatenate([wanted, jnp.zeros((12, LANES), jnp.float32)], axis=0)
        sigmoid = 1.0 / (1.0 + jnp.exp(-value))
        grads.append((sigmoid - wanted) * masks[bx] * scale)
    for q in range(4):
        first = roll(logits[:, plane_cols(2 + 2 * q)], -32)
        second = roll(logits[:, plane_cols(3 + 2 * q)], 32)
        logits_ref[:, plane_cols(q)] = jnp.where(left_half, first, second)[0:8]

    grad_logit = jnp.concatenate(grads, axis=1).astype(jnp.bfloat16)
    back = matmul(ht_ref[...], grad_logit)
    grad2_ref[...] = (back * slope2_ref[...]).astype(jnp.bfloat16)
    own_grads = jnp.concatenate([grads[2 + x] * own_row for x in range(8)], axis=1)
    head_part = matmul_lanes(hid2_ref[:, 2 * LANES : 10 * LANES], own_grads.astype(jnp.bfloat16))

    own_bf16 = jnp.broadcast_to(own_row, (C, LANES)).astype(bf16)
    shifted_ref[...] = jnp.zeros_like(shifted_ref)
    for a in range(3):
        for x in range(8):
            shifted_ref[C * a : C * (a + 1), plane_cols(x + 2 * a)] = (
                grad2_ref[:, plane_cols(x + 2)] * own_bf16
            )
    second_part = matmul_lanes(shifted_ref[...], h9_ref[:, 2 * LANES : 14 * LANES])

    for a in range(3):
        for x in range(8):
            shifted_ref[C * a : C * (a + 1), plane_cols(x)] = grad2_ref[:, plane_cols(x + 4 - 2 * a)]
    for n in range(2):
        cols = slice(512 * n, 512 * (n + 1))
        back_ref[:, cols] = matmul(w2t_ref[...], shifted_ref[:, cols])
    grad1 = []
    for x in range(8):
        total = jnp.zeros((C, LANES), jnp.float32)
        for c in (-1, 0, 1):
            part = jnp.zeros((C, LANES), jnp.float32)
            for b in (-1, 0, 1):
                row = (3 * (b + 1) + c + 1) * C
                step = 16 * b + 2 * c
                piece = back_ref[row : row + C, plane_cols(x)]
                part += roll(piece, step) if step else piece
            if c:
                part = jnp.where(depth48 >= 2 if c == 1 else depth48 <= 5, part, 0.0)
            total += part
        grad1.append((total * slope1_ref[:, plane_cols(x)] * own_row).astype(jnp.bfloat16))

    shifted_ref[...] = jnp.zeros_like(shifted_ref)
    for a in range(3):
        for x in range(8):
            shifted_ref[C * a : C * (a + 1), plane_cols(x + a)] = grad1[x]
    first_part = matmul_lanes(
        shifted_ref[:, 0 : 10 * LANES], x9_ref[:, 4 * LANES : 14 * LANES]
    )

    first_core = (lax.axis_index("dp") & 1) == 0
    head_part = jnp.concatenate([head_part, jnp.zeros((24, 16), jnp.float32)], axis=0)
    nothing = jnp.zeros((72, 16), jnp.float32)
    ends = []
    for part, extra in ((first_part, nothing), (second_part, head_part)):
        tail = jnp.concatenate([part[0:72, 384:], part[72:144, 384:], extra, nothing], axis=1)
        ends.append(jnp.concatenate([tail, jnp.zeros((8, LANES), jnp.float32)], axis=0))
    pieces = [(first_part[:, plane_cols(q)], second_part[:, plane_cols(q)]) for q in range(3)]
    row = 0
    for first, second in pieces + [tuple(ends)]:
        rows = slice(row, row + first.shape[0])
        keep_ref[rows, :] = jnp.where(first_core, first, second)
        send_ref[rows, :] = jnp.where(first_core, second, first)
        row += first.shape[0]


def add_kernel(mine_ref, other_ref, out_ref):
    out_ref[...] = (mine_ref[...] + other_ref[...]).astype(jnp.bfloat16)


def sum_kernel(parts_ref, out_ref):
    total = parts_ref[0].astype(jnp.float32)
    for s in range(1, parts_ref.shape[0]):
        total += parts_ref[s].astype(jnp.float32)
    total = total.astype(jnp.bfloat16)
    for s in range(out_ref.shape[0]):
        out_ref[s] = total


def unpack_kernel(mine_ref, other_ref, logits_ref, first_ref, second_ref, head_ref, out_ref):
    out_ref[:, 0, :] = logits_ref[0:3, :]
    first_core = (lax.axis_index("dp") & 1) == 0
    mine, other = mine_ref[...], other_ref[...]
    for k, out in ((0, first_ref), (1, second_ref)):
        half = jnp.where(first_core, other if k else mine, mine if k else other)
        half = half.astype(jnp.float32)
        tail = jnp.concatenate([half[432:504, 0:C], half[432:504, C : 2 * C]], axis=0)
        tiles = [half[144 * q : 144 * (q + 1), :] for q in range(3)]
        whole = jnp.concatenate(tiles + [tail], axis=1)
        for a in range(3):
            for t in range(9):
                out[9 * a + t] = whole[C * a : C * (a + 1), C * t : C * (t + 1)]
        if k:
            head_ref[...] = half[432 : 432 + C, 96:112].T[0:3]


def on_device_flat(features, device_block, conv_first, conv_second, head_weight, targets):
    space_count = lax.axis_size("space")
    device_count = lax.axis_size("dp") * space_count
    bf16, f32 = jnp.bfloat16, jnp.float32
    small = pltpu.CompilerParams(vmem_limit_bytes=8 * 1024 * 1024)
    shape = jax.ShapeDtypeStruct
    vmem = pl.BlockSpec(memory_space=pltpu.VMEM)

    def swap(values, mask):
        return lax.ppermute(values, "space", [(s, s ^ mask) for s in range(space_count)])

    mate_targets, mate_features = swap(targets, 1), swap(features, 1)
    head, head_t = pl.pallas_call(
        head_kernel,
        out_shape=(shape((16, C), bf16), shape((C, 16), bf16)),
        in_specs=[vmem],
        out_specs=(vmem,) * 2,
        compiler_params=small,
        cost_estimate=pl.CostEstimate(flops=1_000_000, bytes_accessed=2_000_000, transcendentals=0),
        name="lay_out_head",
    )(head_weight)
    lane = pl.pallas_call(
        lanes_kernel,
        out_shape=shape((16, LANES), jnp.int32),
        out_specs=vmem,
        compiler_params=small,
        cost_estimate=pl.CostEstimate(flops=0, bytes_accessed=2_000_000, transcendentals=0),
        name="lane_indices",
    )()
    own, own_slabs = pl.pallas_call(
        pack_own_kernel,
        out_shape=(shape((13, 16, LANES), bf16), shape((3, 8, 16, LANES), bf16)),
        in_specs=[vmem] * 4,
        out_specs=(vmem,) * 2,
        scratch_shapes=[pltpu.VMEM((4, 8, 16, LANES), bf16)],
        compiler_params=small,
        cost_estimate=pl.CostEstimate(flops=1_000_000, bytes_accessed=2_000_000, transcendentals=0),
        name="pack_own",
    )(device_block, features[0, 0], targets[0].transpose(1, 0, 2), lane)
    mate_slab, *pairs = pl.pallas_call(
        pack_mate_kernel,
        out_shape=(
            shape((8, 16, LANES), bf16),
            *[shape((2, 8, 16, LANES), bf16) for _ in PARTNERS],
        ),
        in_specs=[vmem] * 4,
        out_specs=(vmem,) * 4,
        scratch_shapes=[pltpu.VMEM((4, 8, 16, LANES), bf16)],
        compiler_params=small,
        cost_estimate=pl.CostEstimate(flops=1_000_000, bytes_accessed=2_000_000, transcendentals=0),
        name="pack_mate",
    )(device_block, mate_features[0, 0], mate_targets[0].transpose(1, 0, 2), own_slabs)
    pairs = [swap(pair, mask) for pair, mask in zip(pairs, PARTNERS)]

    w1, owners, masks = pl.pallas_call(
        prepare_kernel,
        out_shape=(
            shape((3 * C, 9 * C), bf16),
            shape((1, LANES), jnp.int32),
            shape((8, LANES), f32),
        ),
        in_specs=[vmem] * 2,
        out_specs=(vmem,) * 3,
        scratch_shapes=[pltpu.SMEM((2, 16), jnp.int32)],
        compiler_params=small,
        cost_estimate=pl.CostEstimate(flops=2_000_000, bytes_accessed=4_000_000, transcendentals=0),
        name="prepare",
    )(device_block, conv_first.transpose(1, 0, 2))
    w2, w2t = pl.pallas_call(
        second_kernel,
        out_shape=(shape((3 * C, 9 * C), bf16), shape((9 * C, 3 * C), bf16)),
        in_specs=[vmem],
        out_specs=(vmem,) * 2,
        compiler_params=small,
        cost_estimate=pl.CostEstimate(flops=2_000_000, bytes_accessed=4_000_000, transcendentals=0),
        name="second_weights",
    )(conv_second.transpose(1, 0, 2))

    scale = (device_count * 3 * CELLS) ** (-0.5)
    logits, keep, send = pl.pallas_call(
        functools.partial(crop_kernel, scale),
        out_shape=(shape((8, CELLS), f32), shape((HALF, LANES), f32), shape((HALF, LANES), f32)),
        in_specs=[vmem] * 12,
        out_specs=(vmem,) * 3,
        scratch_shapes=[
            pltpu.VMEM((space_count, 8, 16, LANES), bf16),
            pltpu.VMEM((2, 12, 16, LANES), bf16),
            pltpu.VMEM((6, 3, 16, LANES), bf16),
            pltpu.VMEM((9 * C, 18 * LANES), bf16),
            pltpu.VMEM((9 * C, 16 * LANES), bf16),
            pltpu.VMEM((3 * C, 18 * LANES), f32),
            pltpu.VMEM((C, 8 * LANES), f32),
            pltpu.VMEM((C, 12 * LANES), f32),
            pltpu.VMEM((C, 12 * LANES), bf16),
            pltpu.VMEM((C, 12 * LANES), bf16),
            pltpu.VMEM((3 * C, 12 * LANES), bf16),
            pltpu.VMEM((9 * C, 8 * LANES), f32),
        ],
        compiler_params=pltpu.CompilerParams(vmem_limit_bytes=20 * 1024 * 1024),
        name="forward_backward",
    )(owners, masks, own, mate_slab, *pairs, w1, w2, w2t, head, head_t)

    dp_count = lax.axis_size("dp")

    def swap_cores(values):
        return lax.ppermute(values, "dp", [(d, d ^ 1) for d in range(dp_count)])

    peers = device_count // 2
    groups = [
        [d * space_count + s for d in range(core, dp_count, 2) for s in range(space_count)]
        for core in range(2)
    ]

    def exchange(values):
        return lax.all_to_all(
            values, ("dp", "space"), 0, 0, axis_index_groups=groups, tiled=True
        )

    def step(kernel, out, *operands):
        return pl.pallas_call(
            kernel,
            out_shape=out,
            in_specs=[vmem] * len(operands),
            out_specs=vmem,
            compiler_params=small,
            name="gradient_sum",
        )(*operands)

    term = step(add_kernel, shape((HALF, LANES), bf16), keep, swap_cores(send))
    pieces = shape((peers, HALF // peers, LANES), bf16)
    total = exchange(step(sum_kernel, pieces, exchange(term.reshape(pieces.shape))))
    total = total.reshape(HALF, LANES)
    grad_first, grad_second, grad_head, logits = pl.pallas_call(
        unpack_kernel,
        out_shape=(
            shape((27, C, C), f32),
            shape((27, C, C), f32),
            shape((3, C), f32),
            shape((3, 1, CELLS), f32),
        ),
        in_specs=[vmem] * 3,
        out_specs=(vmem,) * 4,
        compiler_params=small,
        name="unpack_gradients",
    )(total, swap_cores(total), logits)
    return (
        logits.transpose(1, 0, 2)[None],
        grad_first.transpose(1, 0, 2),
        grad_second.transpose(1, 0, 2),
        grad_head,
    )


def solution(mesh):
    in_specs = (
        P("dp", "space", None, None),
        P("dp", None),
        P(),
        P(),
        P(),
        P("dp", "space", None, None),
    )
    out_specs = (P("dp", "space", None, None), P(), P(), P())
    flat = mesh.shape["space"] == 8 and mesh.shape["dp"] in (2, 4)
    return jax.shard_map(
        on_device_flat if flat else on_device_deep,
        mesh=mesh,
        in_specs=in_specs,
        out_specs=out_specs,
        check_vma=False,
    )
```

```python
import functools

import jax
import jax.numpy as jnp
from jax import lax
from jax.experimental import pallas as pl
from jax.experimental.pallas import tpu as pltpu
from jax.sharding import PartitionSpec as P

BS = 8


tap_offsets = [
    (tap_index // 9 - 1, tap_index // 3 % 3 - 1, tap_index % 3 - 1) for tap_index in range(27)
]


def elu_pair(values):
    negative = jnp.exp(jnp.minimum(values, 0.0))
    return (jnp.where(values > 0, values, negative - 1.0), jnp.where(values > 0, 1.0, negative))


def neighbor_tables(device_block):
    space_count = lax.axis_size("space")
    depth_z = space_count // 8
    self_index = lax.axis_index("space")
    blocks = device_block[0]
    coords = jnp.stack([blocks // (4 * depth_z), blocks // depth_z % 4, blocks % depth_z])
    own_coords = lax.dynamic_index_in_dim(coords, self_index, 1, keepdims=False)
    offsets = jnp.array(tap_offsets, jnp.int32)
    limits = jnp.array([4, 4, depth_z], jnp.int32)
    wanted = own_coords[None, :] + offsets
    inside = jnp.all((wanted >= 0) & (wanted < limits[None, :]), axis=1) & (jnp.arange(27) != 13)
    wanted_id = (wanted[:, 0] * 4 + wanted[:, 1]) * depth_z + wanted[:, 2]
    matches = (blocks[None, :] == wanted_id[:, None]) & inside[:, None]
    devices = jnp.arange(space_count, dtype=jnp.int32)
    owner_row = jnp.sum(jnp.where(matches, devices[None, :], 0), axis=1)
    present = jnp.any(matches, axis=1)
    relative = coords - own_coords[:, None]
    adjacent = jnp.all(jnp.abs(relative) <= 1, axis=0) & (devices != self_index)
    send_tap = jnp.where(
        adjacent, (relative[0] + 1) * 9 + (relative[1] + 1) * 3 + relative[2] + 1, 13
    )
    return (owner_row, present, send_tap)


def region_slice(block_data, offset, depth_cells):
    span_list = []
    for step_value in offset:
        if step_value == 1:
            span_list.append(slice(BS - depth_cells, BS))
        elif step_value == -1:
            span_list.append(slice(0, depth_cells))
        else:
            span_list.append(slice(0, BS))
    return block_data[:, span_list[0], span_list[1], span_list[2]]


def surround(block_data, depth_cells, tables):
    owner_row, present, send_tap = tables
    channels = block_data.shape[0]
    length = depth_cells * BS * BS
    pieces = []
    for tap_index in range(27):
        if tap_index == 13:
            pieces.append(jnp.zeros((channels, length), block_data.dtype))
        else:
            region = region_slice(block_data, tap_offsets[tap_index], depth_cells).reshape(
                channels, -1
            )
            pieces.append(jnp.pad(region, ((0, 0), (0, length - region.shape[1]))))
    outgoing = jnp.stack(pieces)
    sending = outgoing[send_tap]
    by_source = lax.all_to_all(sending, "space", split_axis=0, concat_axis=0, tiled=True)
    incoming = jnp.where(
        present[:, None, None], by_source[owner_row], jnp.zeros((), block_data.dtype)
    )
    rows_x = []
    for step_x in range(3):
        rows_y = []
        for step_y in range(3):
            rows_z = []
            for step_z in range(3):
                tap_index = step_x * 9 + step_y * 3 + step_z
                if tap_index == 13:
                    rows_z.append(block_data)
                else:
                    extent_list = [
                        BS if step_value == 1 else depth_cells
                        for step_value in (step_x, step_y, step_z)
                    ]
                    count_cells = extent_list[0] * extent_list[1] * extent_list[2]
                    rows_z.append(
                        incoming[tap_index][:, :count_cells].reshape(
                            channels, extent_list[0], extent_list[1], extent_list[2]
                        )
                    )
            rows_y.append(jnp.concatenate(rows_z, axis=3))
        rows_x.append(jnp.concatenate(rows_y, axis=2))
    return jnp.concatenate(rows_x, axis=1)


def conv_padded(padded, kernel, dilation):
    result = lax.conv_general_dilated(
        padded[None],
        kernel,
        (1, 1, 1),
        "VALID",
        rhs_dilation=(dilation, dilation, dilation),
        dimension_numbers=("NCDHW", "OIDHW", "NCDHW"),
        preferred_element_type=jnp.float32,
    )
    return result[0].reshape(kernel.shape[0], BS * BS * BS)


def kernel_grad(padded, grad_rows, dilation):
    channels = padded.shape[0]
    outputs = grad_rows.shape[0]
    grad_block = grad_rows.reshape(outputs, 1, BS, BS, BS)
    result = lax.conv_general_dilated(
        padded[None],
        grad_block,
        (dilation, dilation, dilation),
        "VALID",
        dimension_numbers=("CNDHW", "OIDHW", "NCDHW"),
        preferred_element_type=jnp.float32,
    )
    return result.reshape(channels, outputs, 27).transpose(1, 2, 0)


def on_device_deep(features, device_block, conv_first, conv_second, head_weight, targets):
    channels = features.shape[2]
    tables = neighbor_tables(device_block)
    kernel_first = conv_first.reshape(channels, 3, 3, 3, channels).transpose(0, 4, 1, 2, 3)
    kernel_second = conv_second.reshape(channels, 3, 3, 3, channels).transpose(0, 4, 1, 2, 3)
    block_in = features[0, 0].reshape(channels, BS, BS, BS)
    padded_in = surround(block_in, 1, tables)
    pre_first = conv_padded(padded_in, kernel_first, 1)
    act_first, slope_first = elu_pair(pre_first)
    hid_first = act_first.astype(jnp.bfloat16)
    padded_first = surround(hid_first.reshape(channels, BS, BS, BS), 2, tables)
    pre_second = conv_padded(padded_first, kernel_second, 2)
    act_second, slope_second = elu_pair(pre_second)
    hid_second = act_second.astype(jnp.bfloat16)
    logits = jnp.dot(head_weight, hid_second, preferred_element_type=jnp.float32)
    scale = (lax.axis_size("dp") * lax.axis_size("space") * 3 * BS * BS * BS) ** (-0.5)
    grad_logit = ((jax.nn.sigmoid(logits) - targets[0, 0].astype(jnp.float32)) * scale).astype(
        jnp.bfloat16
    )
    grad_head = lax.dot_general(
        grad_logit, hid_second, (((1,), (1,)), ((), ())), preferred_element_type=jnp.float32
    )
    back_second = lax.dot_general(
        head_weight, grad_logit, (((0,), (0,)), ((), ())), preferred_element_type=jnp.float32
    )
    grad_pre_second = (back_second * slope_second).astype(jnp.bfloat16)
    grad_second = kernel_grad(padded_first, grad_pre_second, 2)
    padded_grad = surround(grad_pre_second.reshape(channels, BS, BS, BS), 2, tables)
    kernel_back = jnp.transpose(kernel_second[:, :, ::-1, ::-1, ::-1], (1, 0, 2, 3, 4))
    back_first = conv_padded(padded_grad, kernel_back, 2)
    grad_pre_first = (back_first * slope_first).astype(jnp.bfloat16)
    grad_first = kernel_grad(padded_in, grad_pre_first, 1)
    grad_first, grad_second, grad_head = lax.psum(
        (grad_first, grad_second, grad_head), ("dp", "space")
    )
    return (logits[None, None], grad_first, grad_second, grad_head)


C = 48
CELLS = 512
HALF = 512
LANES = 128


def lanes(rows=1):
    return lax.broadcasted_iota(jnp.int32, (rows, LANES), 1)


def roll(values, shift):
    return pltpu.roll(values, shift % LANES, 1) if shift % LANES else values


def listed_blocks(block_ref, me):
    ids = block_ref[...].astype(jnp.float32)
    index = lax.broadcasted_iota(jnp.int32, ids.shape, 1)
    return [
        jnp.sum(jnp.where(index == (me ^ k), ids, 0.0)).astype(jnp.int32)
        for k in range(ids.shape[1])
    ]


def apart(source, target):
    return (target >> 2) - (source >> 2), (target & 3) - (source & 3)


PARTNERS = (4, 6, 2)


def block_tiles(features_ref, targets_ref):
    tiles = [
        [features_ref[16 * ct : 16 * (ct + 1), LANES * q : LANES * (q + 1)] for q in range(4)]
        for ct in range(3)
    ]
    targets = targets_ref[:, 0, :].astype(jnp.float32)
    targets = jnp.concatenate([targets, jnp.zeros((1, CELLS), jnp.float32)], axis=0)
    return tiles, [targets[:, LANES * q : LANES * (q + 1)] for q in range(4)]


def write_cases(tiles, rows, cases_ref, lane):
    left = lane < 64
    cell = lane & 63
    target_tile = jnp.concatenate(rows, axis=0)

    def write(case, pairs, halves, wanted):
        for ct in range(3):
            cases_ref[case, 2 * ct] = pairs[ct][0]
            cases_ref[case, 2 * ct + 1] = pairs[ct][1]
        cases_ref[case, 6] = jnp.where(left, halves[0], halves[1])
        cases_ref[case, 7] = jnp.where(left, halves[2], wanted.astype(jnp.bfloat16))

    for case, pair, single, q in ((0, (2, 3), 1, 3), (1, (0, 1), 2, 0)):
        turns = (64, 0, 64) if case == 0 else (0, 64, 0)
        halves = [roll(tiles[ct][single], turns[ct]) for ct in range(3)]
        both = [roll(rows[q], 64), rows[q], jnp.zeros((8, LANES), jnp.float32)]
        wanted = jnp.concatenate(both, axis=0)
        write(case, [(t[pair[0]], t[pair[1]]) for t in tiles], halves, wanted)
    for case, spare, turn, turns, target_turns in (
        (2, cell < 24, -24, (-48, -96, -16, -64), (16, -32)),
        (3, cell >= 40, 40, (-24, -72, 8, -40), (64, 16)),
    ):
        pairs, halves = [], []
        for ct, t in enumerate(tiles):
            pairs.append([jnp.where(spare, roll(t[q + 2], turn), t[q]) for q in range(2)])
            moved = [roll(t[2 + n // 2], turns[n] + (64 if ct == 1 else 0)) for n in range(4)]
            half = jnp.where(cell < 16, moved[0], jnp.where(cell < 32, moved[1], moved[2]))
            halves.append(jnp.where(cell < 48, half, moved[3]))
        wanted = [roll(target_tile, n) for n in target_turns]
        write(case, pairs, halves, jnp.where(lane < 80, wanted[0], wanted[1]))


def case_of(source, target):
    dx, dy = apart(source, target)
    return jnp.where(dx > 0, 0, jnp.where(dx < 0, 1, jnp.where(dy > 0, 2, 3)))


def head_kernel(head_ref, h_ref, ht_ref):
    head = head_ref[...].astype(jnp.float32)
    head = jnp.concatenate([head, jnp.zeros((13, C), jnp.float32)], axis=0)
    h_ref[...] = head.astype(jnp.bfloat16)
    ht_ref[...] = head.T.astype(jnp.bfloat16)


def lanes_kernel(out_ref):
    out_ref[...] = lanes(16)


def pack_own_kernel(
    block_ref, features_ref, targets_ref, lane_ref, own_ref, slabs_ref, cases_ref
):
    blocks = listed_blocks(block_ref, lax.axis_index("space"))
    tiles, rows = block_tiles(features_ref, targets_ref)
    for ct in range(3):
        for q in range(4):
            own_ref[4 * ct + q] = tiles[ct][q]
    own_ref[12] = jnp.concatenate(rows, axis=0).astype(jnp.bfloat16)
    write_cases(tiles, rows, cases_ref, lane_ref[...])
    for n, k in enumerate(PARTNERS):
        slabs_ref[n] = cases_ref[case_of(blocks[0], blocks[k])]


def pack_mate_kernel(block_ref, features_ref, targets_ref, slabs_ref, mate_ref, *refs):
    *pair_refs, cases_ref = refs
    blocks = listed_blocks(block_ref, lax.axis_index("space"))
    write_cases(*block_tiles(features_ref, targets_ref), cases_ref, lanes(16))
    mate_ref[...] = cases_ref[case_of(blocks[1], blocks[0])]
    for n, (k, ref) in enumerate(zip(PARTNERS, pair_refs)):
        ref[0] = slabs_ref[n]
        ref[1] = cases_ref[case_of(blocks[1], blocks[k])]


def stacked_taps(ref):
    rows = []
    for a in range(3):
        taps = [ref[9 * a + t] for t in range(9)]
        rows.append(jnp.concatenate(taps, axis=1))
    return jnp.concatenate(rows, axis=0)


def second_kernel(second_ref, w2_ref, w2t_ref):
    whole = stacked_taps(second_ref)
    w2_ref[...] = whole
    w2t_ref[...] = whole.T


def prepare_kernel(block_ref, first_ref, w1_ref, owners_ref, masks_ref, table_ref):
    w1_ref[...] = stacked_taps(first_ref)

    blocks = listed_blocks(block_ref, lax.axis_index("space"))
    for slot in range(10):
        table_ref[0, slot] = 1
        table_ref[1, slot] = 0
    table_ref[1, 4] = 1
    for k in range(1, len(blocks)):
        dx, dy = apart(blocks[0], blocks[k])
        near = (dx >= -1) & (dx <= 1) & (dy >= -1) & (dy <= 1)
        slot = jnp.where(near, dx * 3 + dy + 4, 9)
        table_ref[0, slot] = k
        table_ref[1, slot] = 1
    lane = lanes()
    there = [table_ref[1, q].astype(jnp.float32) for q in range(9)]
    owners = jnp.zeros((1, LANES), jnp.int32)
    for q in range(9):
        owners = jnp.where(lane == q, table_ref[0, q], owners)
    owners_ref[...] = owners
    for bx in range(3):
        before, middle, after = there[3 * bx : 3 * bx + 3]
        masks_ref[bx : bx + 1, :] = jnp.where(
            lane < 32, before, jnp.where(lane < 96, middle, after)
        )
        masks_ref[bx + 3 : bx + 4, :] = jnp.where(lane < 64, after, before)


def matmul(left, right):
    return lax.dot_general(
        left, right, (((1,), (0,)), ((), ())), preferred_element_type=jnp.float32
    )


def matmul_lanes(left, right):
    return lax.dot_general(
        left, right, (((1,), (1,)), ((), ())), preferred_element_type=jnp.float32
    )


def crop_kernel(scale, owners_ref, masks_ref, own_ref, mate_ref, *refs):
    crop_body(scale, owners_ref, masks_ref, own_ref, mate_ref, refs[:3], *refs[3:])


def crop_body(
    scale,
    owners_ref,
    masks_ref,
    own_ref,
    mate_ref,
    pairs,
    w1_ref,
    w2_ref,
    w2t_ref,
    h_ref,
    ht_ref,
    logits_ref,
    keep_ref,
    send_ref,
    gathered_ref,
    sides_ref,
    ends_ref,
    x9_ref,
    h9_ref,
    product_ref,
    slope1_ref,
    slope2_ref,
    hid2_ref,
    grad2_ref,
    shifted_ref,
    back_ref,
):
    gathered_ref[1] = mate_ref[...]
    for k, pair in zip(PARTNERS, pairs):
        for j in range(2):
            gathered_ref[k + j] = pair[j]
    owners = owners_ref[...]
    owner = [owners[0, q] for q in range(9)]

    bf16 = jnp.bfloat16
    lane = lanes(16)
    depth = lane & 7
    depth48 = lanes(C) & 7
    low, mid, left_half = lane < 32, lane < 96, lane < 64
    masks = [masks_ref[bx : bx + 1, :] for bx in range(3)]
    main_masks = [jnp.broadcast_to(mask, (16, LANES)).astype(bf16) for mask in masks]
    edge_masks = [
        jnp.broadcast_to(masks_ref[bx + 3 : bx + 4, :], (16, LANES)).astype(bf16)
        for bx in range(3)
    ]
    own_row = jnp.where((lane >= 32) & mid, 1.0, 0.0)[0:1]

    cell = lane & 63
    for side, by, in_place, turn, turns in (
        (0, 0, cell < 48, 24, (48, 96, 16, 64)),
        (1, 2, cell < 24, -40, (24, 72, -8, 40)),
    ):
        slab = owner[3 + by]
        for ct in range(3):
            half = gathered_ref[slab, 6 + ct // 2]
            for q in range(2):
                sides_ref[side, 4 * ct + q] = gathered_ref[slab, 2 * ct + q]
                moved = [roll(half, turns[2 * q + n] - (64 if ct == 1 else 0)) for n in range(2)]
                sides_ref[side, 4 * ct + q + 2] = jnp.where(
                    in_place,
                    roll(gathered_ref[slab, 2 * ct + q], turn),
                    jnp.where(left_half, moved[0], moved[1]),
                )

    for bx in (0, 2):
        for by in range(3):
            for ct in range(3):
                tile = gathered_ref[owner[3 * bx + by], 6 + ct // 2]
                ends_ref[3 * bx // 2 + by, ct] = roll(tile, -64 * (ct % 2))

    def placed(ct, bx, i):
        if bx == 1:
            tile, half = 4 * ct + i // 2, i % 2
            parts = [sides_ref[0, tile], own_ref[tile], sides_ref[1, tile]]
        elif i == (3 if bx == 0 else 4):
            half = 0
            parts = [ends_ref[3 * bx // 2 + by, ct] for by in range(3)]
        else:
            tile, half = 2 * ct + (i // 2 - 2 if bx == 0 else i // 2), i % 2
            parts = [gathered_ref[owner[3 * bx + by], tile] for by in range(3)]
        outer = 96 - 64 * half
        return roll(parts[0], outer), roll(parts[1], 32 - 64 * half), roll(parts[2], outer)

    zero = jnp.zeros((16, LANES), bf16)

    for plane in range(18):
        bx, i = (plane + 3) // 8, (plane + 3) % 8
        for ct in range(3):
            before, middle, after = placed(ct, bx, i)
            main = jnp.where(low, before, jnp.where(mid, middle, after)) * main_masks[bx]
            edge = jnp.where(left_half, after, before) * edge_masks[bx]
            for c in (-1, 0, 1):
                if c == 0:
                    main_c, edge_c = main, edge
                else:
                    keep = depth >= 1 if c == 1 else depth <= 6
                    main_c, edge_c = jnp.where(keep, main, zero), jnp.where(keep, edge, zero)
                for b in (-1, 0, 1):
                    step = 8 * b + c
                    if b == 1:
                        source = jnp.where(lane < step, edge_c, main_c)
                    elif b == -1:
                        source = jnp.where(lane >= LANES + step, edge_c, main_c)
                    else:
                        source = main_c
                    row = (3 * (b + 1) + c + 1) * C + 16 * ct
                    x9_ref[row : row + 16, LANES * plane : LANES * (plane + 1)] = (
                        roll(source, -step) if step else source
                    )

    def plane_cols(plane):
        return slice(LANES * plane, LANES * (plane + 1))

    def summed(plane, stride):
        return (
            product_ref[0:C, plane_cols(plane)]
            + product_ref[C : 2 * C, plane_cols(plane + stride)]
            + product_ref[2 * C : 3 * C, plane_cols(plane + 2 * stride)]
        )

    for n in range(3):
        cols = slice(768 * n, 768 * (n + 1))
        product_ref[:, cols] = matmul(w1_ref[...], x9_ref[:, cols])

    for plane in range(16):
        bx = (plane + 4) // 8
        pre = summed(plane, 1)
        negative = jnp.exp(jnp.minimum(pre, 0.0))
        if 4 <= plane < 12:
            slope1_ref[:, plane_cols(plane - 4)] = negative
        hidden = (jnp.maximum(pre, 0.0) + (negative - 1.0)) * masks[bx]
        hidden = hidden.astype(bf16)
        for c in (-1, 0, 1):
            if c == 0:
                source = hidden
            else:
                keep = depth48 >= 2 if c == 1 else depth48 <= 5
                source = jnp.where(keep, hidden, jnp.zeros((C, LANES), bf16))
            for b in (-1, 0, 1):
                step = 16 * b + 2 * c
                row = (3 * (b + 1) + c + 1) * C
                h9_ref[row : row + C, plane_cols(plane)] = roll(source, -step) if step else source

    for n in range(4):
        cols = slice(512 * n, 512 * (n + 1))
        product_ref[:, cols] = matmul(w2_ref[...], h9_ref[:, cols])

    for plane in range(12):
        bx = (plane + 6) // 8
        pre = summed(plane, 2)
        negative = jnp.exp(jnp.minimum(pre, 0.0))
        slope2_ref[:, plane_cols(plane)] = negative * masks[bx]
        hidden = (jnp.maximum(pre, 0.0) + (negative - 1.0)) * masks[bx]
        hid2_ref[:, plane_cols(plane)] = hidden.astype(jnp.bfloat16)

    logits = matmul(h_ref[...], hid2_ref[...])
    targets = []
    for bx, half in ((0, 1), (1, 0), (1, 1), (2, 1)):
        if bx == 1:
            before = roll(gathered_ref[owner[3], 7], -48 - 16 * half)
            middle = roll(own_ref[12], 32 - 64 * half)
            after = roll(gathered_ref[owner[5], 7], 32 - 16 * half)
        else:
            parts = [gathered_ref[owner[3 * bx + by], 7] for by in range(3)]
            before, middle, after = roll(parts[0], 32), roll(parts[1], -32), roll(parts[2], 32)
        cells = jnp.where(low, before, jnp.where(mid, middle, after))
        targets.append(cells.astype(jnp.float32))
    grads = []
    for plane in range(12):
        bx, i = (plane + 6) // 8, (plane + 6) % 8
        value = logits[:, plane_cols(plane)]
        if bx == 1:
            wanted = targets[1 + i % 2][4 * (i // 2) : 4 * (i // 2) + 4]
        else:
            wanted = targets[0 if bx == 0 else 3][4 * (i % 2) : 4 * (i % 2) + 4]
        wanted = jnp.concatenate([wanted, jnp.zeros((12, LANES), jnp.float32)], axis=0)
        sigmoid = 1.0 / (1.0 + jnp.exp(-value))
        grads.append((sigmoid - wanted) * masks[bx] * scale)
    for q in range(4):
        first = roll(logits[:, plane_cols(2 + 2 * q)], -32)
        second = roll(logits[:, plane_cols(3 + 2 * q)], 32)
        logits_ref[:, plane_cols(q)] = jnp.where(left_half, first, second)[0:8]

    grad_logit = jnp.concatenate(grads, axis=1).astype(jnp.bfloat16)
    back = matmul(ht_ref[...], grad_logit)
    grad2_ref[...] = (back * slope2_ref[...]).astype(jnp.bfloat16)
    own_grads = jnp.concatenate([grads[2 + x] * own_row for x in range(8)], axis=1)
    head_part = matmul_lanes(hid2_ref[:, 2 * LANES : 10 * LANES], own_grads.astype(jnp.bfloat16))

    own_bf16 = jnp.broadcast_to(own_row, (C, LANES)).astype(bf16)
    shifted_ref[...] = jnp.zeros_like(shifted_ref)
    for a in range(3):
        for x in range(8):
            shifted_ref[C * a : C * (a + 1), plane_cols(x + 2 * a)] = (
                grad2_ref[:, plane_cols(x + 2)] * own_bf16
            )
    second_part = matmul_lanes(h9_ref[:, 2 * LANES : 14 * LANES], shifted_ref[...]).T

    for a in range(3):
        for x in range(8):
            shifted_ref[C * a : C * (a + 1), plane_cols(x)] = grad2_ref[:, plane_cols(x + 4 - 2 * a)]
    for n in range(2):
        cols = slice(512 * n, 512 * (n + 1))
        back_ref[:, cols] = matmul(w2t_ref[...], shifted_ref[:, cols])
    grad1 = []
    for x in range(8):
        total = jnp.zeros((C, LANES), jnp.float32)
        for c in (-1, 0, 1):
            part = jnp.zeros((C, LANES), jnp.float32)
            for b in (-1, 0, 1):
                row = (3 * (b + 1) + c + 1) * C
                step = 16 * b + 2 * c
                piece = back_ref[row : row + C, plane_cols(x)]
                part += roll(piece, step) if step else piece
            if c:
                part = jnp.where(depth48 >= 2 if c == 1 else depth48 <= 5, part, 0.0)
            total += part
        grad1.append((total * slope1_ref[:, plane_cols(x)] * own_row).astype(jnp.bfloat16))

    shifted_ref[...] = jnp.zeros_like(shifted_ref)
    for a in range(3):
        for x in range(8):
            shifted_ref[C * a : C * (a + 1), plane_cols(x + a)] = grad1[x]
    first_part = matmul_lanes(
        x9_ref[:, 4 * LANES : 14 * LANES], shifted_ref[:, 0 : 10 * LANES]
    ).T

    first_core = (lax.axis_index("dp") & 1) == 0
    head_part = jnp.concatenate([head_part, jnp.zeros((24, 16), jnp.float32)], axis=0)
    nothing = jnp.zeros((72, 16), jnp.float32)
    ends = []
    for part, extra in ((first_part, nothing), (second_part, head_part)):
        tail = jnp.concatenate([part[0:72, 384:], part[72:144, 384:], extra, nothing], axis=1)
        ends.append(jnp.concatenate([tail, jnp.zeros((8, LANES), jnp.float32)], axis=0))
    pieces = [(first_part[:, plane_cols(q)], second_part[:, plane_cols(q)]) for q in range(3)]
    row = 0
    for first, second in pieces + [tuple(ends)]:
        rows = slice(row, row + first.shape[0])
        keep_ref[rows, :] = jnp.where(first_core, first, second)
        send_ref[rows, :] = jnp.where(first_core, second, first)
        row += first.shape[0]


def add_kernel(mine_ref, other_ref, out_ref):
    out_ref[...] = (mine_ref[...] + other_ref[...]).astype(jnp.bfloat16)


def sum_kernel(parts_ref, out_ref):
    total = parts_ref[0].astype(jnp.float32)
    for s in range(1, parts_ref.shape[0]):
        total += parts_ref[s].astype(jnp.float32)
    total = total.astype(jnp.bfloat16)
    for s in range(out_ref.shape[0]):
        out_ref[s] = total


def unpack_kernel(mine_ref, other_ref, logits_ref, first_ref, second_ref, head_ref, out_ref):
    out_ref[:, 0, :] = logits_ref[0:3, :]
    first_core = (lax.axis_index("dp") & 1) == 0
    mine, other = mine_ref[...], other_ref[...]
    for k, out in ((0, first_ref), (1, second_ref)):
        half = jnp.where(first_core, other if k else mine, mine if k else other)
        half = half.astype(jnp.float32)
        tail = jnp.concatenate([half[432:504, 0:C], half[432:504, C : 2 * C]], axis=0)
        tiles = [half[144 * q : 144 * (q + 1), :] for q in range(3)]
        whole = jnp.concatenate(tiles + [tail], axis=1)
        for a in range(3):
            for t in range(9):
                out[9 * a + t] = whole[C * a : C * (a + 1), C * t : C * (t + 1)]
        if k:
            head_ref[...] = half[432 : 432 + C, 96:112].T[0:3]


def on_device_flat(features, device_block, conv_first, conv_second, head_weight, targets):
    space_count = lax.axis_size("space")
    device_count = lax.axis_size("dp") * space_count
    bf16, f32 = jnp.bfloat16, jnp.float32
    small = pltpu.CompilerParams(vmem_limit_bytes=8 * 1024 * 1024)
    shape = jax.ShapeDtypeStruct
    vmem = pl.BlockSpec(memory_space=pltpu.VMEM)

    def swap(values, mask):
        return lax.ppermute(values, "space", [(s, s ^ mask) for s in range(space_count)])

    mate_targets, mate_features = swap(targets, 1), swap(features, 1)
    head, head_t = pl.pallas_call(
        head_kernel,
        out_shape=(shape((16, C), bf16), shape((C, 16), bf16)),
        in_specs=[vmem],
        out_specs=(vmem,) * 2,
        compiler_params=small,
        cost_estimate=pl.CostEstimate(flops=1_000_000, bytes_accessed=2_000_000, transcendentals=0),
        name="lay_out_head",
    )(head_weight)
    lane = pl.pallas_call(
        lanes_kernel,
        out_shape=shape((16, LANES), jnp.int32),
        out_specs=vmem,
        compiler_params=small,
        cost_estimate=pl.CostEstimate(flops=0, bytes_accessed=2_000_000, transcendentals=0),
        name="lane_indices",
    )()
    own, own_slabs = pl.pallas_call(
        pack_own_kernel,
        out_shape=(shape((13, 16, LANES), bf16), shape((3, 8, 16, LANES), bf16)),
        in_specs=[vmem] * 4,
        out_specs=(vmem,) * 2,
        scratch_shapes=[pltpu.VMEM((4, 8, 16, LANES), bf16)],
        compiler_params=small,
        cost_estimate=pl.CostEstimate(flops=1_000_000, bytes_accessed=2_000_000, transcendentals=0),
        name="pack_own",
    )(device_block, features[0, 0], targets[0].transpose(1, 0, 2), lane)
    mate_slab, *pairs = pl.pallas_call(
        pack_mate_kernel,
        out_shape=(
            shape((8, 16, LANES), bf16),
            *[shape((2, 8, 16, LANES), bf16) for _ in PARTNERS],
        ),
        in_specs=[vmem] * 4,
        out_specs=(vmem,) * 4,
        scratch_shapes=[pltpu.VMEM((4, 8, 16, LANES), bf16)],
        compiler_params=small,
        cost_estimate=pl.CostEstimate(flops=1_000_000, bytes_accessed=2_000_000, transcendentals=0),
        name="pack_mate",
    )(device_block, mate_features[0, 0], mate_targets[0].transpose(1, 0, 2), own_slabs)
    pairs = [swap(pair, mask) for pair, mask in zip(pairs, PARTNERS)]

    w1, owners, masks = pl.pallas_call(
        prepare_kernel,
        out_shape=(
            shape((3 * C, 9 * C), bf16),
            shape((1, LANES), jnp.int32),
            shape((8, LANES), f32),
        ),
        in_specs=[vmem] * 2,
        out_specs=(vmem,) * 3,
        scratch_shapes=[pltpu.SMEM((2, 16), jnp.int32)],
        compiler_params=small,
        cost_estimate=pl.CostEstimate(flops=2_000_000, bytes_accessed=4_000_000, transcendentals=0),
        name="prepare",
    )(device_block, conv_first.transpose(1, 0, 2))
    w2, w2t = pl.pallas_call(
        second_kernel,
        out_shape=(shape((3 * C, 9 * C), bf16), shape((9 * C, 3 * C), bf16)),
        in_specs=[vmem],
        out_specs=(vmem,) * 2,
        compiler_params=small,
        cost_estimate=pl.CostEstimate(flops=2_000_000, bytes_accessed=4_000_000, transcendentals=0),
        name="second_weights",
    )(conv_second.transpose(1, 0, 2))

    scale = (device_count * 3 * CELLS) ** (-0.5)
    logits, keep, send = pl.pallas_call(
        functools.partial(crop_kernel, scale),
        out_shape=(shape((8, CELLS), f32), shape((HALF, LANES), f32), shape((HALF, LANES), f32)),
        in_specs=[vmem] * 12,
        out_specs=(vmem,) * 3,
        scratch_shapes=[
            pltpu.VMEM((space_count, 8, 16, LANES), bf16),
            pltpu.VMEM((2, 12, 16, LANES), bf16),
            pltpu.VMEM((6, 3, 16, LANES), bf16),
            pltpu.VMEM((9 * C, 18 * LANES), bf16),
            pltpu.VMEM((9 * C, 16 * LANES), bf16),
            pltpu.VMEM((3 * C, 18 * LANES), f32),
            pltpu.VMEM((C, 8 * LANES), f32),
            pltpu.VMEM((C, 12 * LANES), f32),
            pltpu.VMEM((C, 12 * LANES), bf16),
            pltpu.VMEM((C, 12 * LANES), bf16),
            pltpu.VMEM((3 * C, 12 * LANES), bf16),
            pltpu.VMEM((9 * C, 8 * LANES), f32),
        ],
        compiler_params=pltpu.CompilerParams(vmem_limit_bytes=20 * 1024 * 1024),
        name="forward_backward",
    )(owners, masks, own, mate_slab, *pairs, w1, w2, w2t, head, head_t)

    dp_count = lax.axis_size("dp")

    def swap_cores(values):
        return lax.ppermute(values, "dp", [(d, d ^ 1) for d in range(dp_count)])

    peers = device_count // 2
    groups = [
        [d * space_count + s for d in range(core, dp_count, 2) for s in range(space_count)]
        for core in range(2)
    ]

    def exchange(values):
        return lax.all_to_all(
            values, ("dp", "space"), 0, 0, axis_index_groups=groups, tiled=True
        )

    def step(kernel, out, *operands):
        return pl.pallas_call(
            kernel,
            out_shape=out,
            in_specs=[vmem] * len(operands),
            out_specs=vmem,
            compiler_params=small,
            name="gradient_sum",
        )(*operands)

    term = step(add_kernel, shape((HALF, LANES), bf16), keep, swap_cores(send))
    pieces = shape((peers, HALF // peers, LANES), bf16)
    total = exchange(step(sum_kernel, pieces, exchange(term.reshape(pieces.shape))))
    total = total.reshape(HALF, LANES)
    grad_first, grad_second, grad_head, logits = pl.pallas_call(
        unpack_kernel,
        out_shape=(
            shape((27, C, C), f32),
            shape((27, C, C), f32),
            shape((3, C), f32),
            shape((3, 1, CELLS), f32),
        ),
        in_specs=[vmem] * 3,
        out_specs=(vmem,) * 4,
        compiler_params=small,
        name="unpack_gradients",
    )(total, swap_cores(total), logits)
    return (
        logits.transpose(1, 0, 2)[None],
        grad_first.transpose(1, 0, 2),
        grad_second.transpose(1, 0, 2),
        grad_head,
    )


def solution(mesh):
    in_specs = (
        P("dp", "space", None, None),
        P("dp", None),
        P(),
        P(),
        P(),
        P("dp", "space", None, None),
    )
    out_specs = (P("dp", "space", None, None), P(), P(), P())
    flat = mesh.shape["space"] == 8 and mesh.shape["dp"] in (2, 4)
    return jax.shard_map(
        on_device_flat if flat else on_device_deep,
        mesh=mesh,
        in_specs=in_specs,
        out_specs=out_specs,
        check_vma=False,
    )
```

```python
import functools

import jax
import jax.numpy as jnp
from jax import lax
from jax.experimental import pallas as pl
from jax.experimental.pallas import tpu as pltpu
from jax.sharding import PartitionSpec as P

BS = 8


tap_offsets = [
    (tap_index // 9 - 1, tap_index // 3 % 3 - 1, tap_index % 3 - 1) for tap_index in range(27)
]


def elu_pair(values):
    negative = jnp.exp(jnp.minimum(values, 0.0))
    return (jnp.where(values > 0, values, negative - 1.0), jnp.where(values > 0, 1.0, negative))


def neighbor_tables(device_block):
    space_count = lax.axis_size("space")
    depth_z = space_count // 8
    self_index = lax.axis_index("space")
    blocks = device_block[0]
    coords = jnp.stack([blocks // (4 * depth_z), blocks // depth_z % 4, blocks % depth_z])
    own_coords = lax.dynamic_index_in_dim(coords, self_index, 1, keepdims=False)
    offsets = jnp.array(tap_offsets, jnp.int32)
    limits = jnp.array([4, 4, depth_z], jnp.int32)
    wanted = own_coords[None, :] + offsets
    inside = jnp.all((wanted >= 0) & (wanted < limits[None, :]), axis=1) & (jnp.arange(27) != 13)
    wanted_id = (wanted[:, 0] * 4 + wanted[:, 1]) * depth_z + wanted[:, 2]
    matches = (blocks[None, :] == wanted_id[:, None]) & inside[:, None]
    devices = jnp.arange(space_count, dtype=jnp.int32)
    owner_row = jnp.sum(jnp.where(matches, devices[None, :], 0), axis=1)
    present = jnp.any(matches, axis=1)
    relative = coords - own_coords[:, None]
    adjacent = jnp.all(jnp.abs(relative) <= 1, axis=0) & (devices != self_index)
    send_tap = jnp.where(
        adjacent, (relative[0] + 1) * 9 + (relative[1] + 1) * 3 + relative[2] + 1, 13
    )
    return (owner_row, present, send_tap)


def region_slice(block_data, offset, depth_cells):
    span_list = []
    for step_value in offset:
        if step_value == 1:
            span_list.append(slice(BS - depth_cells, BS))
        elif step_value == -1:
            span_list.append(slice(0, depth_cells))
        else:
            span_list.append(slice(0, BS))
    return block_data[:, span_list[0], span_list[1], span_list[2]]


def surround(block_data, depth_cells, tables):
    owner_row, present, send_tap = tables
    channels = block_data.shape[0]
    length = depth_cells * BS * BS
    pieces = []
    for tap_index in range(27):
        if tap_index == 13:
            pieces.append(jnp.zeros((channels, length), block_data.dtype))
        else:
            region = region_slice(block_data, tap_offsets[tap_index], depth_cells).reshape(
                channels, -1
            )
            pieces.append(jnp.pad(region, ((0, 0), (0, length - region.shape[1]))))
    outgoing = jnp.stack(pieces)
    sending = outgoing[send_tap]
    by_source = lax.all_to_all(sending, "space", split_axis=0, concat_axis=0, tiled=True)
    incoming = jnp.where(
        present[:, None, None], by_source[owner_row], jnp.zeros((), block_data.dtype)
    )
    rows_x = []
    for step_x in range(3):
        rows_y = []
        for step_y in range(3):
            rows_z = []
            for step_z in range(3):
                tap_index = step_x * 9 + step_y * 3 + step_z
                if tap_index == 13:
                    rows_z.append(block_data)
                else:
                    extent_list = [
                        BS if step_value == 1 else depth_cells
                        for step_value in (step_x, step_y, step_z)
                    ]
                    count_cells = extent_list[0] * extent_list[1] * extent_list[2]
                    rows_z.append(
                        incoming[tap_index][:, :count_cells].reshape(
                            channels, extent_list[0], extent_list[1], extent_list[2]
                        )
                    )
            rows_y.append(jnp.concatenate(rows_z, axis=3))
        rows_x.append(jnp.concatenate(rows_y, axis=2))
    return jnp.concatenate(rows_x, axis=1)


def conv_padded(padded, kernel, dilation):
    result = lax.conv_general_dilated(
        padded[None],
        kernel,
        (1, 1, 1),
        "VALID",
        rhs_dilation=(dilation, dilation, dilation),
        dimension_numbers=("NCDHW", "OIDHW", "NCDHW"),
        preferred_element_type=jnp.float32,
    )
    return result[0].reshape(kernel.shape[0], BS * BS * BS)


def kernel_grad(padded, grad_rows, dilation):
    channels = padded.shape[0]
    outputs = grad_rows.shape[0]
    grad_block = grad_rows.reshape(outputs, 1, BS, BS, BS)
    result = lax.conv_general_dilated(
        padded[None],
        grad_block,
        (dilation, dilation, dilation),
        "VALID",
        dimension_numbers=("CNDHW", "OIDHW", "NCDHW"),
        preferred_element_type=jnp.float32,
    )
    return result.reshape(channels, outputs, 27).transpose(1, 2, 0)


def on_device_deep(features, device_block, conv_first, conv_second, head_weight, targets):
    channels = features.shape[2]
    tables = neighbor_tables(device_block)
    kernel_first = conv_first.reshape(channels, 3, 3, 3, channels).transpose(0, 4, 1, 2, 3)
    kernel_second = conv_second.reshape(channels, 3, 3, 3, channels).transpose(0, 4, 1, 2, 3)
    block_in = features[0, 0].reshape(channels, BS, BS, BS)
    padded_in = surround(block_in, 1, tables)
    pre_first = conv_padded(padded_in, kernel_first, 1)
    act_first, slope_first = elu_pair(pre_first)
    hid_first = act_first.astype(jnp.bfloat16)
    padded_first = surround(hid_first.reshape(channels, BS, BS, BS), 2, tables)
    pre_second = conv_padded(padded_first, kernel_second, 2)
    act_second, slope_second = elu_pair(pre_second)
    hid_second = act_second.astype(jnp.bfloat16)
    logits = jnp.dot(head_weight, hid_second, preferred_element_type=jnp.float32)
    scale = (lax.axis_size("dp") * lax.axis_size("space") * 3 * BS * BS * BS) ** (-0.5)
    grad_logit = ((jax.nn.sigmoid(logits) - targets[0, 0].astype(jnp.float32)) * scale).astype(
        jnp.bfloat16
    )
    grad_head = lax.dot_general(
        grad_logit, hid_second, (((1,), (1,)), ((), ())), preferred_element_type=jnp.float32
    )
    back_second = lax.dot_general(
        head_weight, grad_logit, (((0,), (0,)), ((), ())), preferred_element_type=jnp.float32
    )
    grad_pre_second = (back_second * slope_second).astype(jnp.bfloat16)
    grad_second = kernel_grad(padded_first, grad_pre_second, 2)
    padded_grad = surround(grad_pre_second.reshape(channels, BS, BS, BS), 2, tables)
    kernel_back = jnp.transpose(kernel_second[:, :, ::-1, ::-1, ::-1], (1, 0, 2, 3, 4))
    back_first = conv_padded(padded_grad, kernel_back, 2)
    grad_pre_first = (back_first * slope_first).astype(jnp.bfloat16)
    grad_first = kernel_grad(padded_in, grad_pre_first, 1)
    grad_first, grad_second, grad_head = lax.psum(
        (grad_first, grad_second, grad_head), ("dp", "space")
    )
    return (logits[None, None], grad_first, grad_second, grad_head)


C = 48
CELLS = 512
HALF = 512
LANES = 128


def lanes(rows=1):
    return lax.broadcasted_iota(jnp.int32, (rows, LANES), 1)


def roll(values, shift):
    return pltpu.roll(values, shift % LANES, 1) if shift % LANES else values


def listed_blocks(block_ref, me):
    ids = block_ref[...].astype(jnp.float32)
    index = lax.broadcasted_iota(jnp.int32, ids.shape, 1)
    return [
        jnp.sum(jnp.where(index == (me ^ k), ids, 0.0)).astype(jnp.int32)
        for k in range(ids.shape[1])
    ]


def apart(source, target):
    return (target >> 2) - (source >> 2), (target & 3) - (source & 3)


PARTNERS = (4, 2, 6)


def block_tiles(features_ref, targets_ref):
    tiles = [
        [features_ref[16 * ct : 16 * (ct + 1), LANES * q : LANES * (q + 1)] for q in range(4)]
        for ct in range(3)
    ]
    targets = targets_ref[:, 0, :].astype(jnp.float32)
    targets = jnp.concatenate([targets, jnp.zeros((1, CELLS), jnp.float32)], axis=0)
    return tiles, [targets[:, LANES * q : LANES * (q + 1)] for q in range(4)]


def write_cases(tiles, rows, cases_ref, lane):
    left = lane < 64
    cell = lane & 63
    target_tile = jnp.concatenate(rows, axis=0)

    def write(case, pairs, halves, wanted):
        for ct in range(3):
            cases_ref[case, 2 * ct] = pairs[ct][0]
            cases_ref[case, 2 * ct + 1] = pairs[ct][1]
        cases_ref[case, 6] = jnp.where(left, halves[0], halves[1])
        cases_ref[case, 7] = jnp.where(left, halves[2], wanted.astype(jnp.bfloat16))

    for case, pair, single, q in ((0, (2, 3), 1, 3), (1, (0, 1), 2, 0)):
        turns = (64, 0, 64) if case == 0 else (0, 64, 0)
        halves = [roll(tiles[ct][single], turns[ct]) for ct in range(3)]
        both = [roll(rows[q], 64), rows[q], jnp.zeros((8, LANES), jnp.float32)]
        wanted = jnp.concatenate(both, axis=0)
        write(case, [(t[pair[0]], t[pair[1]]) for t in tiles], halves, wanted)
    for case, spare, turn, turns, target_turns in (
        (2, cell < 24, -24, (-48, -96, -16, -64), (16, -32)),
        (3, cell >= 40, 40, (-24, -72, 8, -40), (64, 16)),
    ):
        pairs, halves = [], []
        for ct, t in enumerate(tiles):
            pairs.append([jnp.where(spare, roll(t[q + 2], turn), t[q]) for q in range(2)])
            moved = [roll(t[2 + n // 2], turns[n] + (64 if ct == 1 else 0)) for n in range(4)]
            half = jnp.where(cell < 16, moved[0], jnp.where(cell < 32, moved[1], moved[2]))
            halves.append(jnp.where(cell < 48, half, moved[3]))
        wanted = [roll(target_tile, n) for n in target_turns]
        write(case, pairs, halves, jnp.where(lane < 80, wanted[0], wanted[1]))


def case_of(source, target):
    dx, dy = apart(source, target)
    return jnp.where(dx > 0, 0, jnp.where(dx < 0, 1, jnp.where(dy > 0, 2, 3)))


def head_kernel(head_ref, h_ref, ht_ref):
    head = head_ref[...].astype(jnp.float32)
    head = jnp.concatenate([head, jnp.zeros((13, C), jnp.float32)], axis=0)
    h_ref[...] = head.astype(jnp.bfloat16)
    ht_ref[...] = head.T.astype(jnp.bfloat16)


def lanes_kernel(out_ref):
    out_ref[...] = lanes(16)


def pack_own_kernel(
    block_ref, features_ref, targets_ref, lane_ref, own_ref, slabs_ref, cases_ref
):
    blocks = listed_blocks(block_ref, lax.axis_index("space"))
    tiles, rows = block_tiles(features_ref, targets_ref)
    for ct in range(3):
        for q in range(4):
            own_ref[4 * ct + q] = tiles[ct][q]
    own_ref[12] = jnp.concatenate(rows, axis=0).astype(jnp.bfloat16)
    write_cases(tiles, rows, cases_ref, lane_ref[...])
    for n, k in enumerate(PARTNERS):
        slabs_ref[n] = cases_ref[case_of(blocks[0], blocks[k])]


def pack_mate_kernel(block_ref, features_ref, targets_ref, slabs_ref, mate_ref, *refs):
    *pair_refs, cases_ref = refs
    blocks = listed_blocks(block_ref, lax.axis_index("space"))
    write_cases(*block_tiles(features_ref, targets_ref), cases_ref, lanes(16))
    mate_ref[...] = cases_ref[case_of(blocks[1], blocks[0])]
    for n, (k, ref) in enumerate(zip(PARTNERS, pair_refs)):
        ref[0] = slabs_ref[n]
        ref[1] = cases_ref[case_of(blocks[1], blocks[k])]


def stacked_taps(ref):
    rows = []
    for a in range(3):
        taps = [ref[9 * a + t] for t in range(9)]
        rows.append(jnp.concatenate(taps, axis=1))
    return jnp.concatenate(rows, axis=0)


def second_kernel(second_ref, w2_ref, w2t_ref):
    whole = stacked_taps(second_ref)
    w2_ref[...] = whole
    w2t_ref[...] = whole.T


def prepare_kernel(block_ref, first_ref, w1_ref, owners_ref, masks_ref, table_ref):
    w1_ref[...] = stacked_taps(first_ref)

    blocks = listed_blocks(block_ref, lax.axis_index("space"))
    for slot in range(10):
        table_ref[0, slot] = 1
        table_ref[1, slot] = 0
    table_ref[1, 4] = 1
    for k in range(1, len(blocks)):
        dx, dy = apart(blocks[0], blocks[k])
        near = (dx >= -1) & (dx <= 1) & (dy >= -1) & (dy <= 1)
        slot = jnp.where(near, dx * 3 + dy + 4, 9)
        table_ref[0, slot] = k
        table_ref[1, slot] = 1
    lane = lanes()
    there = [table_ref[1, q].astype(jnp.float32) for q in range(9)]
    owners = jnp.zeros((1, LANES), jnp.int32)
    for q in range(9):
        owners = jnp.where(lane == q, table_ref[0, q], owners)
    owners_ref[...] = owners
    for bx in range(3):
        before, middle, after = there[3 * bx : 3 * bx + 3]
        masks_ref[bx : bx + 1, :] = jnp.where(
            lane < 32, before, jnp.where(lane < 96, middle, after)
        )
        masks_ref[bx + 3 : bx + 4, :] = jnp.where(lane < 64, after, before)


def matmul(left, right):
    return lax.dot_general(
        left, right, (((1,), (0,)), ((), ())), preferred_element_type=jnp.float32
    )


def matmul_lanes(left, right):
    return lax.dot_general(
        left, right, (((1,), (1,)), ((), ())), preferred_element_type=jnp.float32
    )


def crop_kernel(scale, owners_ref, masks_ref, own_ref, mate_ref, *refs):
    crop_body(scale, owners_ref, masks_ref, own_ref, mate_ref, refs[:3], *refs[3:])


def crop_body(
    scale,
    owners_ref,
    masks_ref,
    own_ref,
    mate_ref,
    pairs,
    w1_ref,
    w2_ref,
    w2t_ref,
    h_ref,
    ht_ref,
    logits_ref,
    keep_ref,
    send_ref,
    gathered_ref,
    sides_ref,
    ends_ref,
    x9_ref,
    h9_ref,
    product_ref,
    slope1_ref,
    slope2_ref,
    hid2_ref,
    grad2_ref,
    shifted_ref,
    back_ref,
):
    gathered_ref[1] = mate_ref[...]
    for k, pair in zip(PARTNERS, pairs):
        for j in range(2):
            gathered_ref[k + j] = pair[j]
    owners = owners_ref[...]
    owner = [owners[0, q] for q in range(9)]

    bf16 = jnp.bfloat16
    lane = lanes(16)
    depth = lane & 7
    depth48 = lanes(C) & 7
    low, mid, left_half = lane < 32, lane < 96, lane < 64
    masks = [masks_ref[bx : bx + 1, :] for bx in range(3)]
    main_masks = [jnp.broadcast_to(mask, (16, LANES)).astype(bf16) for mask in masks]
    edge_masks = [
        jnp.broadcast_to(masks_ref[bx + 3 : bx + 4, :], (16, LANES)).astype(bf16)
        for bx in range(3)
    ]
    own_row = jnp.where((lane >= 32) & mid, 1.0, 0.0)[0:1]

    cell = lane & 63
    for side, by, in_place, turn, turns in (
        (0, 0, cell < 48, 24, (48, 96, 16, 64)),
        (1, 2, cell < 24, -40, (24, 72, -8, 40)),
    ):
        slab = owner[3 + by]
        for ct in range(3):
            half = gathered_ref[slab, 6 + ct // 2]
            for q in range(2):
                sides_ref[side, 4 * ct + q] = gathered_ref[slab, 2 * ct + q]
                moved = [roll(half, turns[2 * q + n] - (64 if ct == 1 else 0)) for n in range(2)]
                sides_ref[side, 4 * ct + q + 2] = jnp.where(
                    in_place,
                    roll(gathered_ref[slab, 2 * ct + q], turn),
                    jnp.where(left_half, moved[0], moved[1]),
                )

    for bx in (0, 2):
        for by in range(3):
            for ct in range(3):
                tile = gathered_ref[owner[3 * bx + by], 6 + ct // 2]
                ends_ref[3 * bx // 2 + by, ct] = roll(tile, -64 * (ct % 2))

    def placed(ct, bx, i):
        if bx == 1:
            tile, half = 4 * ct + i // 2, i % 2
            parts = [sides_ref[0, tile], own_ref[tile], sides_ref[1, tile]]
        elif i == (3 if bx == 0 else 4):
            half = 0
            parts = [ends_ref[3 * bx // 2 + by, ct] for by in range(3)]
        else:
            tile, half = 2 * ct + (i // 2 - 2 if bx == 0 else i // 2), i % 2
            parts = [gathered_ref[owner[3 * bx + by], tile] for by in range(3)]
        outer = 96 - 64 * half
        return roll(parts[0], outer), roll(parts[1], 32 - 64 * half), roll(parts[2], outer)

    zero = jnp.zeros((16, LANES), bf16)

    for plane in range(18):
        bx, i = (plane + 3) // 8, (plane + 3) % 8
        for ct in range(3):
            before, middle, after = placed(ct, bx, i)
            main = jnp.where(low, before, jnp.where(mid, middle, after)) * main_masks[bx]
            edge = jnp.where(left_half, after, before) * edge_masks[bx]
            for c in (-1, 0, 1):
                if c == 0:
                    main_c, edge_c = main, edge
                else:
                    keep = depth >= 1 if c == 1 else depth <= 6
                    main_c, edge_c = jnp.where(keep, main, zero), jnp.where(keep, edge, zero)
                for b in (-1, 0, 1):
                    step = 8 * b + c
                    if b == 1:
                        source = jnp.where(lane < step, edge_c, main_c)
                    elif b == -1:
                        source = jnp.where(lane >= LANES + step, edge_c, main_c)
                    else:
                        source = main_c
                    row = (3 * (b + 1) + c + 1) * C + 16 * ct
                    x9_ref[row : row + 16, LANES * plane : LANES * (plane + 1)] = (
                        roll(source, -step) if step else source
                    )

    def plane_cols(plane):
        return slice(LANES * plane, LANES * (plane + 1))

    def summed(plane, stride):
        return (
            product_ref[0:C, plane_cols(plane)]
            + product_ref[C : 2 * C, plane_cols(plane + stride)]
            + product_ref[2 * C : 3 * C, plane_cols(plane + 2 * stride)]
        )

    for n in range(3):
        cols = slice(768 * n, 768 * (n + 1))
        product_ref[:, cols] = matmul(w1_ref[...], x9_ref[:, cols])

    for plane in range(16):
        bx = (plane + 4) // 8
        pre = summed(plane, 1)
        negative = jnp.exp(jnp.minimum(pre, 0.0))
        if 4 <= plane < 12:
            slope1_ref[:, plane_cols(plane - 4)] = negative
        hidden = (jnp.maximum(pre, 0.0) + (negative - 1.0)) * masks[bx]
        hidden = hidden.astype(bf16)
        for c in (-1, 0, 1):
            if c == 0:
                source = hidden
            else:
                keep = depth48 >= 2 if c == 1 else depth48 <= 5
                source = jnp.where(keep, hidden, jnp.zeros((C, LANES), bf16))
            for b in (-1, 0, 1):
                step = 16 * b + 2 * c
                row = (3 * (b + 1) + c + 1) * C
                h9_ref[row : row + C, plane_cols(plane)] = roll(source, -step) if step else source

    for n in range(4):
        cols = slice(512 * n, 512 * (n + 1))
        product_ref[:, cols] = matmul(w2_ref[...], h9_ref[:, cols])

    for plane in range(12):
        bx = (plane + 6) // 8
        pre = summed(plane, 2)
        negative = jnp.exp(jnp.minimum(pre, 0.0))
        slope2_ref[:, plane_cols(plane)] = negative * masks[bx]
        hidden = (jnp.maximum(pre, 0.0) + (negative - 1.0)) * masks[bx]
        hid2_ref[:, plane_cols(plane)] = hidden.astype(jnp.bfloat16)

    logits = matmul(h_ref[...], hid2_ref[...])
    targets = []
    for bx, half in ((0, 1), (1, 0), (1, 1), (2, 1)):
        if bx == 1:
            before = roll(gathered_ref[owner[3], 7], -48 - 16 * half)
            middle = roll(own_ref[12], 32 - 64 * half)
            after = roll(gathered_ref[owner[5], 7], 32 - 16 * half)
        else:
            parts = [gathered_ref[owner[3 * bx + by], 7] for by in range(3)]
            before, middle, after = roll(parts[0], 32), roll(parts[1], -32), roll(parts[2], 32)
        cells = jnp.where(low, before, jnp.where(mid, middle, after))
        targets.append(cells.astype(jnp.float32))
    grads = []
    for plane in range(12):
        bx, i = (plane + 6) // 8, (plane + 6) % 8
        value = logits[:, plane_cols(plane)]
        if bx == 1:
            wanted = targets[1 + i % 2][4 * (i // 2) : 4 * (i // 2) + 4]
        else:
            wanted = targets[0 if bx == 0 else 3][4 * (i % 2) : 4 * (i % 2) + 4]
        wanted = jnp.concatenate([wanted, jnp.zeros((12, LANES), jnp.float32)], axis=0)
        sigmoid = 1.0 / (1.0 + jnp.exp(-value))
        grads.append((sigmoid - wanted) * masks[bx] * scale)
    for q in range(4):
        first = roll(logits[:, plane_cols(2 + 2 * q)], -32)
        second = roll(logits[:, plane_cols(3 + 2 * q)], 32)
        logits_ref[:, plane_cols(q)] = jnp.where(left_half, first, second)[0:8]

    grad_logit = jnp.concatenate(grads, axis=1).astype(jnp.bfloat16)
    back = matmul(ht_ref[...], grad_logit)
    grad2_ref[...] = (back * slope2_ref[...]).astype(jnp.bfloat16)
    own_grads = jnp.concatenate([grads[2 + x] * own_row for x in range(8)], axis=1)
    head_part = matmul_lanes(hid2_ref[:, 2 * LANES : 10 * LANES], own_grads.astype(jnp.bfloat16))

    own_bf16 = jnp.broadcast_to(own_row, (C, LANES)).astype(bf16)
    shifted_ref[...] = jnp.zeros_like(shifted_ref)
    for a in range(3):
        for x in range(8):
            shifted_ref[C * a : C * (a + 1), plane_cols(x + 2 * a)] = (
                grad2_ref[:, plane_cols(x + 2)] * own_bf16
            )
    second_part = matmul_lanes(shifted_ref[...], h9_ref[:, 2 * LANES : 14 * LANES])

    for a in range(3):
        for x in range(8):
            shifted_ref[C * a : C * (a + 1), plane_cols(x)] = grad2_ref[:, plane_cols(x + 4 - 2 * a)]
    for n in range(2):
        cols = slice(512 * n, 512 * (n + 1))
        back_ref[:, cols] = matmul(w2t_ref[...], shifted_ref[:, cols])
    grad1 = []
    for x in range(8):
        total = jnp.zeros((C, LANES), jnp.float32)
        for c in (-1, 0, 1):
            part = jnp.zeros((C, LANES), jnp.float32)
            for b in (-1, 0, 1):
                row = (3 * (b + 1) + c + 1) * C
                step = 16 * b + 2 * c
                piece = back_ref[row : row + C, plane_cols(x)]
                part += roll(piece, step) if step else piece
            if c:
                part = jnp.where(depth48 >= 2 if c == 1 else depth48 <= 5, part, 0.0)
            total += part
        grad1.append((total * slope1_ref[:, plane_cols(x)] * own_row).astype(jnp.bfloat16))

    shifted_ref[...] = jnp.zeros_like(shifted_ref)
    for a in range(3):
        for x in range(8):
            shifted_ref[C * a : C * (a + 1), plane_cols(x + a)] = grad1[x]
    first_part = matmul_lanes(
        shifted_ref[:, 0 : 10 * LANES], x9_ref[:, 4 * LANES : 14 * LANES]
    )

    first_core = (lax.axis_index("dp") & 1) == 0
    head_part = jnp.concatenate([head_part, jnp.zeros((24, 16), jnp.float32)], axis=0)
    nothing = jnp.zeros((72, 16), jnp.float32)
    ends = []
    for part, extra in ((first_part, nothing), (second_part, head_part)):
        tail = jnp.concatenate([part[0:72, 384:], part[72:144, 384:], extra, nothing], axis=1)
        ends.append(jnp.concatenate([tail, jnp.zeros((8, LANES), jnp.float32)], axis=0))
    pieces = [(first_part[:, plane_cols(q)], second_part[:, plane_cols(q)]) for q in range(3)]
    row = 0
    for first, second in pieces + [tuple(ends)]:
        rows = slice(row, row + first.shape[0])
        keep_ref[rows, :] = jnp.where(first_core, first, second)
        send_ref[rows, :] = jnp.where(first_core, second, first)
        row += first.shape[0]


def add_kernel(mine_ref, other_ref, out_ref):
    out_ref[...] = (mine_ref[...] + other_ref[...]).astype(jnp.bfloat16)


def sum_kernel(parts_ref, out_ref):
    total = parts_ref[0].astype(jnp.float32)
    for s in range(1, parts_ref.shape[0]):
        total += parts_ref[s].astype(jnp.float32)
    total = total.astype(jnp.bfloat16)
    for s in range(out_ref.shape[0]):
        out_ref[s] = total


def unpack_kernel(mine_ref, other_ref, logits_ref, first_ref, second_ref, head_ref, out_ref):
    out_ref[:, 0, :] = logits_ref[0:3, :]
    first_core = (lax.axis_index("dp") & 1) == 0
    mine, other = mine_ref[...], other_ref[...]
    for k, out in ((0, first_ref), (1, second_ref)):
        half = jnp.where(first_core, other if k else mine, mine if k else other)
        half = half.astype(jnp.float32)
        tail = jnp.concatenate([half[432:504, 0:C], half[432:504, C : 2 * C]], axis=0)
        tiles = [half[144 * q : 144 * (q + 1), :] for q in range(3)]
        whole = jnp.concatenate(tiles + [tail], axis=1)
        for a in range(3):
            for t in range(9):
                out[9 * a + t] = whole[C * a : C * (a + 1), C * t : C * (t + 1)]
        if k:
            head_ref[...] = half[432 : 432 + C, 96:112].T[0:3]


def on_device_flat(features, device_block, conv_first, conv_second, head_weight, targets):
    space_count = lax.axis_size("space")
    device_count = lax.axis_size("dp") * space_count
    bf16, f32 = jnp.bfloat16, jnp.float32
    small = pltpu.CompilerParams(vmem_limit_bytes=8 * 1024 * 1024)
    shape = jax.ShapeDtypeStruct
    vmem = pl.BlockSpec(memory_space=pltpu.VMEM)

    def swap(values, mask):
        return lax.ppermute(values, "space", [(s, s ^ mask) for s in range(space_count)])

    mate_targets, mate_features = swap(targets, 1), swap(features, 1)
    head, head_t = pl.pallas_call(
        head_kernel,
        out_shape=(shape((16, C), bf16), shape((C, 16), bf16)),
        in_specs=[vmem],
        out_specs=(vmem,) * 2,
        compiler_params=small,
        cost_estimate=pl.CostEstimate(flops=1_000_000, bytes_accessed=2_000_000, transcendentals=0),
        name="lay_out_head",
    )(head_weight)
    lane = pl.pallas_call(
        lanes_kernel,
        out_shape=shape((16, LANES), jnp.int32),
        out_specs=vmem,
        compiler_params=small,
        cost_estimate=pl.CostEstimate(flops=0, bytes_accessed=2_000_000, transcendentals=0),
        name="lane_indices",
    )()
    own, own_slabs = pl.pallas_call(
        pack_own_kernel,
        out_shape=(shape((13, 16, LANES), bf16), shape((3, 8, 16, LANES), bf16)),
        in_specs=[vmem] * 4,
        out_specs=(vmem,) * 2,
        scratch_shapes=[pltpu.VMEM((4, 8, 16, LANES), bf16)],
        compiler_params=small,
        cost_estimate=pl.CostEstimate(flops=1_000_000, bytes_accessed=2_000_000, transcendentals=0),
        name="pack_own",
    )(device_block, features[0, 0], targets[0].transpose(1, 0, 2), lane)
    mate_slab, *pairs = pl.pallas_call(
        pack_mate_kernel,
        out_shape=(
            shape((8, 16, LANES), bf16),
            *[shape((2, 8, 16, LANES), bf16) for _ in PARTNERS],
        ),
        in_specs=[vmem] * 4,
        out_specs=(vmem,) * 4,
        scratch_shapes=[pltpu.VMEM((4, 8, 16, LANES), bf16)],
        compiler_params=small,
        cost_estimate=pl.CostEstimate(flops=1_000_000, bytes_accessed=2_000_000, transcendentals=0),
        name="pack_mate",
    )(device_block, mate_features[0, 0], mate_targets[0].transpose(1, 0, 2), own_slabs)
    pairs = [swap(pair, mask) for pair, mask in zip(pairs, PARTNERS)]

    w1, owners, masks = pl.pallas_call(
        prepare_kernel,
        out_shape=(
            shape((3 * C, 9 * C), bf16),
            shape((1, LANES), jnp.int32),
            shape((8, LANES), f32),
        ),
        in_specs=[vmem] * 2,
        out_specs=(vmem,) * 3,
        scratch_shapes=[pltpu.SMEM((2, 16), jnp.int32)],
        compiler_params=small,
        cost_estimate=pl.CostEstimate(flops=2_000_000, bytes_accessed=4_000_000, transcendentals=0),
        name="prepare",
    )(device_block, conv_first.transpose(1, 0, 2))
    w2, w2t = pl.pallas_call(
        second_kernel,
        out_shape=(shape((3 * C, 9 * C), bf16), shape((9 * C, 3 * C), bf16)),
        in_specs=[vmem],
        out_specs=(vmem,) * 2,
        compiler_params=small,
        cost_estimate=pl.CostEstimate(flops=2_000_000, bytes_accessed=4_000_000, transcendentals=0),
        name="second_weights",
    )(conv_second.transpose(1, 0, 2))

    scale = (device_count * 3 * CELLS) ** (-0.5)
    logits, keep, send = pl.pallas_call(
        functools.partial(crop_kernel, scale),
        out_shape=(shape((8, CELLS), f32), shape((HALF, LANES), f32), shape((HALF, LANES), f32)),
        in_specs=[vmem] * 12,
        out_specs=(vmem,) * 3,
        scratch_shapes=[
            pltpu.VMEM((space_count, 8, 16, LANES), bf16),
            pltpu.VMEM((2, 12, 16, LANES), bf16),
            pltpu.VMEM((6, 3, 16, LANES), bf16),
            pltpu.VMEM((9 * C, 18 * LANES), bf16),
            pltpu.VMEM((9 * C, 16 * LANES), bf16),
            pltpu.VMEM((3 * C, 18 * LANES), f32),
            pltpu.VMEM((C, 8 * LANES), f32),
            pltpu.VMEM((C, 12 * LANES), f32),
            pltpu.VMEM((C, 12 * LANES), bf16),
            pltpu.VMEM((C, 12 * LANES), bf16),
            pltpu.VMEM((3 * C, 12 * LANES), bf16),
            pltpu.VMEM((9 * C, 8 * LANES), f32),
        ],
        compiler_params=pltpu.CompilerParams(vmem_limit_bytes=20 * 1024 * 1024),
        name="forward_backward",
    )(owners, masks, own, mate_slab, *pairs, w1, w2, w2t, head, head_t)

    dp_count = lax.axis_size("dp")

    def swap_cores(values):
        return lax.ppermute(values, "dp", [(d, d ^ 1) for d in range(dp_count)])

    peers = device_count // 2
    groups = [
        [d * space_count + s for d in range(core, dp_count, 2) for s in range(space_count)]
        for core in range(2)
    ]

    def exchange(values):
        return lax.all_to_all(
            values, ("dp", "space"), 0, 0, axis_index_groups=groups, tiled=True
        )

    def step(kernel, out, *operands):
        return pl.pallas_call(
            kernel,
            out_shape=out,
            in_specs=[vmem] * len(operands),
            out_specs=vmem,
            compiler_params=small,
            name="gradient_sum",
        )(*operands)

    term = step(add_kernel, shape((HALF, LANES), bf16), keep, swap_cores(send))
    pieces = shape((peers, HALF // peers, LANES), bf16)
    total = exchange(step(sum_kernel, pieces, exchange(term.reshape(pieces.shape))))
    total = total.reshape(HALF, LANES)
    grad_first, grad_second, grad_head, logits = pl.pallas_call(
        unpack_kernel,
        out_shape=(
            shape((27, C, C), f32),
            shape((27, C, C), f32),
            shape((3, C), f32),
            shape((3, 1, CELLS), f32),
        ),
        in_specs=[vmem] * 3,
        out_specs=(vmem,) * 4,
        compiler_params=small,
        name="unpack_gradients",
    )(total, swap_cores(total), logits)
    return (
        logits.transpose(1, 0, 2)[None],
        grad_first.transpose(1, 0, 2),
        grad_second.transpose(1, 0, 2),
        grad_head,
    )


def solution(mesh):
    in_specs = (
        P("dp", "space", None, None),
        P("dp", None),
        P(),
        P(),
        P(),
        P("dp", "space", None, None),
    )
    out_specs = (P("dp", "space", None, None), P(), P(), P())
    flat = mesh.shape["space"] == 8 and mesh.shape["dp"] in (2, 4)
    return jax.shard_map(
        on_device_flat if flat else on_device_deep,
        mesh=mesh,
        in_specs=in_specs,
        out_specs=out_specs,
        check_vma=False,
    )
```

```python
import functools

import jax
import jax.numpy as jnp
from jax import lax
from jax.experimental import pallas as pl
from jax.experimental.pallas import tpu as pltpu
from jax.sharding import PartitionSpec as P

BS = 8


tap_offsets = [
    (tap_index // 9 - 1, tap_index // 3 % 3 - 1, tap_index % 3 - 1) for tap_index in range(27)
]


def elu_pair(values):
    negative = jnp.exp(jnp.minimum(values, 0.0))
    return (jnp.where(values > 0, values, negative - 1.0), jnp.where(values > 0, 1.0, negative))


def neighbor_tables(device_block):
    space_count = lax.axis_size("space")
    depth_z = space_count // 8
    self_index = lax.axis_index("space")
    blocks = device_block[0]
    coords = jnp.stack([blocks // (4 * depth_z), blocks // depth_z % 4, blocks % depth_z])
    own_coords = lax.dynamic_index_in_dim(coords, self_index, 1, keepdims=False)
    offsets = jnp.array(tap_offsets, jnp.int32)
    limits = jnp.array([4, 4, depth_z], jnp.int32)
    wanted = own_coords[None, :] + offsets
    inside = jnp.all((wanted >= 0) & (wanted < limits[None, :]), axis=1) & (jnp.arange(27) != 13)
    wanted_id = (wanted[:, 0] * 4 + wanted[:, 1]) * depth_z + wanted[:, 2]
    matches = (blocks[None, :] == wanted_id[:, None]) & inside[:, None]
    devices = jnp.arange(space_count, dtype=jnp.int32)
    owner_row = jnp.sum(jnp.where(matches, devices[None, :], 0), axis=1)
    present = jnp.any(matches, axis=1)
    relative = coords - own_coords[:, None]
    adjacent = jnp.all(jnp.abs(relative) <= 1, axis=0) & (devices != self_index)
    send_tap = jnp.where(
        adjacent, (relative[0] + 1) * 9 + (relative[1] + 1) * 3 + relative[2] + 1, 13
    )
    return (owner_row, present, send_tap)


def region_slice(block_data, offset, depth_cells):
    span_list = []
    for step_value in offset:
        if step_value == 1:
            span_list.append(slice(BS - depth_cells, BS))
        elif step_value == -1:
            span_list.append(slice(0, depth_cells))
        else:
            span_list.append(slice(0, BS))
    return block_data[:, span_list[0], span_list[1], span_list[2]]


def surround(block_data, depth_cells, tables):
    owner_row, present, send_tap = tables
    channels = block_data.shape[0]
    length = depth_cells * BS * BS
    pieces = []
    for tap_index in range(27):
        if tap_index == 13:
            pieces.append(jnp.zeros((channels, length), block_data.dtype))
        else:
            region = region_slice(block_data, tap_offsets[tap_index], depth_cells).reshape(
                channels, -1
            )
            pieces.append(jnp.pad(region, ((0, 0), (0, length - region.shape[1]))))
    outgoing = jnp.stack(pieces)
    sending = outgoing[send_tap]
    by_source = lax.all_to_all(sending, "space", split_axis=0, concat_axis=0, tiled=True)
    incoming = jnp.where(
        present[:, None, None], by_source[owner_row], jnp.zeros((), block_data.dtype)
    )
    rows_x = []
    for step_x in range(3):
        rows_y = []
        for step_y in range(3):
            rows_z = []
            for step_z in range(3):
                tap_index = step_x * 9 + step_y * 3 + step_z
                if tap_index == 13:
                    rows_z.append(block_data)
                else:
                    extent_list = [
                        BS if step_value == 1 else depth_cells
                        for step_value in (step_x, step_y, step_z)
                    ]
                    count_cells = extent_list[0] * extent_list[1] * extent_list[2]
                    rows_z.append(
                        incoming[tap_index][:, :count_cells].reshape(
                            channels, extent_list[0], extent_list[1], extent_list[2]
                        )
                    )
            rows_y.append(jnp.concatenate(rows_z, axis=3))
        rows_x.append(jnp.concatenate(rows_y, axis=2))
    return jnp.concatenate(rows_x, axis=1)


def conv_padded(padded, kernel, dilation):
    result = lax.conv_general_dilated(
        padded[None],
        kernel,
        (1, 1, 1),
        "VALID",
        rhs_dilation=(dilation, dilation, dilation),
        dimension_numbers=("NCDHW", "OIDHW", "NCDHW"),
        preferred_element_type=jnp.float32,
    )
    return result[0].reshape(kernel.shape[0], BS * BS * BS)


def kernel_grad(padded, grad_rows, dilation):
    channels = padded.shape[0]
    outputs = grad_rows.shape[0]
    grad_block = grad_rows.reshape(outputs, 1, BS, BS, BS)
    result = lax.conv_general_dilated(
        padded[None],
        grad_block,
        (dilation, dilation, dilation),
        "VALID",
        dimension_numbers=("CNDHW", "OIDHW", "NCDHW"),
        preferred_element_type=jnp.float32,
    )
    return result.reshape(channels, outputs, 27).transpose(1, 2, 0)


def on_device_deep(features, device_block, conv_first, conv_second, head_weight, targets):
    channels = features.shape[2]
    tables = neighbor_tables(device_block)
    kernel_first = conv_first.reshape(channels, 3, 3, 3, channels).transpose(0, 4, 1, 2, 3)
    kernel_second = conv_second.reshape(channels, 3, 3, 3, channels).transpose(0, 4, 1, 2, 3)
    block_in = features[0, 0].reshape(channels, BS, BS, BS)
    padded_in = surround(block_in, 1, tables)
    pre_first = conv_padded(padded_in, kernel_first, 1)
    act_first, slope_first = elu_pair(pre_first)
    hid_first = act_first.astype(jnp.bfloat16)
    padded_first = surround(hid_first.reshape(channels, BS, BS, BS), 2, tables)
    pre_second = conv_padded(padded_first, kernel_second, 2)
    act_second, slope_second = elu_pair(pre_second)
    hid_second = act_second.astype(jnp.bfloat16)
    logits = jnp.dot(head_weight, hid_second, preferred_element_type=jnp.float32)
    scale = (lax.axis_size("dp") * lax.axis_size("space") * 3 * BS * BS * BS) ** (-0.5)
    grad_logit = ((jax.nn.sigmoid(logits) - targets[0, 0].astype(jnp.float32)) * scale).astype(
        jnp.bfloat16
    )
    grad_head = lax.dot_general(
        grad_logit, hid_second, (((1,), (1,)), ((), ())), preferred_element_type=jnp.float32
    )
    back_second = lax.dot_general(
        head_weight, grad_logit, (((0,), (0,)), ((), ())), preferred_element_type=jnp.float32
    )
    grad_pre_second = (back_second * slope_second).astype(jnp.bfloat16)
    grad_second = kernel_grad(padded_first, grad_pre_second, 2)
    padded_grad = surround(grad_pre_second.reshape(channels, BS, BS, BS), 2, tables)
    kernel_back = jnp.transpose(kernel_second[:, :, ::-1, ::-1, ::-1], (1, 0, 2, 3, 4))
    back_first = conv_padded(padded_grad, kernel_back, 2)
    grad_pre_first = (back_first * slope_first).astype(jnp.bfloat16)
    grad_first = kernel_grad(padded_in, grad_pre_first, 1)
    grad_first, grad_second, grad_head = lax.psum(
        (grad_first, grad_second, grad_head), ("dp", "space")
    )
    return (logits[None, None], grad_first, grad_second, grad_head)


C = 48
CELLS = 512
HALF = 512
LANES = 128


def lanes(rows=1):
    return lax.broadcasted_iota(jnp.int32, (rows, LANES), 1)


def roll(values, shift):
    return pltpu.roll(values, shift % LANES, 1) if shift % LANES else values


def listed_blocks(block_ref, me):
    ids = block_ref[...].astype(jnp.float32)
    index = lax.broadcasted_iota(jnp.int32, ids.shape, 1)
    return [
        jnp.sum(jnp.where(index == (me ^ k), ids, 0.0)).astype(jnp.int32)
        for k in range(ids.shape[1])
    ]


def apart(source, target):
    return (target >> 2) - (source >> 2), (target & 3) - (source & 3)


PARTNERS = (4, 6, 2)


def block_tiles(features_ref, targets_ref):
    tiles = [
        [features_ref[16 * ct : 16 * (ct + 1), LANES * q : LANES * (q + 1)] for q in range(4)]
        for ct in range(3)
    ]
    targets = targets_ref[:, 0, :].astype(jnp.float32)
    targets = jnp.concatenate([targets, jnp.zeros((1, CELLS), jnp.float32)], axis=0)
    return tiles, [targets[:, LANES * q : LANES * (q + 1)] for q in range(4)]


def write_cases(tiles, rows, cases_ref, lane):
    left = lane < 64
    cell = lane & 63
    target_tile = jnp.concatenate(rows, axis=0)

    def write(case, pairs, halves, wanted):
        for ct in range(3):
            cases_ref[case, 2 * ct] = pairs[ct][0]
            cases_ref[case, 2 * ct + 1] = pairs[ct][1]
        cases_ref[case, 6] = jnp.where(left, halves[0], halves[1])
        cases_ref[case, 7] = jnp.where(left, halves[2], wanted.astype(jnp.bfloat16))

    for case, pair, single, q in ((0, (2, 3), 1, 3), (1, (0, 1), 2, 0)):
        turns = (64, 0, 64) if case == 0 else (0, 64, 0)
        halves = [roll(tiles[ct][single], turns[ct]) for ct in range(3)]
        both = [roll(rows[q], 64), rows[q], jnp.zeros((8, LANES), jnp.float32)]
        wanted = jnp.concatenate(both, axis=0)
        write(case, [(t[pair[0]], t[pair[1]]) for t in tiles], halves, wanted)
    for case, spare, turn, turns, target_turns in (
        (2, cell < 24, -24, (-48, -96, -16, -64), (16, -32)),
        (3, cell >= 40, 40, (-24, -72, 8, -40), (64, 16)),
    ):
        pairs, halves = [], []
        for ct, t in enumerate(tiles):
            pairs.append([jnp.where(spare, roll(t[q + 2], turn), t[q]) for q in range(2)])
            moved = [roll(t[2 + n // 2], turns[n] + (64 if ct == 1 else 0)) for n in range(4)]
            half = jnp.where(cell < 16, moved[0], jnp.where(cell < 32, moved[1], moved[2]))
            halves.append(jnp.where(cell < 48, half, moved[3]))
        wanted = [roll(target_tile, n) for n in target_turns]
        write(case, pairs, halves, jnp.where(lane < 80, wanted[0], wanted[1]))


def case_of(source, target):
    dx, dy = apart(source, target)
    return jnp.where(dx > 0, 0, jnp.where(dx < 0, 1, jnp.where(dy > 0, 2, 3)))


def head_kernel(head_ref, h_ref, ht_ref):
    head = head_ref[...].astype(jnp.float32)
    head = jnp.concatenate([head, jnp.zeros((13, C), jnp.float32)], axis=0)
    h_ref[...] = head.astype(jnp.bfloat16)
    ht_ref[...] = head.T.astype(jnp.bfloat16)


def lanes_kernel(out_ref):
    out_ref[...] = lanes(16)


def pack_own_kernel(
    block_ref, features_ref, targets_ref, lane_ref, own_ref, slabs_ref, cases_ref
):
    blocks = listed_blocks(block_ref, lax.axis_index("space"))
    tiles, rows = block_tiles(features_ref, targets_ref)
    for ct in range(3):
        for q in range(4):
            own_ref[4 * ct + q] = tiles[ct][q]
    own_ref[12] = jnp.concatenate(rows, axis=0).astype(jnp.bfloat16)
    write_cases(tiles, rows, cases_ref, lane_ref[...])
    for n, k in enumerate(PARTNERS):
        slabs_ref[n] = cases_ref[case_of(blocks[0], blocks[k])]


def pack_mate_kernel(block_ref, features_ref, targets_ref, slabs_ref, mate_ref, *refs):
    *pair_refs, cases_ref = refs
    blocks = listed_blocks(block_ref, lax.axis_index("space"))
    write_cases(*block_tiles(features_ref, targets_ref), cases_ref, lanes(16))
    mate_ref[...] = cases_ref[case_of(blocks[1], blocks[0])]
    for n, (k, ref) in enumerate(zip(PARTNERS, pair_refs)):
        ref[0] = slabs_ref[n]
        ref[1] = cases_ref[case_of(blocks[1], blocks[k])]


def stacked_taps(ref):
    rows = []
    for a in range(3):
        taps = [ref[9 * a + t] for t in range(9)]
        rows.append(jnp.concatenate(taps, axis=1))
    return jnp.concatenate(rows, axis=0)


def second_kernel(second_ref, w2_ref, w2t_ref):
    whole = stacked_taps(second_ref)
    w2_ref[...] = whole
    w2t_ref[...] = whole.T


def prepare_kernel(block_ref, first_ref, w1_ref, owners_ref, masks_ref, table_ref):
    w1_ref[...] = stacked_taps(first_ref)

    blocks = listed_blocks(block_ref, lax.axis_index("space"))
    for slot in range(10):
        table_ref[0, slot] = 1
        table_ref[1, slot] = 0
    table_ref[1, 4] = 1
    for k in range(1, len(blocks)):
        dx, dy = apart(blocks[0], blocks[k])
        near = (dx >= -1) & (dx <= 1) & (dy >= -1) & (dy <= 1)
        slot = jnp.where(near, dx * 3 + dy + 4, 9)
        table_ref[0, slot] = k
        table_ref[1, slot] = 1
    lane = lanes()
    there = [table_ref[1, q].astype(jnp.float32) for q in range(9)]
    owners = jnp.zeros((1, LANES), jnp.int32)
    for q in range(9):
        owners = jnp.where(lane == q, table_ref[0, q], owners)
    owners_ref[...] = owners
    for bx in range(3):
        before, middle, after = there[3 * bx : 3 * bx + 3]
        masks_ref[bx : bx + 1, :] = jnp.where(
            lane < 32, before, jnp.where(lane < 96, middle, after)
        )
        masks_ref[bx + 3 : bx + 4, :] = jnp.where(lane < 64, after, before)


def matmul(left, right):
    return lax.dot_general(
        left, right, (((1,), (0,)), ((), ())), preferred_element_type=jnp.float32
    )


def matmul_lanes(left, right):
    return lax.dot_general(
        left, right, (((1,), (1,)), ((), ())), preferred_element_type=jnp.float32
    )


def crop_kernel(scale, owners_ref, masks_ref, own_ref, mate_ref, *refs):
    crop_body(scale, owners_ref, masks_ref, own_ref, mate_ref, refs[:3], *refs[3:])


def crop_body(
    scale,
    owners_ref,
    masks_ref,
    own_ref,
    mate_ref,
    pairs,
    w1_ref,
    w2_ref,
    w2t_ref,
    h_ref,
    ht_ref,
    logits_ref,
    keep_ref,
    send_ref,
    gathered_ref,
    sides_ref,
    ends_ref,
    x9_ref,
    h9_ref,
    product_ref,
    slope1_ref,
    slope2_ref,
    hid2_ref,
    grad2_ref,
    shifted_ref,
    back_ref,
):
    gathered_ref[1] = mate_ref[...]
    for k, pair in zip(PARTNERS, pairs):
        for j in range(2):
            gathered_ref[k + j] = pair[j]
    owners = owners_ref[...]
    owner = [owners[0, q] for q in range(9)]

    bf16 = jnp.bfloat16
    lane = lanes(16)
    depth = lane & 7
    depth48 = lanes(C) & 7
    low, mid, left_half = lane < 32, lane < 96, lane < 64
    masks = [masks_ref[bx : bx + 1, :] for bx in range(3)]
    main_masks = [jnp.broadcast_to(mask, (16, LANES)).astype(bf16) for mask in masks]
    edge_masks = [
        jnp.broadcast_to(masks_ref[bx + 3 : bx + 4, :], (16, LANES)).astype(bf16)
        for bx in range(3)
    ]
    own_row = jnp.where((lane >= 32) & mid, 1.0, 0.0)[0:1]

    cell = lane & 63
    for side, by, in_place, turn, turns in (
        (0, 0, cell < 48, 24, (48, 96, 16, 64)),
        (1, 2, cell < 24, -40, (24, 72, -8, 40)),
    ):
        slab = owner[3 + by]
        for ct in range(3):
            half = gathered_ref[slab, 6 + ct // 2]
            for q in range(2):
                sides_ref[side, 4 * ct + q] = gathered_ref[slab, 2 * ct + q]
                moved = [roll(half, turns[2 * q + n] - (64 if ct == 1 else 0)) for n in range(2)]
                sides_ref[side, 4 * ct + q + 2] = jnp.where(
                    in_place,
                    roll(gathered_ref[slab, 2 * ct + q], turn),
                    jnp.where(left_half, moved[0], moved[1]),
                )

    for bx in (0, 2):
        for by in range(3):
            for ct in range(3):
                tile = gathered_ref[owner[3 * bx + by], 6 + ct // 2]
                ends_ref[3 * bx // 2 + by, ct] = roll(tile, -64 * (ct % 2))

    def placed(ct, bx, i):
        if bx == 1:
            tile, half = 4 * ct + i // 2, i % 2
            parts = [sides_ref[0, tile], own_ref[tile], sides_ref[1, tile]]
        elif i == (3 if bx == 0 else 4):
            half = 0
            parts = [ends_ref[3 * bx // 2 + by, ct] for by in range(3)]
        else:
            tile, half = 2 * ct + (i // 2 - 2 if bx == 0 else i // 2), i % 2
            parts = [gathered_ref[owner[3 * bx + by], tile] for by in range(3)]
        outer = 96 - 64 * half
        return roll(parts[0], outer), roll(parts[1], 32 - 64 * half), roll(parts[2], outer)

    zero = jnp.zeros((16, LANES), bf16)

    for plane in range(18):
        bx, i = (plane + 3) // 8, (plane + 3) % 8
        for ct in range(3):
            before, middle, after = placed(ct, bx, i)
            main = jnp.where(low, before, jnp.where(mid, middle, after)) * main_masks[bx]
            edge = jnp.where(left_half, after, before) * edge_masks[bx]
            for c in (-1, 0, 1):
                if c == 0:
                    main_c, edge_c = main, edge
                else:
                    keep = depth >= 1 if c == 1 else depth <= 6
                    main_c, edge_c = jnp.where(keep, main, zero), jnp.where(keep, edge, zero)
                for b in (-1, 0, 1):
                    step = 8 * b + c
                    if b == 1:
                        source = jnp.where(lane < step, edge_c, main_c)
                    elif b == -1:
                        source = jnp.where(lane >= LANES + step, edge_c, main_c)
                    else:
                        source = main_c
                    row = (3 * (b + 1) + c + 1) * C + 16 * ct
                    x9_ref[row : row + 16, LANES * plane : LANES * (plane + 1)] = (
                        roll(source, -step) if step else source
                    )

    def plane_cols(plane):
        return slice(LANES * plane, LANES * (plane + 1))

    def summed(plane, stride):
        return (
            product_ref[0:C, plane_cols(plane)]
            + product_ref[C : 2 * C, plane_cols(plane + stride)]
            + product_ref[2 * C : 3 * C, plane_cols(plane + 2 * stride)]
        )

    for top, bottom, start, stop in (
        (0, 2, 0, 2), (0, 3, 2, 6), (0, 3, 6, 10), (0, 3, 10, 16), (1, 3, 16, 18)
    ):
        rows, cols = slice(C * top, C * bottom), slice(LANES * start, LANES * stop)
        product_ref[rows, cols] = matmul(w1_ref[rows, :], x9_ref[:, cols])

    for plane in range(16):
        bx = (plane + 4) // 8
        pre = summed(plane, 1)
        negative = jnp.exp(jnp.minimum(pre, 0.0))
        if 4 <= plane < 12:
            slope1_ref[:, plane_cols(plane - 4)] = negative
        hidden = (jnp.maximum(pre, 0.0) + (negative - 1.0)) * masks[bx]
        hidden = hidden.astype(bf16)
        for c in (-1, 0, 1):
            if c == 0:
                source = hidden
            else:
                keep = depth48 >= 2 if c == 1 else depth48 <= 5
                source = jnp.where(keep, hidden, jnp.zeros((C, LANES), bf16))
            for b in (-1, 0, 1):
                step = 16 * b + 2 * c
                row = (3 * (b + 1) + c + 1) * C
                h9_ref[row : row + C, plane_cols(plane)] = roll(source, -step) if step else source

    for top, bottom, start, stop in (
        (0, 1, 0, 2), (0, 2, 2, 4), (0, 3, 4, 8), (0, 3, 8, 12), (1, 3, 12, 14), (2, 3, 14, 16)
    ):
        rows, cols = slice(C * top, C * bottom), slice(LANES * start, LANES * stop)
        product_ref[rows, cols] = matmul(w2_ref[rows, :], h9_ref[:, cols])

    for plane in range(12):
        bx = (plane + 6) // 8
        pre = summed(plane, 2)
        negative = jnp.exp(jnp.minimum(pre, 0.0))
        slope2_ref[:, plane_cols(plane)] = negative * masks[bx]
        hidden = (jnp.maximum(pre, 0.0) + (negative - 1.0)) * masks[bx]
        hid2_ref[:, plane_cols(plane)] = hidden.astype(jnp.bfloat16)

    logits = matmul(h_ref[...], hid2_ref[...])
    targets = []
    for bx, half in ((0, 1), (1, 0), (1, 1), (2, 1)):
        if bx == 1:
            before = roll(gathered_ref[owner[3], 7], -48 - 16 * half)
            middle = roll(own_ref[12], 32 - 64 * half)
            after = roll(gathered_ref[owner[5], 7], 32 - 16 * half)
        else:
            parts = [gathered_ref[owner[3 * bx + by], 7] for by in range(3)]
            before, middle, after = roll(parts[0], 32), roll(parts[1], -32), roll(parts[2], 32)
        cells = jnp.where(low, before, jnp.where(mid, middle, after))
        targets.append(cells.astype(jnp.float32))
    grads = []
    for plane in range(12):
        bx, i = (plane + 6) // 8, (plane + 6) % 8
        value = logits[:, plane_cols(plane)]
        if bx == 1:
            wanted = targets[1 + i % 2][4 * (i // 2) : 4 * (i // 2) + 4]
        else:
            wanted = targets[0 if bx == 0 else 3][4 * (i % 2) : 4 * (i % 2) + 4]
        wanted = jnp.concatenate([wanted, jnp.zeros((12, LANES), jnp.float32)], axis=0)
        sigmoid = 1.0 / (1.0 + jnp.exp(-value))
        grads.append((sigmoid - wanted) * masks[bx] * scale)
    for q in range(4):
        first = roll(logits[:, plane_cols(2 + 2 * q)], -32)
        second = roll(logits[:, plane_cols(3 + 2 * q)], 32)
        logits_ref[:, plane_cols(q)] = jnp.where(left_half, first, second)[0:8]

    grad_logit = jnp.concatenate(grads, axis=1).astype(jnp.bfloat16)
    back = matmul(ht_ref[...], grad_logit)
    grad2_ref[...] = (back * slope2_ref[...]).astype(jnp.bfloat16)
    own_grads = jnp.concatenate([grads[2 + x] * own_row for x in range(8)], axis=1)
    head_part = matmul_lanes(hid2_ref[:, 2 * LANES : 10 * LANES], own_grads.astype(jnp.bfloat16))

    own_bf16 = jnp.broadcast_to(own_row, (C, LANES)).astype(bf16)
    shifted_ref[...] = jnp.zeros_like(shifted_ref)
    for a in range(3):
        for x in range(8):
            shifted_ref[C * a : C * (a + 1), plane_cols(x + 2 * a)] = (
                grad2_ref[:, plane_cols(x + 2)] * own_bf16
            )
    second_part = matmul_lanes(shifted_ref[...], h9_ref[:, 2 * LANES : 14 * LANES])

    for a in range(3):
        for x in range(8):
            shifted_ref[C * a : C * (a + 1), plane_cols(x)] = grad2_ref[:, plane_cols(x + 4 - 2 * a)]
    for n in range(2):
        cols = slice(512 * n, 512 * (n + 1))
        back_ref[:, cols] = matmul(w2t_ref[...], shifted_ref[:, cols])
    grad1 = []
    for x in range(8):
        total = jnp.zeros((C, LANES), jnp.float32)
        for c in (-1, 0, 1):
            part = jnp.zeros((C, LANES), jnp.float32)
            for b in (-1, 0, 1):
                row = (3 * (b + 1) + c + 1) * C
                step = 16 * b + 2 * c
                piece = back_ref[row : row + C, plane_cols(x)]
                part += roll(piece, step) if step else piece
            if c:
                part = jnp.where(depth48 >= 2 if c == 1 else depth48 <= 5, part, 0.0)
            total += part
        grad1.append((total * slope1_ref[:, plane_cols(x)] * own_row).astype(jnp.bfloat16))

    shifted_ref[...] = jnp.zeros_like(shifted_ref)
    for a in range(3):
        for x in range(8):
            shifted_ref[C * a : C * (a + 1), plane_cols(x + a)] = grad1[x]
    first_part = matmul_lanes(
        shifted_ref[:, 0 : 10 * LANES], x9_ref[:, 4 * LANES : 14 * LANES]
    )

    first_core = (lax.axis_index("dp") & 1) == 0
    head_part = jnp.concatenate([head_part, jnp.zeros((24, 16), jnp.float32)], axis=0)
    nothing = jnp.zeros((72, 16), jnp.float32)
    ends = []
    for part, extra in ((first_part, nothing), (second_part, head_part)):
        tail = jnp.concatenate([part[0:72, 384:], part[72:144, 384:], extra, nothing], axis=1)
        ends.append(jnp.concatenate([tail, jnp.zeros((8, LANES), jnp.float32)], axis=0))
    pieces = [(first_part[:, plane_cols(q)], second_part[:, plane_cols(q)]) for q in range(3)]
    row = 0
    for first, second in pieces + [tuple(ends)]:
        rows = slice(row, row + first.shape[0])
        keep_ref[rows, :] = jnp.where(first_core, first, second)
        send_ref[rows, :] = jnp.where(first_core, second, first)
        row += first.shape[0]


def add_kernel(mine_ref, other_ref, out_ref):
    out_ref[...] = (mine_ref[...] + other_ref[...]).astype(jnp.bfloat16)


def sum_kernel(parts_ref, out_ref):
    total = parts_ref[0].astype(jnp.float32)
    for s in range(1, parts_ref.shape[0]):
        total += parts_ref[s].astype(jnp.float32)
    total = total.astype(jnp.bfloat16)
    for s in range(out_ref.shape[0]):
        out_ref[s] = total


def unpack_kernel(mine_ref, other_ref, logits_ref, first_ref, second_ref, head_ref, out_ref):
    out_ref[:, 0, :] = logits_ref[0:3, :]
    first_core = (lax.axis_index("dp") & 1) == 0
    mine, other = mine_ref[...], other_ref[...]
    for k, out in ((0, first_ref), (1, second_ref)):
        half = jnp.where(first_core, other if k else mine, mine if k else other)
        half = half.astype(jnp.float32)
        tail = jnp.concatenate([half[432:504, 0:C], half[432:504, C : 2 * C]], axis=0)
        tiles = [half[144 * q : 144 * (q + 1), :] for q in range(3)]
        whole = jnp.concatenate(tiles + [tail], axis=1)
        for a in range(3):
            for t in range(9):
                out[9 * a + t] = whole[C * a : C * (a + 1), C * t : C * (t + 1)]
        if k:
            head_ref[...] = half[432 : 432 + C, 96:112].T[0:3]


def on_device_flat(features, device_block, conv_first, conv_second, head_weight, targets):
    space_count = lax.axis_size("space")
    device_count = lax.axis_size("dp") * space_count
    bf16, f32 = jnp.bfloat16, jnp.float32
    small = pltpu.CompilerParams(vmem_limit_bytes=8 * 1024 * 1024)
    shape = jax.ShapeDtypeStruct
    vmem = pl.BlockSpec(memory_space=pltpu.VMEM)

    def swap(values, mask):
        return lax.ppermute(values, "space", [(s, s ^ mask) for s in range(space_count)])

    mate_targets, mate_features = swap(targets, 1), swap(features, 1)
    head, head_t = pl.pallas_call(
        head_kernel,
        out_shape=(shape((16, C), bf16), shape((C, 16), bf16)),
        in_specs=[vmem],
        out_specs=(vmem,) * 2,
        compiler_params=small,
        cost_estimate=pl.CostEstimate(flops=1_000_000, bytes_accessed=2_000_000, transcendentals=0),
        name="lay_out_head",
    )(head_weight)
    lane = pl.pallas_call(
        lanes_kernel,
        out_shape=shape((16, LANES), jnp.int32),
        out_specs=vmem,
        compiler_params=small,
        cost_estimate=pl.CostEstimate(flops=0, bytes_accessed=2_000_000, transcendentals=0),
        name="lane_indices",
    )()
    own, own_slabs = pl.pallas_call(
        pack_own_kernel,
        out_shape=(shape((13, 16, LANES), bf16), shape((3, 8, 16, LANES), bf16)),
        in_specs=[vmem] * 4,
        out_specs=(vmem,) * 2,
        scratch_shapes=[pltpu.VMEM((4, 8, 16, LANES), bf16)],
        compiler_params=small,
        cost_estimate=pl.CostEstimate(flops=1_000_000, bytes_accessed=2_000_000, transcendentals=0),
        name="pack_own",
    )(device_block, features[0, 0], targets[0].transpose(1, 0, 2), lane)
    mate_slab, *pairs = pl.pallas_call(
        pack_mate_kernel,
        out_shape=(
            shape((8, 16, LANES), bf16),
            *[shape((2, 8, 16, LANES), bf16) for _ in PARTNERS],
        ),
        in_specs=[vmem] * 4,
        out_specs=(vmem,) * 4,
        scratch_shapes=[pltpu.VMEM((4, 8, 16, LANES), bf16)],
        compiler_params=small,
        cost_estimate=pl.CostEstimate(flops=1_000_000, bytes_accessed=2_000_000, transcendentals=0),
        name="pack_mate",
    )(device_block, mate_features[0, 0], mate_targets[0].transpose(1, 0, 2), own_slabs)
    pairs = [swap(pair, mask) for pair, mask in zip(pairs, PARTNERS)]

    w1, owners, masks = pl.pallas_call(
        prepare_kernel,
        out_shape=(
            shape((3 * C, 9 * C), bf16),
            shape((1, LANES), jnp.int32),
            shape((8, LANES), f32),
        ),
        in_specs=[vmem] * 2,
        out_specs=(vmem,) * 3,
        scratch_shapes=[pltpu.SMEM((2, 16), jnp.int32)],
        compiler_params=small,
        cost_estimate=pl.CostEstimate(flops=2_000_000, bytes_accessed=4_000_000, transcendentals=0),
        name="prepare",
    )(device_block, conv_first.transpose(1, 0, 2))
    w2, w2t = pl.pallas_call(
        second_kernel,
        out_shape=(shape((3 * C, 9 * C), bf16), shape((9 * C, 3 * C), bf16)),
        in_specs=[vmem],
        out_specs=(vmem,) * 2,
        compiler_params=small,
        cost_estimate=pl.CostEstimate(flops=2_000_000, bytes_accessed=4_000_000, transcendentals=0),
        name="second_weights",
    )(conv_second.transpose(1, 0, 2))

    scale = (device_count * 3 * CELLS) ** (-0.5)
    logits, keep, send = pl.pallas_call(
        functools.partial(crop_kernel, scale),
        out_shape=(shape((8, CELLS), f32), shape((HALF, LANES), f32), shape((HALF, LANES), f32)),
        in_specs=[vmem] * 12,
        out_specs=(vmem,) * 3,
        scratch_shapes=[
            pltpu.VMEM((space_count, 8, 16, LANES), bf16),
            pltpu.VMEM((2, 12, 16, LANES), bf16),
            pltpu.VMEM((6, 3, 16, LANES), bf16),
            pltpu.VMEM((9 * C, 18 * LANES), bf16),
            pltpu.VMEM((9 * C, 16 * LANES), bf16),
            pltpu.VMEM((3 * C, 18 * LANES), f32),
            pltpu.VMEM((C, 8 * LANES), f32),
            pltpu.VMEM((C, 12 * LANES), f32),
            pltpu.VMEM((C, 12 * LANES), bf16),
            pltpu.VMEM((C, 12 * LANES), bf16),
            pltpu.VMEM((3 * C, 12 * LANES), bf16),
            pltpu.VMEM((9 * C, 8 * LANES), f32),
        ],
        compiler_params=pltpu.CompilerParams(vmem_limit_bytes=20 * 1024 * 1024),
        name="forward_backward",
    )(owners, masks, own, mate_slab, *pairs, w1, w2, w2t, head, head_t)

    dp_count = lax.axis_size("dp")

    def swap_cores(values):
        return lax.ppermute(values, "dp", [(d, d ^ 1) for d in range(dp_count)])

    peers = device_count // 2
    groups = [
        [d * space_count + s for d in range(core, dp_count, 2) for s in range(space_count)]
        for core in range(2)
    ]

    def exchange(values):
        return lax.all_to_all(
            values, ("dp", "space"), 0, 0, axis_index_groups=groups, tiled=True
        )

    def step(kernel, out, *operands):
        return pl.pallas_call(
            kernel,
            out_shape=out,
            in_specs=[vmem] * len(operands),
            out_specs=vmem,
            compiler_params=small,
            name="gradient_sum",
        )(*operands)

    term = step(add_kernel, shape((HALF, LANES), bf16), keep, swap_cores(send))
    pieces = shape((peers, HALF // peers, LANES), bf16)
    total = exchange(step(sum_kernel, pieces, exchange(term.reshape(pieces.shape))))
    total = total.reshape(HALF, LANES)
    grad_first, grad_second, grad_head, logits = pl.pallas_call(
        unpack_kernel,
        out_shape=(
            shape((27, C, C), f32),
            shape((27, C, C), f32),
            shape((3, C), f32),
            shape((3, 1, CELLS), f32),
        ),
        in_specs=[vmem] * 3,
        out_specs=(vmem,) * 4,
        compiler_params=small,
        name="unpack_gradients",
    )(total, swap_cores(total), logits)
    return (
        logits.transpose(1, 0, 2)[None],
        grad_first.transpose(1, 0, 2),
        grad_second.transpose(1, 0, 2),
        grad_head,
    )


def solution(mesh):
    in_specs = (
        P("dp", "space", None, None),
        P("dp", None),
        P(),
        P(),
        P(),
        P("dp", "space", None, None),
    )
    out_specs = (P("dp", "space", None, None), P(), P(), P())
    flat = mesh.shape["space"] == 8 and mesh.shape["dp"] in (2, 4)
    return jax.shard_map(
        on_device_flat if flat else on_device_deep,
        mesh=mesh,
        in_specs=in_specs,
        out_specs=out_specs,
        check_vma=False,
    )
```

```python
import functools

import jax
import jax.numpy as jnp
from jax import lax
from jax.experimental import pallas as pl
from jax.experimental.pallas import tpu as pltpu
from jax.sharding import PartitionSpec as P

BS = 8


tap_offsets = [
    (tap_index // 9 - 1, tap_index // 3 % 3 - 1, tap_index % 3 - 1) for tap_index in range(27)
]


def elu_pair(values):
    negative = jnp.exp(jnp.minimum(values, 0.0))
    return (jnp.where(values > 0, values, negative - 1.0), jnp.where(values > 0, 1.0, negative))


def neighbor_tables(device_block):
    space_count = lax.axis_size("space")
    depth_z = space_count // 8
    self_index = lax.axis_index("space")
    blocks = device_block[0]
    coords = jnp.stack([blocks // (4 * depth_z), blocks // depth_z % 4, blocks % depth_z])
    own_coords = lax.dynamic_index_in_dim(coords, self_index, 1, keepdims=False)
    offsets = jnp.array(tap_offsets, jnp.int32)
    limits = jnp.array([4, 4, depth_z], jnp.int32)
    wanted = own_coords[None, :] + offsets
    inside = jnp.all((wanted >= 0) & (wanted < limits[None, :]), axis=1) & (jnp.arange(27) != 13)
    wanted_id = (wanted[:, 0] * 4 + wanted[:, 1]) * depth_z + wanted[:, 2]
    matches = (blocks[None, :] == wanted_id[:, None]) & inside[:, None]
    devices = jnp.arange(space_count, dtype=jnp.int32)
    owner_row = jnp.sum(jnp.where(matches, devices[None, :], 0), axis=1)
    present = jnp.any(matches, axis=1)
    relative = coords - own_coords[:, None]
    adjacent = jnp.all(jnp.abs(relative) <= 1, axis=0) & (devices != self_index)
    send_tap = jnp.where(
        adjacent, (relative[0] + 1) * 9 + (relative[1] + 1) * 3 + relative[2] + 1, 13
    )
    return (owner_row, present, send_tap)


def region_slice(block_data, offset, depth_cells):
    span_list = []
    for step_value in offset:
        if step_value == 1:
            span_list.append(slice(BS - depth_cells, BS))
        elif step_value == -1:
            span_list.append(slice(0, depth_cells))
        else:
            span_list.append(slice(0, BS))
    return block_data[:, span_list[0], span_list[1], span_list[2]]


def surround(block_data, depth_cells, tables):
    owner_row, present, send_tap = tables
    channels = block_data.shape[0]
    length = depth_cells * BS * BS
    pieces = []
    for tap_index in range(27):
        if tap_index == 13:
            pieces.append(jnp.zeros((channels, length), block_data.dtype))
        else:
            region = region_slice(block_data, tap_offsets[tap_index], depth_cells).reshape(
                channels, -1
            )
            pieces.append(jnp.pad(region, ((0, 0), (0, length - region.shape[1]))))
    outgoing = jnp.stack(pieces)
    sending = outgoing[send_tap]
    by_source = lax.all_to_all(sending, "space", split_axis=0, concat_axis=0, tiled=True)
    incoming = jnp.where(
        present[:, None, None], by_source[owner_row], jnp.zeros((), block_data.dtype)
    )
    rows_x = []
    for step_x in range(3):
        rows_y = []
        for step_y in range(3):
            rows_z = []
            for step_z in range(3):
                tap_index = step_x * 9 + step_y * 3 + step_z
                if tap_index == 13:
                    rows_z.append(block_data)
                else:
                    extent_list = [
                        BS if step_value == 1 else depth_cells
                        for step_value in (step_x, step_y, step_z)
                    ]
                    count_cells = extent_list[0] * extent_list[1] * extent_list[2]
                    rows_z.append(
                        incoming[tap_index][:, :count_cells].reshape(
                            channels, extent_list[0], extent_list[1], extent_list[2]
                        )
                    )
            rows_y.append(jnp.concatenate(rows_z, axis=3))
        rows_x.append(jnp.concatenate(rows_y, axis=2))
    return jnp.concatenate(rows_x, axis=1)


def conv_padded(padded, kernel, dilation):
    result = lax.conv_general_dilated(
        padded[None],
        kernel,
        (1, 1, 1),
        "VALID",
        rhs_dilation=(dilation, dilation, dilation),
        dimension_numbers=("NCDHW", "OIDHW", "NCDHW"),
        preferred_element_type=jnp.float32,
    )
    return result[0].reshape(kernel.shape[0], BS * BS * BS)


def kernel_grad(padded, grad_rows, dilation):
    channels = padded.shape[0]
    outputs = grad_rows.shape[0]
    grad_block = grad_rows.reshape(outputs, 1, BS, BS, BS)
    result = lax.conv_general_dilated(
        padded[None],
        grad_block,
        (dilation, dilation, dilation),
        "VALID",
        dimension_numbers=("CNDHW", "OIDHW", "NCDHW"),
        preferred_element_type=jnp.float32,
    )
    return result.reshape(channels, outputs, 27).transpose(1, 2, 0)


def on_device_deep(features, device_block, conv_first, conv_second, head_weight, targets):
    channels = features.shape[2]
    tables = neighbor_tables(device_block)
    kernel_first = conv_first.reshape(channels, 3, 3, 3, channels).transpose(0, 4, 1, 2, 3)
    kernel_second = conv_second.reshape(channels, 3, 3, 3, channels).transpose(0, 4, 1, 2, 3)
    block_in = features[0, 0].reshape(channels, BS, BS, BS)
    padded_in = surround(block_in, 1, tables)
    pre_first = conv_padded(padded_in, kernel_first, 1)
    act_first, slope_first = elu_pair(pre_first)
    hid_first = act_first.astype(jnp.bfloat16)
    padded_first = surround(hid_first.reshape(channels, BS, BS, BS), 2, tables)
    pre_second = conv_padded(padded_first, kernel_second, 2)
    act_second, slope_second = elu_pair(pre_second)
    hid_second = act_second.astype(jnp.bfloat16)
    logits = jnp.dot(head_weight, hid_second, preferred_element_type=jnp.float32)
    scale = (lax.axis_size("dp") * lax.axis_size("space") * 3 * BS * BS * BS) ** (-0.5)
    grad_logit = ((jax.nn.sigmoid(logits) - targets[0, 0].astype(jnp.float32)) * scale).astype(
        jnp.bfloat16
    )
    grad_head = lax.dot_general(
        grad_logit, hid_second, (((1,), (1,)), ((), ())), preferred_element_type=jnp.float32
    )
    back_second = lax.dot_general(
        head_weight, grad_logit, (((0,), (0,)), ((), ())), preferred_element_type=jnp.float32
    )
    grad_pre_second = (back_second * slope_second).astype(jnp.bfloat16)
    grad_second = kernel_grad(padded_first, grad_pre_second, 2)
    padded_grad = surround(grad_pre_second.reshape(channels, BS, BS, BS), 2, tables)
    kernel_back = jnp.transpose(kernel_second[:, :, ::-1, ::-1, ::-1], (1, 0, 2, 3, 4))
    back_first = conv_padded(padded_grad, kernel_back, 2)
    grad_pre_first = (back_first * slope_first).astype(jnp.bfloat16)
    grad_first = kernel_grad(padded_in, grad_pre_first, 1)
    grad_first, grad_second, grad_head = lax.psum(
        (grad_first, grad_second, grad_head), ("dp", "space")
    )
    return (logits[None, None], grad_first, grad_second, grad_head)


C = 48
CELLS = 512
HALF = 512
LANES = 128


def lanes(rows=1):
    return lax.broadcasted_iota(jnp.int32, (rows, LANES), 1)


def roll(values, shift):
    return pltpu.roll(values, shift % LANES, 1) if shift % LANES else values


def listed_blocks(block_ref, me):
    ids = block_ref[...].astype(jnp.float32)
    index = lax.broadcasted_iota(jnp.int32, ids.shape, 1)
    return [
        jnp.sum(jnp.where(index == (me ^ k), ids, 0.0)).astype(jnp.int32)
        for k in range(ids.shape[1])
    ]


def apart(source, target):
    return (target >> 2) - (source >> 2), (target & 3) - (source & 3)


PARTNERS = (6, 4, 2)


def block_tiles(features_ref, targets_ref):
    tiles = [
        [features_ref[16 * ct : 16 * (ct + 1), LANES * q : LANES * (q + 1)] for q in range(4)]
        for ct in range(3)
    ]
    targets = targets_ref[:, 0, :].astype(jnp.float32)
    targets = jnp.concatenate([targets, jnp.zeros((1, CELLS), jnp.float32)], axis=0)
    return tiles, [targets[:, LANES * q : LANES * (q + 1)] for q in range(4)]


def write_cases(tiles, rows, cases_ref, lane):
    left = lane < 64
    cell = lane & 63
    target_tile = jnp.concatenate(rows, axis=0)

    def write(case, pairs, halves, wanted):
        for ct in range(3):
            cases_ref[case, 2 * ct] = pairs[ct][0]
            cases_ref[case, 2 * ct + 1] = pairs[ct][1]
        cases_ref[case, 6] = jnp.where(left, halves[0], halves[1])
        cases_ref[case, 7] = jnp.where(left, halves[2], wanted.astype(jnp.bfloat16))

    for case, pair, single, q in ((0, (2, 3), 1, 3), (1, (0, 1), 2, 0)):
        turns = (64, 0, 64) if case == 0 else (0, 64, 0)
        halves = [roll(tiles[ct][single], turns[ct]) for ct in range(3)]
        both = [roll(rows[q], 64), rows[q], jnp.zeros((8, LANES), jnp.float32)]
        wanted = jnp.concatenate(both, axis=0)
        write(case, [(t[pair[0]], t[pair[1]]) for t in tiles], halves, wanted)
    for case, spare, turn, turns, target_turns in (
        (2, cell < 24, -24, (-48, -96, -16, -64), (16, -32)),
        (3, cell >= 40, 40, (-24, -72, 8, -40), (64, 16)),
    ):
        pairs, halves = [], []
        for ct, t in enumerate(tiles):
            pairs.append([jnp.where(spare, roll(t[q + 2], turn), t[q]) for q in range(2)])
            moved = [roll(t[2 + n // 2], turns[n] + (64 if ct == 1 else 0)) for n in range(4)]
            half = jnp.where(cell < 16, moved[0], jnp.where(cell < 32, moved[1], moved[2]))
            halves.append(jnp.where(cell < 48, half, moved[3]))
        wanted = [roll(target_tile, n) for n in target_turns]
        write(case, pairs, halves, jnp.where(lane < 80, wanted[0], wanted[1]))


def case_of(source, target):
    dx, dy = apart(source, target)
    return jnp.where(dx > 0, 0, jnp.where(dx < 0, 1, jnp.where(dy > 0, 2, 3)))


def head_kernel(head_ref, h_ref, ht_ref):
    head = head_ref[...].astype(jnp.float32)
    head = jnp.concatenate([head, jnp.zeros((13, C), jnp.float32)], axis=0)
    h_ref[...] = head.astype(jnp.bfloat16)
    ht_ref[...] = head.T.astype(jnp.bfloat16)


def lanes_kernel(out_ref):
    out_ref[...] = lanes(16)


def pack_own_kernel(
    block_ref, features_ref, targets_ref, lane_ref, own_ref, slabs_ref, cases_ref
):
    blocks = listed_blocks(block_ref, lax.axis_index("space"))
    tiles, rows = block_tiles(features_ref, targets_ref)
    for ct in range(3):
        for q in range(4):
            own_ref[4 * ct + q] = tiles[ct][q]
    own_ref[12] = jnp.concatenate(rows, axis=0).astype(jnp.bfloat16)
    write_cases(tiles, rows, cases_ref, lane_ref[...])
    for n, k in enumerate(PARTNERS):
        slabs_ref[n] = cases_ref[case_of(blocks[0], blocks[k])]


def pack_mate_kernel(block_ref, features_ref, targets_ref, slabs_ref, mate_ref, *refs):
    *pair_refs, cases_ref = refs
    blocks = listed_blocks(block_ref, lax.axis_index("space"))
    write_cases(*block_tiles(features_ref, targets_ref), cases_ref, lanes(16))
    mate_ref[...] = cases_ref[case_of(blocks[1], blocks[0])]
    for n, (k, ref) in enumerate(zip(PARTNERS, pair_refs)):
        ref[0] = slabs_ref[n]
        ref[1] = cases_ref[case_of(blocks[1], blocks[k])]


def stacked_taps(ref):
    rows = []
    for a in range(3):
        taps = [ref[9 * a + t] for t in range(9)]
        rows.append(jnp.concatenate(taps, axis=1))
    return jnp.concatenate(rows, axis=0)


def second_kernel(second_ref, w2_ref, w2t_ref):
    whole = stacked_taps(second_ref)
    w2_ref[...] = whole
    w2t_ref[...] = whole.T


def prepare_kernel(block_ref, first_ref, w1_ref, owners_ref, masks_ref, table_ref):
    w1_ref[...] = stacked_taps(first_ref)

    blocks = listed_blocks(block_ref, lax.axis_index("space"))
    for slot in range(10):
        table_ref[0, slot] = 1
        table_ref[1, slot] = 0
    table_ref[1, 4] = 1
    for k in range(1, len(blocks)):
        dx, dy = apart(blocks[0], blocks[k])
        near = (dx >= -1) & (dx <= 1) & (dy >= -1) & (dy <= 1)
        slot = jnp.where(near, dx * 3 + dy + 4, 9)
        table_ref[0, slot] = k
        table_ref[1, slot] = 1
    lane = lanes()
    there = [table_ref[1, q].astype(jnp.float32) for q in range(9)]
    owners = jnp.zeros((1, LANES), jnp.int32)
    for q in range(9):
        owners = jnp.where(lane == q, table_ref[0, q], owners)
    owners_ref[...] = owners
    for bx in range(3):
        before, middle, after = there[3 * bx : 3 * bx + 3]
        masks_ref[bx : bx + 1, :] = jnp.where(
            lane < 32, before, jnp.where(lane < 96, middle, after)
        )
        masks_ref[bx + 3 : bx + 4, :] = jnp.where(lane < 64, after, before)


def matmul(left, right):
    return lax.dot_general(
        left, right, (((1,), (0,)), ((), ())), preferred_element_type=jnp.float32
    )


def matmul_lanes(left, right):
    return lax.dot_general(
        left, right, (((1,), (1,)), ((), ())), preferred_element_type=jnp.float32
    )


def crop_kernel(scale, owners_ref, masks_ref, own_ref, mate_ref, *refs):
    crop_body(scale, owners_ref, masks_ref, own_ref, mate_ref, refs[:3], *refs[3:])


def crop_body(
    scale,
    owners_ref,
    masks_ref,
    own_ref,
    mate_ref,
    pairs,
    w1_ref,
    w2_ref,
    w2t_ref,
    h_ref,
    ht_ref,
    logits_ref,
    keep_ref,
    send_ref,
    gathered_ref,
    sides_ref,
    ends_ref,
    x9_ref,
    h9_ref,
    product_ref,
    slope1_ref,
    slope2_ref,
    hid2_ref,
    grad2_ref,
    shifted_ref,
    back_ref,
):
    gathered_ref[1] = mate_ref[...]
    for k, pair in zip(PARTNERS, pairs):
        for j in range(2):
            gathered_ref[k + j] = pair[j]
    owners = owners_ref[...]
    owner = [owners[0, q] for q in range(9)]

    bf16 = jnp.bfloat16
    lane = lanes(16)
    depth = lane & 7
    depth48 = lanes(C) & 7
    low, mid, left_half = lane < 32, lane < 96, lane < 64
    masks = [masks_ref[bx : bx + 1, :] for bx in range(3)]
    main_masks = [jnp.broadcast_to(mask, (16, LANES)).astype(bf16) for mask in masks]
    edge_masks = [
        jnp.broadcast_to(masks_ref[bx + 3 : bx + 4, :], (16, LANES)).astype(bf16)
        for bx in range(3)
    ]
    own_row = jnp.where((lane >= 32) & mid, 1.0, 0.0)[0:1]

    cell = lane & 63
    for side, by, in_place, turn, turns in (
        (0, 0, cell < 48, 24, (48, 96, 16, 64)),
        (1, 2, cell < 24, -40, (24, 72, -8, 40)),
    ):
        slab = owner[3 + by]
        for ct in range(3):
            half = gathered_ref[slab, 6 + ct // 2]
            for q in range(2):
                sides_ref[side, 4 * ct + q] = gathered_ref[slab, 2 * ct + q]
                moved = [roll(half, turns[2 * q + n] - (64 if ct == 1 else 0)) for n in range(2)]
                sides_ref[side, 4 * ct + q + 2] = jnp.where(
                    in_place,
                    roll(gathered_ref[slab, 2 * ct + q], turn),
                    jnp.where(left_half, moved[0], moved[1]),
                )

    for bx in (0, 2):
        for by in range(3):
            for ct in range(3):
                tile = gathered_ref[owner[3 * bx + by], 6 + ct // 2]
                ends_ref[3 * bx // 2 + by, ct] = roll(tile, -64 * (ct % 2))

    def placed(ct, bx, i):
        if bx == 1:
            tile, half = 4 * ct + i // 2, i % 2
            parts = [sides_ref[0, tile], own_ref[tile], sides_ref[1, tile]]
        elif i == (3 if bx == 0 else 4):
            half = 0
            parts = [ends_ref[3 * bx // 2 + by, ct] for by in range(3)]
        else:
            tile, half = 2 * ct + (i // 2 - 2 if bx == 0 else i // 2), i % 2
            parts = [gathered_ref[owner[3 * bx + by], tile] for by in range(3)]
        outer = 96 - 64 * half
        return roll(parts[0], outer), roll(parts[1], 32 - 64 * half), roll(parts[2], outer)

    zero = jnp.zeros((16, LANES), bf16)

    for plane in range(18):
        bx, i = (plane + 3) // 8, (plane + 3) % 8
        for ct in range(3):
            before, middle, after = placed(ct, bx, i)
            main = jnp.where(low, before, jnp.where(mid, middle, after)) * main_masks[bx]
            edge = jnp.where(left_half, after, before) * edge_masks[bx]
            for c in (-1, 0, 1):
                if c == 0:
                    main_c, edge_c = main, edge
                else:
                    keep = depth >= 1 if c == 1 else depth <= 6
                    main_c, edge_c = jnp.where(keep, main, zero), jnp.where(keep, edge, zero)
                for b in (-1, 0, 1):
                    step = 8 * b + c
                    if b == 1:
                        source = jnp.where(lane < step, edge_c, main_c)
                    elif b == -1:
                        source = jnp.where(lane >= LANES + step, edge_c, main_c)
                    else:
                        source = main_c
                    row = (3 * (b + 1) + c + 1) * C + 16 * ct
                    x9_ref[row : row + 16, LANES * plane : LANES * (plane + 1)] = (
                        roll(source, -step) if step else source
                    )

    def plane_cols(plane):
        return slice(LANES * plane, LANES * (plane + 1))

    def summed(plane, stride):
        return (
            product_ref[0:C, plane_cols(plane)]
            + product_ref[C : 2 * C, plane_cols(plane + stride)]
            + product_ref[2 * C : 3 * C, plane_cols(plane + 2 * stride)]
        )

    for top, bottom, start, stop in (
        (0, 2, 0, 2), (0, 3, 2, 6), (0, 3, 6, 10), (0, 3, 10, 16), (1, 3, 16, 18)
    ):
        rows, cols = slice(C * top, C * bottom), slice(LANES * start, LANES * stop)
        product_ref[rows, cols] = matmul(w1_ref[rows, :], x9_ref[:, cols])

    for plane in range(16):
        bx = (plane + 4) // 8
        pre = summed(plane, 1)
        negative = jnp.exp(jnp.minimum(pre, 0.0))
        if 4 <= plane < 12:
            slope1_ref[:, plane_cols(plane - 4)] = negative
        hidden = (jnp.maximum(pre, 0.0) + (negative - 1.0)) * masks[bx]
        hidden = hidden.astype(bf16)
        for c in (-1, 0, 1):
            if c == 0:
                source = hidden
            else:
                keep = depth48 >= 2 if c == 1 else depth48 <= 5
                source = jnp.where(keep, hidden, jnp.zeros((C, LANES), bf16))
            for b in (-1, 0, 1):
                step = 16 * b + 2 * c
                row = (3 * (b + 1) + c + 1) * C
                h9_ref[row : row + C, plane_cols(plane)] = roll(source, -step) if step else source

    for top, bottom, start, stop in (
        (0, 1, 0, 2), (0, 2, 2, 4), (0, 3, 4, 8), (0, 3, 8, 12), (1, 3, 12, 14), (2, 3, 14, 16)
    ):
        rows, cols = slice(C * top, C * bottom), slice(LANES * start, LANES * stop)
        product_ref[rows, cols] = matmul(w2_ref[rows, :], h9_ref[:, cols])

    for plane in range(12):
        bx = (plane + 6) // 8
        pre = summed(plane, 2)
        negative = jnp.exp(jnp.minimum(pre, 0.0))
        slope2_ref[:, plane_cols(plane)] = negative * masks[bx]
        hidden = (jnp.maximum(pre, 0.0) + (negative - 1.0)) * masks[bx]
        hid2_ref[:, plane_cols(plane)] = hidden.astype(jnp.bfloat16)

    logits = matmul(h_ref[...], hid2_ref[...])
    targets = []
    for bx, half in ((0, 1), (1, 0), (1, 1), (2, 1)):
        if bx == 1:
            before = roll(gathered_ref[owner[3], 7], -48 - 16 * half)
            middle = roll(own_ref[12], 32 - 64 * half)
            after = roll(gathered_ref[owner[5], 7], 32 - 16 * half)
        else:
            parts = [gathered_ref[owner[3 * bx + by], 7] for by in range(3)]
            before, middle, after = roll(parts[0], 32), roll(parts[1], -32), roll(parts[2], 32)
        cells = jnp.where(low, before, jnp.where(mid, middle, after))
        targets.append(cells.astype(jnp.float32))
    grads = []
    for plane in range(12):
        bx, i = (plane + 6) // 8, (plane + 6) % 8
        value = logits[:, plane_cols(plane)]
        if bx == 1:
            wanted = targets[1 + i % 2][4 * (i // 2) : 4 * (i // 2) + 4]
        else:
            wanted = targets[0 if bx == 0 else 3][4 * (i % 2) : 4 * (i % 2) + 4]
        wanted = jnp.concatenate([wanted, jnp.zeros((12, LANES), jnp.float32)], axis=0)
        sigmoid = 1.0 / (1.0 + jnp.exp(-value))
        grads.append((sigmoid - wanted) * masks[bx] * scale)
    for q in range(4):
        first = roll(logits[:, plane_cols(2 + 2 * q)], -32)
        second = roll(logits[:, plane_cols(3 + 2 * q)], 32)
        logits_ref[:, plane_cols(q)] = jnp.where(left_half, first, second)[0:8]

    grad_logit = jnp.concatenate(grads, axis=1).astype(jnp.bfloat16)
    back = matmul(ht_ref[...], grad_logit)
    grad2_ref[...] = (back * slope2_ref[...]).astype(jnp.bfloat16)
    own_grads = jnp.concatenate([grads[2 + x] * own_row for x in range(8)], axis=1)
    head_part = matmul_lanes(hid2_ref[:, 2 * LANES : 10 * LANES], own_grads.astype(jnp.bfloat16))

    own_bf16 = jnp.broadcast_to(own_row, (C, LANES)).astype(bf16)
    shifted_ref[...] = jnp.zeros_like(shifted_ref)
    for a in range(3):
        for x in range(8):
            shifted_ref[C * a : C * (a + 1), plane_cols(x + 2 * a)] = (
                grad2_ref[:, plane_cols(x + 2)] * own_bf16
            )
    second_part = matmul_lanes(shifted_ref[...], h9_ref[:, 2 * LANES : 14 * LANES])

    for a in range(3):
        for x in range(8):
            shifted_ref[C * a : C * (a + 1), plane_cols(x)] = grad2_ref[:, plane_cols(x + 4 - 2 * a)]
    for n in range(2):
        cols = slice(512 * n, 512 * (n + 1))
        back_ref[:, cols] = matmul(w2t_ref[...], shifted_ref[:, cols])
    grad1 = []
    for x in range(8):
        total = jnp.zeros((C, LANES), jnp.float32)
        for c in (-1, 0, 1):
            part = jnp.zeros((C, LANES), jnp.float32)
            for b in (-1, 0, 1):
                row = (3 * (b + 1) + c + 1) * C
                step = 16 * b + 2 * c
                piece = back_ref[row : row + C, plane_cols(x)]
                part += roll(piece, step) if step else piece
            if c:
                part = jnp.where(depth48 >= 2 if c == 1 else depth48 <= 5, part, 0.0)
            total += part
        grad1.append((total * slope1_ref[:, plane_cols(x)] * own_row).astype(jnp.bfloat16))

    shifted_ref[...] = jnp.zeros_like(shifted_ref)
    for a in range(3):
        for x in range(8):
            shifted_ref[C * a : C * (a + 1), plane_cols(x + a)] = grad1[x]
    first_part = matmul_lanes(
        shifted_ref[:, 0 : 10 * LANES], x9_ref[:, 4 * LANES : 14 * LANES]
    )

    first_core = (lax.axis_index("dp") & 1) == 0
    head_part = jnp.concatenate([head_part, jnp.zeros((24, 16), jnp.float32)], axis=0)
    nothing = jnp.zeros((72, 16), jnp.float32)
    ends = []
    for part, extra in ((first_part, nothing), (second_part, head_part)):
        tail = jnp.concatenate([part[0:72, 384:], part[72:144, 384:], extra, nothing], axis=1)
        ends.append(jnp.concatenate([tail, jnp.zeros((8, LANES), jnp.float32)], axis=0))
    pieces = [(first_part[:, plane_cols(q)], second_part[:, plane_cols(q)]) for q in range(3)]
    row = 0
    for first, second in pieces + [tuple(ends)]:
        rows = slice(row, row + first.shape[0])
        keep_ref[rows, :] = jnp.where(first_core, first, second)
        send_ref[rows, :] = jnp.where(first_core, second, first)
        row += first.shape[0]


def add_kernel(mine_ref, other_ref, out_ref):
    out_ref[...] = (mine_ref[...] + other_ref[...]).astype(jnp.bfloat16)


def sum_kernel(parts_ref, out_ref):
    total = parts_ref[0].astype(jnp.float32)
    for s in range(1, parts_ref.shape[0]):
        total += parts_ref[s].astype(jnp.float32)
    total = total.astype(jnp.bfloat16)
    for s in range(out_ref.shape[0]):
        out_ref[s] = total


def unpack_kernel(mine_ref, other_ref, logits_ref, first_ref, second_ref, head_ref, out_ref):
    out_ref[:, 0, :] = logits_ref[0:3, :]
    first_core = (lax.axis_index("dp") & 1) == 0
    mine, other = mine_ref[...], other_ref[...]
    for k, out in ((0, first_ref), (1, second_ref)):
        half = jnp.where(first_core, other if k else mine, mine if k else other)
        half = half.astype(jnp.float32)
        tail = jnp.concatenate([half[432:504, 0:C], half[432:504, C : 2 * C]], axis=0)
        tiles = [half[144 * q : 144 * (q + 1), :] for q in range(3)]
        whole = jnp.concatenate(tiles + [tail], axis=1)
        for a in range(3):
            for t in range(9):
                out[9 * a + t] = whole[C * a : C * (a + 1), C * t : C * (t + 1)]
        if k:
            head_ref[...] = half[432 : 432 + C, 96:112].T[0:3]


def on_device_flat(features, device_block, conv_first, conv_second, head_weight, targets):
    space_count = lax.axis_size("space")
    device_count = lax.axis_size("dp") * space_count
    bf16, f32 = jnp.bfloat16, jnp.float32
    small = pltpu.CompilerParams(vmem_limit_bytes=8 * 1024 * 1024)
    shape = jax.ShapeDtypeStruct
    vmem = pl.BlockSpec(memory_space=pltpu.VMEM)

    def swap(values, mask):
        return lax.ppermute(values, "space", [(s, s ^ mask) for s in range(space_count)])

    mate_targets, mate_features = swap(targets, 1), swap(features, 1)
    head, head_t = pl.pallas_call(
        head_kernel,
        out_shape=(shape((16, C), bf16), shape((C, 16), bf16)),
        in_specs=[vmem],
        out_specs=(vmem,) * 2,
        compiler_params=small,
        cost_estimate=pl.CostEstimate(flops=1_000_000, bytes_accessed=2_000_000, transcendentals=0),
        name="lay_out_head",
    )(head_weight)
    lane = pl.pallas_call(
        lanes_kernel,
        out_shape=shape((16, LANES), jnp.int32),
        out_specs=vmem,
        compiler_params=small,
        cost_estimate=pl.CostEstimate(flops=0, bytes_accessed=2_000_000, transcendentals=0),
        name="lane_indices",
    )()
    own, own_slabs = pl.pallas_call(
        pack_own_kernel,
        out_shape=(shape((13, 16, LANES), bf16), shape((3, 8, 16, LANES), bf16)),
        in_specs=[vmem] * 4,
        out_specs=(vmem,) * 2,
        scratch_shapes=[pltpu.VMEM((4, 8, 16, LANES), bf16)],
        compiler_params=small,
        cost_estimate=pl.CostEstimate(flops=1_000_000, bytes_accessed=2_000_000, transcendentals=0),
        name="pack_own",
    )(device_block, features[0, 0], targets[0].transpose(1, 0, 2), lane)
    mate_slab, *pairs = pl.pallas_call(
        pack_mate_kernel,
        out_shape=(
            shape((8, 16, LANES), bf16),
            *[shape((2, 8, 16, LANES), bf16) for _ in PARTNERS],
        ),
        in_specs=[vmem] * 4,
        out_specs=(vmem,) * 4,
        scratch_shapes=[pltpu.VMEM((4, 8, 16, LANES), bf16)],
        compiler_params=small,
        cost_estimate=pl.CostEstimate(flops=1_000_000, bytes_accessed=2_000_000, transcendentals=0),
        name="pack_mate",
    )(device_block, mate_features[0, 0], mate_targets[0].transpose(1, 0, 2), own_slabs)
    pairs = [swap(pair, mask) for pair, mask in zip(pairs, PARTNERS)]

    w1, owners, masks = pl.pallas_call(
        prepare_kernel,
        out_shape=(
            shape((3 * C, 9 * C), bf16),
            shape((1, LANES), jnp.int32),
            shape((8, LANES), f32),
        ),
        in_specs=[vmem] * 2,
        out_specs=(vmem,) * 3,
        scratch_shapes=[pltpu.SMEM((2, 16), jnp.int32)],
        compiler_params=small,
        cost_estimate=pl.CostEstimate(flops=2_000_000, bytes_accessed=4_000_000, transcendentals=0),
        name="prepare",
    )(device_block, conv_first.transpose(1, 0, 2))
    w2, w2t = pl.pallas_call(
        second_kernel,
        out_shape=(shape((3 * C, 9 * C), bf16), shape((9 * C, 3 * C), bf16)),
        in_specs=[vmem],
        out_specs=(vmem,) * 2,
        compiler_params=small,
        cost_estimate=pl.CostEstimate(flops=2_000_000, bytes_accessed=4_000_000, transcendentals=0),
        name="second_weights",
    )(conv_second.transpose(1, 0, 2))

    scale = (device_count * 3 * CELLS) ** (-0.5)
    logits, keep, send = pl.pallas_call(
        functools.partial(crop_kernel, scale),
        out_shape=(shape((8, CELLS), f32), shape((HALF, LANES), f32), shape((HALF, LANES), f32)),
        in_specs=[vmem] * 12,
        out_specs=(vmem,) * 3,
        scratch_shapes=[
            pltpu.VMEM((space_count, 8, 16, LANES), bf16),
            pltpu.VMEM((2, 12, 16, LANES), bf16),
            pltpu.VMEM((6, 3, 16, LANES), bf16),
            pltpu.VMEM((9 * C, 18 * LANES), bf16),
            pltpu.VMEM((9 * C, 16 * LANES), bf16),
            pltpu.VMEM((3 * C, 18 * LANES), f32),
            pltpu.VMEM((C, 8 * LANES), f32),
            pltpu.VMEM((C, 12 * LANES), f32),
            pltpu.VMEM((C, 12 * LANES), bf16),
            pltpu.VMEM((C, 12 * LANES), bf16),
            pltpu.VMEM((3 * C, 12 * LANES), bf16),
            pltpu.VMEM((9 * C, 8 * LANES), f32),
        ],
        compiler_params=pltpu.CompilerParams(vmem_limit_bytes=20 * 1024 * 1024),
        name="forward_backward",
    )(owners, masks, own, mate_slab, *pairs, w1, w2, w2t, head, head_t)

    dp_count = lax.axis_size("dp")

    def swap_cores(values):
        return lax.ppermute(values, "dp", [(d, d ^ 1) for d in range(dp_count)])

    peers = device_count // 2
    groups = [
        [d * space_count + s for d in range(core, dp_count, 2) for s in range(space_count)]
        for core in range(2)
    ]

    def exchange(values):
        return lax.all_to_all(
            values, ("dp", "space"), 0, 0, axis_index_groups=groups, tiled=True
        )

    def step(kernel, out, *operands):
        return pl.pallas_call(
            kernel,
            out_shape=out,
            in_specs=[vmem] * len(operands),
            out_specs=vmem,
            compiler_params=small,
            name="gradient_sum",
        )(*operands)

    term = step(add_kernel, shape((HALF, LANES), bf16), keep, swap_cores(send))
    pieces = shape((peers, HALF // peers, LANES), bf16)
    total = exchange(step(sum_kernel, pieces, exchange(term.reshape(pieces.shape))))
    total = total.reshape(HALF, LANES)
    grad_first, grad_second, grad_head, logits = pl.pallas_call(
        unpack_kernel,
        out_shape=(
            shape((27, C, C), f32),
            shape((27, C, C), f32),
            shape((3, C), f32),
            shape((3, 1, CELLS), f32),
        ),
        in_specs=[vmem] * 3,
        out_specs=(vmem,) * 4,
        compiler_params=small,
        name="unpack_gradients",
    )(total, swap_cores(total), logits)
    return (
        logits.transpose(1, 0, 2)[None],
        grad_first.transpose(1, 0, 2),
        grad_second.transpose(1, 0, 2),
        grad_head,
    )


def solution(mesh):
    in_specs = (
        P("dp", "space", None, None),
        P("dp", None),
        P(),
        P(),
        P(),
        P("dp", "space", None, None),
    )
    out_specs = (P("dp", "space", None, None), P(), P(), P())
    flat = mesh.shape["space"] == 8 and mesh.shape["dp"] in (2, 4)
    return jax.shard_map(
        on_device_flat if flat else on_device_deep,
        mesh=mesh,
        in_specs=in_specs,
        out_specs=out_specs,
        check_vma=False,
    )
```
